32 devices in a mesh: gx: 4 (over x, core), gy: 8 (over z, y).
Axes of the slice: x: 2, y: 2, z: 4, core: 2. Of those that a mesh axis runs over, the one named last changes fastest.
Arguments:
- damage: float32 [64, 64, 512], P('gx', 'gy'), may hold values from 0 to 0.9
- strain: float32 [3, 64, 64, 512], P(None, 'gx', 'gy'), may hold values from -3 to 3
- seed_damage: float32 [64, 64, 512], P('gx', 'gy'), may hold values from -6 to 6
- seed_disp: float32 [3, 64, 64, 512], P(None, 'gx', 'gy'), may hold values from -6 to 6
- brick_work: int32 [4, 8], P('gx', 'gy'), may hold values from 1 to 4, as said below
Outputs:
- adjoint_damage: float32 [64, 64, 512], P('gx', 'gy')
- adjoint_disp: float32 [3, 64, 64, 512], P(None, 'gx', 'gy')
The draws below stay inside these ranges and needn't reach their ends.
Inputs may be any that keep to these rules, and one draw needn't show every extreme that they name: brick_work is 1 on ordinary bricks and 2 to 4 on crack-band bricks. In every row of bricks (one gx index) the crack-band bricks form one run of 2 neighbouring bricks, all with gy index below 4. Some brick has weight 4.
All inputs are finite; a program needn't handle non-finite values.
Results may differ from the reference program's by a relative error of at most 0.0001.
Values sent between devices are 32-bit elements; how exact they have to be, the bound alone decides.
No kernel may reach another device: no remote copies, remote signals or barrier semaphores. Data moves between devices by JAX's collectives and lax.ppermute only.
A program may use at most 64 MiB of HBM per device.

```python
import jax
import jax.numpy as jnp
from jax import lax

CX = 16
CY = 8
SWEEPS = 3
WORK_MAX = 4
RELAX_INNER = 8
NX = 64
NY = 64
NZ = 512
BRICKS_X = 4
BRICKS_Y = 8


def draw_brick_work(key, part):
    start_key = jax.random.fold_in(key, 11)
    load_key = jax.random.fold_in(key, 23)
    band = BRICKS_Y // 4
    starts = jax.random.randint(start_key, (BRICKS_X,), 0, band + 1)
    columns = jnp.arange(BRICKS_Y)[None, :]
    inside = (columns >= starts[:, None]) & (columns < starts[:, None] + band)
    loads = jax.random.randint(load_key, (BRICKS_X, BRICKS_Y), 2, WORK_MAX + 1)
    first_row = jnp.arange(BRICKS_X)[:, None] == 0
    loads = jnp.where(first_row & (columns == starts[0]), WORK_MAX, loads)
    return jnp.where(inside, loads, 1).astype(jnp.int32)


def levels(key, shape, split, smallest, largest):
    factor_of = 1.0
    for position, blocks in split:
        steps = jax.random.uniform(jax.random.fold_in(jax.random.fold_in(key, 6), position), (blocks,), jnp.float32, smallest / len(split), largest / len(split))
        factor_of = factor_of * jnp.repeat(jnp.exp(steps), shape[position] // blocks).reshape((-1,) + (1,) * (len(shape) - 1 - position))
    return factor_of


def bell_draw(own_key, shape, scale, bound, cuts=(), held_as=jnp.bfloat16):
    drawn = jax.random.normal(own_key, shape, jnp.float32) * scale
    if len(cuts) > 0:
        drawn = levels(own_key, shape, cuts, -0.22, 0.18) * drawn
    return jnp.clip(drawn, min=-bound, max=bound).astype(held_as)


def setup_inputs(seed: int = 0) -> dict:
    seeds = jax.random.split(jax.random.key(seed), 6)
    return {
        "damage": jnp.clip(0.9 * jax.random.uniform(seeds[0], (NX, NY, NZ), jnp.float32) ** levels(seeds[0], (NX, NY, NZ), ((0, 4), (1, 8)), -0.2, 0.2), 0.0, 0.9),
        "strain": bell_draw(seeds[1], (3, NX, NY, NZ), 0.5, 3.0, ((1, 4), (2, 8)), jnp.float32),
        "seed_damage": bell_draw(seeds[2], (NX, NY, NZ), 1.0, 6.0, ((0, 4), (1, 8)), jnp.float32),
        "seed_disp": bell_draw(seeds[3], (3, NX, NY, NZ), 1.0, 6.0, ((1, 4), (2, 8)), jnp.float32),
        "brick_work": draw_brick_work(jax.random.fold_in(seeds[5], 71), 0),
    }


RESIDUAL_STIFFNESS = 0.001
TOUGH_OVER_LENGTH = 0.5
TOUGH_TIMES_LENGTH = 0.25
MASS_SHIFT = 0.5
STIFF_SCALE = 0.25
CENTER_VALUE = 1.0
HALF_WIDTH = 0.75
NORMAL_WEIGHT = 1.5
RELAX_STEP = 0.5
NORMAL_FLOOR = 0.05

def shifted(field):
    center = field[..., 1:-1, 1:-1, :]
    widths = [(0, 0)] * (center.ndim - 1) + [(1, 1)]
    padded = jnp.pad(center, widths)
    sides = [field[..., 2:, 1:-1, :], field[..., :-2, 1:-1, :], field[..., 1:-1, 2:, :], field[..., 1:-1, :-2, :], padded[..., 2:], padded[..., :-2]]
    return (center, sides)

def prepare(framed_damage, framed_strain):
    center, sides = shifted(framed_damage)
    soft_center = (1.0 - center) ** 2 + RESIDUAL_STIFFNESS
    faces = jnp.stack([0.5 * (soft_center + (1.0 - side) ** 2 + RESIDUAL_STIFFNESS) for side in sides])
    energy = 0.5 * lax.optimization_barrier(jnp.sum(framed_strain[:, 1:-1, 1:-1, :] ** 2, axis=0))
    coupling = 2.0 * (framed_damage - 1.0)[None] * framed_strain
    inverse_damage = 1.0 / (TOUGH_OVER_LENGTH + 2.0 * energy + 6.0 * TOUGH_TIMES_LENGTH)
    inverse_disp = 1.0 / (MASS_SHIFT + STIFF_SCALE * lax.optimization_barrier(jnp.sum(faces, axis=0)))
    inverse = jnp.stack([inverse_damage, inverse_disp, inverse_disp, inverse_disp])
    return (faces, energy, coupling, inverse)

def operate(faces, energy, coupling, state):
    mu_center, mu_sides = shifted(state[0])
    damage_part = (TOUGH_OVER_LENGTH + 2.0 * energy) * mu_center + TOUGH_TIMES_LENGTH * sum((mu_center - side for side in mu_sides))
    lam_center, lam_sides = shifted(state[1:])
    disp_part = MASS_SHIFT * lam_center + STIFF_SCALE * sum((faces[slot] * (lam_center - lam_sides[slot]) for slot in range(6)))
    weighted = coupling * state[0][None]
    along_x = 0.5 * (weighted[0, :-2, 1:-1, :] - weighted[0, 2:, 1:-1, :])
    along_y = 0.5 * (weighted[1, 1:-1, :-2, :] - weighted[1, 1:-1, 2:, :])
    padded = jnp.pad(weighted[2, 1:-1, 1:-1, :], ((0, 0), (0, 0), (1, 1)))
    along_z = 0.5 * (padded[..., :-2] - padded[..., 2:])
    transfer = jnp.stack([along_x, along_y, along_z])
    return jnp.concatenate([damage_part[None], disp_part + transfer], axis=0)

def chebyshev(faces, energy, coupling, inverse, source, widen, keep):
    ratio = CENTER_VALUE / HALF_WIDTH
    rho = 1.0 / ratio
    update = inverse * source / CENTER_VALUE
    state = keep(update)
    for sweep in range(SWEEPS):
        residual = source - operate(faces, energy, coupling, widen(state))
        rho_next = 1.0 / (2.0 * ratio - rho)
        update = rho_next * rho * update + 2.0 * rho_next / HALF_WIDTH * inverse * residual
        state = keep(state + update)
        rho = rho_next
    return state

def crack_normal(framed_damage):
    center, sides = shifted(framed_damage)
    grad = jnp.stack([0.5 * (sides[0] - sides[1]), 0.5 * (sides[2] - sides[3]), 0.5 * (sides[4] - sides[5])])
    length = jnp.sqrt(jnp.maximum(lax.optimization_barrier(jnp.sum(grad * grad, axis=0, keepdims=True)), NORMAL_FLOOR))
    return grad / length

def relax_once(target, normal, relaxed):
    along = lax.optimization_barrier(jnp.sum(normal * relaxed, axis=0, keepdims=True))
    return relaxed + RELAX_STEP / RELAX_INNER * (target - relaxed - NORMAL_WEIGHT * along * normal)

def widen_zero(state):
    return jnp.pad(state, ((0, 0), (1, 1), (1, 1), (0, 0)))

def unchanged(state):
    return state

def reference(damage, strain, seed_damage, seed_disp, brick_work):
    framed_damage = jnp.pad(damage, ((1, 1), (1, 1), (0, 0)))
    framed_strain = jnp.pad(strain, ((0, 0), (1, 1), (1, 1), (0, 0)))
    faces, energy, coupling, inverse = prepare(framed_damage, framed_strain)
    source = jnp.concatenate([seed_damage[None], seed_disp], axis=0)
    state = chebyshev(faces, energy, coupling, inverse, source, widen_zero, unchanged)
    normal = crack_normal(framed_damage)
    counts = jnp.repeat(jnp.repeat(brick_work * RELAX_INNER, CX, axis=0), CY, axis=1)[:, :, None]
    target = state[1:]

    def advance(level, relaxed):
        moved = relax_once(target, normal, relaxed)
        return jnp.where(level < counts, moved, relaxed)
    relaxed = lax.fori_loop(0, WORK_MAX * RELAX_INNER, advance, target)
    return (state[0], relaxed)
```

```python
import functools

import jax
import jax.numpy as jnp
from jax import lax
from jax.experimental import pallas as pl
from jax.experimental.pallas import tpu as pltpu
from jax.sharding import PartitionSpec as P

RELAX_INNER = 8
RESIDUAL_STIFFNESS = 0.001
CENTER_VALUE = 1.0
HALF_WIDTH = 0.75
NORMAL_WEIGHT = 1.5
RELAX_RATE = 0.5 / RELAX_INNER
NORMAL_FLOOR = 0.05
OUTSIDE = 1.0 + RESIDUAL_STIFFNESS
F32 = jnp.float32


def weights():
    ratio = CENTER_VALUE / HALF_WIDTH
    rho = 1.0 / ratio
    found = []
    for _ in range(3):
        rho_next = 1.0 / (2.0 * ratio - rho)
        found.append((rho_next * rho, 2.0 * rho_next / HALF_WIDTH))
        rho = rho_next
    return found


def soft_of(damage):
    return (1.0 - damage) ** 2 + RESIDUAL_STIFFNESS


def row_up(plane, beyond):
    rows = plane.shape[0]
    at = lax.broadcasted_iota(jnp.int32, plane.shape, 0)
    return jnp.where(at == rows - 1, beyond, pltpu.roll(plane, rows - 1, 0))


def row_down(plane, beyond):
    at = lax.broadcasted_iota(jnp.int32, plane.shape, 0)
    return jnp.where(at == 0, beyond, pltpu.roll(plane, 1, 0))


def lane_up(plane, beyond):
    cells = plane.shape[1]
    at = lax.broadcasted_iota(jnp.int32, plane.shape, 1)
    return jnp.where(at == cells - 1, beyond, pltpu.roll(plane, cells - 1, 1))


def lane_down(plane, beyond):
    at = lax.broadcasted_iota(jnp.int32, plane.shape, 1)
    return jnp.where(at == 0, beyond, pltpu.roll(plane, 1, 1))


def mu_inverse(ex, ey, ez):
    return 1.0 / (2.0 + (ex * ex + ey * ey + ez * ez))


def lam_inverse(center, total):
    return 1.0 / (0.5 + 0.125 * (6.0 * center + total))


def faces_x_kernel(damage, strain, seed_damage, seed_disp, low, high):
    nx = damage.shape[0]
    for out, first, second in ((low, 0, 1), (high, nx - 1, nx - 2)):
        out[0] = damage[first]
        out[1] = damage[second]
        out[2] = strain[0, first]
        out[3] = seed_damage[first] * mu_inverse(strain[0, first], strain[1, first], strain[2, first])
        for c in range(3):
            out[4 + c] = seed_disp[c, first]


def faces_y_kernel(damage, strain, seed_damage, seed_disp, from_low, from_high, low, high):
    nx, ny, _ = damage.shape
    for out, first, second in ((low, 0, 1), (high, ny - 1, ny - 2)):
        for i in range(nx):
            def put(slot, row):
                out[slot * nx + i : slot * nx + i + 1, :] = row
            here = slice(first, first + 1)
            put(0, damage[i, here, :])
            put(1, damage[i, second : second + 1, :])
            sx, sy, sz = (strain[c, i, here, :] for c in range(3))
            put(2, sy)
            put(3, seed_damage[i, here, :] * mu_inverse(sx, sy, sz))
            for c in range(3):
                put(4 + c, seed_disp[c, i, here, :])
        out[7 * nx : 7 * nx + 1, :] = from_low[0, here, :]
        out[7 * nx + 1 : 7 * nx + 2, :] = from_high[0, here, :]


def first_kernel(
    damage, strain, seed_damage, seed_disp, x_low, x_high, y_low, y_high,
    g, k, mu_scale, state0, state1, sx_low, sx_high, sy_low, sy_high,
    soft, y_soft, x_state, y_state,
):
    nx, ny, nz = damage.shape
    y_in = (y_low, y_high)
    x_in = (x_low, x_high)

    def fill(i, _):
        soft[i + 1] = soft_of(damage[i])
        return 0

    lax.fori_loop(0, nx, fill, 0)
    soft[0] = soft_of(x_low[0])
    soft[nx + 1] = soft_of(x_high[0])
    for s in range(2):
        y_soft[s, 1 : nx + 1, :] = soft_of(y_in[s][0:nx, :])
        y_soft[s, 0:1, :] = soft_of(y_in[s][7 * nx : 7 * nx + 1, :])
        y_soft[s, nx + 1 : nx + 2, :] = soft_of(y_in[s][7 * nx + 1 : 7 * nx + 2, :])

    for s in range(2):
        at = 0 if s == 0 else nx + 1
        inner = 1 if s == 0 else nx
        center = soft[at]
        total = soft[inner] + soft_of(x_in[s][1])
        total += row_up(center, y_soft[1, at : at + 1, :]) + row_down(center, y_soft[0, at : at + 1, :])
        total += lane_up(center, OUTSIDE) + lane_down(center, OUTSIDE)
        inverse = lam_inverse(center, total)
        x_state[s, 0] = x_in[s][3]
        for c in range(3):
            x_state[s, 1 + c] = inverse * x_in[s][4 + c]

        center = y_soft[s, 1 : nx + 1, :]
        edge = 0 if s == 0 else ny - 1
        total = soft[1 : nx + 1, edge, :] + soft_of(y_in[s][nx : 2 * nx, :])
        total += y_soft[s, 0:nx, :] + y_soft[s, 2 : nx + 2, :]
        total += lane_up(center, OUTSIDE) + lane_down(center, OUTSIDE)
        inverse = lam_inverse(center, total)
        y_state[s, 0:nx, :] = y_in[s][3 * nx : 4 * nx, :]
        for c in range(3):
            y_state[s, (1 + c) * nx : (2 + c) * nx, :] = inverse * y_in[s][(4 + c) * nx : (5 + c) * nx, :]

    lane = lax.broadcasted_iota(jnp.int32, (ny, nz), 1)

    def prepare(i, dx_up, dx_down, sx_up, sx_down):
        center = soft[i + 1]
        sides = [
            soft[i + 2],
            soft[i],
            row_up(center, y_soft[1, pl.ds(i + 1, 1), :]),
            row_down(center, y_soft[0, pl.ds(i + 1, 1), :]),
            lane_up(center, OUTSIDE),
            lane_down(center, OUTSIDE),
        ]
        inverse = lam_inverse(center, sum(sides))
        eighth = 0.125 * inverse
        for j in range(6):
            face = eighth * (center + sides[j])
            if j == 4:
                face = jnp.where(lane == nz - 1, 0.0, face)
            if j == 5:
                face = jnp.where(lane == 0, 0.0, face)
            g[j, i] = face
        k[0, i] = inverse * (dx_up - 1.0) * sx_up
        k[1, i] = inverse * (1.0 - dx_down) * sx_down
        own = damage[i] - 1.0
        low, high = pl.ds(i, 1), pl.ds(2 * nx + i, 1)
        wy = own * strain[1, i]
        k[2, i] = inverse * row_up(wy, (y_high[low, :] - 1.0) * y_high[high, :])
        k[3, i] = -inverse * row_down(wy, (y_low[low, :] - 1.0) * y_low[high, :])
        wz = own * strain[2, i]
        k[4, i] = inverse * lane_up(wz, 0.0)
        k[5, i] = -inverse * lane_down(wz, 0.0)
        mu_inv = mu_inverse(strain[0, i], strain[1, i], strain[2, i])
        mu_scale[i] = 0.25 * mu_inv
        state0[0, i] = mu_inv * seed_damage[i]
        for c in range(3):
            state0[1 + c, i] = inverse * seed_disp[c, i]

    def prepare_inner(i, _):
        prepare(i, damage[i + 1], damage[i - 1], strain[0, i + 1], strain[0, i - 1])
        return 0

    prepare(0, damage[1], x_low[0], strain[0, 1], x_low[2])
    lax.fori_loop(1, nx - 1, prepare_inner, 0)
    prepare(nx - 1, x_high[0], damage[nx - 2], x_high[2], strain[0, nx - 2])

    (c1, c2), _, _ = weights()

    def advance(i, f, own, moved):
        return (1.0 + c1) * own + c2 * moved

    sweep(
        state0, state1, g, k, mu_scale, x_state.at[0], x_state.at[1], y_state.at[0], y_state.at[1], advance
    )
    send_faces(state1, sx_low, sx_high, sy_low, sy_high)


def send_faces(state, sx_low, sx_high, sy_low, sy_high):
    nx, ny = state.shape[1:3]
    for f in range(4):
        sx_low[f] = state[f, 0]
        sx_high[f] = state[f, nx - 1]
        sy_low[f * nx : (f + 1) * nx, :] = state[f, :, 0, :]
        sy_high[f * nx : (f + 1) * nx, :] = state[f, :, ny - 1, :]


def sweep(state, out, g, k, mu_scale, x_low, x_high, y_low, y_high, advance):
    nx, ny, nz = mu_scale.shape
    lane = lax.broadcasted_iota(jnp.int32, (ny, nz), 1)

    def plane(i, up, down):
        def around(f):
            own = state[f, i]
            row = pl.ds(f * nx + i, 1)
            return own, [
                up(f),
                down(f),
                row_up(own, y_high[row, :]),
                row_down(own, y_low[row, :]),
                pltpu.roll(own, nz - 1, 1),
                pltpu.roll(own, 1, 1),
            ]

        mu, mu_sides = around(0)
        ends = [
            jnp.where(lane == nz - 1, 0.0, mu_sides[4]),
            jnp.where(lane == 0, 0.0, mu_sides[5]),
        ]
        out[0, i] = advance(i, 0, mu, mu_scale[i] * sum(mu_sides[:4] + ends))
        faces = [g[j, i] for j in range(6)]
        for c in range(3):
            lam, lam_sides = around(1 + c)
            moved = sum(faces[j] * lam_sides[j] for j in range(6))
            moved += k[2 * c, i] * mu_sides[2 * c] + k[2 * c + 1, i] * mu_sides[2 * c + 1]
            out[1 + c, i] = advance(i, 1 + c, lam, moved)

    def inner(i, _):
        plane(i, lambda f: state[f, i + 1], lambda f: state[f, i - 1])
        return 0

    plane(0, lambda f: state[f, 1], lambda f: x_low[f])
    lax.fori_loop(1, nx - 1, inner, 0)
    plane(nx - 1, lambda f: x_high[f], lambda f: state[f, nx - 2])


def second_kernel(
    g, k, mu_scale, state0, state1, x_low, x_high, y_low, y_high,
    state2, sx_low, sx_high, sy_low, sy_high,
):
    _, (c1, c2), _ = weights()

    def advance(i, f, own, moved):
        return own + (c1 - c2) * (own - state0[f, i]) + c2 * moved

    sweep(state1, state2, g, k, mu_scale, x_low, x_high, y_low, y_high, advance)
    send_faces(state2, sx_low, sx_high, sy_low, sy_high)


def third_kernel(
    work, damage, dx_low, dx_high, dy_low, dy_high,
    g, k, mu_scale, state0, state1, state2, x_low, x_high, y_low, y_high,
    out_mu, out_lam, state3,
):
    nx, ny, nz = damage.shape
    _, _, (c1, c2) = weights()

    def advance(i, f, own, moved):
        return own + c1 * (own - state1[f, i]) + c2 * (state0[f, i] - own + moved)

    sweep(state2, state3, g, k, mu_scale, x_low, x_high, y_low, y_high, advance)

    count = work[0, 0]

    def finish(i, dx_up, dx_down):
        out_mu[i] = state3[0, i]
        own = damage[i]
        grad = [
            0.5 * (dx_up - dx_down),
            0.5 * (row_up(own, dy_high[pl.ds(i, 1), :]) - row_down(own, dy_low[pl.ds(i, 1), :])),
            0.5 * (lane_up(own, 0.0) - lane_down(own, 0.0)),
        ]
        square = sum(part * part for part in grad)
        scale = 1.0 / jnp.maximum(square, NORMAL_FLOOR)
        stretch = 1.0 + NORMAL_WEIGHT * square * scale
        power = 1.0 - RELAX_RATE * stretch
        for _ in range(3):
            power = power * power
        left = jnp.where((count & 1) > 0, power, 1.0)
        power = power * power
        left = left * jnp.where((count & 2) > 0, power, 1.0)
        power = power * power
        left = left * jnp.where((count & 4) > 0, power, 1.0)
        along = sum(grad[c] * state3[1 + c, i] for c in range(3))
        along = along * (NORMAL_WEIGHT * scale) * (1.0 - left) / stretch
        for c in range(3):
            out_lam[c, i] = state3[1 + c, i] - along * grad[c]

    def inner(i, _):
        finish(i, damage[i + 1], damage[i - 1])
        return 0

    finish(0, damage[1], dx_low[0])
    lax.fori_loop(1, nx - 1, inner, 0)
    finish(nx - 1, dx_high[0], damage[nx - 2])


def call(kernel, ins, outs, scratch=(), smem_first=False):
    in_specs = [pl.BlockSpec(memory_space=pltpu.VMEM)] * len(ins)
    if smem_first:
        in_specs[0] = pl.BlockSpec(memory_space=pltpu.SMEM)
    return pl.pallas_call(
        kernel,
        out_shape=[jax.ShapeDtypeStruct(shape, F32) for shape in outs],
        in_specs=in_specs,
        out_specs=[pl.BlockSpec(memory_space=pltpu.VMEM)] * len(outs),
        scratch_shapes=[pltpu.VMEM(shape, F32) for shape in scratch],
        compiler_params=pltpu.CompilerParams(vmem_limit_bytes=24 * 1024 * 1024),
    )(*ins)


def swap(low, high, axis):
    count = lax.axis_size(axis)
    up = [(i, i + 1) for i in range(count - 1)]
    down = [(i + 1, i) for i in range(count - 1)]
    return lax.ppermute(high, axis, up), lax.ppermute(low, axis, down)


def body(damage, strain, seed_damage, seed_disp, brick_work):
    nx, ny, nz = damage.shape
    brick = (nx, ny, nz)
    fields = (damage, strain, seed_damage, seed_disp)
    x_face, y_face = (7, ny, nz), (7 * nx + 8, nz)
    x_pair = call(faces_x_kernel, fields, [x_face, x_face])
    x_in = swap(*x_pair, "gx")
    y_pair = call(faces_y_kernel, fields + x_in, [y_face, y_face])
    y_in = swap(*y_pair, "gy")

    state = (4,) + brick
    sent = [(4, ny, nz), (4, ny, nz), (4 * nx, nz), (4 * nx, nz)]
    g, k, mu_scale, state0, state1, *faces = call(
        first_kernel,
        fields + x_in + y_in,
        [(6,) + brick, (6,) + brick, brick, state, state] + sent,
        [(nx + 2, ny, nz), (2, nx + 2, nz), (2, 4, ny, nz), (2, 4 * nx, nz)],
    )
    halo = swap(*faces[2:], "gy")
    halo = swap(*faces[:2], "gx") + halo
    state2, *faces = call(
        second_kernel, (g, k, mu_scale, state0, state1) + halo, [state] + sent
    )
    halo = swap(*faces[2:], "gy")
    halo = swap(*faces[:2], "gx") + halo
    return tuple(
        call(
            third_kernel,
            (brick_work, damage) + x_in + y_in + (g, k, mu_scale, state0, state1, state2) + halo,
            [brick, (3,) + brick],
            [state],
            smem_first=True,
        )
    )


def solution(mesh):
    placed = (
        P("gx", "gy", None),
        P(None, "gx", "gy", None),
        P("gx", "gy", None),
        P(None, "gx", "gy", None),
        P("gx", "gy"),
    )
    return jax.shard_map(
        body,
        mesh=mesh,
        in_specs=placed,
        out_specs=(P("gx", "gy", None), P(None, "gx", "gy", None)),
        check_vma=False,
    )
```

```python
import functools

import jax
import jax.numpy as jnp
from jax import lax
from jax.experimental import pallas as pl
from jax.experimental.pallas import tpu as pltpu
from jax.sharding import PartitionSpec as P

RELAX_INNER = 8
RESIDUAL_STIFFNESS = 0.001
CENTER_VALUE = 1.0
HALF_WIDTH = 0.75
NORMAL_WEIGHT = 1.5
RELAX_RATE = 0.5 / RELAX_INNER
NORMAL_FLOOR = 0.05
OUTSIDE = 1.0 + RESIDUAL_STIFFNESS
F32 = jnp.float32


def weights():
    ratio = CENTER_VALUE / HALF_WIDTH
    rho = 1.0 / ratio
    found = []
    for _ in range(3):
        rho_next = 1.0 / (2.0 * ratio - rho)
        found.append((rho_next * rho, 2.0 * rho_next / HALF_WIDTH))
        rho = rho_next
    return found


def soft_of(damage):
    return (1.0 - damage) ** 2 + RESIDUAL_STIFFNESS


def row_up(plane, beyond):
    rows = plane.shape[0]
    at = lax.broadcasted_iota(jnp.int32, plane.shape, 0)
    return jnp.where(at == rows - 1, beyond, pltpu.roll(plane, rows - 1, 0))


def row_down(plane, beyond):
    at = lax.broadcasted_iota(jnp.int32, plane.shape, 0)
    return jnp.where(at == 0, beyond, pltpu.roll(plane, 1, 0))


def lane_up(plane, beyond):
    cells = plane.shape[1]
    at = lax.broadcasted_iota(jnp.int32, plane.shape, 1)
    return jnp.where(at == cells - 1, beyond, pltpu.roll(plane, cells - 1, 1))


def lane_down(plane, beyond):
    at = lax.broadcasted_iota(jnp.int32, plane.shape, 1)
    return jnp.where(at == 0, beyond, pltpu.roll(plane, 1, 1))


def mu_inverse(ex, ey, ez):
    return 1.0 / (2.0 + (ex * ex + ey * ey + ez * ez))


def lam_inverse(center, total):
    return 1.0 / (0.5 + 0.125 * (6.0 * center + total))


def faces_x_kernel(damage, strain, seed_damage, seed_disp, low, high, ends, pulls, seed_ends, source_ends, sems):
    nx = damage.shape[0]
    copies = []
    for s, first in enumerate((0, nx - 2)):
        copies.append(pltpu.make_async_copy(damage.at[pl.ds(first, 2)], ends.at[s], sems.at[4 * s]))
    for s, edge in enumerate((0, nx - 1)):
        copies.append(pltpu.make_async_copy(strain.at[:, edge], pulls.at[s], sems.at[4 * s + 1]))
        copies.append(pltpu.make_async_copy(seed_damage.at[edge], seed_ends.at[s], sems.at[4 * s + 2]))
        copies.append(pltpu.make_async_copy(seed_disp.at[:, edge], source_ends.at[s], sems.at[4 * s + 3]))
    for copy in copies:
        copy.start()
    for copy in copies:
        copy.wait()
    for s, out in enumerate((low, high)):
        out[0] = ends[s, s]
        out[1] = ends[s, 1 - s]
        out[2] = pulls[s, 0]
        out[3] = seed_ends[s] * mu_inverse(pulls[s, 0], pulls[s, 1], pulls[s, 2])
        for c in range(3):
            out[4 + c] = source_ends[s, c]


def faces_y_kernel(damage, strain, seed_damage, seed_disp, from_low, from_high, low, high):
    nx, ny, _ = damage.shape
    for out, first, second in ((low, 0, 1), (high, ny - 1, ny - 2)):
        here = slice(first, first + 1)

        def rows(i, _):
            def put(slot, row):
                out[pl.ds(slot * nx + i, 1), :] = row

            put(0, damage[i, here, :])
            put(1, damage[i, second : second + 1, :])
            sx, sy, sz = (strain[c, i, here, :] for c in range(3))
            put(2, sy)
            put(3, seed_damage[i, here, :] * mu_inverse(sx, sy, sz))
            for c in range(3):
                put(4 + c, seed_disp[c, i, here, :])
            return 0

        lax.fori_loop(0, nx, rows, 0)
        out[7 * nx : 7 * nx + 1, :] = from_low[0, here, :]
        out[7 * nx + 1 : 7 * nx + 2, :] = from_high[0, here, :]


def first_kernel(
    damage, strain, seed_damage, seed_disp, x_low, x_high, y_low, y_high,
    g, k, mu_scale, state0, state1, sx, sy_low, sy_high,
    soft, pull_x, y_soft, y_state,
):
    nx, ny, nz = damage.shape
    y_in = (y_low, y_high)
    x_in = (x_low, x_high)

    def fill(i, _):
        soft[i + 1] = soft_of(damage[i])
        pull_x[i + 1] = (damage[i] - 1.0) * strain[0, i]
        return 0

    lax.fori_loop(0, nx, fill, 0)
    for s in range(2):
        at = 0 if s == 0 else nx + 1
        soft[at] = soft_of(x_in[s][0])
        pull_x[at] = (x_in[s][0] - 1.0) * x_in[s][2]
        y_soft[s, 1 : nx + 1, :] = soft_of(y_in[s][0:nx, :])
        y_soft[s, 0:1, :] = soft_of(y_in[s][7 * nx : 7 * nx + 1, :])
        y_soft[s, nx + 1 : nx + 2, :] = soft_of(y_in[s][7 * nx + 1 : 7 * nx + 2, :])

    for s in range(2):
        at = 0 if s == 0 else nx + 1
        inner = 1 if s == 0 else nx
        center = soft[at]
        total = soft[inner] + soft_of(x_in[s][1])
        total += row_up(center, y_soft[1, at : at + 1, :]) + row_down(center, y_soft[0, at : at + 1, :])
        total += lane_up(center, OUTSIDE) + lane_down(center, OUTSIDE)
        inverse = lam_inverse(center, total)
        state0[0, at] = x_in[s][3]
        for c in range(3):
            state0[1 + c, at] = inverse * x_in[s][4 + c]

        center = y_soft[s, 1 : nx + 1, :]
        edge = 0 if s == 0 else ny - 1
        total = soft[1 : nx + 1, edge, :] + soft_of(y_in[s][nx : 2 * nx, :])
        total += y_soft[s, 0:nx, :] + y_soft[s, 2 : nx + 2, :]
        total += lane_up(center, OUTSIDE) + lane_down(center, OUTSIDE)
        inverse = lam_inverse(center, total)
        y_state[s, 0:nx, :] = y_in[s][3 * nx : 4 * nx, :]
        for c in range(3):
            y_state[s, (1 + c) * nx : (2 + c) * nx, :] = inverse * y_in[s][(4 + c) * nx : (5 + c) * nx, :]

    lane = lax.broadcasted_iota(jnp.int32, (ny, nz), 1)

    def prepare(i, _):
        center = soft[i + 1]
        sides = [
            soft[i + 2],
            soft[i],
            row_up(center, y_soft[1, pl.ds(i + 1, 1), :]),
            row_down(center, y_soft[0, pl.ds(i + 1, 1), :]),
            lane_up(center, OUTSIDE),
            lane_down(center, OUTSIDE),
        ]
        inverse = lam_inverse(center, sum(sides))
        eighth = 0.125 * inverse
        for j in range(6):
            face = eighth * (center + sides[j])
            if j == 4:
                face = jnp.where(lane == nz - 1, 0.0, face)
            if j == 5:
                face = jnp.where(lane == 0, 0.0, face)
            g[j, i] = face
        k[0, i] = inverse * pull_x[i + 2]
        k[1, i] = -inverse * pull_x[i]
        own = damage[i] - 1.0
        low, high = pl.ds(i, 1), pl.ds(2 * nx + i, 1)
        wy = own * strain[1, i]
        k[2, i] = inverse * row_up(wy, (y_high[low, :] - 1.0) * y_high[high, :])
        k[3, i] = -inverse * row_down(wy, (y_low[low, :] - 1.0) * y_low[high, :])
        wz = own * strain[2, i]
        k[4, i] = inverse * lane_up(wz, 0.0)
        k[5, i] = -inverse * lane_down(wz, 0.0)
        mu_inv = mu_inverse(strain[0, i], strain[1, i], strain[2, i])
        mu_scale[i] = 0.25 * mu_inv
        state0[0, i + 1] = mu_inv * seed_damage[i]
        for c in range(3):
            state0[1 + c, i + 1] = inverse * seed_disp[c, i]
        return 0

    lax.fori_loop(0, nx, prepare, 0)
    (c1, c2), _, _ = weights()

    def advance(i, f, own, moved):
        state1[f, i + 1] = (1.0 + c1) * own + c2 * moved

    sweep(state0, g, k, mu_scale, y_state.at[0], y_state.at[1], advance)
    send_faces(state1, sx, sy_low, sy_high)


def send_faces(state, sx, sy_low, sy_high):
    nx, ny = state.shape[1] - 2, state.shape[2]
    for f in range(4):
        sx[f] = state[f, 1]
        sx[4 + f] = state[f, nx]
        sy_low[f * nx : (f + 1) * nx, :] = state[f, 1 : nx + 1, 0, :]
        sy_high[f * nx : (f + 1) * nx, :] = state[f, 1 : nx + 1, ny - 1, :]


def take_faces(state, x_all):
    nx = state.shape[1] - 2
    bricks = x_all.shape[0]
    here = lax.axis_index("gx")
    low = jnp.maximum(here - 1, 0)
    high = jnp.minimum(here + 1, bricks - 1)
    for f in range(4):
        state[f, 0] = jnp.where(here > 0, x_all[low, 4 + f], 0.0)
        state[f, nx + 1] = jnp.where(here < bricks - 1, x_all[high, f], 0.0)


def sweep(state, g, k, mu_scale, y_low, y_high, advance, finish=None):
    nx, ny, nz = mu_scale.shape
    lane = lax.broadcasted_iota(jnp.int32, (ny, nz), 1)

    def plane(i, _):
        def around(f):
            own = state[f, i + 1]
            row = pl.ds(f * nx + i, 1)
            return own, [
                state[f, i + 2],
                state[f, i],
                row_up(own, y_high[row, :]),
                row_down(own, y_low[row, :]),
                pltpu.roll(own, nz - 1, 1),
                pltpu.roll(own, 1, 1),
            ]

        mu, mu_sides = around(0)
        ends = [
            jnp.where(lane == nz - 1, 0.0, mu_sides[4]),
            jnp.where(lane == 0, 0.0, mu_sides[5]),
        ]
        results = [advance(i, 0, mu, mu_scale[i] * sum(mu_sides[:4] + ends))]
        faces = [g[j, i] for j in range(6)]
        for c in range(3):
            lam, lam_sides = around(1 + c)
            moved = sum(faces[j] * lam_sides[j] for j in range(6))
            moved += k[2 * c, i] * mu_sides[2 * c] + k[2 * c + 1, i] * mu_sides[2 * c + 1]
            results.append(advance(i, 1 + c, lam, moved))
        if finish is not None:
            finish(i, results)
        return 0

    lax.fori_loop(0, nx, plane, 0)


def second_kernel(
    g, k, mu_scale, state0, state1, x_all, y_low, y_high,
    whole1, state2, sx, sy_low, sy_high,
):
    _, (c1, c2), _ = weights()
    take_faces(whole1, x_all)

    def advance(i, f, own, moved):
        state2[f, i + 1] = own + (c1 - c2) * (own - state0[f, i + 1]) + c2 * moved

    sweep(whole1, g, k, mu_scale, y_low, y_high, advance)
    send_faces(state2, sx, sy_low, sy_high)


def third_kernel(
    work, damage, dx_low, dx_high, dy_low, dy_high,
    g, k, mu_scale, state0, state1, state2, x_all, y_low, y_high,
    out_mu, out_lam, whole2,
    framed, mu_tile, lam_tile, sems,
):
    nx, ny, nz = damage.shape
    _, _, (c1, c2) = weights()
    take_faces(whole2, x_all)
    framed[0] = dx_low[0]
    framed[nx + 1] = dx_high[0]

    def fill(i, _):
        framed[i + 1] = damage[i]
        return 0

    lax.fori_loop(0, nx, fill, 0)
    count = work[0, 0]

    def copies(i):
        return (
            pltpu.make_async_copy(mu_tile.at[i], out_mu.at[i], sems.at[0, i]),
            pltpu.make_async_copy(lam_tile.at[:, i], out_lam.at[:, i], sems.at[1, i]),
        )

    def advance(i, f, own, moved):
        return own + c1 * (own - state1[f, i + 1]) + c2 * (state0[f, i + 1] - own + moved)

    def finish(i, results):
        mu_tile[i] = results[0]
        own = framed[i + 1]
        grad = [
            0.5 * (framed[i + 2] - framed[i]),
            0.5 * (row_up(own, dy_high[pl.ds(i, 1), :]) - row_down(own, dy_low[pl.ds(i, 1), :])),
            0.5 * (lane_up(own, 0.0) - lane_down(own, 0.0)),
        ]
        square = sum(part * part for part in grad)
        scale = 1.0 / jnp.maximum(square, NORMAL_FLOOR)
        power = 1.0 - RELAX_RATE * (1.0 + NORMAL_WEIGHT * square * scale)
        series = 1.0 + power
        for _ in range(2):
            power = power * power
            series = series * (1.0 + power)
        power = power * power
        repeats = jnp.ones_like(power)
        for level in range(1, 4):
            repeats = jnp.where(count > level, 1.0 + power * repeats, repeats)
        along = sum(grad[c] * results[1 + c] for c in range(3))
        along = along * (RELAX_RATE * NORMAL_WEIGHT * scale) * (series * repeats)
        for c in range(3):
            lam_tile[c, i] = results[1 + c] - along * grad[c]
        for copy in copies(i):
            copy.start()

    sweep(whole2, g, k, mu_scale, y_low, y_high, advance, finish)

    def settle(i, _):
        for copy in copies(i):
            copy.wait()
        return 0

    lax.fori_loop(0, nx, settle, 0)


VMEM = pl.BlockSpec(memory_space=pltpu.VMEM)
SMEM = pl.BlockSpec(memory_space=pltpu.SMEM)
ANY = pl.BlockSpec(memory_space=pl.ANY)
MIB = 1024 * 1024


def call(kernel, ins, outs, scratch=(), in_specs=None, out_specs=None, grant=24 * MIB, aliases=None):
    return pl.pallas_call(
        kernel,
        out_shape=[jax.ShapeDtypeStruct(shape, F32) for shape in outs],
        in_specs=in_specs or [VMEM] * len(ins),
        out_specs=out_specs or [VMEM] * len(outs),
        scratch_shapes=[pltpu.VMEM(shape, F32) if isinstance(shape, tuple) else shape for shape in scratch],
        input_output_aliases=aliases or {},
        compiler_params=pltpu.CompilerParams(vmem_limit_bytes=grant),
    )(*ins)


def swap(low, high, axis):
    count = lax.axis_size(axis)
    up = [(i, i + 1) for i in range(count - 1)]
    down = [(i + 1, i) for i in range(count - 1)]
    return lax.ppermute(high, axis, up), lax.ppermute(low, axis, down)


def body(damage, strain, seed_damage, seed_disp, brick_work):
    nx, ny, nz = damage.shape
    brick = (nx, ny, nz)
    fields = (damage, strain, seed_damage, seed_disp)
    x_face, y_face = (7, ny, nz), (7 * nx + 8, nz)
    plane = (ny, nz)
    x_pair = call(
        faces_x_kernel, fields, [x_face, x_face],
        [(2, 2) + plane, (2, 3) + plane, (2,) + plane, (2, 3) + plane, pltpu.SemaphoreType.DMA((8,))],
        in_specs=[ANY] * 4, grant=56 * MIB,
    )
    x_in = swap(*x_pair, "gx")
    y_pair = call(faces_y_kernel, fields + x_in, [y_face, y_face])
    y_in = swap(*y_pair, "gy")

    state = (4, nx + 2) + plane
    sent = [(8,) + plane, (4 * nx, nz), (4 * nx, nz)]
    g, k, mu_scale, state0, state1, sx, *sy = call(
        first_kernel,
        fields + x_in + y_in,
        [(6,) + brick, (6,) + brick, brick, state, state] + sent,
        [(nx + 2,) + plane, (nx + 2,) + plane, (2, nx + 2, nz), (2, 4 * nx, nz)],
    )
    halo = (lax.all_gather(sx, "gx"),) + swap(*sy, "gy")
    state1, state2, sx, *sy = call(
        second_kernel, (g, k, mu_scale, state0, state1) + halo, [state, state] + sent, aliases={4: 0}
    )
    halo = (lax.all_gather(sx, "gx"),) + swap(*sy, "gy")
    ins = (brick_work, damage) + x_in + y_in + (g, k, mu_scale, state0, state1, state2) + halo
    out_mu, out_lam, _ = call(
        third_kernel, ins, [brick, (3,) + brick, state],
        [(nx + 2,) + plane, brick, (3,) + brick, pltpu.SemaphoreType.DMA((2, nx))],
        in_specs=[SMEM] + [VMEM] * (len(ins) - 1), out_specs=[ANY, ANY, VMEM], aliases={11: 2},
    )
    return out_mu, out_lam


def solution(mesh):
    placed = (
        P("gx", "gy", None),
        P(None, "gx", "gy", None),
        P("gx", "gy", None),
        P(None, "gx", "gy", None),
        P("gx", "gy"),
    )
    return jax.shard_map(
        body,
        mesh=mesh,
        in_specs=placed,
        out_specs=(P("gx", "gy", None), P(None, "gx", "gy", None)),
        check_vma=False,
    )
```

```python
import functools

import jax
import jax.numpy as jnp
from jax import lax
from jax.experimental import pallas as pl
from jax.experimental.pallas import tpu as pltpu
from jax.sharding import PartitionSpec as P

RELAX_INNER = 8
RESIDUAL_STIFFNESS = 0.001
CENTER_VALUE = 1.0
HALF_WIDTH = 0.75
NORMAL_WEIGHT = 1.5
RELAX_RATE = 0.5 / RELAX_INNER
NORMAL_FLOOR = 0.05
OUTSIDE = 1.0 + RESIDUAL_STIFFNESS
F32 = jnp.float32


def weights():
    ratio = CENTER_VALUE / HALF_WIDTH
    rho = 1.0 / ratio
    found = []
    for _ in range(3):
        rho_next = 1.0 / (2.0 * ratio - rho)
        found.append((rho_next * rho, 2.0 * rho_next / HALF_WIDTH))
        rho = rho_next
    return found


def soft_of(damage):
    return (1.0 - damage) ** 2 + RESIDUAL_STIFFNESS


def row_up(plane, beyond):
    rows = plane.shape[0]
    at = lax.broadcasted_iota(jnp.int32, plane.shape, 0)
    return jnp.where(at == rows - 1, beyond, pltpu.roll(plane, rows - 1, 0))


def row_down(plane, beyond):
    at = lax.broadcasted_iota(jnp.int32, plane.shape, 0)
    return jnp.where(at == 0, beyond, pltpu.roll(plane, 1, 0))


def lane_up(plane, beyond):
    cells = plane.shape[1]
    at = lax.broadcasted_iota(jnp.int32, plane.shape, 1)
    return jnp.where(at == cells - 1, beyond, pltpu.roll(plane, cells - 1, 1))


def lane_down(plane, beyond):
    at = lax.broadcasted_iota(jnp.int32, plane.shape, 1)
    return jnp.where(at == 0, beyond, pltpu.roll(plane, 1, 1))


def mu_inverse(ex, ey, ez):
    return 1.0 / (2.0 + (ex * ex + ey * ey + ez * ez))


def lam_inverse(center, total):
    return 1.0 / (0.5 + 0.125 * (6.0 * center + total))


HALO = 4
X_DAMAGE, X_PULL, X_PULL_Y, X_PULL_Z, X_MU, X_SOURCE, X_SLOTS = 0, 4, 7, 9, 11, 14, 23
Y_FIELDS = 7
CORNER_ROWS = 32


def faces_x_kernel(damage, strain, seed_damage, seed_disp, low, high, pulls, seeds, sems):
    nx = damage.shape[0]
    copies = []
    for s, out in enumerate((low, high)):

        def planes(count):
            return pl.ds(0 if s == 0 else nx - count, count)

        moves = [
            (damage.at[planes(4)], out.at[pl.ds(X_DAMAGE, 4)]),
            (strain.at[0, planes(3)], out.at[pl.ds(X_PULL, 3)]),
            (strain.at[1, planes(2)], out.at[pl.ds(X_PULL_Y, 2)]),
            (strain.at[2, planes(2)], out.at[pl.ds(X_PULL_Z, 2)]),
            (strain.at[:, planes(3)], pulls.at[s]),
            (seed_damage.at[planes(3)], seeds.at[s]),
        ]
        for c in range(3):
            moves.append((seed_disp.at[c, planes(3)], out.at[pl.ds(X_SOURCE + 3 * c, 3)]))
        for slot, (source, target) in enumerate(moves):
            copies.append(pltpu.make_async_copy(source, target, sems.at[9 * s + slot]))
    for copy in copies:
        copy.start()
    for copy in copies:
        copy.wait()
    for s, out in enumerate((low, high)):
        out[X_MU : X_MU + 3] = seeds[s] * mu_inverse(pulls[s, 0], pulls[s, 1], pulls[s, 2])


def faces_y_kernel(damage, strain, seed_damage, seed_disp, low, high):
    nx, ny, _ = damage.shape
    for out, first, second in ((low, 0, 1), (high, ny - 1, ny - 2)):
        here = slice(first, first + 1)

        def rows(i, _):
            def put(slot, row):
                out[pl.ds(slot * nx + i, 1), :] = row

            put(0, damage[i, here, :])
            put(1, damage[i, second : second + 1, :])
            sx, sy, sz = (strain[c, i, here, :] for c in range(3))
            put(2, sy)
            put(3, seed_damage[i, here, :] * mu_inverse(sx, sy, sz))
            for c in range(3):
                put(4 + c, seed_disp[c, i, here, :])
            return 0

        lax.fori_loop(0, nx, rows, 0)


def corners_kernel(x_low, x_high, low, high):
    ny = x_low.shape[1]
    for out, first, second in ((low, 0, 1), (high, ny - 1, ny - 2)):
        for s, x_in in enumerate((x_low, x_high)):
            start = 1 - s
            out[3 * s : 3 * s + 3, :] = x_in[X_DAMAGE + start : X_DAMAGE + start + 3, first, :]
            out[6 + 2 * s : 8 + 2 * s, :] = x_in[X_DAMAGE + 2 * start : X_DAMAGE + 2 * start + 2, second, :]
            out[10 + 2 * s : 12 + 2 * s, :] = x_in[X_PULL_Y : X_PULL_Y + 2, first, :]
            out[14 + 2 * s : 16 + 2 * s, :] = x_in[X_MU + start : X_MU + start + 2, first, :]
            for c in range(3):
                slot = X_SOURCE + 3 * c + start
                row = 18 + 4 * c + 2 * s
                out[row : row + 2, :] = x_in[slot : slot + 2, first, :]
        out[30:32, :] = jnp.zeros((2, out.shape[1]), F32)


def gather_kernel(
    damage, strain, seed_damage, seed_disp, x_low, x_high, soft, pull, mu_scale, raw
):
    nx = damage.shape[0]

    def fill(i, _):
        at = HALO + i
        own = damage[i]
        sx, sy, sz = strain[0, i], strain[1, i], strain[2, i]
        soft[at] = soft_of(own)
        own = own - 1.0
        pull[0, at] = own * sx
        pull[1, at] = own * sy
        pull[2, at] = own * sz
        mu_inv = mu_inverse(sx, sy, sz)
        mu_scale[at] = 0.25 * mu_inv
        raw[0, at] = mu_inv * seed_damage[i]
        for c in range(3):
            raw[1 + c, at] = seed_disp[c, i]
        return 0

    lax.fori_loop(0, nx, fill, 0)
    here = lax.axis_index("gx")
    inside = (here > 0, here < lax.axis_size("gx") - 1)
    for s, x_in in enumerate((x_low, x_high)):

        def planes(count):
            first = HALO - count if s == 0 else HALO + nx
            return slice(first, first + count)

        def nearest(slot, held, count):
            first = slot + (held - count if s == 0 else 0)
            return x_in[first : first + count]

        soft[planes(4)] = soft_of(nearest(X_DAMAGE, 4, 4))
        pull[0, planes(3)] = (nearest(X_DAMAGE, 4, 3) - 1.0) * nearest(X_PULL, 3, 3)
        own = nearest(X_DAMAGE, 4, 2) - 1.0
        sx, sy, sz = nearest(X_PULL, 3, 2), nearest(X_PULL_Y, 2, 2), nearest(X_PULL_Z, 2, 2)
        pull[1, planes(2)] = own * sy
        pull[2, planes(2)] = own * sz
        mu_scale[planes(2)] = jnp.where(inside[s], 0.25 * mu_inverse(sx, sy, sz), 0.0)
        raw[0, planes(3)] = nearest(X_MU, 3, 3)
        for c in range(3):
            raw[1 + c, planes(3)] = nearest(X_SOURCE + 3 * c, 3, 3)


def first_kernel(
    soft, pull, mu_scale, raw, y_low, y_high, c_low, c_high,
    g, k, state0, state1, sy_low, sy_high,
    y_soft, y_pull, y_state,
):
    planes, ny, nz = soft.shape
    nx = planes - 2 * HALO
    inner = slice(HALO, HALO + nx)

    for s, (y_in, c_in) in enumerate(((y_low, c_low), (y_high, c_high))):
        def field(slot):
            return y_in[slot * nx : (slot + 1) * nx, :]

        y_soft[s, inner, :] = soft_of(field(0))
        y_soft[s, HALO - 3 : HALO, :] = soft_of(c_in[0:3, :])
        y_soft[s, HALO + nx : HALO + nx + 3, :] = soft_of(c_in[3:6, :])
        y_pull[s, inner, :] = (field(0) - 1.0) * field(2)
        y_pull[s, HALO - 2 : HALO, :] = (c_in[1:3, :] - 1.0) * c_in[10:12, :]
        y_pull[s, HALO + nx : HALO + nx + 2, :] = (c_in[3:5, :] - 1.0) * c_in[12:14, :]
        edge = 0 if s == 0 else ny - 1
        for first, count, behind, sources in (
            (HALO, nx, field(1), [field(3 + f) for f in range(4)]),
            (HALO - 2, 2, c_in[6:8, :], [c_in[14 + 4 * f : 16 + 4 * f, :] for f in range(4)]),
            (HALO + nx, 2, c_in[8:10, :], [c_in[16 + 4 * f : 18 + 4 * f, :] for f in range(4)]),
        ):
            center = y_soft[s, first : first + count, :]
            total = soft[first : first + count, edge, :] + soft_of(behind)
            total += y_soft[s, first - 1 : first - 1 + count, :] + y_soft[s, first + 1 : first + 1 + count, :]
            total += lane_up(center, OUTSIDE) + lane_down(center, OUTSIDE)
            inverse = lam_inverse(center, total)
            y_state[s, 0, first : first + count, :] = sources[0]
            for c in range(3):
                y_state[s, 1 + c, first : first + count, :] = inverse * sources[1 + c]

    lane = lax.broadcasted_iota(jnp.int32, (ny, nz), 1)
    here = lax.axis_index("gx")
    low_inside, high_inside = here > 0, here < lax.axis_size("gx") - 1

    def prepare(at, _):
        row = pl.ds(at, 1)
        center = soft[at]
        sides = [
            soft[at + 1],
            soft[at - 1],
            row_up(center, y_soft[1, row, :]),
            row_down(center, y_soft[0, row, :]),
            lane_up(center, OUTSIDE),
            lane_down(center, OUTSIDE),
        ]
        outside = ((at < HALO) & ~low_inside) | ((at >= HALO + nx) & ~high_inside)
        inverse = jnp.where(outside, 0.0, lam_inverse(center, sum(sides)))
        eighth = 0.125 * inverse
        for j in range(6):
            face = eighth * (center + sides[j])
            if j == 4:
                face = jnp.where(lane == nz - 1, 0.0, face)
            if j == 5:
                face = jnp.where(lane == 0, 0.0, face)
            g[j, at] = face
        k[0, at] = inverse * pull[0, at + 1]
        k[1, at] = -inverse * pull[0, at - 1]
        k[2, at] = inverse * row_up(pull[1, at], y_pull[1, row, :])
        k[3, at] = -inverse * row_down(pull[1, at], y_pull[0, row, :])
        k[4, at] = inverse * lane_up(pull[2, at], 0.0)
        k[5, at] = -inverse * lane_down(pull[2, at], 0.0)
        state0[0, at] = raw[0, at]
        for c in range(3):
            state0[1 + c, at] = inverse * raw[1 + c, at]
        return 0

    lax.fori_loop(HALO - 3, HALO + nx + 3, prepare, 0)
    (c1, c2), _, _ = weights()

    def advance(at, f, own, moved):
        state1[f, at] = (1.0 + c1) * own + c2 * moved

    def rows(s, f, at):
        return y_state[s, f, pl.ds(at, 1), :]

    sweep(2, state0, g, k, mu_scale, rows, advance)
    send_rows(1, state1, sy_low, sy_high)


def send_rows(wide, state, sy_low, sy_high):
    planes, ny = state.shape[1:3]
    count = planes - 2 * HALO + 2 * wide
    inner = slice(HALO - wide, HALO - wide + count)
    for f in range(4):
        sy_low[f * count : (f + 1) * count, :] = state[f, inner, 0, :]
        sy_high[f * count : (f + 1) * count, :] = state[f, inner, ny - 1, :]


def received_rows(wide, y_low, y_high):
    count = y_low.shape[0] // 4

    def rows(s, f, at):
        return (y_low, y_high)[s][pl.ds(f * count + at - (HALO - wide), 1), :]

    return rows


def sweep(wide, state, g, k, mu_scale, rows, advance, finish=None):
    planes, ny, nz = mu_scale.shape
    lane = lax.broadcasted_iota(jnp.int32, (ny, nz), 1)

    def plane(at, _):
        def around(f):
            own = state[f, at]
            return own, [
                state[f, at + 1],
                state[f, at - 1],
                row_up(own, rows(1, f, at)),
                row_down(own, rows(0, f, at)),
                pltpu.roll(own, nz - 1, 1),
                pltpu.roll(own, 1, 1),
            ]

        mu, mu_sides = around(0)
        ends = [
            jnp.where(lane == nz - 1, 0.0, mu_sides[4]),
            jnp.where(lane == 0, 0.0, mu_sides[5]),
        ]
        results = [advance(at, 0, mu, mu_scale[at] * sum(mu_sides[:4] + ends))]
        faces = [g[j, at] for j in range(6)]
        for c in range(3):
            lam, lam_sides = around(1 + c)
            moved = sum(faces[j] * lam_sides[j] for j in range(6))
            moved += k[2 * c, at] * mu_sides[2 * c] + k[2 * c + 1, at] * mu_sides[2 * c + 1]
            results.append(advance(at, 1 + c, lam, moved))
        if finish is not None:
            finish(at - HALO, results)
        return 0

    lax.fori_loop(HALO - wide, planes - HALO + wide, plane, 0)


def second_kernel(g, k, mu_scale, state0, state1, y_low, y_high, state2, sy_low, sy_high):
    _, (c1, c2), _ = weights()

    def advance(at, f, own, moved):
        state2[f, at] = own + (c1 - c2) * (own - state0[f, at]) + c2 * moved

    sweep(1, state1, g, k, mu_scale, received_rows(1, y_low, y_high), advance)
    send_rows(0, state2, sy_low, sy_high)


def third_kernel(
    work, damage, dx_low, dx_high, dy_low, dy_high,
    g, k, mu_scale, state0, state1, state2, y_low, y_high,
    out_mu, out_lam,
    framed, mu_tile, lam_tile, sems,
):
    nx, ny, nz = damage.shape
    _, _, (c1, c2) = weights()
    framed[0] = dx_low[X_DAMAGE + 3]
    framed[nx + 1] = dx_high[X_DAMAGE]

    def fill(i, _):
        framed[i + 1] = damage[i]
        return 0

    lax.fori_loop(0, nx, fill, 0)
    count = work[0, 0]

    def copies(i):
        return (
            pltpu.make_async_copy(mu_tile.at[i], out_mu.at[i], sems.at[0, i]),
            pltpu.make_async_copy(lam_tile.at[:, i], out_lam.at[:, i], sems.at[1, i]),
        )

    def advance(at, f, own, moved):
        return own + c1 * (own - state1[f, at]) + c2 * (state0[f, at] - own + moved)

    def finish(i, results):
        mu_tile[i] = results[0]
        own = framed[i + 1]
        grad = [
            0.5 * (framed[i + 2] - framed[i]),
            0.5 * (row_up(own, dy_high[pl.ds(i, 1), :]) - row_down(own, dy_low[pl.ds(i, 1), :])),
            0.5 * (lane_up(own, 0.0) - lane_down(own, 0.0)),
        ]
        square = sum(part * part for part in grad)
        scale = 1.0 / jnp.maximum(square, NORMAL_FLOOR)
        power = 1.0 - RELAX_RATE * (1.0 + NORMAL_WEIGHT * square * scale)
        series = 1.0 + power
        for _ in range(2):
            power = power * power
            series = series * (1.0 + power)
        power = power * power
        repeats = jnp.ones_like(power)
        for level in range(1, 4):
            repeats = jnp.where(count > level, 1.0 + power * repeats, repeats)
        along = sum(grad[c] * results[1 + c] for c in range(3))
        along = along * (RELAX_RATE * NORMAL_WEIGHT * scale) * (series * repeats)
        for c in range(3):
            lam_tile[c, i] = results[1 + c] - along * grad[c]
        for copy in copies(i):
            copy.start()

    sweep(0, state2, g, k, mu_scale, received_rows(0, y_low, y_high), advance, finish)

    def settle(i, _):
        for copy in copies(i):
            copy.wait()
        return 0

    lax.fori_loop(0, nx, settle, 0)


VMEM = pl.BlockSpec(memory_space=pltpu.VMEM)
SMEM = pl.BlockSpec(memory_space=pltpu.SMEM)
ANY = pl.BlockSpec(memory_space=pl.ANY)
MIB = 1024 * 1024


def call(kernel, ins, outs, scratch=(), in_specs=None, out_specs=None, grant=24 * MIB):
    return pl.pallas_call(
        kernel,
        out_shape=[jax.ShapeDtypeStruct(shape, F32) for shape in outs],
        in_specs=in_specs or [VMEM] * len(ins),
        out_specs=out_specs or [VMEM] * len(outs),
        scratch_shapes=[pltpu.VMEM(shape, F32) if isinstance(shape, tuple) else shape for shape in scratch],
        compiler_params=pltpu.CompilerParams(vmem_limit_bytes=grant),
    )(*ins)


def swap(low, high, axis):
    count = lax.axis_size(axis)
    up = [(i, i + 1) for i in range(count - 1)]
    down = [(i + 1, i) for i in range(count - 1)]
    return lax.ppermute(high, axis, up), lax.ppermute(low, axis, down)


def body(damage, strain, seed_damage, seed_disp, brick_work):
    nx, ny, nz = damage.shape
    plane = (ny, nz)
    brick = (nx,) + plane
    framed = (nx + 2 * HALO,) + plane
    state = (4,) + framed
    fields = (damage, strain, seed_damage, seed_disp)

    x_pair = call(
        faces_x_kernel, fields, [(X_SLOTS,) + plane] * 2,
        [(2, 3, 3) + plane, (2, 3) + plane, pltpu.SemaphoreType.DMA((18,))],
        in_specs=[ANY] * 4, grant=56 * MIB,
    )
    x_in = swap(*x_pair, "gx")
    y_in = swap(*call(faces_y_kernel, fields, [(Y_FIELDS * nx, nz)] * 2), "gy")
    c_in = swap(*call(corners_kernel, x_in, [(CORNER_ROWS, nz)] * 2), "gy")
    soft, pull, mu_scale, raw = call(
        gather_kernel, fields + x_in, [framed, (3,) + framed, framed, state]
    )

    def rows(wide):
        return [(4 * (nx + 2 * wide), nz)] * 2

    g, k, state0, state1, *sent = call(
        first_kernel,
        (soft, pull, mu_scale, raw) + y_in + c_in,
        [(6,) + framed, (6,) + framed, state, state] + rows(1),
        [(2, nx + 2 * HALO, nz), (2, nx + 2 * HALO, nz), (2, 4, nx + 2 * HALO, nz)],
    )
    halo = swap(*sent, "gy")
    state2, *sent = call(
        second_kernel, (g, k, mu_scale, state0, state1) + halo, [state] + rows(0)
    )
    halo = swap(*sent, "gy")
    ins = (brick_work, damage) + x_in + y_in + (g, k, mu_scale, state0, state1, state2) + halo
    return tuple(
        call(
            third_kernel, ins, [brick, (3,) + brick],
            [(nx + 2,) + plane, brick, (3,) + brick, pltpu.SemaphoreType.DMA((2, nx))],
            in_specs=[SMEM] + [VMEM] * (len(ins) - 1), out_specs=[ANY, ANY],
        )
    )


def solution(mesh):
    placed = (
        P("gx", "gy", None),
        P(None, "gx", "gy", None),
        P("gx", "gy", None),
        P(None, "gx", "gy", None),
        P("gx", "gy"),
    )
    return jax.shard_map(
        body,
        mesh=mesh,
        in_specs=placed,
        out_specs=(P("gx", "gy", None), P(None, "gx", "gy", None)),
        check_vma=False,
    )
```

```python
import functools

import jax
import jax.numpy as jnp
from jax import lax
from jax.experimental import pallas as pl
from jax.experimental.pallas import tpu as pltpu
from jax.sharding import PartitionSpec as P

RELAX_INNER = 8
RESIDUAL_STIFFNESS = 0.001
CENTER_VALUE = 1.0
HALF_WIDTH = 0.75
NORMAL_WEIGHT = 1.5
RELAX_RATE = 0.5 / RELAX_INNER
NORMAL_FLOOR = 0.05
OUTSIDE = 1.0 + RESIDUAL_STIFFNESS
F32 = jnp.float32


def weights():
    ratio = CENTER_VALUE / HALF_WIDTH
    rho = 1.0 / ratio
    found = []
    for _ in range(3):
        rho_next = 1.0 / (2.0 * ratio - rho)
        found.append((rho_next * rho, 2.0 * rho_next / HALF_WIDTH))
        rho = rho_next
    return found


def soft_of(damage):
    return (1.0 - damage) ** 2 + RESIDUAL_STIFFNESS


def row_up(plane, beyond):
    rows = plane.shape[0]
    at = lax.broadcasted_iota(jnp.int32, plane.shape, 0)
    return jnp.where(at == rows - 1, beyond, pltpu.roll(plane, rows - 1, 0))


def row_down(plane, beyond):
    at = lax.broadcasted_iota(jnp.int32, plane.shape, 0)
    return jnp.where(at == 0, beyond, pltpu.roll(plane, 1, 0))


def lane_up(plane, beyond):
    cells = plane.shape[1]
    at = lax.broadcasted_iota(jnp.int32, plane.shape, 1)
    return jnp.where(at == cells - 1, beyond, pltpu.roll(plane, cells - 1, 1))


def lane_down(plane, beyond):
    at = lax.broadcasted_iota(jnp.int32, plane.shape, 1)
    return jnp.where(at == 0, beyond, pltpu.roll(plane, 1, 1))


def mu_inverse(ex, ey, ez):
    return 1.0 / (2.0 + (ex * ex + ey * ey + ez * ez))


def lam_inverse(center, total):
    return 1.0 / (0.5 + 0.125 * (6.0 * center + total))


HALO = 4
X_DAMAGE, X_PULL, X_PULL_Y, X_PULL_Z, X_MU, X_SOURCE, X_SLOTS = 0, 4, 7, 9, 11, 14, 23
Y_ROWS = (
    (X_DAMAGE, 4, 0, 3),
    (X_DAMAGE, 4, 1, 2),
    (X_DAMAGE, 4, 2, 1),
    (X_PULL, 3, 0, 2),
    (X_PULL_Y, 2, 0, 2),
    (X_PULL_Y, 2, 1, 1),
    (X_PULL_Z, 2, 0, 1),
    (X_MU, 3, 0, 2),
    (X_MU, 3, 1, 1),
    (X_SOURCE, 3, 0, 2),
    (X_SOURCE + 3, 3, 0, 2),
    (X_SOURCE + 6, 3, 0, 2),
    (X_SOURCE, 3, 1, 1),
    (X_SOURCE + 3, 3, 1, 1),
    (X_SOURCE + 6, 3, 1, 1),
)
CORNER_ROWS = sum(entry[3] for entry in Y_ROWS)


def edge_row(s, ny, depth):
    return depth if s == 0 else ny - 1 - depth


def faces_y_kernel(
    damage_in, strain_in, seed_in, sources_in, low, high, damage, strain, seed_damage, seed_disp, sems
):
    nx, ny, _ = damage.shape
    copies = [
        pltpu.make_async_copy(damage_in, damage, sems.at[0]),
        pltpu.make_async_copy(seed_in, seed_damage, sems.at[1]),
    ]
    for c in range(3):
        copies.append(pltpu.make_async_copy(strain_in.at[c], strain.at[c], sems.at[2 + c]))
        copies.append(pltpu.make_async_copy(sources_in.at[c], seed_disp.at[c], sems.at[5 + c]))
    for copy in copies:
        copy.start()
    for copy in copies:
        copy.wait()
    for s, out in enumerate((low, high)):
        first, second, third = (edge_row(s, ny, depth) for depth in range(3))

        def put(slot, value):
            out[slot * nx : (slot + 1) * nx, :] = value

        put(0, damage[:, first, :])
        put(1, damage[:, second, :])
        put(2, damage[:, third, :])
        for depth, row in enumerate((first, second)):
            sx, sy, sz = (strain[c, :, row, :] for c in range(3))
            if depth == 0:
                put(3, sx)
                put(6, sz)
            put(4 + depth, sy)
            put(7 + depth, seed_damage[:, row, :] * mu_inverse(sx, sy, sz))
            for c in range(3):
                put(9 + 3 * depth + c, seed_disp[c, :, row, :])


def faces_x_kernel(damage, strain, seed_damage, seed_disp, low, high):
    nx = damage.shape[0]
    for s, out in enumerate((low, high)):

        def planes(count):
            first = 0 if s == 0 else nx - count
            return slice(first, first + count)

        out[X_DAMAGE : X_DAMAGE + 4] = damage[planes(4)]
        sx, sy, sz = (strain[c, planes(3)] for c in range(3))
        out[X_PULL : X_PULL + 3] = sx
        out[X_PULL_Y : X_PULL_Y + 2] = strain[1, planes(2)]
        out[X_PULL_Z : X_PULL_Z + 2] = strain[2, planes(2)]
        out[X_MU : X_MU + 3] = seed_damage[planes(3)] * mu_inverse(sx, sy, sz)
        for c in range(3):
            slot = X_SOURCE + 3 * c
            out[slot : slot + 3] = seed_disp[c, planes(3)]


def corners_kernel(x_low, x_high, low, high):
    ny = x_low.shape[1]
    for s, out in enumerate((low, high)):
        row = 0
        for slot, held, depth, count in Y_ROWS:
            for side, x_in in enumerate((x_low, x_high)):
                first = slot + (held - count if side == 0 else 0)
                at = side * CORNER_ROWS + row
                out[at : at + count, :] = x_in[first : first + count, edge_row(s, ny, depth), :]
            row += count


def sides_of(center, beyond_up, beyond_down):
    return [
        row_up(center, beyond_up),
        row_down(center, beyond_down),
        lane_up(center, OUTSIDE),
        lane_down(center, OUTSIDE),
    ]


def inner_kernel(
    damage, strain, seed_damage, seed_disp, x_low, x_high,
    soft, pull, mu_scale, raw, g, k, state0, state1,
):
    nx, ny, nz = damage.shape

    def fill(i, _):
        at = HALO + i
        own = damage[i]
        sx, sy, sz = strain[0, i], strain[1, i], strain[2, i]
        soft[at] = soft_of(own)
        own = own - 1.0
        pull[0, at] = own * sx
        pull[1, at] = own * sy
        pull[2, at] = own * sz
        mu_inv = mu_inverse(sx, sy, sz)
        mu_scale[at] = 0.25 * mu_inv
        state0[0, at] = mu_inv * seed_damage[i]
        for c in range(3):
            raw[c, at] = seed_disp[c, i]
        return 0

    lax.fori_loop(0, nx, fill, 0)
    here = lax.axis_index("gx")
    inside = (here > 0, here < lax.axis_size("gx") - 1)
    for s, x_in in enumerate((x_low, x_high)):

        def planes(count):
            first = HALO - count if s == 0 else HALO + nx
            return slice(first, first + count)

        def nearest(slot, held, count):
            first = slot + (held - count if s == 0 else 0)
            return x_in[first : first + count]

        soft[planes(4)] = soft_of(nearest(X_DAMAGE, 4, 4))
        pull[0, planes(3)] = (nearest(X_DAMAGE, 4, 3) - 1.0) * nearest(X_PULL, 3, 3)
        own = nearest(X_DAMAGE, 4, 2) - 1.0
        sx, sy, sz = nearest(X_PULL, 3, 2), nearest(X_PULL_Y, 2, 2), nearest(X_PULL_Z, 2, 2)
        pull[1, planes(2)] = own * sy
        pull[2, planes(2)] = own * sz
        mu_scale[planes(2)] = jnp.where(inside[s], 0.25 * mu_inverse(sx, sy, sz), 0.0)
        state0[0, planes(3)] = nearest(X_MU, 3, 3)
        for c in range(3):
            raw[c, planes(3)] = nearest(X_SOURCE + 3 * c, 3, 3)

    lane = lax.broadcasted_iota(jnp.int32, (ny, nz), 1)
    row = lax.broadcasted_iota(jnp.int32, (ny, nz), 0)
    inner = (row > 0) & (row < ny - 1)

    def prepare(at, _):
        center = soft[at]
        sides = [soft[at + 1], soft[at - 1]] + sides_of(center, 1.0, 1.0)
        outside = ((at < HALO) & ~inside[0]) | ((at >= HALO + nx) & ~inside[1])
        inverse = jnp.where(inner & ~outside, lam_inverse(center, sum(sides)), 0.0)
        eighth = 0.125 * inverse
        for j in range(6):
            face = eighth * (center + sides[j])
            if j == 4:
                face = jnp.where(lane == nz - 1, 0.0, face)
            if j == 5:
                face = jnp.where(lane == 0, 0.0, face)
            g[j, at] = face
        k[0, at] = inverse * pull[0, at + 1]
        k[1, at] = -inverse * pull[0, at - 1]
        k[2, at] = inverse * pltpu.roll(pull[1, at], ny - 1, 0)
        k[3, at] = -inverse * pltpu.roll(pull[1, at], 1, 0)
        k[4, at] = inverse * lane_up(pull[2, at], 0.0)
        k[5, at] = -inverse * lane_down(pull[2, at], 0.0)
        for c in range(3):
            state0[1 + c, at] = inverse * raw[c, at]
        return 0

    lax.fori_loop(HALO - 3, HALO + nx + 3, prepare, 0)
    (c1, c2), _, _ = weights()

    def advance(at, f, own, moved):
        state1[f, at] = (1.0 + c1) * own + c2 * moved

    sweep(2, state0, g, k, mu_scale, None, advance)


def edges_kernel(
    soft, pull, mu_scale, raw, g, state0, state1, y_low, y_high, c_low, c_high,
    sy_low, sy_high, coefficients, firsts, seconds, outer,
    field,
):
    planes, ny, nz = soft.shape
    nx = planes - 2 * HALO
    (c1, c2), (d1, d2), _ = weights()
    lane = lax.broadcasted_iota(jnp.int32, (planes, nz), 1)
    plane = lax.broadcasted_iota(jnp.int32, (planes, nz), 0)
    here, there = lax.axis_index("gx"), lax.axis_index("gy")
    in_x = ((plane >= HALO) | (here > 0)) & ((plane < HALO + nx) | (here < lax.axis_size("gx") - 1))
    in_y = (there > 0, there < lax.axis_size("gy") - 1)

    def around_x(value):
        return [pltpu.roll(value, planes - 1, 0), pltpu.roll(value, 1, 0)]

    def around_z(value, fill):
        return [lane_up(value, fill), lane_down(value, fill)]

    for s, (y_in, c_in, sent) in enumerate(((y_low, c_low, sy_low), (y_high, c_high, sy_high))):
        e0, e1 = edge_row(s, ny, 0), edge_row(s, ny, 1)

        def ordered(inward, outward):
            return [inward, outward] if s == 0 else [outward, inward]

        row = 0
        for f, entry in enumerate(Y_ROWS):
            count = entry[3]
            field[f, HALO : HALO + nx, :] = y_in[f * nx : (f + 1) * nx, :]
            field[f, HALO - count : HALO, :] = c_in[row : row + count, :]
            field[f, HALO + nx : HALO + nx + count, :] = c_in[CORNER_ROWS + row : CORNER_ROWS + row + count, :]
            row += count

        soft_1, soft_2, soft_3 = (soft_of(field[f]) for f in range(3))
        soft_e0, soft_e1 = soft[:, e0, :], soft[:, e1, :]

        def total(center, inward, outward):
            return sum(around_x(center) + [inward, outward] + around_z(center, OUTSIDE))

        inverse_2 = lam_inverse(soft_2, total(soft_2, soft_1, soft_3))
        lam_2 = [inverse_2 * field[12 + c] for c in range(3)]
        inverse_1 = lam_inverse(soft_1, total(soft_1, soft_e0, soft_2))
        inverse_1 = jnp.where(in_x & in_y[s], inverse_1, 0.0)
        lam_1 = [inverse_1 * field[9 + c] for c in range(3)]
        inverse_e0 = jnp.where(in_x, lam_inverse(soft_e0, total(soft_e0, soft_e1, soft_1)), 0.0)
        lam_e0 = [inverse_e0 * raw[c, :, e0, :] for c in range(3)]
        mu_1, mu_2 = field[7], field[8]
        mu_e0, mu_e1 = state0[0, :, e0, :], state0[0, :, e1, :]
        lam_e1 = [state0[1 + c, :, e1, :] for c in range(3)]

        def coefficients_of(center, inverse, inward, outward, wx, wy, wz):
            sides = around_x(center) + ordered(inward, outward) + around_z(center, OUTSIDE)
            eighth = 0.125 * inverse
            faces = [eighth * (center + side) for side in sides]
            faces[4] = jnp.where(lane == nz - 1, 0.0, faces[4])
            faces[5] = jnp.where(lane == 0, 0.0, faces[5])
            pulls = around_x(wx) + wy + around_z(wz, 0.0)
            return faces, [inverse * w if j % 2 == 0 else -inverse * w for j, w in enumerate(pulls)]

        def moved_of(faces, pulls, scale, own, inward, outward):
            sides = [
                around_x(own[f]) + ordered(inward[f], outward[f]) + around_z(own[f], 0.0) for f in range(4)
            ]
            moved = [scale * sum(sides[0])]
            for c in range(3):
                part = sum(faces[j] * sides[1 + c][j] for j in range(6))
                moved.append(part + pulls[2 * c] * sides[0][2 * c] + pulls[2 * c + 1] * sides[0][2 * c + 1])
            return moved

        less = field[0] - 1.0
        scale_1 = jnp.where(in_x & in_y[s], 0.25 * mu_inverse(field[3], field[4], field[6]), 0.0)
        wy = ordered(pull[1, :, e0, :], (field[1] - 1.0) * field[5])
        faces, pulls = coefficients_of(soft_1, inverse_1, soft_e0, soft_2, less * field[3], wy, less * field[6])
        own_1 = [mu_1] + lam_1
        own_e0 = [mu_e0] + lam_e0
        moved = moved_of(faces, pulls, scale_1, own_1, own_e0, [mu_2] + lam_2)
        first_1 = [(1.0 + c1) * own_1[f] + c2 * moved[f] for f in range(4)]

        scale_e0 = mu_scale[:, e0, :]
        wy = ordered(pull[1, :, e1, :], less * field[4])
        faces, pulls = coefficients_of(
            soft_e0, inverse_e0, soft_e1, soft_1, pull[0, :, e0, :], wy, pull[2, :, e0, :]
        )
        moved = moved_of(faces, pulls, scale_e0, own_e0, [mu_e1] + lam_e1, own_1)
        first_e0 = [(1.0 + c1) * own_e0[f] + c2 * moved[f] for f in range(4)]

        outward_face = g[3 if s == 0 else 2, :, e1, :]
        first_e1 = [state1[0, :, e1, :]]
        for c in range(3):
            first_e1.append(state1[1 + c, :, e1, :] + c2 * outward_face * lam_e0[c])

        moved = moved_of(faces, pulls, scale_e0, first_e0, first_e1, first_1)
        for f in range(4):
            second = first_e0[f] + (d1 - d2) * (first_e0[f] - own_e0[f]) + d2 * moved[f]
            sent[f * nx : (f + 1) * nx, :] = second[HALO : HALO + nx, :]
            firsts[s, f] = first_e0[f]
            outer[s, f] = first_1[f]
        for j in range(6):
            coefficients[s, j] = faces[j]
            coefficients[s, 6 + j] = pulls[j]
        for c in range(3):
            coefficients[s, 12 + c] = lam_e0[c]
            seconds[s, c] = first_e1[1 + c]


def sweep(wide, state, g, k, mu_scale, rows, advance, finish=None):
    planes, ny, nz = mu_scale.shape
    lane = lax.broadcasted_iota(jnp.int32, (ny, nz), 1)
    if rows is None:

        def rows(s, f, at):
            return 0.0

    def plane(at, _):
        def around(f):
            own = state[f, at]
            return own, [
                state[f, at + 1],
                state[f, at - 1],
                row_up(own, rows(1, f, at)),
                row_down(own, rows(0, f, at)),
                pltpu.roll(own, nz - 1, 1),
                pltpu.roll(own, 1, 1),
            ]

        mu, mu_sides = around(0)
        ends = [
            jnp.where(lane == nz - 1, 0.0, mu_sides[4]),
            jnp.where(lane == 0, 0.0, mu_sides[5]),
        ]
        results = [advance(at, 0, mu, mu_scale[at] * sum(mu_sides[:4] + ends))]
        faces = [g[j, at] for j in range(6)]
        for c in range(3):
            lam, lam_sides = around(1 + c)
            moved = sum(faces[j] * lam_sides[j] for j in range(6))
            moved += k[2 * c, at] * mu_sides[2 * c] + k[2 * c + 1, at] * mu_sides[2 * c + 1]
            results.append(advance(at, 1 + c, lam, moved))
        if finish is not None:
            finish(at - HALO, results)
        return 0

    lax.fori_loop(HALO - wide, planes - HALO + wide, plane, 0)


def wait_kernel(
    work, damage, dx_low, dx_high, dy_low, dy_high,
    mu_scale, coefficients, firsts, seconds, outer, g_in, k_in, state0_in, state1_in,
    out_mu, out_lam, edges, g, k, state0, state1,
    state2, framed, grads, states,
):
    nx, ny, nz = damage.shape
    planes = nx + 2 * HALO
    _, (d1, d2), (c1, c2) = weights()
    held = slice(HALO - 2, HALO + nx + 2)
    for s in range(2):
        e0, e1 = edge_row(s, ny, 0), edge_row(s, ny, 1)
        for j in range(6):
            g[j, held, e0, :] = coefficients[s, j, held, :]
            k[j, held, e0, :] = coefficients[s, 6 + j, held, :]
        for c in range(3):
            state0[1 + c, held, e0, :] = coefficients[s, 12 + c, held, :]
            state1[1 + c, held, e1, :] = seconds[s, c, held, :]
        for f in range(4):
            state1[f, held, e0, :] = firsts[s, f, held, :]

    def rows(s, f, at):
        return outer[s, f, pl.ds(at, 1), :]

    def advance_2(at, f, own, moved):
        state2[f, at] = own + (d1 - d2) * (own - state0[f, at]) + d2 * moved

    sweep(1, state1, g, k, mu_scale, rows, advance_2)

    framed[0] = dx_low[X_DAMAGE + 3]
    framed[nx + 1] = dx_high[X_DAMAGE]

    def fill(i, _):
        framed[i + 1] = damage[i]
        return 0

    lax.fori_loop(0, nx, fill, 0)
    count = work[0, 0]

    def advance_3(at, f, own, moved):
        return own + c1 * (own - state1[f, at]) + c2 * (state0[f, at] - own + moved)

    def finish(i, results):
        out_mu[i] = results[0]
        own = framed[i + 1]
        grad = [
            0.5 * (framed[i + 2] - framed[i]),
            0.5 * (row_up(own, dy_high[pl.ds(i, 1), :]) - row_down(own, dy_low[pl.ds(i, 1), :])),
            0.5 * (lane_up(own, 0.0) - lane_down(own, 0.0)),
        ]
        square = sum(part * part for part in grad)
        scale = 1.0 / jnp.maximum(square, NORMAL_FLOOR)
        power = 1.0 - RELAX_RATE * (1.0 + NORMAL_WEIGHT * square * scale)
        series = 1.0 + power
        for _ in range(2):
            power = power * power
            series = series * (1.0 + power)
        power = power * power
        repeats = jnp.ones_like(power)
        for level in range(1, 4):
            repeats = jnp.where(count > level, 1.0 + power * repeats, repeats)
        reach = (RELAX_RATE * NORMAL_WEIGHT * scale) * (series * repeats)
        along = reach * sum(grad[c] * results[1 + c] for c in range(3))
        grads[3, i] = reach
        for c in range(3):
            out_lam[c, i] = results[1 + c] - along * grad[c]
            grads[c, i] = grad[c]
            states[c, i] = results[1 + c]

    sweep(0, state2, g, k, mu_scale, None, advance_3, finish)
    for s in range(2):
        e0 = edge_row(s, ny, 0)
        for f in range(4):
            edges[s, f] = grads[f, :, e0, :]
        for c in range(3):
            edges[s, 4 + c] = states[c, :, e0, :]


def last_kernel(
    mu_scale, coefficients, edges, y_low, y_high, mu_in, lam_in,
    out_mu, out_lam, mu, lam,
    sems,
):
    nx, ny, nz = mu.shape
    inner = slice(HALO, HALO + nx)
    _, _, (_, c2) = weights()
    for s, y_in in enumerate((y_low, y_high)):
        e0 = edge_row(s, ny, 0)
        outward = 3 if s == 0 else 2

        def got(f):
            return y_in[f * nx : (f + 1) * nx, :]

        mu[:, e0, :] = mu[:, e0, :] + c2 * mu_scale[inner, e0, :] * got(0)
        face = c2 * coefficients[s, outward, inner, :]
        ends = []
        for c in range(3):
            end = edges[s, 4 + c] + face * got(1 + c)
            if c == 1:
                end += c2 * coefficients[s, 6 + outward, inner, :] * got(0)
            ends.append(end)
        along = edges[s, 3] * sum(edges[s, c] * ends[c] for c in range(3))
        for c in range(3):
            lam[c, :, e0, :] = ends[c] - along * edges[s, c]
    copies = [
        pltpu.make_async_copy(mu, out_mu, sems.at[0]),
        pltpu.make_async_copy(lam, out_lam, sems.at[1]),
    ]
    for copy in copies:
        copy.start()
    for copy in copies:
        copy.wait()


VMEM = pl.BlockSpec(memory_space=pltpu.VMEM)
SMEM = pl.BlockSpec(memory_space=pltpu.SMEM)
HBM = pl.BlockSpec(memory_space=pltpu.HBM)
MIB = 1024 * 1024


def call(kernel, ins, outs, scratch=(), in_specs=None, out_specs=None, aliases=None, grant=24 * MIB):
    return pl.pallas_call(
        kernel,
        out_shape=[jax.ShapeDtypeStruct(shape, F32) for shape in outs],
        in_specs=in_specs or [VMEM] * len(ins),
        out_specs=out_specs or [VMEM] * len(outs),
        scratch_shapes=[pltpu.VMEM(shape, F32) if isinstance(shape, tuple) else shape for shape in scratch],
        input_output_aliases=aliases or {},
        compiler_params=pltpu.CompilerParams(vmem_limit_bytes=grant),
    )(*ins)


def swap(low, high, axis):
    count = lax.axis_size(axis)
    up = [(i, i + 1) for i in range(count - 1)]
    down = [(i + 1, i) for i in range(count - 1)]
    return lax.ppermute(high, axis, up), lax.ppermute(low, axis, down)


def body(damage, strain, seed_damage, seed_disp, brick_work):
    nx, ny, nz = damage.shape
    plane = (ny, nz)
    brick = (nx,) + plane
    bricks = (3,) + brick
    framed = (nx + 2 * HALO,) + plane
    state = (4,) + framed
    row = (nx + 2 * HALO, nz)

    fields = (damage, strain, seed_damage, seed_disp)
    y_pair = call(
        faces_y_kernel, fields, [(len(Y_ROWS) * nx, nz)] * 2,
        [brick, bricks, brick, bricks, pltpu.SemaphoreType.DMA((8,))],
        in_specs=[HBM] * 4, grant=56 * MIB,
    )
    y_in = swap(*y_pair, "gy")
    x_in = swap(*call(faces_x_kernel, fields, [(X_SLOTS,) + plane] * 2), "gx")
    c_in = swap(*call(corners_kernel, x_in, [(2 * CORNER_ROWS, nz)] * 2), "gy")
    soft, pull, mu_scale, raw, g, k, state0, state1 = call(
        inner_kernel, fields + x_in,
        [framed, (3,) + framed, framed, (3,) + framed, (6,) + framed, (6,) + framed, state, state],
    )
    low, high, coefficients, firsts, seconds, outer = call(
        edges_kernel, (soft, pull, mu_scale, raw, g, state0, state1) + y_in + c_in,
        [(4 * nx, nz)] * 2 + [(2, 15) + row, (2, 4) + row, (2, 3) + row, (2, 4) + row],
        [(len(Y_ROWS),) + row],
    )
    halo = swap(low, high, "gy")
    ins = (brick_work, fields[0]) + x_in + y_in
    ins += (mu_scale, coefficients, firsts, seconds, outer, g, k, state0, state1)
    mu, lam, edges, *_ = call(
        wait_kernel, ins,
        [brick, bricks, (2, 7, nx, nz), (6,) + framed, (6,) + framed, state, state],
        [state, (nx + 2,) + plane, (4,) + brick, bricks],
        in_specs=[SMEM] + [VMEM] * (len(ins) - 1),
        aliases={11: 3, 12: 4, 13: 5, 14: 6},
    )
    out_mu, out_lam, *_ = call(
        last_kernel, (mu_scale, coefficients, edges) + halo + (mu, lam),
        [brick, bricks, brick, bricks], [pltpu.SemaphoreType.DMA((2,))],
        out_specs=[HBM, HBM, VMEM, VMEM], aliases={5: 2, 6: 3},
    )
    return out_mu, out_lam


def solution(mesh):
    placed = (
        P("gx", "gy", None),
        P(None, "gx", "gy", None),
        P("gx", "gy", None),
        P(None, "gx", "gy", None),
        P("gx", "gy"),
    )
    return jax.shard_map(
        body,
        mesh=mesh,
        in_specs=placed,
        out_specs=(P("gx", "gy", None), P(None, "gx", "gy", None)),
        check_vma=False,
    )
```

```python
import functools

import jax
import jax.numpy as jnp
from jax import lax
from jax.experimental import pallas as pl
from jax.experimental.pallas import tpu as pltpu
from jax.sharding import PartitionSpec as P

RELAX_INNER = 8
RESIDUAL_STIFFNESS = 0.001
CENTER_VALUE = 1.0
HALF_WIDTH = 0.75
NORMAL_WEIGHT = 1.5
RELAX_RATE = 0.5 / RELAX_INNER
NORMAL_FLOOR = 0.05
OUTSIDE = 1.0 + RESIDUAL_STIFFNESS
F32 = jnp.float32


def weights():
    ratio = CENTER_VALUE / HALF_WIDTH
    rho = 1.0 / ratio
    found = []
    for _ in range(3):
        rho_next = 1.0 / (2.0 * ratio - rho)
        found.append((rho_next * rho, 2.0 * rho_next / HALF_WIDTH))
        rho = rho_next
    return found


def soft_of(damage):
    return (1.0 - damage) ** 2 + RESIDUAL_STIFFNESS


def row_up(plane, beyond):
    rows = plane.shape[0]
    at = lax.broadcasted_iota(jnp.int32, plane.shape, 0)
    return jnp.where(at == rows - 1, beyond, pltpu.roll(plane, rows - 1, 0))


def row_down(plane, beyond):
    at = lax.broadcasted_iota(jnp.int32, plane.shape, 0)
    return jnp.where(at == 0, beyond, pltpu.roll(plane, 1, 0))


def lane_up(plane, beyond):
    cells = plane.shape[1]
    at = lax.broadcasted_iota(jnp.int32, plane.shape, 1)
    return jnp.where(at == cells - 1, beyond, pltpu.roll(plane, cells - 1, 1))


def lane_down(plane, beyond):
    at = lax.broadcasted_iota(jnp.int32, plane.shape, 1)
    return jnp.where(at == 0, beyond, pltpu.roll(plane, 1, 1))


def mu_inverse(ex, ey, ez):
    return 1.0 / (2.0 + (ex * ex + ey * ey + ez * ez))


def lam_inverse(center, total):
    return 1.0 / (0.5 + 0.125 * (6.0 * center + total))


HALO = 4
X_DAMAGE, X_PULL, X_PULL_Y, X_PULL_Z, X_MU, X_SOURCE, X_SLOTS = 0, 4, 7, 9, 11, 14, 23
Y_ROWS = (
    (X_DAMAGE, 4, 0, 3),
    (X_DAMAGE, 4, 1, 2),
    (None, 2, 0, 2),
    (X_MU, 3, 0, 2),
    (None, 2, 0, 1),
    (X_SOURCE, 3, 0, 2),
    (X_SOURCE + 3, 3, 0, 2),
    (X_SOURCE + 6, 3, 0, 2),
)
Y_KNOWN, Y_FIELDS, Y_SPARE = 8, 12, 3
CORNER_ROWS = sum(entry[3] for entry in Y_ROWS) + 8


def edge_row(s, ny, depth):
    return depth if s == 0 else ny - 1 - depth


def known_of(s, damages, pulls, behind_pull, mus, sources, behind):
    planes = damages[0].shape[0]
    (c1, c2), _, _ = weights()
    soft = [soft_of(part) for part in damages]
    less = damages[0] - 1.0
    wx, wy, wz = (less * pull for pull in pulls)
    wy_behind = (damages[1] - 1.0) * behind_pull

    def across(value):
        return pltpu.roll(value, planes - 1, 0), pltpu.roll(value, 1, 0)

    def along(value, fill):
        return lane_up(value, fill), lane_down(value, fill)

    total = soft[0] + soft[2] + sum(across(soft[1])) + sum(along(soft[1], OUTSIDE))
    inverse = lam_inverse(soft[1], total)
    face = 0.125 * (soft[0] + soft[1])
    scale = 0.25 * mu_inverse(*pulls)
    known = [(1.0 + c1) * mus[0] + c2 * scale * (mus[1] + sum(across(mus[0])) + sum(along(mus[0], 0.0)))]
    x_up, x_down = across(wx * mus[0])
    z_up, z_down = along(wz * mus[0], 0.0)
    y_behind = wy_behind * mus[1]
    transfers = (x_up - x_down, y_behind if s == 0 else -y_behind, z_up - z_down)
    for c in range(3):
        known.append((1.0 + c1) * sources[c] + c2 * (face * (inverse * behind[c]) + transfers[c]))
    return scale, wy, known


def put_rows(s, put, damage, strain, seed_damage, seed_disp):
    ny = damage.shape[1]
    first, second, third = (edge_row(s, ny, depth) for depth in range(3))
    damages = [damage[:, row, :] for row in (first, second, third)]
    pulls = [strain[c, :, first, :] for c in range(3)]
    pulls_behind = [strain[c, :, second, :] for c in range(3)]
    mus = [
        seed_damage[:, first, :] * mu_inverse(*pulls),
        seed_damage[:, second, :] * mu_inverse(*pulls_behind),
    ]
    sources = [seed_disp[c, :, first, :] for c in range(3)]
    behind = [seed_disp[c, :, second, :] for c in range(3)]
    scale, wy, known = known_of(s, damages, pulls, pulls_behind[1], mus, sources, behind)
    for slot, value in enumerate(damages[:2] + [wy, mus[0], scale] + sources + known):
        put(slot, value)


def high_rows_kernel(
    damage_in, strain_in, seed_in, sources_in, out, token,
    damage, strain, seed_damage, seed_disp, rows, sems, out_sem,
):
    nx = damage.shape[0]
    token[0, 0] = 0.0
    copies = [
        pltpu.make_async_copy(damage_in, damage, sems.at[0]),
        pltpu.make_async_copy(strain_in, strain, sems.at[1]),
        pltpu.make_async_copy(seed_in, seed_damage, sems.at[2]),
        pltpu.make_async_copy(sources_in, seed_disp, sems.at[3]),
    ]
    for copy in copies:
        copy.start()
    for copy in copies:
        copy.wait()

    def put(slot, value):
        rows[slot * nx : (slot + 1) * nx, :] = value

    put_rows(1, put, damage, strain, seed_damage, seed_disp)
    copy = pltpu.make_async_copy(rows, out.at[pl.ds(0, Y_FIELDS * nx)], out_sem)
    copy.start()
    copy.wait()


def even_brick():
    return lax.rem(lax.axis_index("gx"), 2) == 0


def faces_kernel(damage, strain, seed_damage, seed_disp, _, near, far, low):
    nx = damage.shape[0]

    def put(slot, value):
        low[slot * nx : (slot + 1) * nx, :] = value

    put_rows(0, put, damage, strain, seed_damage, seed_disp)
    even = even_brick()
    for out, high in ((near, even), (far, ~even)):

        def planes(count):
            return pl.ds(jnp.where(high, nx - count, 0), count)

        out[X_DAMAGE : X_DAMAGE + 4] = damage[planes(4)]
        sx, sy, sz = (strain[c, planes(3)] for c in range(3))
        out[X_PULL : X_PULL + 3] = sx
        out[X_PULL_Y : X_PULL_Y + 2] = strain[1, planes(2)]
        out[X_PULL_Z : X_PULL_Z + 2] = strain[2, planes(2)]
        out[X_MU : X_MU + 3] = seed_damage[planes(3)] * mu_inverse(sx, sy, sz)
        for c in range(3):
            slot = X_SOURCE + 3 * c
            out[slot : slot + 3] = seed_disp[c, planes(3)]


def received_x(near, far, side):
    from_near = even_brick() == (side == 1)

    def planes(first, count, row=None):
        at = slice(first, first + count) if row is None else (slice(first, first + count), row)
        return jnp.where(from_near, near[at], far[at])

    return planes


def corners_kernel(
    damage, strain, seed_damage, seed_disp, far, near, _, low, high, field
):
    nx, ny, _ = damage.shape
    for s, out in enumerate((low, high)):
        first, second, third = (edge_row(s, ny, depth) for depth in range(3))
        for side in range(2):
            x_in = received_x(near, far, side)
            theirs, ours = (slice(0, 3), slice(3, 8)) if side == 0 else (slice(5, 8), slice(0, 5))
            planes = slice(0, 5) if side == 0 else slice(nx - 5, nx)

            def x_rows(slot, held, row):
                start = slot + (held - 3 if side == 0 else 0)
                return x_in(start, 3, row)

            def x_pair(slot, row):
                return x_in(slot, 2, row)

            for depth, row in enumerate((first, second, third)):
                field[depth, ours, :] = damage[planes, row, :]
                field[depth, theirs, :] = x_rows(X_DAMAGE, 4, row)
            pair = slice(1, 3) if side == 0 else slice(5, 7)
            for depth, row in enumerate((first, second)):
                sx, sy, sz = (strain[c, planes, row, :] for c in range(3))
                if depth == 0:
                    field[3, ours, :] = sx
                    field[3, theirs, :] = x_rows(X_PULL, 3, row)
                    field[5, ours, :] = sz
                    field[5, pair, :] = x_pair(X_PULL_Z, row)
                slot = 4 if depth == 0 else 6
                field[slot, ours, :] = sy
                field[slot, pair, :] = x_pair(X_PULL_Y, row)
                field[7 + depth, ours, :] = seed_damage[planes, row, :] * mu_inverse(sx, sy, sz)
                field[7 + depth, theirs, :] = x_rows(X_MU, 3, row)
                for c in range(3):
                    slot = 9 + 3 * depth + c
                    field[slot, ours, :] = seed_disp[c, planes, row, :]
                    field[slot, theirs, :] = x_rows(X_SOURCE + 3 * c, 3, row)
            got = [field[slot] for slot in range(15)]
            scale, wy, known = known_of(s, got[:3], got[3:6], got[6], got[7:9], got[9:12], got[12:15])
            row = side * CORNER_ROWS
            for slot, value in enumerate(got[:2] + [wy, got[7], scale] + got[9:12]):
                count = Y_ROWS[slot][3]
                start = 3 - count if side == 0 else 5
                out[row : row + count, :] = value[start : start + count, :]
                row += count
            for value in known:
                start = 2 if side == 0 else 4
                out[row : row + 2, :] = value[start : start + 2, :]
                row += 2


def in_grid():
    here = lax.axis_index("gx")
    return here > 0, here < lax.axis_size("gx") - 1


def prepare(first, last, soft, pull, raw, g, k, state0):
    planes, ny, nz = soft.shape
    inside = in_grid()
    lane = lax.broadcasted_iota(jnp.int32, (ny, nz), 1)
    row = lax.broadcasted_iota(jnp.int32, (ny, nz), 0)
    inner = (row > 0) & (row < ny - 1)

    def step(at, _):
        center = soft[at]
        sides = [
            soft[at + 1],
            soft[at - 1],
            pltpu.roll(center, ny - 1, 0),
            pltpu.roll(center, 1, 0),
            lane_up(center, OUTSIDE),
            lane_down(center, OUTSIDE),
        ]
        outside = ((at < HALO) & ~inside[0]) | ((at >= planes - HALO) & ~inside[1])
        inverse = jnp.where(inner & ~outside, lam_inverse(center, sum(sides)), 0.0)
        eighth = 0.125 * inverse
        for j in range(6):
            face = eighth * (center + sides[j])
            if j == 4:
                face = jnp.where(lane == nz - 1, 0.0, face)
            if j == 5:
                face = jnp.where(lane == 0, 0.0, face)
            g[j, at] = face
        k[0, at] = inverse * pull[0, at + 1]
        k[1, at] = -inverse * pull[0, at - 1]
        k[2, at] = inverse * pltpu.roll(pull[1, at], ny - 1, 0)
        k[3, at] = -inverse * pltpu.roll(pull[1, at], 1, 0)
        k[4, at] = inverse * lane_up(pull[2, at], 0.0)
        k[5, at] = -inverse * lane_down(pull[2, at], 0.0)
        for c in range(3):
            state0[1 + c, at] = inverse * raw[c, at]
        return 0

    lax.fori_loop(first, last, step, 0)


def reach_of(grad, count):
    square = sum(part * part for part in grad)
    scale = 1.0 / jnp.maximum(square, NORMAL_FLOOR)
    power = 1.0 - RELAX_RATE * (1.0 + NORMAL_WEIGHT * square * scale)
    series = 1.0 + power
    for _ in range(2):
        power = power * power
        series = series * (1.0 + power)
    power = power * power
    repeats = jnp.ones_like(power)
    for level in range(1, 4):
        repeats = jnp.where(count > level, 1.0 + power * repeats, repeats)
    return (RELAX_RATE * NORMAL_WEIGHT * scale) * (series * repeats)


def slopes(first, last, count, less, grads):
    ny = less.shape[1]

    def step(at, _):
        own = less[at]
        grad = [
            0.5 * (less[at + 1] - less[at - 1]),
            0.5 * (pltpu.roll(own, ny - 1, 0) - pltpu.roll(own, 1, 0)),
            0.5 * (lane_up(own, -1.0) - lane_down(own, -1.0)),
        ]
        for c in range(3):
            grads[c, at - HALO] = grad[c]
        grads[3, at - HALO] = reach_of(grad, count)
        return 0

    lax.fori_loop(first, last, step, 0)


def first_sweep(ranges, state0, state1, g, k, mu_scale):
    (c1, c2), _, _ = weights()

    def advance(at, f, own, moved):
        state1[f, at] = (1.0 + c1) * own + c2 * moved

    for first, last in ranges:
        sweep(first, last, state0, g, k, mu_scale, None, advance)


def inner_kernel(
    work, damage, strain, seed_damage, seed_disp,
    less, soft, pull, mu_scale, raw, g, k, state0, state1, grads,
):
    nx = damage.shape[0]

    def fill(i, _):
        at = HALO + i
        own = damage[i]
        sx, sy, sz = strain[0, i], strain[1, i], strain[2, i]
        soft[at] = soft_of(own)
        own = own - 1.0
        less[at] = own
        pull[0, at] = own * sx
        pull[1, at] = own * sy
        pull[2, at] = own * sz
        mu_inv = mu_inverse(sx, sy, sz)
        mu_scale[at] = 0.25 * mu_inv
        state0[0, at] = mu_inv * seed_damage[i]
        for c in range(3):
            raw[c, at] = seed_disp[c, i]
        return 0

    lax.fori_loop(0, nx, fill, 0)
    low, high = HALO, HALO + nx
    prepare(low + 1, high - 1, soft, pull, raw, g, k, state0)
    slopes(low + 1, high - 1, work[0, 0], less, grads)
    first_sweep([(low + 2, high - 2)], state0, state1, g, k, mu_scale)


def sides_kernel(
    work, far, near, less_in, soft_in, pull_in, scale_in, raw_in, g_in, k_in, state0_in, state1_in, grads_in,
    less, soft, pull, mu_scale, raw, g, k, state0, state1, grads,
):
    nx = soft.shape[0] - 2 * HALO
    inside = in_grid()
    for s in range(2):
        x_in = received_x(near, far, s)

        def planes(count):
            first = HALO - count if s == 0 else HALO + nx
            return slice(first, first + count)

        def nearest(slot, held, count):
            return x_in(slot + (held - count if s == 0 else 0), count)

        soft[planes(4)] = soft_of(nearest(X_DAMAGE, 4, 4))
        less[planes(1)] = nearest(X_DAMAGE, 4, 1) - 1.0
        pull[0, planes(3)] = (nearest(X_DAMAGE, 4, 3) - 1.0) * nearest(X_PULL, 3, 3)
        own = nearest(X_DAMAGE, 4, 2) - 1.0
        sx, sy, sz = nearest(X_PULL, 3, 2), nearest(X_PULL_Y, 2, 2), nearest(X_PULL_Z, 2, 2)
        pull[1, planes(2)] = own * sy
        pull[2, planes(2)] = own * sz
        mu_scale[planes(2)] = jnp.where(inside[s], 0.25 * mu_inverse(sx, sy, sz), 0.0)
        state0[0, planes(3)] = nearest(X_MU, 3, 3)
        for c in range(3):
            raw[c, planes(3)] = nearest(X_SOURCE + 3 * c, 3, 3)

    low, high = HALO, HALO + nx
    for first, last in ((low - 3, low + 1), (high - 1, high + 3)):
        prepare(first, last, soft, pull, raw, g, k, state0)
    for first, last in ((low, low + 1), (high - 1, high)):
        slopes(first, last, work[0, 0], less, grads)
    first_sweep([(low - 2, low + 2), (high - 2, high + 2)], state0, state1, g, k, mu_scale)


def edges_kernel(
    soft, pull, mu_scale, raw, g, state0, state1, y_low, y_high, c_low, c_high,
    sy_low, sy_high, coefficients, firsts, seconds, outer,
    field,
):
    planes, ny, nz = soft.shape
    nx = planes - 2 * HALO
    (c1, c2), (d1, d2), _ = weights()
    lane = lax.broadcasted_iota(jnp.int32, (planes, nz), 1)
    plane = lax.broadcasted_iota(jnp.int32, (planes, nz), 0)
    here, there = lax.axis_index("gx"), lax.axis_index("gy")
    in_x = ((plane >= HALO) | (here > 0)) & ((plane < HALO + nx) | (here < lax.axis_size("gx") - 1))
    in_y = (there > 0, there < lax.axis_size("gy") - 1)

    def around_x(value):
        return [pltpu.roll(value, planes - 1, 0), pltpu.roll(value, 1, 0)]

    def around_z(value, fill):
        return [lane_up(value, fill), lane_down(value, fill)]

    for s, (y_in, c_in, sent) in enumerate(((y_low, c_low, sy_low), (y_high, c_high, sy_high))):
        e0, e1 = edge_row(s, ny, 0), edge_row(s, ny, 1)

        def ordered(inward, outward):
            return [inward, outward] if s == 0 else [outward, inward]

        row = 0
        for f in range(Y_FIELDS):
            field[f, HALO : HALO + nx, :] = y_in[f * nx : (f + 1) * nx, :]
            count, shift = (Y_ROWS[f][3], 0) if f < Y_KNOWN else (2, 1)
            field[f, HALO - count + shift : HALO + shift, :] = c_in[row : row + count, :]
            high = HALO + nx - shift
            field[f, high : high + count, :] = c_in[CORNER_ROWS + row : CORNER_ROWS + row + count, :]
            row += count

        soft_1, soft_2 = soft_of(field[0]), soft_of(field[1])
        soft_e0, soft_e1 = soft[:, e0, :], soft[:, e1, :]

        def total(center, inward, outward):
            return sum(around_x(center) + [inward, outward] + around_z(center, OUTSIDE))

        inverse_1 = lam_inverse(soft_1, total(soft_1, soft_e0, soft_2))
        inverse_1 = jnp.where(in_x & in_y[s], inverse_1, 0.0)
        lam_1 = [inverse_1 * field[5 + c] for c in range(3)]
        inverse_e0 = jnp.where(in_x, lam_inverse(soft_e0, total(soft_e0, soft_e1, soft_1)), 0.0)
        lam_e0 = [inverse_e0 * raw[c, :, e0, :] for c in range(3)]
        mu_1, wy_1 = field[3], field[2]
        mu_e0, mu_e1 = state0[0, :, e0, :], state0[0, :, e1, :]
        lam_e1 = [state0[1 + c, :, e1, :] for c in range(3)]

        def coefficients_of(center, inverse, inward, outward, wx, wy, wz):
            sides = around_x(center) + ordered(inward, outward) + around_z(center, OUTSIDE)
            eighth = 0.125 * inverse
            faces = [eighth * (center + side) for side in sides]
            faces[4] = jnp.where(lane == nz - 1, 0.0, faces[4])
            faces[5] = jnp.where(lane == 0, 0.0, faces[5])
            pulls = around_x(wx) + wy + around_z(wz, 0.0)
            return faces, [inverse * w if j % 2 == 0 else -inverse * w for j, w in enumerate(pulls)]

        def moved_of(faces, pulls, scale, own, inward, outward):
            sides = [
                around_x(own[f]) + ordered(inward[f], outward[f]) + around_z(own[f], 0.0) for f in range(4)
            ]
            moved = [scale * sum(sides[0])]
            for c in range(3):
                part = sum(faces[j] * sides[1 + c][j] for j in range(6))
                moved.append(part + pulls[2 * c] * sides[0][2 * c] + pulls[2 * c + 1] * sides[0][2 * c + 1])
            return moved

        first_1 = [jnp.where(in_x, field[Y_KNOWN] + c2 * field[4] * mu_e0, 0.0)]
        sides = around_x(soft_1) + around_z(soft_1, OUTSIDE) + [soft_e0]
        faces = [0.125 * (soft_1 + side) for side in sides]
        wy_e0 = pull[1, :, e0, :] * mu_e0
        own_1 = [mu_1] + lam_1
        own_e0 = [mu_e0] + lam_e0
        for c in range(3):
            sides = around_x(lam_1[c]) + around_z(lam_1[c], 0.0) + [lam_e0[c]]
            lacked = sum(faces[j] * sides[j] for j in range(5))
            if c == 1:
                lacked += wy_e0 if s == 0 else -wy_e0
            first_1.append(inverse_1 * (field[Y_KNOWN + 1 + c] + c2 * lacked))

        scale_e0 = mu_scale[:, e0, :]
        wy = ordered(pull[1, :, e1, :], wy_1)
        faces, pulls = coefficients_of(
            soft_e0, inverse_e0, soft_e1, soft_1, pull[0, :, e0, :], wy, pull[2, :, e0, :]
        )
        moved = moved_of(faces, pulls, scale_e0, own_e0, [mu_e1] + lam_e1, own_1)
        first_e0 = [(1.0 + c1) * own_e0[f] + c2 * moved[f] for f in range(4)]

        outward_face = g[3 if s == 0 else 2, :, e1, :]
        first_e1 = [state1[0, :, e1, :]]
        for c in range(3):
            first_e1.append(state1[1 + c, :, e1, :] + c2 * outward_face * lam_e0[c])

        moved = moved_of(faces, pulls, scale_e0, first_e0, first_e1, first_1)
        for f in range(4):
            second = first_e0[f] + (d1 - d2) * (first_e0[f] - own_e0[f]) + d2 * moved[f]
            sent[f * nx : (f + 1) * nx, :] = second[HALO : HALO + nx, :]
            firsts[s, f] = first_e0[f]
            outer[s, f] = first_1[f]
        for j in range(6):
            coefficients[s, j] = faces[j]
            coefficients[s, 6 + j] = pulls[j]
        for c in range(3):
            coefficients[s, 12 + c] = lam_e0[c]
            seconds[s, c] = first_e1[1 + c]


def sweep(first, last, state, g, k, mu_scale, rows, advance, finish=None):
    _, ny, nz = mu_scale.shape
    lane = lax.broadcasted_iota(jnp.int32, (ny, nz), 1)
    if rows is None:

        def rows(s, f, at):
            return 0.0

    def plane(at, _):
        def around(f):
            own = state[f, at]
            return own, [
                state[f, at + 1],
                state[f, at - 1],
                row_up(own, rows(1, f, at)),
                row_down(own, rows(0, f, at)),
                pltpu.roll(own, nz - 1, 1),
                pltpu.roll(own, 1, 1),
            ]

        mu, mu_sides = around(0)
        ends = [
            jnp.where(lane == nz - 1, 0.0, mu_sides[4]),
            jnp.where(lane == 0, 0.0, mu_sides[5]),
        ]
        results = [advance(at, 0, mu, mu_scale[at] * sum(mu_sides[:4] + ends))]
        faces = [g[j, at] for j in range(6)]
        for c in range(3):
            lam, lam_sides = around(1 + c)
            moved = sum(faces[j] * lam_sides[j] for j in range(6))
            moved += k[2 * c, at] * mu_sides[2 * c] + k[2 * c + 1, at] * mu_sides[2 * c + 1]
            results.append(advance(at, 1 + c, lam, moved))
        if finish is not None:
            finish(at - HALO, results)
        return 0

    lax.fori_loop(first, last, plane, 0)


def wait_kernel(
    work, less, grads, y_low, y_high,
    mu_scale, coefficients, firsts, seconds, outer, g_in, k_in, state0_in, state1_in,
    out_mu, out_lam, edges, g, k, state0, state1,
    state2, states,
):
    _, nx, ny, _ = grads.shape
    planes = nx + 2 * HALO
    _, (d1, d2), (c1, c2) = weights()
    held = slice(HALO - 2, HALO + nx + 2)
    for s in range(2):
        e0, e1 = edge_row(s, ny, 0), edge_row(s, ny, 1)
        for j in range(6):
            g[j, held, e0, :] = coefficients[s, j, held, :]
            k[j, held, e0, :] = coefficients[s, 6 + j, held, :]
        for c in range(3):
            state0[1 + c, held, e0, :] = coefficients[s, 12 + c, held, :]
            state1[1 + c, held, e1, :] = seconds[s, c, held, :]
        for f in range(4):
            state1[f, held, e0, :] = firsts[s, f, held, :]

    def rows(s, f, at):
        return outer[s, f, pl.ds(at, 1), :]

    def advance_2(at, f, own, moved):
        state2[f, at] = own + (d1 - d2) * (own - state0[f, at]) + d2 * moved

    sweep(HALO - 1, HALO + nx + 1, state1, g, k, mu_scale, rows, advance_2)

    def advance_3(at, f, own, moved):
        return own + c1 * (own - state1[f, at]) + c2 * (state0[f, at] - own + moved)

    def finish(i, results):
        out_mu[i] = results[0]
        along = grads[3, i] * sum(grads[c, i] * results[1 + c] for c in range(3))
        for c in range(3):
            out_lam[c, i] = results[1 + c] - along * grads[c, i]
            states[c, i] = results[1 + c]

    sweep(HALO, HALO + nx, state2, g, k, mu_scale, None, advance_3, finish)

    for s, y_in in enumerate((y_low, y_high)):
        e0, e1 = edge_row(s, ny, 0), edge_row(s, ny, 1)
        own = less[HALO : HALO + nx, e0, :]
        inward, outward = less[HALO : HALO + nx, e1, :], y_in[0:nx, :] - 1.0
        grad = [
            0.5 * (less[HALO + 1 : HALO + nx + 1, e0, :] - less[HALO - 1 : HALO + nx - 1, e0, :]),
            0.5 * (inward - outward if s == 0 else outward - inward),
            0.5 * (lane_up(own, -1.0) - lane_down(own, -1.0)),
        ]
        for c in range(3):
            edges[s, c] = grad[c]
            edges[s, 4 + c] = states[c, :, e0, :]
        edges[s, 3] = reach_of(grad, work[0, 0])


def last_kernel(
    mu_scale, coefficients, edges, y_low, y_high, mu_in, lam_in,
    out_mu, out_lam, mu, lam,
    sems,
):
    nx, ny, nz = mu.shape
    inner = slice(HALO, HALO + nx)
    _, _, (_, c2) = weights()
    for s, y_in in enumerate((y_low, y_high)):
        e0 = edge_row(s, ny, 0)
        outward = 3 if s == 0 else 2

        def got(f):
            return y_in[f * nx : (f + 1) * nx, :]

        mu[:, e0, :] = mu[:, e0, :] + c2 * mu_scale[inner, e0, :] * got(0)
        face = c2 * coefficients[s, outward, inner, :]
        ends = []
        for c in range(3):
            end = edges[s, 4 + c] + face * got(1 + c)
            if c == 1:
                end += c2 * coefficients[s, 6 + outward, inner, :] * got(0)
            ends.append(end)
        along = edges[s, 3] * sum(edges[s, c] * ends[c] for c in range(3))
        for c in range(3):
            lam[c, :, e0, :] = ends[c] - along * edges[s, c]
    copies = [
        pltpu.make_async_copy(mu, out_mu, sems.at[0]),
        pltpu.make_async_copy(lam, out_lam, sems.at[1]),
    ]
    for copy in copies:
        copy.start()
    for copy in copies:
        copy.wait()


VMEM = pl.BlockSpec(memory_space=pltpu.VMEM)
SMEM = pl.BlockSpec(memory_space=pltpu.SMEM)
HBM = pl.BlockSpec(memory_space=pltpu.HBM)
ANY = pl.BlockSpec(memory_space=pl.ANY)
MIB = 1024 * 1024


def call(kernel, ins, outs, scratch=(), in_specs=None, out_specs=None, aliases=None, grant=24 * MIB):
    return pl.pallas_call(
        kernel,
        out_shape=[jax.ShapeDtypeStruct(shape, F32) for shape in outs],
        in_specs=in_specs or [VMEM] * len(ins),
        out_specs=out_specs or [VMEM] * len(outs),
        scratch_shapes=[pltpu.VMEM(shape, F32) if isinstance(shape, tuple) else shape for shape in scratch],
        input_output_aliases=aliases or {},
        compiler_params=pltpu.CompilerParams(vmem_limit_bytes=grant),
    )(*ins)


def send_up(high, axis):
    return lax.ppermute(high, axis, [(i, i + 1) for i in range(lax.axis_size(axis) - 1)])


def send_down(low, axis):
    return lax.ppermute(low, axis, [(i + 1, i) for i in range(lax.axis_size(axis) - 1)])


def swap(low, high, axis):
    return send_up(high, axis), send_down(low, axis)


def body(damage, strain, seed_damage, seed_disp, brick_work):
    nx, ny, nz = damage.shape
    plane = (ny, nz)
    brick = (nx,) + plane
    bricks = (3,) + brick
    framed = (nx + 2 * HALO,) + plane
    state = (4,) + framed
    row = (nx + 2 * HALO, nz)
    fields = (damage, strain, seed_damage, seed_disp)

    y_rows = (Y_FIELDS * nx, nz)
    high, token = call(
        high_rows_kernel, fields, [((Y_FIELDS + Y_SPARE) * nx, nz), (1, 1)],
        [brick, bricks, brick, bricks, y_rows, pltpu.SemaphoreType.DMA((4,)), pltpu.SemaphoreType.DMA],
        in_specs=[HBM] * 4, out_specs=[HBM, SMEM], grant=56 * MIB,
    )
    y_up = send_up(high, "gy")
    near, far, low = call(
        faces_kernel, fields + (token,), [(X_SLOTS,) + plane] * 2 + [y_rows], in_specs=[VMEM] * 4 + [SMEM]
    )
    y_in = (y_up, send_down(low, "gy"))
    last = lax.axis_size("gx")
    pairs = [(i, i + 1) for i in range(0, last - 1, 2)]
    near = lax.ppermute(near, "gx", pairs + [(j, i) for i, j in pairs])
    pairs = [(i, i + 1) for i in range(1, last - 1, 2)]
    far = lax.ppermute(far, "gx", pairs + [(j, i) for i, j in pairs])
    x_in = (far, near)
    work = brick_work
    inner = tuple(call(
        inner_kernel, (work,) + fields,
        [framed, framed, (3,) + framed, framed, (3,) + framed]
        + [(6,) + framed, (6,) + framed, state, state, (4,) + brick],
        in_specs=[SMEM] + [VMEM] * 4,
    ))
    c_pair = call(
        corners_kernel, fields + x_in + (inner[0],), [(2 * CORNER_ROWS, nz)] * 2, [(15,) + plane],
        in_specs=[VMEM] * 6 + [ANY],
    )
    c_in = swap(*c_pair, "gy")
    less, soft, pull, mu_scale, raw, g, k, state0, state1, grads = call(
        sides_kernel, (work,) + x_in + inner, [part.shape for part in inner],
        in_specs=[SMEM] + [VMEM] * 12, aliases={3 + part: part for part in range(10)},
    )
    low, high, coefficients, firsts, seconds, outer = call(
        edges_kernel, (soft, pull, mu_scale, raw, g, state0, state1) + y_in + c_in,
        [(4 * nx, nz)] * 2 + [(2, 15) + row, (2, 4) + row, (2, 3) + row, (2, 4) + row],
        [(Y_FIELDS,) + row],
    )
    halo = swap(low, high, "gy")
    ins = (work, less, grads) + y_in + (mu_scale, coefficients, firsts, seconds, outer, g, k, state0, state1)
    mu, lam, edges, *_ = call(
        wait_kernel, ins,
        [brick, bricks, (2, 7, nx, nz), (6,) + framed, (6,) + framed, state, state],
        [state, bricks],
        in_specs=[SMEM] + [VMEM] * (len(ins) - 1),
        aliases={10: 3, 11: 4, 12: 5, 13: 6},
    )
    out_mu, out_lam, *_ = call(
        last_kernel, (mu_scale, coefficients, edges) + halo + (mu, lam),
        [brick, bricks, brick, bricks], [pltpu.SemaphoreType.DMA((2,))],
        out_specs=[HBM, HBM, VMEM, VMEM], aliases={5: 2, 6: 3},
    )
    return out_mu, out_lam


def solution(mesh):
    placed = (
        P("gx", "gy", None),
        P(None, "gx", "gy", None),
        P("gx", "gy", None),
        P(None, "gx", "gy", None),
        P("gx", "gy"),
    )
    return jax.shard_map(
        body,
        mesh=mesh,
        in_specs=placed,
        out_specs=(P("gx", "gy", None), P(None, "gx", "gy", None)),
        check_vma=False,
    )
```

```python
import functools

import jax
import jax.numpy as jnp
from jax import lax
from jax.experimental import pallas as pl
from jax.experimental.pallas import tpu as pltpu
from jax.sharding import PartitionSpec as P

RELAX_INNER = 8
RESIDUAL_STIFFNESS = 0.001
CENTER_VALUE = 1.0
HALF_WIDTH = 0.75
NORMAL_WEIGHT = 1.5
RELAX_RATE = 0.5 / RELAX_INNER
NORMAL_FLOOR = 0.05
OUTSIDE = 1.0 + RESIDUAL_STIFFNESS
F32 = jnp.float32


def weights():
    ratio = CENTER_VALUE / HALF_WIDTH
    rho = 1.0 / ratio
    found = []
    for _ in range(3):
        rho_next = 1.0 / (2.0 * ratio - rho)
        found.append((rho_next * rho, 2.0 * rho_next / HALF_WIDTH))
        rho = rho_next
    return found


def soft_of(damage):
    return (1.0 - damage) ** 2 + RESIDUAL_STIFFNESS


def row_up(plane, beyond):
    rows = plane.shape[0]
    at = lax.broadcasted_iota(jnp.int32, plane.shape, 0)
    return jnp.where(at == rows - 1, beyond, pltpu.roll(plane, rows - 1, 0))


def row_down(plane, beyond):
    at = lax.broadcasted_iota(jnp.int32, plane.shape, 0)
    return jnp.where(at == 0, beyond, pltpu.roll(plane, 1, 0))


def lane_up(plane, beyond):
    cells = plane.shape[1]
    at = lax.broadcasted_iota(jnp.int32, plane.shape, 1)
    return jnp.where(at == cells - 1, beyond, pltpu.roll(plane, cells - 1, 1))


def lane_down(plane, beyond):
    at = lax.broadcasted_iota(jnp.int32, plane.shape, 1)
    return jnp.where(at == 0, beyond, pltpu.roll(plane, 1, 1))


def mu_inverse(ex, ey, ez):
    return 1.0 / (2.0 + (ex * ex + ey * ey + ez * ez))


def lam_inverse(center, total):
    return 1.0 / (0.5 + 0.125 * (6.0 * center + total))


HALO = 4
X_DAMAGE, X_PULL, X_PULL_Y, X_PULL_Z, X_MU, X_SOURCE, X_SLOTS = 0, 4, 7, 9, 11, 14, 23
NEAR_CUT, FAR_CUT = 17, 11
Y_ROWS = (
    (X_DAMAGE, 4, 0, 3),
    (X_DAMAGE, 4, 1, 2),
    (None, 2, 0, 2),
    (X_MU, 3, 0, 2),
    (None, 2, 0, 1),
    (X_SOURCE, 3, 0, 2),
    (X_SOURCE + 3, 3, 0, 2),
    (X_SOURCE + 6, 3, 0, 2),
)
Y_KNOWN, Y_FIELDS = 8, 12
CORNER_ROWS = sum(entry[3] for entry in Y_ROWS) + 8


def edge_row(s, ny, depth):
    return depth if s == 0 else ny - 1 - depth


def known_of(s, damages, pulls, behind_pull, mus, sources, behind):
    planes = damages[0].shape[0]
    (c1, c2), _, _ = weights()
    soft = [soft_of(part) for part in damages]
    less = damages[0] - 1.0
    wx, wy, wz = (less * pull for pull in pulls)
    wy_behind = (damages[1] - 1.0) * behind_pull

    def across(value):
        return pltpu.roll(value, planes - 1, 0), pltpu.roll(value, 1, 0)

    def along(value, fill):
        return lane_up(value, fill), lane_down(value, fill)

    total = soft[0] + soft[2] + sum(across(soft[1])) + sum(along(soft[1], OUTSIDE))
    inverse = lam_inverse(soft[1], total)
    face = 0.125 * (soft[0] + soft[1])
    scale = 0.25 * mu_inverse(*pulls)
    known = [(1.0 + c1) * mus[0] + c2 * scale * (mus[1] + sum(across(mus[0])) + sum(along(mus[0], 0.0)))]
    x_up, x_down = across(wx * mus[0])
    z_up, z_down = along(wz * mus[0], 0.0)
    y_behind = wy_behind * mus[1]
    transfers = (x_up - x_down, y_behind if s == 0 else -y_behind, z_up - z_down)
    for c in range(3):
        known.append((1.0 + c1) * sources[c] + c2 * (face * (inverse * behind[c]) + transfers[c]))
    return scale, wy, known


def put_rows(s, put, damage, strain, seed_damage, seed_disp):
    ny = damage.shape[1]
    first, second, third = (edge_row(s, ny, depth) for depth in range(3))
    damages = [damage[:, row, :] for row in (first, second, third)]
    pulls = [strain[c, :, first, :] for c in range(3)]
    pulls_behind = [strain[c, :, second, :] for c in range(3)]
    mus = [
        seed_damage[:, first, :] * mu_inverse(*pulls),
        seed_damage[:, second, :] * mu_inverse(*pulls_behind),
    ]
    sources = [seed_disp[c, :, first, :] for c in range(3)]
    behind = [seed_disp[c, :, second, :] for c in range(3)]
    scale, wy, known = known_of(s, damages, pulls, pulls_behind[1], mus, sources, behind)
    for slot, value in enumerate(damages[:2] + [wy, mus[0], scale] + sources + known):
        put(slot, value)


def even(axis):
    return lax.rem(lax.axis_index(axis), 2) == 0


def pal_rows_kernel(
    damage_in, strain_in, seed_in, sources_in, out, token,
    damage, strain, seed_damage, seed_disp, rows, sems, out_sem,
):
    nx = damage.shape[0]
    token[0, 0] = 0.0
    copies = [
        pltpu.make_async_copy(damage_in, damage, sems.at[0]),
        pltpu.make_async_copy(strain_in, strain, sems.at[1]),
        pltpu.make_async_copy(seed_in, seed_damage, sems.at[2]),
        pltpu.make_async_copy(sources_in, seed_disp, sems.at[3]),
    ]
    for copy in copies:
        copy.start()
    for copy in copies:
        copy.wait()

    def put(slot, value):
        rows[slot * nx : (slot + 1) * nx, :] = value

    for s in range(2):

        @pl.when(even("gy") == (s == 1))
        def _():
            put_rows(s, put, damage, strain, seed_damage, seed_disp)

    copy = pltpu.make_async_copy(rows, out, out_sem)
    copy.start()
    copy.wait()


def faces_kernel(damage, strain, seed_damage, seed_disp, _, near_1, near_2, far_1, far_2, rows):
    nx = damage.shape[0]

    def put(slot, value):
        rows[slot * nx : (slot + 1) * nx, :] = value

    for s in range(2):

        @pl.when(even("gy") == (s == 0))
        def _():
            put_rows(s, put, damage, strain, seed_damage, seed_disp)

    for parts, cut, high in (((near_2, near_1), NEAR_CUT, even("gx")), ((far_1, far_2), FAR_CUT, ~even("gx"))):

        def put_planes(first, value):
            out, first = (parts[0], first) if first < cut else (parts[1], first - cut)
            out[first : first + value.shape[0]] = value

        def planes(count):
            return pl.ds(jnp.where(high, nx - count, 0), count)

        sx, sy, sz = (strain[c, planes(3)] for c in range(3))
        put_planes(X_DAMAGE, damage[planes(4)])
        put_planes(X_PULL, sx)
        put_planes(X_PULL_Y, strain[1, planes(2)])
        put_planes(X_PULL_Z, strain[2, planes(2)])
        put_planes(X_MU, seed_damage[planes(3)] * mu_inverse(sx, sy, sz))
        for c in range(3):
            put_planes(X_SOURCE + 3 * c, seed_disp[c, planes(3)])


def received_x(near_1, near_2, far_1, far_2, side):
    from_near = even("gx") == (side == 1)

    def part(lower, upper, cut, first, count, row):
        held, first = (lower, first) if first < cut else (upper, first - cut)
        planes = slice(first, first + count)
        return held[planes] if row is None else held[planes, row]

    def planes(first, count, row=None):
        near = part(near_2, near_1, NEAR_CUT, first, count, row)
        return jnp.where(from_near, near, part(far_1, far_2, FAR_CUT, first, count, row))

    return planes


def received_y(pal, other, side):
    from_pal = even("gy") == (side == 1)
    return lambda first, count: jnp.where(from_pal, pal[first : first + count, :], other[first : first + count, :])


def deal(pal, other, low, high):
    first = even("gy")
    low, high = low[...], high[...]
    pal[...] = jnp.where(first, high, low)
    other[...] = jnp.where(first, low, high)


def corners_kernel(
    damage, strain, seed_damage, seed_disp, near_1, near_2, far_1, far_2, _, pal, other, field, low, high
):
    nx, ny, _ = damage.shape
    for s, out in enumerate((low, high)):
        first, second, third = (edge_row(s, ny, depth) for depth in range(3))
        for side in range(2):
            x_in = received_x(near_1, near_2, far_1, far_2, side)
            theirs, ours = (slice(0, 3), slice(3, 8)) if side == 0 else (slice(5, 8), slice(0, 5))
            planes = slice(0, 5) if side == 0 else slice(nx - 5, nx)

            def x_rows(slot, held, row):
                start = slot + (held - 3 if side == 0 else 0)
                return x_in(start, 3, row)

            def x_pair(slot, row):
                return x_in(slot, 2, row)

            for depth, row in enumerate((first, second, third)):
                field[depth, ours, :] = damage[planes, row, :]
                field[depth, theirs, :] = x_rows(X_DAMAGE, 4, row)
            pair = slice(1, 3) if side == 0 else slice(5, 7)
            for depth, row in enumerate((first, second)):
                sx, sy, sz = (strain[c, planes, row, :] for c in range(3))
                if depth == 0:
                    field[3, ours, :] = sx
                    field[3, theirs, :] = x_rows(X_PULL, 3, row)
                    field[5, ours, :] = sz
                    field[5, pair, :] = x_pair(X_PULL_Z, row)
                slot = 4 if depth == 0 else 6
                field[slot, ours, :] = sy
                field[slot, pair, :] = x_pair(X_PULL_Y, row)
                field[7 + depth, ours, :] = seed_damage[planes, row, :] * mu_inverse(sx, sy, sz)
                field[7 + depth, theirs, :] = x_rows(X_MU, 3, row)
                for c in range(3):
                    slot = 9 + 3 * depth + c
                    field[slot, ours, :] = seed_disp[c, planes, row, :]
                    field[slot, theirs, :] = x_rows(X_SOURCE + 3 * c, 3, row)
            got = [field[slot] for slot in range(15)]
            scale, wy, known = known_of(s, got[:3], got[3:6], got[6], got[7:9], got[9:12], got[12:15])
            row = side * CORNER_ROWS
            for slot, value in enumerate(got[:2] + [wy, got[7], scale] + got[9:12]):
                count = Y_ROWS[slot][3]
                start = 3 - count if side == 0 else 5
                out[row : row + count, :] = value[start : start + count, :]
                row += count
            for value in known:
                start = 2 if side == 0 else 4
                out[row : row + 2, :] = value[start : start + 2, :]
                row += 2
    deal(pal, other, low, high)


def in_grid():
    here = lax.axis_index("gx")
    return here > 0, here < lax.axis_size("gx") - 1


def prepare(first, last, soft, pull, raw, g, k, state0):
    planes, ny, nz = soft.shape
    inside = in_grid()
    lane = lax.broadcasted_iota(jnp.int32, (ny, nz), 1)
    row = lax.broadcasted_iota(jnp.int32, (ny, nz), 0)
    inner = (row > 0) & (row < ny - 1)

    def step(at, _):
        center = soft[at]
        sides = [
            soft[at + 1],
            soft[at - 1],
            pltpu.roll(center, ny - 1, 0),
            pltpu.roll(center, 1, 0),
            lane_up(center, OUTSIDE),
            lane_down(center, OUTSIDE),
        ]
        outside = ((at < HALO) & ~inside[0]) | ((at >= planes - HALO) & ~inside[1])
        inverse = jnp.where(inner & ~outside, lam_inverse(center, sum(sides)), 0.0)
        eighth = 0.125 * inverse
        for j in range(6):
            face = eighth * (center + sides[j])
            if j == 4:
                face = jnp.where(lane == nz - 1, 0.0, face)
            if j == 5:
                face = jnp.where(lane == 0, 0.0, face)
            g[j, at] = face
        k[0, at] = inverse * pull[0, at + 1]
        k[1, at] = -inverse * pull[0, at - 1]
        k[2, at] = inverse * pltpu.roll(pull[1, at], ny - 1, 0)
        k[3, at] = -inverse * pltpu.roll(pull[1, at], 1, 0)
        k[4, at] = inverse * lane_up(pull[2, at], 0.0)
        k[5, at] = -inverse * lane_down(pull[2, at], 0.0)
        for c in range(3):
            state0[1 + c, at] = inverse * raw[c, at]
        return 0

    lax.fori_loop(first, last, step, 0)


def reach_of(grad, count):
    square = sum(part * part for part in grad)
    scale = 1.0 / jnp.maximum(square, NORMAL_FLOOR)
    power = 1.0 - RELAX_RATE * (1.0 + NORMAL_WEIGHT * square * scale)
    series = 1.0 + power
    for _ in range(2):
        power = power * power
        series = series * (1.0 + power)
    power = power * power
    repeats = jnp.ones_like(power)
    for level in range(1, 4):
        repeats = jnp.where(count > level, 1.0 + power * repeats, repeats)
    return (RELAX_RATE * NORMAL_WEIGHT * scale) * (series * repeats)


def slopes(first, last, count, less, grads):
    ny = less.shape[1]

    def step(at, _):
        own = less[at]
        grad = [
            0.5 * (less[at + 1] - less[at - 1]),
            0.5 * (pltpu.roll(own, ny - 1, 0) - pltpu.roll(own, 1, 0)),
            0.5 * (lane_up(own, -1.0) - lane_down(own, -1.0)),
        ]
        for c in range(3):
            grads[c, at - HALO] = grad[c]
        grads[3, at - HALO] = reach_of(grad, count)
        return 0

    lax.fori_loop(first, last, step, 0)


def first_sweep(ranges, state0, state1, g, k, mu_scale):
    (c1, c2), _, _ = weights()

    def advance(at, f, own, moved):
        state1[f, at] = (1.0 + c1) * own + c2 * moved

    for first, last in ranges:
        sweep(first, last, state0, g, k, mu_scale, None, advance)


def inner_kernel(
    work, damage, strain, seed_damage, seed_disp,
    less, soft, pull, mu_scale, raw, g, k, state0, state1, grads,
):
    nx = damage.shape[0]

    def fill(i, _):
        at = HALO + i
        own = damage[i]
        sx, sy, sz = strain[0, i], strain[1, i], strain[2, i]
        soft[at] = soft_of(own)
        own = own - 1.0
        less[at] = own
        pull[0, at] = own * sx
        pull[1, at] = own * sy
        pull[2, at] = own * sz
        mu_inv = mu_inverse(sx, sy, sz)
        mu_scale[at] = 0.25 * mu_inv
        state0[0, at] = mu_inv * seed_damage[i]
        for c in range(3):
            raw[c, at] = seed_disp[c, i]
        return 0

    lax.fori_loop(0, nx, fill, 0)
    low, high = HALO, HALO + nx
    prepare(low + 1, high - 1, soft, pull, raw, g, k, state0)
    slopes(low + 1, high - 1, work[...], less, grads)
    first_sweep([(low + 2, high - 2)], state0, state1, g, k, mu_scale)


def sides_kernel(
    work, near_1, near_2, far_1, far_2, less_in, soft_in, pull_in, scale_in, raw_in, g_in, k_in, state0_in, state1_in, grads_in,
    less, soft, pull, mu_scale, raw, g, k, state0, state1, grads,
):
    nx = soft.shape[0] - 2 * HALO
    inside = in_grid()
    for s in range(2):
        x_in = received_x(near_1, near_2, far_1, far_2, s)

        def planes(count):
            first = HALO - count if s == 0 else HALO + nx
            return slice(first, first + count)

        def nearest(slot, held, count):
            return x_in(slot + (held - count if s == 0 else 0), count)

        soft[planes(4)] = soft_of(nearest(X_DAMAGE, 4, 4))
        less[planes(1)] = nearest(X_DAMAGE, 4, 1) - 1.0
        pull[0, planes(3)] = (nearest(X_DAMAGE, 4, 3) - 1.0) * nearest(X_PULL, 3, 3)
        own = nearest(X_DAMAGE, 4, 2) - 1.0
        sx, sy, sz = nearest(X_PULL, 3, 2), nearest(X_PULL_Y, 2, 2), nearest(X_PULL_Z, 2, 2)
        pull[1, planes(2)] = own * sy
        pull[2, planes(2)] = own * sz
        mu_scale[planes(2)] = jnp.where(inside[s], 0.25 * mu_inverse(sx, sy, sz), 0.0)
        state0[0, planes(3)] = nearest(X_MU, 3, 3)
        for c in range(3):
            raw[c, planes(3)] = nearest(X_SOURCE + 3 * c, 3, 3)

    low, high = HALO, HALO + nx
    for first, last in ((low - 3, low + 1), (high - 1, high + 3)):
        prepare(first, last, soft, pull, raw, g, k, state0)
    for first, last in ((low, low + 1), (high - 1, high)):
        slopes(first, last, work[...], less, grads)
    first_sweep([(low - 2, low + 2), (high - 2, high + 2)], state0, state1, g, k, mu_scale)


def edges_kernel(
    soft, pull, mu_scale, raw, g, state0, state1, y_pal, y_other, c_pal, c_other,
    sent_pal, sent_other, coefficients, firsts, seconds, outer,
    field, sent_low, sent_high,
):
    planes, ny, nz = soft.shape
    nx = planes - 2 * HALO
    (c1, c2), (d1, d2), _ = weights()
    lane = lax.broadcasted_iota(jnp.int32, (planes, nz), 1)
    plane = lax.broadcasted_iota(jnp.int32, (planes, nz), 0)
    here, there = lax.axis_index("gx"), lax.axis_index("gy")
    in_x = ((plane >= HALO) | (here > 0)) & ((plane < HALO + nx) | (here < lax.axis_size("gx") - 1))
    in_y = (there > 0, there < lax.axis_size("gy") - 1)

    def around_x(value):
        return [pltpu.roll(value, planes - 1, 0), pltpu.roll(value, 1, 0)]

    def around_z(value, fill):
        return [lane_up(value, fill), lane_down(value, fill)]

    for s, sent in enumerate((sent_low, sent_high)):
        y_in, c_in = received_y(y_pal, y_other, s), received_y(c_pal, c_other, s)
        e0, e1 = edge_row(s, ny, 0), edge_row(s, ny, 1)

        def ordered(inward, outward):
            return [inward, outward] if s == 0 else [outward, inward]

        row = 0
        for f in range(Y_FIELDS):
            field[f, HALO : HALO + nx, :] = y_in(f * nx, nx)
            count, shift = (Y_ROWS[f][3], 0) if f < Y_KNOWN else (2, 1)
            field[f, HALO - count + shift : HALO + shift, :] = c_in(row, count)
            high = HALO + nx - shift
            field[f, high : high + count, :] = c_in(CORNER_ROWS + row, count)
            row += count

        soft_1, soft_2 = soft_of(field[0]), soft_of(field[1])
        soft_e0, soft_e1 = soft[:, e0, :], soft[:, e1, :]

        def total(center, inward, outward):
            return sum(around_x(center) + [inward, outward] + around_z(center, OUTSIDE))

        inverse_1 = lam_inverse(soft_1, total(soft_1, soft_e0, soft_2))
        inverse_1 = jnp.where(in_x & in_y[s], inverse_1, 0.0)
        lam_1 = [inverse_1 * field[5 + c] for c in range(3)]
        inverse_e0 = jnp.where(in_x, lam_inverse(soft_e0, total(soft_e0, soft_e1, soft_1)), 0.0)
        lam_e0 = [inverse_e0 * raw[c, :, e0, :] for c in range(3)]
        mu_1, wy_1 = field[3], field[2]
        mu_e0, mu_e1 = state0[0, :, e0, :], state0[0, :, e1, :]
        lam_e1 = [state0[1 + c, :, e1, :] for c in range(3)]

        def coefficients_of(center, inverse, inward, outward, wx, wy, wz):
            sides = around_x(center) + ordered(inward, outward) + around_z(center, OUTSIDE)
            eighth = 0.125 * inverse
            faces = [eighth * (center + side) for side in sides]
            faces[4] = jnp.where(lane == nz - 1, 0.0, faces[4])
            faces[5] = jnp.where(lane == 0, 0.0, faces[5])
            pulls = around_x(wx) + wy + around_z(wz, 0.0)
            return faces, [inverse * w if j % 2 == 0 else -inverse * w for j, w in enumerate(pulls)]

        def moved_of(faces, pulls, scale, own, inward, outward):
            sides = [
                around_x(own[f]) + ordered(inward[f], outward[f]) + around_z(own[f], 0.0) for f in range(4)
            ]
            moved = [scale * sum(sides[0])]
            for c in range(3):
                part = sum(faces[j] * sides[1 + c][j] for j in range(6))
                moved.append(part + pulls[2 * c] * sides[0][2 * c] + pulls[2 * c + 1] * sides[0][2 * c + 1])
            return moved

        first_1 = [jnp.where(in_x, field[Y_KNOWN] + c2 * field[4] * mu_e0, 0.0)]
        sides = around_x(soft_1) + around_z(soft_1, OUTSIDE) + [soft_e0]
        faces = [0.125 * (soft_1 + side) for side in sides]
        wy_e0 = pull[1, :, e0, :] * mu_e0
        own_1 = [mu_1] + lam_1
        own_e0 = [mu_e0] + lam_e0
        for c in range(3):
            sides = around_x(lam_1[c]) + around_z(lam_1[c], 0.0) + [lam_e0[c]]
            lacked = sum(faces[j] * sides[j] for j in range(5))
            if c == 1:
                lacked += wy_e0 if s == 0 else -wy_e0
            first_1.append(inverse_1 * (field[Y_KNOWN + 1 + c] + c2 * lacked))

        scale_e0 = mu_scale[:, e0, :]
        wy = ordered(pull[1, :, e1, :], wy_1)
        faces, pulls = coefficients_of(
            soft_e0, inverse_e0, soft_e1, soft_1, pull[0, :, e0, :], wy, pull[2, :, e0, :]
        )
        moved = moved_of(faces, pulls, scale_e0, own_e0, [mu_e1] + lam_e1, own_1)
        first_e0 = [(1.0 + c1) * own_e0[f] + c2 * moved[f] for f in range(4)]

        outward_face = g[3 if s == 0 else 2, :, e1, :]
        first_e1 = [state1[0, :, e1, :]]
        for c in range(3):
            first_e1.append(state1[1 + c, :, e1, :] + c2 * outward_face * lam_e0[c])

        moved = moved_of(faces, pulls, scale_e0, first_e0, first_e1, first_1)
        for f in range(4):
            second = first_e0[f] + (d1 - d2) * (first_e0[f] - own_e0[f]) + d2 * moved[f]
            sent[f * nx : (f + 1) * nx, :] = second[HALO : HALO + nx, :]
            firsts[s, f] = first_e0[f]
            outer[s, f] = first_1[f]
        for j in range(6):
            coefficients[s, j] = faces[j]
            coefficients[s, 6 + j] = pulls[j]
        for c in range(3):
            coefficients[s, 12 + c] = lam_e0[c]
            seconds[s, c] = first_e1[1 + c]
    deal(sent_pal, sent_other, sent_low, sent_high)


def sweep(first, last, state, g, k, mu_scale, rows, advance, finish=None):
    _, ny, nz = mu_scale.shape
    lane = lax.broadcasted_iota(jnp.int32, (ny, nz), 1)
    if rows is None:

        def rows(s, f, at):
            return 0.0

    def plane(at, _):
        def around(f):
            own = state[f, at]
            return own, [
                state[f, at + 1],
                state[f, at - 1],
                row_up(own, rows(1, f, at)),
                row_down(own, rows(0, f, at)),
                pltpu.roll(own, nz - 1, 1),
                pltpu.roll(own, 1, 1),
            ]

        mu, mu_sides = around(0)
        ends = [
            jnp.where(lane == nz - 1, 0.0, mu_sides[4]),
            jnp.where(lane == 0, 0.0, mu_sides[5]),
        ]
        results = [advance(at, 0, mu, mu_scale[at] * sum(mu_sides[:4] + ends))]
        faces = [g[j, at] for j in range(6)]
        for c in range(3):
            lam, lam_sides = around(1 + c)
            moved = sum(faces[j] * lam_sides[j] for j in range(6))
            moved += k[2 * c, at] * mu_sides[2 * c] + k[2 * c + 1, at] * mu_sides[2 * c + 1]
            results.append(advance(at, 1 + c, lam, moved))
        if finish is not None:
            finish(at - HALO, results)
        return 0

    lax.fori_loop(first, last, plane, 0)


def wait_kernel(
    work, less, grads, y_pal, y_other,
    mu_scale, coefficients, firsts, seconds, outer, g_in, k_in, state0_in, state1_in,
    out_mu, out_lam, edges, g, k, state0, state1,
    state2, states,
):
    _, nx, ny, _ = grads.shape
    planes = nx + 2 * HALO
    _, (d1, d2), (c1, c2) = weights()
    held = slice(HALO - 2, HALO + nx + 2)
    for s in range(2):
        e0, e1 = edge_row(s, ny, 0), edge_row(s, ny, 1)
        for j in range(6):
            g[j, held, e0, :] = coefficients[s, j, held, :]
            k[j, held, e0, :] = coefficients[s, 6 + j, held, :]
        for c in range(3):
            state0[1 + c, held, e0, :] = coefficients[s, 12 + c, held, :]
            state1[1 + c, held, e1, :] = seconds[s, c, held, :]
        for f in range(4):
            state1[f, held, e0, :] = firsts[s, f, held, :]

    def rows(s, f, at):
        return outer[s, f, pl.ds(at, 1), :]

    def advance_2(at, f, own, moved):
        state2[f, at] = own + (d1 - d2) * (own - state0[f, at]) + d2 * moved

    sweep(HALO - 1, HALO + nx + 1, state1, g, k, mu_scale, rows, advance_2)

    def advance_3(at, f, own, moved):
        return own + c1 * (own - state1[f, at]) + c2 * (state0[f, at] - own + moved)

    def finish(i, results):
        out_mu[i] = results[0]
        along = grads[3, i] * sum(grads[c, i] * results[1 + c] for c in range(3))
        for c in range(3):
            out_lam[c, i] = results[1 + c] - along * grads[c, i]
            states[c, i] = results[1 + c]

    sweep(HALO, HALO + nx, state2, g, k, mu_scale, None, advance_3, finish)

    for s in range(2):
        y_in = received_y(y_pal, y_other, s)
        e0, e1 = edge_row(s, ny, 0), edge_row(s, ny, 1)
        own = less[HALO : HALO + nx, e0, :]
        inward, outward = less[HALO : HALO + nx, e1, :], y_in(0, nx) - 1.0
        grad = [
            0.5 * (less[HALO + 1 : HALO + nx + 1, e0, :] - less[HALO - 1 : HALO + nx - 1, e0, :]),
            0.5 * (inward - outward if s == 0 else outward - inward),
            0.5 * (lane_up(own, -1.0) - lane_down(own, -1.0)),
        ]
        for c in range(3):
            edges[s, c] = grad[c]
            edges[s, 4 + c] = states[c, :, e0, :]
        edges[s, 3] = reach_of(grad, work[...])


def last_kernel(
    mu_scale, coefficients, edges, y_pal, y_other, mu_in, lam_in,
    out_mu, out_lam, mu, lam,
    sems,
):
    nx, ny, nz = mu.shape
    inner = slice(HALO, HALO + nx)
    _, _, (_, c2) = weights()
    for s in range(2):
        y_in = received_y(y_pal, y_other, s)
        e0 = edge_row(s, ny, 0)
        outward = 3 if s == 0 else 2

        def got(f):
            return y_in(f * nx, nx)

        mu[:, e0, :] = mu[:, e0, :] + c2 * mu_scale[inner, e0, :] * got(0)
        face = c2 * coefficients[s, outward, inner, :]
        ends = []
        for c in range(3):
            end = edges[s, 4 + c] + face * got(1 + c)
            if c == 1:
                end += c2 * coefficients[s, 6 + outward, inner, :] * got(0)
            ends.append(end)
        along = edges[s, 3] * sum(edges[s, c] * ends[c] for c in range(3))
        for c in range(3):
            lam[c, :, e0, :] = ends[c] - along * edges[s, c]
    copies = [
        pltpu.make_async_copy(mu, out_mu, sems.at[0]),
        pltpu.make_async_copy(lam, out_lam, sems.at[1]),
    ]
    for copy in copies:
        copy.start()
    for copy in copies:
        copy.wait()


VMEM = pl.BlockSpec(memory_space=pltpu.VMEM)
SMEM = pl.BlockSpec(memory_space=pltpu.SMEM)
HBM = pl.BlockSpec(memory_space=pltpu.HBM)
ANY = pl.BlockSpec(memory_space=pl.ANY)
MIB = 1024 * 1024


def call(kernel, ins, outs, scratch=(), in_specs=None, out_specs=None, aliases=None, grant=24 * MIB):
    return pl.pallas_call(
        kernel,
        out_shape=[jax.ShapeDtypeStruct(shape, F32) for shape in outs],
        in_specs=in_specs or [VMEM] * len(ins),
        out_specs=out_specs or [VMEM] * len(outs),
        scratch_shapes=[pltpu.VMEM(shape, F32) if isinstance(shape, tuple) else shape for shape in scratch],
        input_output_aliases=aliases or {},
        compiler_params=pltpu.CompilerParams(vmem_limit_bytes=grant),
    )(*ins)


def trade(value, axis, first):
    pairs = [(i, i + 1) for i in range(first, lax.axis_size(axis) - 1, 2)]
    return lax.ppermute(value, axis, pairs + [(j, i) for i, j in pairs])


def body(damage, strain, seed_damage, seed_disp, brick_work):
    nx, ny, nz = damage.shape
    plane = (ny, nz)
    brick = (nx,) + plane
    bricks = (3,) + brick
    framed = (nx + 2 * HALO,) + plane
    state = (4,) + framed
    row = (nx + 2 * HALO, nz)
    fields = (damage, strain, seed_damage, seed_disp)

    y_rows = (Y_FIELDS * nx, nz)
    pal, token = call(
        pal_rows_kernel, fields, [y_rows, (1, 1)],
        [brick, bricks, brick, bricks, y_rows, pltpu.SemaphoreType.DMA((4,)), pltpu.SemaphoreType.DMA],
        in_specs=[HBM] * 4, out_specs=[HBM, SMEM], grant=56 * MIB,
    )
    near_1, near_2, far_1, far_2, other = call(
        faces_kernel, fields + (token,), [(count,) + plane for count in (X_SLOTS - NEAR_CUT, NEAR_CUT, FAR_CUT, X_SLOTS - FAR_CUT)] + [y_rows],
        in_specs=[VMEM] * 4 + [SMEM],
    )
    y_in = (trade(pal, "gy", 0), trade(other, "gy", 1))
    near = (trade(near_1, "gx", 0), trade(near_2, "gx", 0))
    x_in = near + (trade(far_1, "gx", 1), trade(far_2, "gx", 1))
    work = brick_work
    inner = tuple(call(
        inner_kernel, (work,) + fields,
        [framed, framed, (3,) + framed, framed, (3,) + framed]
        + [(6,) + framed, (6,) + framed, state, state, (4,) + brick],
    ))
    c_rows = (2 * CORNER_ROWS, nz)
    pal, other = call(
        corners_kernel, fields + x_in + (inner[0],), [c_rows] * 2, [(15,) + plane, c_rows, c_rows],
        in_specs=[VMEM] * 8 + [ANY],
    )
    c_in = (trade(pal, "gy", 0), trade(other, "gy", 1))
    less, soft, pull, mu_scale, raw, g, k, state0, state1, grads = call(
        sides_kernel, (work,) + x_in + inner, [part.shape for part in inner],
        aliases={5 + part: part for part in range(10)},
    )
    sent = (4 * nx, nz)
    pal, other, coefficients, firsts, seconds, outer = call(
        edges_kernel, (soft, pull, mu_scale, raw, g, state0, state1) + y_in + c_in,
        [sent] * 2 + [(2, 15) + row, (2, 4) + row, (2, 3) + row, (2, 4) + row],
        [(Y_FIELDS,) + row, sent, sent],
    )
    halo = (trade(pal, "gy", 0), trade(other, "gy", 1))
    ins = (work, less, grads) + y_in + (mu_scale, coefficients, firsts, seconds, outer, g, k, state0, state1)
    mu, lam, edges, *_ = call(
        wait_kernel, ins,
        [brick, bricks, (2, 7, nx, nz), (6,) + framed, (6,) + framed, state, state],
        [state, bricks],
        aliases={10: 3, 11: 4, 12: 5, 13: 6},
    )
    out_mu, out_lam, *_ = call(
        last_kernel, (mu_scale, coefficients, edges) + halo + (mu, lam),
        [brick, bricks, brick, bricks], [pltpu.SemaphoreType.DMA((2,))],
        out_specs=[HBM, HBM, VMEM, VMEM], aliases={5: 2, 6: 3},
    )
    return out_mu, out_lam


def solution(mesh):
    placed = (
        P("gx", "gy", None),
        P(None, "gx", "gy", None),
        P("gx", "gy", None),
        P(None, "gx", "gy", None),
        P("gx", "gy"),
    )
    return jax.shard_map(
        body,
        mesh=mesh,
        in_specs=placed,
        out_specs=(P("gx", "gy", None), P(None, "gx", "gy", None)),
        check_vma=False,
    )
```

```python
import functools

import jax
import jax.numpy as jnp
from jax import lax
from jax.experimental import pallas as pl
from jax.experimental.pallas import tpu as pltpu
from jax.sharding import PartitionSpec as P

RELAX_INNER = 8
RESIDUAL_STIFFNESS = 0.001
CENTER_VALUE = 1.0
HALF_WIDTH = 0.75
NORMAL_WEIGHT = 1.5
RELAX_RATE = 0.5 / RELAX_INNER
NORMAL_FLOOR = 0.05
OUTSIDE = 1.0 + RESIDUAL_STIFFNESS
F32 = jnp.float32


def weights():
    ratio = CENTER_VALUE / HALF_WIDTH
    rho = 1.0 / ratio
    found = []
    for _ in range(3):
        rho_next = 1.0 / (2.0 * ratio - rho)
        found.append((rho_next * rho, 2.0 * rho_next / HALF_WIDTH))
        rho = rho_next
    return found


def soft_of(damage):
    return (1.0 - damage) ** 2 + RESIDUAL_STIFFNESS


def row_up(plane, beyond):
    rows = plane.shape[0]
    at = lax.broadcasted_iota(jnp.int32, plane.shape, 0)
    return jnp.where(at == rows - 1, beyond, pltpu.roll(plane, rows - 1, 0))


def row_down(plane, beyond):
    at = lax.broadcasted_iota(jnp.int32, plane.shape, 0)
    return jnp.where(at == 0, beyond, pltpu.roll(plane, 1, 0))


def lane_up(plane, beyond):
    cells = plane.shape[1]
    at = lax.broadcasted_iota(jnp.int32, plane.shape, 1)
    return jnp.where(at == cells - 1, beyond, pltpu.roll(plane, cells - 1, 1))


def lane_down(plane, beyond):
    at = lax.broadcasted_iota(jnp.int32, plane.shape, 1)
    return jnp.where(at == 0, beyond, pltpu.roll(plane, 1, 1))


def mu_inverse(ex, ey, ez):
    return 1.0 / (2.0 + (ex * ex + ey * ey + ez * ez))


def lam_inverse(center, total):
    return 1.0 / (0.5 + 0.125 * (6.0 * center + total))


HALO = 4
X_DAMAGE, X_PULL, X_PULL_Y, X_PULL_Z, X_MU, X_SOURCE, X_SLOTS = 0, 4, 7, 9, 11, 14, 23
NEAR_CUT, FAR_CUT = 17, 7
Y_ROWS = (
    (X_DAMAGE, 4, 0, 3),
    (X_DAMAGE, 4, 1, 2),
    (None, 2, 0, 2),
    (X_MU, 3, 0, 2),
    (None, 2, 0, 1),
    (X_SOURCE, 3, 0, 2),
    (X_SOURCE + 3, 3, 0, 2),
    (X_SOURCE + 6, 3, 0, 2),
)
Y_KNOWN, Y_FIELDS = 8, 12
CORNER_ROWS = sum(entry[3] for entry in Y_ROWS) + 8


def edge_row(s, ny, depth):
    return depth if s == 0 else ny - 1 - depth


def known_of(s, damages, pulls, behind_pull, mus, sources, behind):
    planes = damages[0].shape[0]
    (c1, c2), _, _ = weights()
    soft = [soft_of(part) for part in damages]
    less = damages[0] - 1.0
    wx, wy, wz = (less * pull for pull in pulls)
    wy_behind = (damages[1] - 1.0) * behind_pull

    def across(value):
        return pltpu.roll(value, planes - 1, 0), pltpu.roll(value, 1, 0)

    def along(value, fill):
        return lane_up(value, fill), lane_down(value, fill)

    total = soft[0] + soft[2] + sum(across(soft[1])) + sum(along(soft[1], OUTSIDE))
    inverse = lam_inverse(soft[1], total)
    face = 0.125 * (soft[0] + soft[1])
    scale = 0.25 * mu_inverse(*pulls)
    known = [(1.0 + c1) * mus[0] + c2 * scale * (mus[1] + sum(across(mus[0])) + sum(along(mus[0], 0.0)))]
    x_up, x_down = across(wx * mus[0])
    z_up, z_down = along(wz * mus[0], 0.0)
    y_behind = wy_behind * mus[1]
    transfers = (x_up - x_down, y_behind if s == 0 else -y_behind, z_up - z_down)
    for c in range(3):
        known.append((1.0 + c1) * sources[c] + c2 * (face * (inverse * behind[c]) + transfers[c]))
    return scale, wy, known


def put_rows(s, put, damage, strain, seed_damage, seed_disp, ready=lambda field: None):
    ny = damage.shape[1]
    first, second, third = (edge_row(s, ny, depth) for depth in range(3))
    ready(0)
    damages = [damage[:, row, :] for row in (first, second, third)]
    ready(1)
    pulls = [strain[c, :, first, :] for c in range(3)]
    pulls_behind = [strain[c, :, second, :] for c in range(3)]
    ready(2)
    mus = [
        seed_damage[:, first, :] * mu_inverse(*pulls),
        seed_damage[:, second, :] * mu_inverse(*pulls_behind),
    ]
    ready(3)
    sources = [seed_disp[c, :, first, :] for c in range(3)]
    behind = [seed_disp[c, :, second, :] for c in range(3)]
    scale, wy, known = known_of(s, damages, pulls, pulls_behind[1], mus, sources, behind)
    for slot, value in enumerate(damages[:2] + [wy, mus[0], scale] + sources + known):
        put(slot, value)


def even(axis):
    return lax.rem(lax.axis_index(axis), 2) == 0


def pal_rows_kernel(
    damage_in, strain_in, seed_in, sources_in, out, token,
    damage, strain, seed_damage, seed_disp, rows, sems, out_sem,
):
    nx = damage.shape[0]
    token[0, 0] = 0.0
    copies = [
        pltpu.make_async_copy(damage_in, damage, sems.at[0]),
        pltpu.make_async_copy(strain_in, strain, sems.at[1]),
        pltpu.make_async_copy(seed_in, seed_damage, sems.at[2]),
        pltpu.make_async_copy(sources_in, seed_disp, sems.at[3]),
    ]
    for copy in copies:
        copy.start()

    def put(slot, value):
        rows[slot * nx : (slot + 1) * nx, :] = value

    for s in range(2):

        @pl.when(even("gy") == (s == 1))
        def _():
            put_rows(s, put, damage, strain, seed_damage, seed_disp, lambda field: copies[field].wait())

    copy = pltpu.make_async_copy(rows, out, out_sem)
    copy.start()
    copy.wait()


def faces_kernel(damage, strain, seed_damage, seed_disp, _, near_1, near_2, far_1, far_2, rows):
    nx = damage.shape[0]

    def put(slot, value):
        rows[slot * nx : (slot + 1) * nx, :] = value

    for s in range(2):

        @pl.when(even("gy") == (s == 0))
        def _():
            put_rows(s, put, damage, strain, seed_damage, seed_disp)

    for parts, cut, high in (((near_1, near_2), NEAR_CUT, even("gx")), ((far_1, far_2), FAR_CUT, ~even("gx"))):

        def put_planes(first, value):
            out, first = (parts[0], first) if first < cut else (parts[1], first - cut)
            out[first : first + value.shape[0]] = value

        def planes(count):
            return pl.ds(jnp.where(high, nx - count, 0), count)

        sx, sy, sz = (strain[c, planes(3)] for c in range(3))
        put_planes(X_DAMAGE, damage[planes(4)])
        put_planes(X_PULL, sx)
        put_planes(X_PULL_Y, strain[1, planes(2)])
        put_planes(X_PULL_Z, strain[2, planes(2)])
        put_planes(X_MU, seed_damage[planes(3)] * mu_inverse(sx, sy, sz))
        for c in range(3):
            put_planes(X_SOURCE + 3 * c, seed_disp[c, planes(3)])


def received_x(near_1, near_2, far_1, far_2, side):
    from_near = even("gx") == (side == 1)

    def part(lower, upper, cut, first, count, row):
        held, first = (lower, first) if first < cut else (upper, first - cut)
        planes = slice(first, first + count)
        return held[planes] if row is None else held[planes, row]

    def planes(first, count, row=None):
        near = part(near_1, near_2, NEAR_CUT, first, count, row)
        return jnp.where(from_near, near, part(far_1, far_2, FAR_CUT, first, count, row))

    return planes


def received_y(pal, other, side):
    from_pal = even("gy") == (side == 1)
    return lambda first, count: jnp.where(from_pal, pal[first : first + count, :], other[first : first + count, :])


def deal(pal, other, low, high):
    first = even("gy")
    low, high = low[...], high[...]
    pal[...] = jnp.where(first, high, low)
    other[...] = jnp.where(first, low, high)


def corners_kernel(
    damage, strain, seed_damage, seed_disp, near_1, near_2, far_1, far_2, _, pal, other, field, low, high
):
    nx, ny, _ = damage.shape
    for s, out in enumerate((low, high)):
        first, second, third = (edge_row(s, ny, depth) for depth in range(3))
        for side in range(2):
            x_in = received_x(near_1, near_2, far_1, far_2, side)
            theirs, ours = (slice(0, 3), slice(3, 8)) if side == 0 else (slice(5, 8), slice(0, 5))
            planes = slice(0, 5) if side == 0 else slice(nx - 5, nx)

            def x_rows(slot, held, row):
                start = slot + (held - 3 if side == 0 else 0)
                return x_in(start, 3, row)

            def x_pair(slot, row):
                return x_in(slot, 2, row)

            for depth, row in enumerate((first, second, third)):
                field[depth, ours, :] = damage[planes, row, :]
                field[depth, theirs, :] = x_rows(X_DAMAGE, 4, row)
            pair = slice(1, 3) if side == 0 else slice(5, 7)
            for depth, row in enumerate((first, second)):
                sx, sy, sz = (strain[c, planes, row, :] for c in range(3))
                if depth == 0:
                    field[3, ours, :] = sx
                    field[3, theirs, :] = x_rows(X_PULL, 3, row)
                    field[5, ours, :] = sz
                    field[5, pair, :] = x_pair(X_PULL_Z, row)
                slot = 4 if depth == 0 else 6
                field[slot, ours, :] = sy
                field[slot, pair, :] = x_pair(X_PULL_Y, row)
                field[7 + depth, ours, :] = seed_damage[planes, row, :] * mu_inverse(sx, sy, sz)
                field[7 + depth, theirs, :] = x_rows(X_MU, 3, row)
                for c in range(3):
                    slot = 9 + 3 * depth + c
                    field[slot, ours, :] = seed_disp[c, planes, row, :]
                    field[slot, theirs, :] = x_rows(X_SOURCE + 3 * c, 3, row)
            got = [field[slot] for slot in range(15)]
            scale, wy, known = known_of(s, got[:3], got[3:6], got[6], got[7:9], got[9:12], got[12:15])
            row = side * CORNER_ROWS
            for slot, value in enumerate(got[:2] + [wy, got[7], scale] + got[9:12]):
                count = Y_ROWS[slot][3]
                start = 3 - count if side == 0 else 5
                out[row : row + count, :] = value[start : start + count, :]
                row += count
            for value in known:
                start = 2 if side == 0 else 4
                out[row : row + 2, :] = value[start : start + 2, :]
                row += 2
    deal(pal, other, low, high)


def in_grid():
    here = lax.axis_index("gx")
    return here > 0, here < lax.axis_size("gx") - 1


def prepare(first, last, soft, pull, raw, g, k, state0):
    planes, ny, nz = soft.shape
    inside = in_grid()
    lane = lax.broadcasted_iota(jnp.int32, (ny, nz), 1)
    row = lax.broadcasted_iota(jnp.int32, (ny, nz), 0)
    inner = (row > 0) & (row < ny - 1)

    def step(at, _):
        center = soft[at]
        sides = [
            soft[at + 1],
            soft[at - 1],
            pltpu.roll(center, ny - 1, 0),
            pltpu.roll(center, 1, 0),
            lane_up(center, OUTSIDE),
            lane_down(center, OUTSIDE),
        ]
        outside = ((at < HALO) & ~inside[0]) | ((at >= planes - HALO) & ~inside[1])
        inverse = jnp.where(inner & ~outside, lam_inverse(center, sum(sides)), 0.0)
        eighth = 0.125 * inverse
        for j in range(6):
            face = eighth * (center + sides[j])
            if j == 4:
                face = jnp.where(lane == nz - 1, 0.0, face)
            if j == 5:
                face = jnp.where(lane == 0, 0.0, face)
            g[j, at] = face
        k[0, at] = inverse * pull[0, at + 1]
        k[1, at] = -inverse * pull[0, at - 1]
        k[2, at] = inverse * pltpu.roll(pull[1, at], ny - 1, 0)
        k[3, at] = -inverse * pltpu.roll(pull[1, at], 1, 0)
        k[4, at] = inverse * lane_up(pull[2, at], 0.0)
        k[5, at] = -inverse * lane_down(pull[2, at], 0.0)
        for c in range(3):
            state0[1 + c, at] = inverse * raw[c, at]
        return 0

    lax.fori_loop(first, last, step, 0)


def reach_of(grad, count):
    square = sum(part * part for part in grad)
    scale = 1.0 / jnp.maximum(square, NORMAL_FLOOR)
    power = 1.0 - RELAX_RATE * (1.0 + NORMAL_WEIGHT * square * scale)
    series = 1.0 + power
    for _ in range(2):
        power = power * power
        series = series * (1.0 + power)
    power = power * power
    repeats = jnp.ones_like(power)
    for level in range(1, 4):
        repeats = jnp.where(count > level, 1.0 + power * repeats, repeats)
    return (RELAX_RATE * NORMAL_WEIGHT * scale) * (series * repeats)


def slopes(first, last, count, less, grads):
    ny = less.shape[1]

    def step(at, _):
        own = less[at]
        grad = [
            0.5 * (less[at + 1] - less[at - 1]),
            0.5 * (pltpu.roll(own, ny - 1, 0) - pltpu.roll(own, 1, 0)),
            0.5 * (lane_up(own, -1.0) - lane_down(own, -1.0)),
        ]
        for c in range(3):
            grads[c, at - HALO] = grad[c]
        grads[3, at - HALO] = reach_of(grad, count)
        return 0

    lax.fori_loop(first, last, step, 0)


def inner_kernel(damage, strain, seed_damage, seed_disp, less, soft, pull, mu_scale, raw, g, k, state0):
    nx = damage.shape[0]

    def fill(i, _):
        at = HALO + i
        own = damage[i]
        sx, sy, sz = strain[0, i], strain[1, i], strain[2, i]
        soft[at] = soft_of(own)
        own = own - 1.0
        less[at] = own
        pull[0, at] = own * sx
        pull[1, at] = own * sy
        pull[2, at] = own * sz
        mu_inv = mu_inverse(sx, sy, sz)
        mu_scale[at] = 0.25 * mu_inv
        state0[0, at] = mu_inv * seed_damage[i]
        for c in range(3):
            raw[c, at] = seed_disp[c, i]
        return 0

    lax.fori_loop(0, nx, fill, 0)
    low, high = HALO, HALO + nx
    prepare(low + 1, high - 1, soft, pull, raw, g, k, state0)


def sides_kernel(
    work, near_1, near_2, far_1, far_2, less_in, soft_in, pull_in, scale_in, raw_in, g_in, k_in, state0_in,
    less, soft, pull, mu_scale, raw, g, k, state0, state1, grads,
):
    nx = soft.shape[0] - 2 * HALO
    inside = in_grid()
    for s in range(2):
        x_in = received_x(near_1, near_2, far_1, far_2, s)

        def planes(count):
            first = HALO - count if s == 0 else HALO + nx
            return slice(first, first + count)

        def nearest(slot, held, count):
            return x_in(slot + (held - count if s == 0 else 0), count)

        soft[planes(4)] = soft_of(nearest(X_DAMAGE, 4, 4))
        less[planes(1)] = nearest(X_DAMAGE, 4, 1) - 1.0
        pull[0, planes(3)] = (nearest(X_DAMAGE, 4, 3) - 1.0) * nearest(X_PULL, 3, 3)
        own = nearest(X_DAMAGE, 4, 2) - 1.0
        sx, sy, sz = nearest(X_PULL, 3, 2), nearest(X_PULL_Y, 2, 2), nearest(X_PULL_Z, 2, 2)
        pull[1, planes(2)] = own * sy
        pull[2, planes(2)] = own * sz
        mu_scale[planes(2)] = jnp.where(inside[s], 0.25 * mu_inverse(sx, sy, sz), 0.0)
        state0[0, planes(3)] = nearest(X_MU, 3, 3)
        for c in range(3):
            raw[c, planes(3)] = nearest(X_SOURCE + 3 * c, 3, 3)

    low, high = HALO, HALO + nx
    for first, last in ((low - 3, low + 1), (high - 1, high + 3)):
        prepare(first, last, soft, pull, raw, g, k, state0)
    slopes(low, high, work[0, 0], less, grads)
    (c1, c2), _, _ = weights()

    def advance(at, f, own, moved):
        state1[f, at] = (1.0 + c1) * own + c2 * moved

    sweep(low - 2, high + 2, state0, g, k, mu_scale, None, advance)


def edges_kernel(
    soft, pull, mu_scale, raw, g, state0, state1, y_pal, y_other, c_pal, c_other,
    sent_pal, sent_other, coefficients, firsts, seconds, outer,
    field, sent_low, sent_high,
):
    planes, ny, nz = soft.shape
    nx = planes - 2 * HALO
    (c1, c2), (d1, d2), _ = weights()
    lane = lax.broadcasted_iota(jnp.int32, (planes, nz), 1)
    plane = lax.broadcasted_iota(jnp.int32, (planes, nz), 0)
    here, there = lax.axis_index("gx"), lax.axis_index("gy")
    in_x = ((plane >= HALO) | (here > 0)) & ((plane < HALO + nx) | (here < lax.axis_size("gx") - 1))
    in_y = (there > 0, there < lax.axis_size("gy") - 1)

    def around_x(value):
        return [pltpu.roll(value, planes - 1, 0), pltpu.roll(value, 1, 0)]

    def around_z(value, fill):
        return [lane_up(value, fill), lane_down(value, fill)]

    for s, sent in enumerate((sent_low, sent_high)):
        y_in, c_in = received_y(y_pal, y_other, s), received_y(c_pal, c_other, s)
        e0, e1 = edge_row(s, ny, 0), edge_row(s, ny, 1)

        def ordered(inward, outward):
            return [inward, outward] if s == 0 else [outward, inward]

        row = 0
        for f in range(Y_FIELDS):
            field[f, HALO : HALO + nx, :] = y_in(f * nx, nx)
            count, shift = (Y_ROWS[f][3], 0) if f < Y_KNOWN else (2, 1)
            field[f, HALO - count + shift : HALO + shift, :] = c_in(row, count)
            high = HALO + nx - shift
            field[f, high : high + count, :] = c_in(CORNER_ROWS + row, count)
            row += count

        soft_1, soft_2 = soft_of(field[0]), soft_of(field[1])
        soft_e0, soft_e1 = soft[:, e0, :], soft[:, e1, :]

        def total(center, inward, outward):
            return sum(around_x(center) + [inward, outward] + around_z(center, OUTSIDE))

        inverse_1 = lam_inverse(soft_1, total(soft_1, soft_e0, soft_2))
        inverse_1 = jnp.where(in_x & in_y[s], inverse_1, 0.0)
        lam_1 = [inverse_1 * field[5 + c] for c in range(3)]
        inverse_e0 = jnp.where(in_x, lam_inverse(soft_e0, total(soft_e0, soft_e1, soft_1)), 0.0)
        lam_e0 = [inverse_e0 * raw[c, :, e0, :] for c in range(3)]
        mu_1, wy_1 = field[3], field[2]
        mu_e0, mu_e1 = state0[0, :, e0, :], state0[0, :, e1, :]
        lam_e1 = [state0[1 + c, :, e1, :] for c in range(3)]

        def coefficients_of(center, inverse, inward, outward, wx, wy, wz):
            sides = around_x(center) + ordered(inward, outward) + around_z(center, OUTSIDE)
            eighth = 0.125 * inverse
            faces = [eighth * (center + side) for side in sides]
            faces[4] = jnp.where(lane == nz - 1, 0.0, faces[4])
            faces[5] = jnp.where(lane == 0, 0.0, faces[5])
            pulls = around_x(wx) + wy + around_z(wz, 0.0)
            return faces, [inverse * w if j % 2 == 0 else -inverse * w for j, w in enumerate(pulls)]

        def moved_of(faces, pulls, scale, own, inward, outward):
            sides = [
                around_x(own[f]) + ordered(inward[f], outward[f]) + around_z(own[f], 0.0) for f in range(4)
            ]
            moved = [scale * sum(sides[0])]
            for c in range(3):
                part = sum(faces[j] * sides[1 + c][j] for j in range(6))
                moved.append(part + pulls[2 * c] * sides[0][2 * c] + pulls[2 * c + 1] * sides[0][2 * c + 1])
            return moved

        first_1 = [jnp.where(in_x, field[Y_KNOWN] + c2 * field[4] * mu_e0, 0.0)]
        sides = around_x(soft_1) + around_z(soft_1, OUTSIDE) + [soft_e0]
        faces = [0.125 * (soft_1 + side) for side in sides]
        wy_e0 = pull[1, :, e0, :] * mu_e0
        own_1 = [mu_1] + lam_1
        own_e0 = [mu_e0] + lam_e0
        for c in range(3):
            sides = around_x(lam_1[c]) + around_z(lam_1[c], 0.0) + [lam_e0[c]]
            lacked = sum(faces[j] * sides[j] for j in range(5))
            if c == 1:
                lacked += wy_e0 if s == 0 else -wy_e0
            first_1.append(inverse_1 * (field[Y_KNOWN + 1 + c] + c2 * lacked))

        scale_e0 = mu_scale[:, e0, :]
        wy = ordered(pull[1, :, e1, :], wy_1)
        faces, pulls = coefficients_of(
            soft_e0, inverse_e0, soft_e1, soft_1, pull[0, :, e0, :], wy, pull[2, :, e0, :]
        )
        moved = moved_of(faces, pulls, scale_e0, own_e0, [mu_e1] + lam_e1, own_1)
        first_e0 = [(1.0 + c1) * own_e0[f] + c2 * moved[f] for f in range(4)]

        outward_face = g[3 if s == 0 else 2, :, e1, :]
        first_e1 = [state1[0, :, e1, :]]
        for c in range(3):
            first_e1.append(state1[1 + c, :, e1, :] + c2 * outward_face * lam_e0[c])

        moved = moved_of(faces, pulls, scale_e0, first_e0, first_e1, first_1)
        for f in range(4):
            second = first_e0[f] + (d1 - d2) * (first_e0[f] - own_e0[f]) + d2 * moved[f]
            sent[f * nx : (f + 1) * nx, :] = second[HALO : HALO + nx, :]
            firsts[s, f] = first_e0[f]
            outer[s, f] = first_1[f]
        for j in range(6):
            coefficients[s, j] = faces[j]
            coefficients[s, 6 + j] = pulls[j]
        for c in range(3):
            coefficients[s, 12 + c] = lam_e0[c]
            seconds[s, c] = first_e1[1 + c]
    deal(sent_pal, sent_other, sent_low, sent_high)


def sweep(first, last, state, g, k, mu_scale, rows, advance, finish=None):
    _, ny, nz = mu_scale.shape
    lane = lax.broadcasted_iota(jnp.int32, (ny, nz), 1)
    if rows is None:

        def rows(s, f, at):
            return 0.0

    def plane(at, _):
        def around(f):
            own = state[f, at]
            return own, [
                state[f, at + 1],
                state[f, at - 1],
                row_up(own, rows(1, f, at)),
                row_down(own, rows(0, f, at)),
                pltpu.roll(own, nz - 1, 1),
                pltpu.roll(own, 1, 1),
            ]

        mu, mu_sides = around(0)
        ends = [
            jnp.where(lane == nz - 1, 0.0, mu_sides[4]),
            jnp.where(lane == 0, 0.0, mu_sides[5]),
        ]
        results = [advance(at, 0, mu, mu_scale[at] * sum(mu_sides[:4] + ends))]
        faces = [g[j, at] for j in range(6)]
        for c in range(3):
            lam, lam_sides = around(1 + c)
            moved = sum(faces[j] * lam_sides[j] for j in range(6))
            moved += k[2 * c, at] * mu_sides[2 * c] + k[2 * c + 1, at] * mu_sides[2 * c + 1]
            results.append(advance(at, 1 + c, lam, moved))
        if finish is not None:
            finish(at - HALO, results)
        return 0

    lax.fori_loop(first, last, plane, 0)


def wait_kernel(
    work, less, grads, y_pal, y_other,
    mu_scale, coefficients, firsts, seconds, outer, g_in, k_in, state0_in, state1_in,
    out_mu, out_lam, edges, g, k, state0, state1,
    state2, states,
):
    _, nx, ny, _ = grads.shape
    planes = nx + 2 * HALO
    _, (d1, d2), (c1, c2) = weights()
    held = slice(HALO - 2, HALO + nx + 2)
    for s in range(2):
        e0, e1 = edge_row(s, ny, 0), edge_row(s, ny, 1)
        for j in range(6):
            g[j, held, e0, :] = coefficients[s, j, held, :]
            k[j, held, e0, :] = coefficients[s, 6 + j, held, :]
        for c in range(3):
            state0[1 + c, held, e0, :] = coefficients[s, 12 + c, held, :]
            state1[1 + c, held, e1, :] = seconds[s, c, held, :]
        for f in range(4):
            state1[f, held, e0, :] = firsts[s, f, held, :]

    def rows(s, f, at):
        return outer[s, f, pl.ds(at, 1), :]

    def advance_2(at, f, own, moved):
        state2[f, at] = own + (d1 - d2) * (own - state0[f, at]) + d2 * moved

    sweep(HALO - 1, HALO + nx + 1, state1, g, k, mu_scale, rows, advance_2)

    def advance_3(at, f, own, moved):
        return own + c1 * (own - state1[f, at]) + c2 * (state0[f, at] - own + moved)

    def finish(i, results):
        out_mu[i] = results[0]
        along = grads[3, i] * sum(grads[c, i] * results[1 + c] for c in range(3))
        for c in range(3):
            out_lam[c, i] = results[1 + c] - along * grads[c, i]
            states[c, i] = results[1 + c]

    sweep(HALO, HALO + nx, state2, g, k, mu_scale, None, advance_3, finish)

    for s in range(2):
        y_in = received_y(y_pal, y_other, s)
        e0, e1 = edge_row(s, ny, 0), edge_row(s, ny, 1)
        own = less[HALO : HALO + nx, e0, :]
        inward, outward = less[HALO : HALO + nx, e1, :], y_in(0, nx) - 1.0
        grad = [
            0.5 * (less[HALO + 1 : HALO + nx + 1, e0, :] - less[HALO - 1 : HALO + nx - 1, e0, :]),
            0.5 * (inward - outward if s == 0 else outward - inward),
            0.5 * (lane_up(own, -1.0) - lane_down(own, -1.0)),
        ]
        for c in range(3):
            edges[s, c] = grad[c]
            edges[s, 4 + c] = states[c, :, e0, :]
        edges[s, 3] = reach_of(grad, work[0, 0])


def last_kernel(
    mu_scale, coefficients, edges, y_pal, y_other, mu_in, lam_in,
    out_mu, out_lam, mu, lam,
    sems,
):
    nx, ny, nz = mu.shape
    inner = slice(HALO, HALO + nx)
    _, _, (_, c2) = weights()
    for s in range(2):
        y_in = received_y(y_pal, y_other, s)
        e0 = edge_row(s, ny, 0)
        outward = 3 if s == 0 else 2

        def got(f):
            return y_in(f * nx, nx)

        mu[:, e0, :] = mu[:, e0, :] + c2 * mu_scale[inner, e0, :] * got(0)
        face = c2 * coefficients[s, outward, inner, :]
        ends = []
        for c in range(3):
            end = edges[s, 4 + c] + face * got(1 + c)
            if c == 1:
                end += c2 * coefficients[s, 6 + outward, inner, :] * got(0)
            ends.append(end)
        along = edges[s, 3] * sum(edges[s, c] * ends[c] for c in range(3))
        for c in range(3):
            lam[c, :, e0, :] = ends[c] - along * edges[s, c]
    copies = [
        pltpu.make_async_copy(mu, out_mu, sems.at[0]),
        pltpu.make_async_copy(lam, out_lam, sems.at[1]),
    ]
    for copy in copies:
        copy.start()
    for copy in copies:
        copy.wait()


VMEM = pl.BlockSpec(memory_space=pltpu.VMEM)
SMEM = pl.BlockSpec(memory_space=pltpu.SMEM)
HBM = pl.BlockSpec(memory_space=pltpu.HBM)
ANY = pl.BlockSpec(memory_space=pl.ANY)
MIB = 1024 * 1024


def call(kernel, ins, outs, scratch=(), in_specs=None, out_specs=None, aliases=None, grant=24 * MIB):
    return pl.pallas_call(
        kernel,
        out_shape=[jax.ShapeDtypeStruct(shape, F32) for shape in outs],
        in_specs=in_specs or [VMEM] * len(ins),
        out_specs=out_specs or [VMEM] * len(outs),
        scratch_shapes=[pltpu.VMEM(shape, F32) if isinstance(shape, tuple) else shape for shape in scratch],
        input_output_aliases=aliases or {},
        compiler_params=pltpu.CompilerParams(vmem_limit_bytes=grant),
    )(*ins)


def trade(value, axis, first):
    pairs = [(i, i + 1) for i in range(first, lax.axis_size(axis) - 1, 2)]
    return lax.ppermute(value, axis, pairs + [(j, i) for i, j in pairs])


def body(damage, strain, seed_damage, seed_disp, brick_work):
    nx, ny, nz = damage.shape
    plane = (ny, nz)
    brick = (nx,) + plane
    bricks = (3,) + brick
    framed = (nx + 2 * HALO,) + plane
    state = (4,) + framed
    row = (nx + 2 * HALO, nz)
    fields = (damage, strain, seed_damage, seed_disp)

    y_rows = (Y_FIELDS * nx, nz)
    pal, token = call(
        pal_rows_kernel, fields, [y_rows, (1, 1)],
        [brick, bricks, brick, bricks, y_rows, pltpu.SemaphoreType.DMA((4,)), pltpu.SemaphoreType.DMA],
        in_specs=[HBM] * 4, out_specs=[HBM, SMEM], grant=56 * MIB,
    )
    near_1, near_2, far_1, far_2, other = call(
        faces_kernel, fields + (token,), [(count,) + plane for count in (NEAR_CUT, X_SLOTS - NEAR_CUT, FAR_CUT, X_SLOTS - FAR_CUT)] + [y_rows],
        in_specs=[VMEM] * 4 + [SMEM],
    )
    y_in = (trade(pal, "gy", 0), trade(other, "gy", 1))
    near = (trade(near_1, "gx", 0), trade(near_2, "gx", 0))
    x_in = near + (trade(far_1, "gx", 1), trade(far_2, "gx", 1))
    inner = tuple(call(
        inner_kernel, fields,
        [framed, framed, (3,) + framed, framed, (3,) + framed, (6,) + framed, (6,) + framed, state],
    ))
    c_rows = (2 * CORNER_ROWS, nz)
    pal, other = call(
        corners_kernel, fields + x_in + (inner[0],), [c_rows] * 2, [(15,) + plane, c_rows, c_rows],
        in_specs=[VMEM] * 8 + [ANY],
    )
    c_in = (trade(pal, "gy", 0), trade(other, "gy", 1))
    less, soft, pull, mu_scale, raw, g, k, state0, state1, grads = call(
        sides_kernel, (brick_work,) + x_in + inner, [part.shape for part in inner] + [state, (4,) + brick],
        in_specs=[SMEM] + [VMEM] * 12, aliases={5 + part: part for part in range(8)},
    )
    sent = (4 * nx, nz)
    pal, other, coefficients, firsts, seconds, outer = call(
        edges_kernel, (soft, pull, mu_scale, raw, g, state0, state1) + y_in + c_in,
        [sent] * 2 + [(2, 15) + row, (2, 4) + row, (2, 3) + row, (2, 4) + row],
        [(Y_FIELDS,) + row, sent, sent],
    )
    halo = (trade(pal, "gy", 0), trade(other, "gy", 1))
    ins = (brick_work, less, grads) + y_in + (mu_scale, coefficients, firsts, seconds, outer, g, k, state0, state1)
    mu, lam, edges, *_ = call(
        wait_kernel, ins,
        [brick, bricks, (2, 7, nx, nz), (6,) + framed, (6,) + framed, state, state],
        [state, bricks],
        in_specs=[SMEM] + [VMEM] * (len(ins) - 1),
        aliases={10: 3, 11: 4, 12: 5, 13: 6},
    )
    out_mu, out_lam, *_ = call(
        last_kernel, (mu_scale, coefficients, edges) + halo + (mu, lam),
        [brick, bricks, brick, bricks], [pltpu.SemaphoreType.DMA((2,))],
        out_specs=[HBM, HBM, VMEM, VMEM], aliases={5: 2, 6: 3},
    )
    return out_mu, out_lam


def solution(mesh):
    placed = (
        P("gx", "gy", None),
        P(None, "gx", "gy", None),
        P("gx", "gy", None),
        P(None, "gx", "gy", None),
        P("gx", "gy"),
    )
    return jax.shard_map(
        body,
        mesh=mesh,
        in_specs=placed,
        out_specs=(P("gx", "gy", None), P(None, "gx", "gy", None)),
        check_vma=False,
    )
```

```python
import functools

import jax
import jax.numpy as jnp
from jax import lax
from jax.experimental import pallas as pl
from jax.experimental.pallas import tpu as pltpu
from jax.sharding import PartitionSpec as P

RELAX_INNER = 8
RESIDUAL_STIFFNESS = 0.001
CENTER_VALUE = 1.0
HALF_WIDTH = 0.75
NORMAL_WEIGHT = 1.5
RELAX_RATE = 0.5 / RELAX_INNER
NORMAL_FLOOR = 0.05
OUTSIDE = 1.0 + RESIDUAL_STIFFNESS
F32 = jnp.float32


def weights():
    ratio = CENTER_VALUE / HALF_WIDTH
    rho = 1.0 / ratio
    found = []
    for _ in range(3):
        rho_next = 1.0 / (2.0 * ratio - rho)
        found.append((rho_next * rho, 2.0 * rho_next / HALF_WIDTH))
        rho = rho_next
    return found


def soft_of(damage):
    return (1.0 - damage) ** 2 + RESIDUAL_STIFFNESS


def row_up(plane, beyond):
    rows = plane.shape[0]
    at = lax.broadcasted_iota(jnp.int32, plane.shape, 0)
    return jnp.where(at == rows - 1, beyond, pltpu.roll(plane, rows - 1, 0))


def row_down(plane, beyond):
    at = lax.broadcasted_iota(jnp.int32, plane.shape, 0)
    return jnp.where(at == 0, beyond, pltpu.roll(plane, 1, 0))


def lane_up(plane, beyond):
    cells = plane.shape[1]
    at = lax.broadcasted_iota(jnp.int32, plane.shape, 1)
    return jnp.where(at == cells - 1, beyond, pltpu.roll(plane, cells - 1, 1))


def lane_down(plane, beyond):
    at = lax.broadcasted_iota(jnp.int32, plane.shape, 1)
    return jnp.where(at == 0, beyond, pltpu.roll(plane, 1, 1))


def mu_inverse(ex, ey, ez):
    return 1.0 / (2.0 + (ex * ex + ey * ey + ez * ez))


def lam_inverse(center, total):
    return 1.0 / (0.5 + 0.125 * (6.0 * center + total))


HALO = 4
X_DAMAGE, X_PULL, X_MU, X_SOURCE, X_SLOTS = 0, 3, 9, 11, 17
LATE_DAMAGE, LATE_PULL, LATE_MU, LATE_SOURCE, LATE_SLOTS = 0, 1, 2, 3, 6
Y_HALO = (3, 2, 2, 2, 1, 2, 2, 2)
Y_KNOWN, Y_FIELDS = 8, 12
CORNER_ROWS = sum(Y_HALO) + 8


def edge_row(s, ny, depth):
    return depth if s == 0 else ny - 1 - depth


def known_of(s, damages, pulls, behind_pull, mus, sources, behind):
    planes = damages[0].shape[0]
    (c1, c2), _, _ = weights()
    soft = [soft_of(part) for part in damages]
    less = damages[0] - 1.0
    wx, wy, wz = (less * pull for pull in pulls)
    wy_behind = (damages[1] - 1.0) * behind_pull

    def across(value):
        return pltpu.roll(value, planes - 1, 0), pltpu.roll(value, 1, 0)

    def along(value, fill):
        return lane_up(value, fill), lane_down(value, fill)

    total = soft[0] + soft[2] + sum(across(soft[1])) + sum(along(soft[1], OUTSIDE))
    inverse = lam_inverse(soft[1], total)
    face = 0.125 * (soft[0] + soft[1])
    scale = 0.25 * mu_inverse(*pulls)
    known = [(1.0 + c1) * mus[0] + c2 * scale * (mus[1] + sum(across(mus[0])) + sum(along(mus[0], 0.0)))]
    x_up, x_down = across(wx * mus[0])
    z_up, z_down = along(wz * mus[0], 0.0)
    y_behind = wy_behind * mus[1]
    transfers = (x_up - x_down, y_behind if s == 0 else -y_behind, z_up - z_down)
    for c in range(3):
        known.append((1.0 + c1) * sources[c] + c2 * (face * (inverse * behind[c]) + transfers[c]))
    return scale, wy, known


def put_rows(s, put, damage, strain, seed_damage, seed_disp, ready=lambda field: None):
    ny = damage.shape[1]
    first, second, third = (edge_row(s, ny, depth) for depth in range(3))
    ready(0)
    damages = [damage[:, row, :] for row in (first, second, third)]
    ready(1)
    pulls = [strain[c, :, first, :] for c in range(3)]
    pulls_behind = [strain[c, :, second, :] for c in range(3)]
    ready(2)
    mus = [
        seed_damage[:, first, :] * mu_inverse(*pulls),
        seed_damage[:, second, :] * mu_inverse(*pulls_behind),
    ]
    ready(3)
    sources = [seed_disp[c, :, first, :] for c in range(3)]
    behind = [seed_disp[c, :, second, :] for c in range(3)]
    scale, wy, known = known_of(s, damages, pulls, pulls_behind[1], mus, sources, behind)
    for slot, value in enumerate(damages[:2] + [wy, mus[0], scale] + sources + known):
        put(slot, value)


def even(axis):
    return lax.rem(lax.axis_index(axis), 2) == 0


def pal_rows_kernel(
    damage_in, strain_in, seed_in, sources_in, out, token,
    damage, strain, seed_damage, seed_disp, rows, sems, out_sem,
):
    nx = damage.shape[0]
    token[0, 0] = 0.0
    copies = [
        pltpu.make_async_copy(damage_in, damage, sems.at[0]),
        pltpu.make_async_copy(strain_in, strain, sems.at[1]),
        pltpu.make_async_copy(seed_in, seed_damage, sems.at[2]),
        pltpu.make_async_copy(sources_in, seed_disp, sems.at[3]),
    ]
    for copy in copies:
        copy.start()

    def put(slot, value):
        rows[slot * nx : (slot + 1) * nx, :] = value

    for s in range(2):

        @pl.when(even("gy") == (s == 1))
        def _():
            put_rows(s, put, damage, strain, seed_damage, seed_disp, lambda field: copies[field].wait())

    copy = pltpu.make_async_copy(rows, out, out_sem)
    copy.start()
    copy.wait()


def faces_kernel(
    damage, strain, seed_damage, seed_disp, _, near, near_late, far, far_late, rows
):
    nx = damage.shape[0]

    def put(slot, value):
        rows[slot * nx : (slot + 1) * nx, :] = value

    for s in range(2):

        @pl.when(even("gy") == (s == 0))
        def _():
            put_rows(s, put, damage, strain, seed_damage, seed_disp)

    for out, late, high in ((near, near_late, even("gx")), (far, far_late, ~even("gx"))):
        for depth in range(4):
            at = jnp.where(high, nx - 1 - depth, depth)
            if depth == 3:
                late[LATE_DAMAGE] = damage[at]
                continue
            out[X_DAMAGE + depth] = damage[at]
            pulls = [strain[c, at] for c in range(3)]
            mu = seed_damage[at] * mu_inverse(*pulls)
            if depth == 2:
                late[LATE_PULL] = pulls[0]
                late[LATE_MU] = mu
            else:
                out[X_MU + depth] = mu
            for c in range(3):
                if depth == 2:
                    late[LATE_SOURCE + c] = seed_disp[c, at]
                else:
                    out[X_PULL + 2 * c + depth] = pulls[c]
                    out[X_SOURCE + 2 * c + depth] = seed_disp[c, at]


def received_x(near, far, side):
    from_near = even("gx") == (side == 1)

    def plane(slot, row=None):
        at = slot if row is None else (slice(slot, slot + 1), row)
        return jnp.where(from_near, near[at], far[at])

    return plane


def received_y(pal, other, side):
    from_pal = even("gy") == (side == 1)
    return lambda first, count: jnp.where(from_pal, pal[first : first + count, :], other[first : first + count, :])


def deal(pal, other, low, high):
    first = even("gy")
    low, high = low[...], high[...]
    pal[...] = jnp.where(first, high, low)
    other[...] = jnp.where(first, low, high)


def corners_kernel(
    damage, strain, seed_damage, seed_disp, near, far, _, pal, other, field, low, high
):
    nx, ny, _ = damage.shape
    for s, out in enumerate((low, high)):
        first, second, third = (edge_row(s, ny, depth) for depth in range(3))
        for side in range(2):
            x_in = received_x(near, far, side)
            ours = slice(3, 8) if side == 0 else slice(0, 5)
            planes = slice(0, 5) if side == 0 else slice(nx - 5, nx)

            def put_x(slot, first, count, row):
                for far_off in range(count):
                    at = 2 - far_off if side == 0 else 5 + far_off
                    field[slot, at : at + 1, :] = x_in(first + far_off, row)

            for depth, row in enumerate((first, second, third)):
                field[depth, ours, :] = damage[planes, row, :]
                put_x(depth, X_DAMAGE, 3, row)
            for depth, row in enumerate((first, second)):
                pulls = [strain[c, planes, row, :] for c in range(3)]
                for c in range(3):
                    if depth == 0:
                        field[3 + c, ours, :] = pulls[c]
                        put_x(3 + c, X_PULL + 2 * c, 2, row)
                    field[9 + 3 * depth + c, ours, :] = seed_disp[c, planes, row, :]
                    put_x(9 + 3 * depth + c, X_SOURCE + 2 * c, 2, row)
                if depth == 1:
                    field[6, ours, :] = pulls[1]
                    put_x(6, X_PULL + 2, 2, row)
                field[7 + depth, ours, :] = seed_damage[planes, row, :] * mu_inverse(*pulls)
                put_x(7 + depth, X_MU, 2, row)
            got = [field[slot] for slot in range(15)]
            scale, wy, known = known_of(s, got[:3], got[3:6], got[6], got[7:9], got[9:12], got[12:15])
            row = side * CORNER_ROWS
            for slot, value in enumerate(got[:2] + [wy, got[7], scale] + got[9:12]):
                count = Y_HALO[slot]
                start = 3 - count if side == 0 else 5
                out[row : row + count, :] = value[start : start + count, :]
                row += count
            for value in known:
                start = 2 if side == 0 else 4
                out[row : row + 2, :] = value[start : start + 2, :]
                row += 2
    deal(pal, other, low, high)


def in_grid():
    here = lax.axis_index("gx")
    return here > 0, here < lax.axis_size("gx") - 1


def prepare(first, last, soft, pull, raw, g, k, state0):
    planes, ny, nz = soft.shape
    inside = in_grid()
    lane = lax.broadcasted_iota(jnp.int32, (ny, nz), 1)
    row = lax.broadcasted_iota(jnp.int32, (ny, nz), 0)
    inner = (row > 0) & (row < ny - 1)

    def step(at, _):
        center = soft[at]
        sides = [
            soft[at + 1],
            soft[at - 1],
            pltpu.roll(center, ny - 1, 0),
            pltpu.roll(center, 1, 0),
            lane_up(center, OUTSIDE),
            lane_down(center, OUTSIDE),
        ]
        outside = ((at < HALO) & ~inside[0]) | ((at >= planes - HALO) & ~inside[1])
        inverse = jnp.where(inner & ~outside, lam_inverse(center, sum(sides)), 0.0)
        eighth = 0.125 * inverse
        for j in range(6):
            face = eighth * (center + sides[j])
            if j == 4:
                face = jnp.where(lane == nz - 1, 0.0, face)
            if j == 5:
                face = jnp.where(lane == 0, 0.0, face)
            g[j, at] = face
        k[0, at] = inverse * pull[0, at + 1]
        k[1, at] = -inverse * pull[0, at - 1]
        k[2, at] = inverse * pltpu.roll(pull[1, at], ny - 1, 0)
        k[3, at] = -inverse * pltpu.roll(pull[1, at], 1, 0)
        k[4, at] = inverse * lane_up(pull[2, at], 0.0)
        k[5, at] = -inverse * lane_down(pull[2, at], 0.0)
        for c in range(3):
            state0[1 + c, at] = inverse * raw[c, at]
        return 0

    lax.fori_loop(first, last, step, 0)


def reach_of(grad, count):
    square = sum(part * part for part in grad)
    scale = 1.0 / jnp.maximum(square, NORMAL_FLOOR)
    power = 1.0 - RELAX_RATE * (1.0 + NORMAL_WEIGHT * square * scale)
    series = 1.0 + power
    for _ in range(2):
        power = power * power
        series = series * (1.0 + power)
    power = power * power
    repeats = jnp.ones_like(power)
    for level in range(1, 4):
        repeats = jnp.where(count > level, 1.0 + power * repeats, repeats)
    return (RELAX_RATE * NORMAL_WEIGHT * scale) * (series * repeats)


def slopes(first, last, count, less, grads):
    ny = less.shape[1]

    def step(at, _):
        own = less[at]
        grad = [
            0.5 * (less[at + 1] - less[at - 1]),
            0.5 * (pltpu.roll(own, ny - 1, 0) - pltpu.roll(own, 1, 0)),
            0.5 * (lane_up(own, -1.0) - lane_down(own, -1.0)),
        ]
        for c in range(3):
            grads[c, at - HALO] = grad[c]
        grads[3, at - HALO] = reach_of(grad, count)
        return 0

    lax.fori_loop(first, last, step, 0)


def first_sweep(ranges, state0, state1, g, k, mu_scale):
    (c1, c2), _, _ = weights()

    def advance(at, f, own, moved):
        state1[f, at] = (1.0 + c1) * own + c2 * moved

    for first, last in ranges:
        sweep(first, last, state0, g, k, mu_scale, None, advance)


def inner_kernel(
    damage, strain, seed_damage, seed_disp, less, soft, pull, mu_scale, raw, g, k, state0, state1
):
    nx = damage.shape[0]

    def fill(i, _):
        at = HALO + i
        own = damage[i]
        sx, sy, sz = strain[0, i], strain[1, i], strain[2, i]
        soft[at] = soft_of(own)
        own = own - 1.0
        less[at] = own
        pull[0, at] = own * sx
        pull[1, at] = own * sy
        pull[2, at] = own * sz
        mu_inv = mu_inverse(sx, sy, sz)
        mu_scale[at] = 0.25 * mu_inv
        state0[0, at] = mu_inv * seed_damage[i]
        for c in range(3):
            raw[c, at] = seed_disp[c, i]
        return 0

    lax.fori_loop(0, nx, fill, 0)
    low, high = HALO, HALO + nx
    prepare(low + 1, high - 1, soft, pull, raw, g, k, state0)
    first_sweep([(low + 2, high - 2)], state0, state1, g, k, mu_scale)


def sides_kernel(
    work, near, near_late, far, far_late,
    less_in, soft_in, pull_in, scale_in, raw_in, g_in, k_in, state0_in, state1_in,
    less, soft, pull, mu_scale, raw, g, k, state0, state1, grads,
):
    nx = soft.shape[0] - 2 * HALO
    low, high = HALO, HALO + nx
    inside = in_grid()
    for s in range(2):
        x_in, late = received_x(near, far, s), received_x(near_late, far_late, s)
        for depth in range(4):
            at = low - 1 - depth if s == 0 else high + depth
            own = late(LATE_DAMAGE) if depth == 3 else x_in(X_DAMAGE + depth)
            soft[at] = soft_of(own)
            if depth == 3:
                continue
            own = own - 1.0
            if depth == 0:
                less[at] = own
            if depth == 2:
                pull[0, at] = own * late(LATE_PULL)
                state0[0, at] = late(LATE_MU)
            else:
                pulls = [x_in(X_PULL + 2 * c + depth) for c in range(3)]
                mu_scale[at] = jnp.where(inside[s], 0.25 * mu_inverse(*pulls), 0.0)
                state0[0, at] = x_in(X_MU + depth)
            for c in range(3):
                if depth == 2:
                    raw[c, at] = late(LATE_SOURCE + c)
                else:
                    pull[c, at] = own * pulls[c]
                    raw[c, at] = x_in(X_SOURCE + 2 * c + depth)

    for first, last in ((low - 3, low + 1), (high - 1, high + 3)):
        prepare(first, last, soft, pull, raw, g, k, state0)
    slopes(low, high, work[0, 0], less, grads)
    first_sweep([(low - 2, low + 2), (high - 2, high + 2)], state0, state1, g, k, mu_scale)


def edges_kernel(
    soft, pull, mu_scale, raw, g, state0, state1, y_pal, y_other, c_pal, c_other,
    sent_pal, sent_other, coefficients, firsts, seconds, outer,
    field, sent_low, sent_high,
):
    planes, ny, nz = soft.shape
    nx = planes - 2 * HALO
    (c1, c2), (d1, d2), _ = weights()
    lane = lax.broadcasted_iota(jnp.int32, (planes, nz), 1)
    plane = lax.broadcasted_iota(jnp.int32, (planes, nz), 0)
    here, there = lax.axis_index("gx"), lax.axis_index("gy")
    in_x = ((plane >= HALO) | (here > 0)) & ((plane < HALO + nx) | (here < lax.axis_size("gx") - 1))
    in_y = (there > 0, there < lax.axis_size("gy") - 1)

    def around_x(value):
        return [pltpu.roll(value, planes - 1, 0), pltpu.roll(value, 1, 0)]

    def around_z(value, fill):
        return [lane_up(value, fill), lane_down(value, fill)]

    for s, sent in enumerate((sent_low, sent_high)):
        y_in, c_in = received_y(y_pal, y_other, s), received_y(c_pal, c_other, s)
        e0, e1 = edge_row(s, ny, 0), edge_row(s, ny, 1)

        def ordered(inward, outward):
            return [inward, outward] if s == 0 else [outward, inward]

        row = 0
        for f in range(Y_FIELDS):
            field[f, HALO : HALO + nx, :] = y_in(f * nx, nx)
            count, shift = (Y_HALO[f], 0) if f < Y_KNOWN else (2, 1)
            field[f, HALO - count + shift : HALO + shift, :] = c_in(row, count)
            high = HALO + nx - shift
            field[f, high : high + count, :] = c_in(CORNER_ROWS + row, count)
            row += count

        soft_1, soft_2 = soft_of(field[0]), soft_of(field[1])
        soft_e0, soft_e1 = soft[:, e0, :], soft[:, e1, :]

        def total(center, inward, outward):
            return sum(around_x(center) + [inward, outward] + around_z(center, OUTSIDE))

        inverse_1 = lam_inverse(soft_1, total(soft_1, soft_e0, soft_2))
        inverse_1 = jnp.where(in_x & in_y[s], inverse_1, 0.0)
        lam_1 = [inverse_1 * field[5 + c] for c in range(3)]
        inverse_e0 = jnp.where(in_x, lam_inverse(soft_e0, total(soft_e0, soft_e1, soft_1)), 0.0)
        lam_e0 = [inverse_e0 * raw[c, :, e0, :] for c in range(3)]
        mu_1, wy_1 = field[3], field[2]
        mu_e0, mu_e1 = state0[0, :, e0, :], state0[0, :, e1, :]
        lam_e1 = [state0[1 + c, :, e1, :] for c in range(3)]

        def coefficients_of(center, inverse, inward, outward, wx, wy, wz):
            sides = around_x(center) + ordered(inward, outward) + around_z(center, OUTSIDE)
            eighth = 0.125 * inverse
            faces = [eighth * (center + side) for side in sides]
            faces[4] = jnp.where(lane == nz - 1, 0.0, faces[4])
            faces[5] = jnp.where(lane == 0, 0.0, faces[5])
            pulls = around_x(wx) + wy + around_z(wz, 0.0)
            return faces, [inverse * w if j % 2 == 0 else -inverse * w for j, w in enumerate(pulls)]

        def moved_of(faces, pulls, scale, own, inward, outward):
            sides = [
                around_x(own[f]) + ordered(inward[f], outward[f]) + around_z(own[f], 0.0) for f in range(4)
            ]
            moved = [scale * sum(sides[0])]
            for c in range(3):
                part = sum(faces[j] * sides[1 + c][j] for j in range(6))
                moved.append(part + pulls[2 * c] * sides[0][2 * c] + pulls[2 * c + 1] * sides[0][2 * c + 1])
            return moved

        first_1 = [jnp.where(in_x, field[Y_KNOWN] + c2 * field[4] * mu_e0, 0.0)]
        sides = around_x(soft_1) + around_z(soft_1, OUTSIDE) + [soft_e0]
        faces = [0.125 * (soft_1 + side) for side in sides]
        wy_e0 = pull[1, :, e0, :] * mu_e0
        own_1 = [mu_1] + lam_1
        own_e0 = [mu_e0] + lam_e0
        for c in range(3):
            sides = around_x(lam_1[c]) + around_z(lam_1[c], 0.0) + [lam_e0[c]]
            lacked = sum(faces[j] * sides[j] for j in range(5))
            if c == 1:
                lacked += wy_e0 if s == 0 else -wy_e0
            first_1.append(inverse_1 * (field[Y_KNOWN + 1 + c] + c2 * lacked))

        scale_e0 = mu_scale[:, e0, :]
        wy = ordered(pull[1, :, e1, :], wy_1)
        faces, pulls = coefficients_of(
            soft_e0, inverse_e0, soft_e1, soft_1, pull[0, :, e0, :], wy, pull[2, :, e0, :]
        )
        moved = moved_of(faces, pulls, scale_e0, own_e0, [mu_e1] + lam_e1, own_1)
        first_e0 = [(1.0 + c1) * own_e0[f] + c2 * moved[f] for f in range(4)]

        outward_face = g[3 if s == 0 else 2, :, e1, :]
        first_e1 = [state1[0, :, e1, :]]
        for c in range(3):
            first_e1.append(state1[1 + c, :, e1, :] + c2 * outward_face * lam_e0[c])

        moved = moved_of(faces, pulls, scale_e0, first_e0, first_e1, first_1)
        for f in range(4):
            second = first_e0[f] + (d1 - d2) * (first_e0[f] - own_e0[f]) + d2 * moved[f]
            sent[f * nx : (f + 1) * nx, :] = second[HALO : HALO + nx, :]
            firsts[s, f] = first_e0[f]
            outer[s, f] = first_1[f]
        for j in range(6):
            coefficients[s, j] = faces[j]
            coefficients[s, 6 + j] = pulls[j]
        for c in range(3):
            coefficients[s, 12 + c] = lam_e0[c]
            seconds[s, c] = first_e1[1 + c]
    deal(sent_pal, sent_other, sent_low, sent_high)


def sweep(first, last, state, g, k, mu_scale, rows, advance, finish=None):
    _, ny, nz = mu_scale.shape
    lane = lax.broadcasted_iota(jnp.int32, (ny, nz), 1)
    if rows is None:

        def rows(s, f, at):
            return 0.0

    def plane(at, _):
        def around(f):
            own = state[f, at]
            return own, [
                state[f, at + 1],
                state[f, at - 1],
                row_up(own, rows(1, f, at)),
                row_down(own, rows(0, f, at)),
                pltpu.roll(own, nz - 1, 1),
                pltpu.roll(own, 1, 1),
            ]

        mu, mu_sides = around(0)
        ends = [
            jnp.where(lane == nz - 1, 0.0, mu_sides[4]),
            jnp.where(lane == 0, 0.0, mu_sides[5]),
        ]
        results = [advance(at, 0, mu, mu_scale[at] * sum(mu_sides[:4] + ends))]
        faces = [g[j, at] for j in range(6)]
        for c in range(3):
            lam, lam_sides = around(1 + c)
            moved = sum(faces[j] * lam_sides[j] for j in range(6))
            moved += k[2 * c, at] * mu_sides[2 * c] + k[2 * c + 1, at] * mu_sides[2 * c + 1]
            results.append(advance(at, 1 + c, lam, moved))
        if finish is not None:
            finish(at - HALO, results)
        return 0

    lax.fori_loop(first, last, plane, 0)


def wait_kernel(
    work, less, grads, y_pal, y_other,
    mu_scale, coefficients, firsts, seconds, outer, g_in, k_in, state0_in, state1_in,
    out_mu, out_lam, edges, g, k, state0, state1,
    state2, states,
):
    _, nx, ny, _ = grads.shape
    planes = nx + 2 * HALO
    _, (d1, d2), (c1, c2) = weights()
    held = slice(HALO - 2, HALO + nx + 2)
    for s in range(2):
        e0, e1 = edge_row(s, ny, 0), edge_row(s, ny, 1)
        for j in range(6):
            g[j, held, e0, :] = coefficients[s, j, held, :]
            k[j, held, e0, :] = coefficients[s, 6 + j, held, :]
        for c in range(3):
            state0[1 + c, held, e0, :] = coefficients[s, 12 + c, held, :]
            state1[1 + c, held, e1, :] = seconds[s, c, held, :]
        for f in range(4):
            state1[f, held, e0, :] = firsts[s, f, held, :]

    def rows(s, f, at):
        return outer[s, f, pl.ds(at, 1), :]

    def advance_2(at, f, own, moved):
        state2[f, at] = own + (d1 - d2) * (own - state0[f, at]) + d2 * moved

    sweep(HALO - 1, HALO + nx + 1, state1, g, k, mu_scale, rows, advance_2)

    def advance_3(at, f, own, moved):
        return own + c1 * (own - state1[f, at]) + c2 * (state0[f, at] - own + moved)

    def finish(i, results):
        out_mu[i] = results[0]
        along = grads[3, i] * sum(grads[c, i] * results[1 + c] for c in range(3))
        for c in range(3):
            out_lam[c, i] = results[1 + c] - along * grads[c, i]
            states[c, i] = results[1 + c]

    sweep(HALO, HALO + nx, state2, g, k, mu_scale, None, advance_3, finish)

    for s in range(2):
        y_in = received_y(y_pal, y_other, s)
        e0, e1 = edge_row(s, ny, 0), edge_row(s, ny, 1)
        own = less[HALO : HALO + nx, e0, :]
        inward, outward = less[HALO : HALO + nx, e1, :], y_in(0, nx) - 1.0
        grad = [
            0.5 * (less[HALO + 1 : HALO + nx + 1, e0, :] - less[HALO - 1 : HALO + nx - 1, e0, :]),
            0.5 * (inward - outward if s == 0 else outward - inward),
            0.5 * (lane_up(own, -1.0) - lane_down(own, -1.0)),
        ]
        for c in range(3):
            edges[s, c] = grad[c]
            edges[s, 4 + c] = states[c, :, e0, :]
        edges[s, 3] = reach_of(grad, work[0, 0])


def last_kernel(
    mu_scale, coefficients, edges, y_pal, y_other, mu_in, lam_in,
    out_mu, out_lam, mu, lam,
    sems,
):
    nx, ny, nz = mu.shape
    inner = slice(HALO, HALO + nx)
    _, _, (_, c2) = weights()
    for s in range(2):
        y_in = received_y(y_pal, y_other, s)
        e0 = edge_row(s, ny, 0)
        outward = 3 if s == 0 else 2

        def got(f):
            return y_in(f * nx, nx)

        mu[:, e0, :] = mu[:, e0, :] + c2 * mu_scale[inner, e0, :] * got(0)
        face = c2 * coefficients[s, outward, inner, :]
        ends = []
        for c in range(3):
            end = edges[s, 4 + c] + face * got(1 + c)
            if c == 1:
                end += c2 * coefficients[s, 6 + outward, inner, :] * got(0)
            ends.append(end)
        along = edges[s, 3] * sum(edges[s, c] * ends[c] for c in range(3))
        for c in range(3):
            lam[c, :, e0, :] = ends[c] - along * edges[s, c]
    copies = [
        pltpu.make_async_copy(mu, out_mu, sems.at[0]),
        pltpu.make_async_copy(lam, out_lam, sems.at[1]),
    ]
    for copy in copies:
        copy.start()
    for copy in copies:
        copy.wait()


VMEM = pl.BlockSpec(memory_space=pltpu.VMEM)
SMEM = pl.BlockSpec(memory_space=pltpu.SMEM)
HBM = pl.BlockSpec(memory_space=pltpu.HBM)
ANY = pl.BlockSpec(memory_space=pl.ANY)
MIB = 1024 * 1024


def call(kernel, ins, outs, scratch=(), in_specs=None, out_specs=None, aliases=None, grant=24 * MIB):
    return pl.pallas_call(
        kernel,
        out_shape=[jax.ShapeDtypeStruct(shape, F32) for shape in outs],
        in_specs=in_specs or [VMEM] * len(ins),
        out_specs=out_specs or [VMEM] * len(outs),
        scratch_shapes=[pltpu.VMEM(shape, F32) if isinstance(shape, tuple) else shape for shape in scratch],
        input_output_aliases=aliases or {},
        compiler_params=pltpu.CompilerParams(vmem_limit_bytes=grant),
    )(*ins)


def trade(value, axis, first):
    pairs = [(i, i + 1) for i in range(first, lax.axis_size(axis) - 1, 2)]
    return lax.ppermute(value, axis, pairs + [(j, i) for i, j in pairs])


def body(damage, strain, seed_damage, seed_disp, brick_work):
    nx, ny, nz = damage.shape
    plane = (ny, nz)
    brick = (nx,) + plane
    bricks = (3,) + brick
    framed = (nx + 2 * HALO,) + plane
    state = (4,) + framed
    row = (nx + 2 * HALO, nz)
    fields = (damage, strain, seed_damage, seed_disp)

    y_rows = (Y_FIELDS * nx, nz)
    pal, token = call(
        pal_rows_kernel, fields, [y_rows, (1, 1)],
        [brick, bricks, brick, bricks, y_rows, pltpu.SemaphoreType.DMA((4,)), pltpu.SemaphoreType.DMA],
        in_specs=[HBM] * 4, out_specs=[HBM, SMEM], grant=56 * MIB,
    )
    x_faces = [(X_SLOTS,) + plane, (LATE_SLOTS,) + plane]
    near, near_late, far, far_late, other = call(
        faces_kernel, fields + (token,), x_faces * 2 + [y_rows], in_specs=[VMEM] * 4 + [SMEM]
    )
    y_in = (trade(pal, "gy", 0), trade(other, "gy", 1))
    far, far_late = trade(far, "gx", 1), trade(far_late, "gx", 1)
    near, near_late = trade(near, "gx", 0), trade(near_late, "gx", 0)
    inner = tuple(call(
        inner_kernel, fields,
        [framed, framed, (3,) + framed, framed, (3,) + framed, (6,) + framed, (6,) + framed, state, state],
    ))
    c_rows = (2 * CORNER_ROWS, nz)
    pal, other = call(
        corners_kernel, fields + (near, far, inner[0]), [c_rows] * 2,
        [(15,) + plane, c_rows, c_rows], in_specs=[VMEM] * 6 + [ANY],
    )
    c_in = (trade(pal, "gy", 0), trade(other, "gy", 1))
    less, soft, pull, mu_scale, raw, g, k, state0, state1, grads = call(
        sides_kernel, (brick_work, near, near_late, far, far_late) + inner,
        [part.shape for part in inner] + [(4,) + brick],
        in_specs=[SMEM] + [VMEM] * 13, aliases={5 + part: part for part in range(9)},
    )
    sent = (4 * nx, nz)
    pal, other, coefficients, firsts, seconds, outer = call(
        edges_kernel, (soft, pull, mu_scale, raw, g, state0, state1) + y_in + c_in,
        [sent] * 2 + [(2, 15) + row, (2, 4) + row, (2, 3) + row, (2, 4) + row],
        [(Y_FIELDS,) + row, sent, sent],
    )
    halo = (trade(pal, "gy", 0), trade(other, "gy", 1))
    ins = (brick_work, less, grads) + y_in + (mu_scale, coefficients, firsts, seconds, outer, g, k, state0, state1)
    mu, lam, edges, *_ = call(
        wait_kernel, ins,
        [brick, bricks, (2, 7, nx, nz), (6,) + framed, (6,) + framed, state, state],
        [state, bricks],
        in_specs=[SMEM] + [VMEM] * (len(ins) - 1),
        aliases={10: 3, 11: 4, 12: 5, 13: 6},
    )
    out_mu, out_lam, *_ = call(
        last_kernel, (mu_scale, coefficients, edges) + halo + (mu, lam),
        [brick, bricks, brick, bricks], [pltpu.SemaphoreType.DMA((2,))],
        out_specs=[HBM, HBM, VMEM, VMEM], aliases={5: 2, 6: 3},
    )
    return out_mu, out_lam


def solution(mesh):
    placed = (
        P("gx", "gy", None),
        P(None, "gx", "gy", None),
        P("gx", "gy", None),
        P(None, "gx", "gy", None),
        P("gx", "gy"),
    )
    return jax.shard_map(
        body,
        mesh=mesh,
        in_specs=placed,
        out_specs=(P("gx", "gy", None), P(None, "gx", "gy", None)),
        check_vma=False,
    )
```

```python
import functools

import jax
import jax.numpy as jnp
from jax import lax
from jax.experimental import pallas as pl
from jax.experimental.pallas import tpu as pltpu
from jax.sharding import PartitionSpec as P

RELAX_INNER = 8
RESIDUAL_STIFFNESS = 0.001
CENTER_VALUE = 1.0
HALF_WIDTH = 0.75
NORMAL_WEIGHT = 1.5
RELAX_RATE = 0.5 / RELAX_INNER
NORMAL_FLOOR = 0.05
OUTSIDE = 1.0 + RESIDUAL_STIFFNESS
F32 = jnp.float32


def weights():
    ratio = CENTER_VALUE / HALF_WIDTH
    rho = 1.0 / ratio
    found = []
    for _ in range(3):
        rho_next = 1.0 / (2.0 * ratio - rho)
        found.append((rho_next * rho, 2.0 * rho_next / HALF_WIDTH))
        rho = rho_next
    return found


def soft_of(damage):
    return (1.0 - damage) ** 2 + RESIDUAL_STIFFNESS


def row_up(plane, beyond):
    rows = plane.shape[0]
    at = lax.broadcasted_iota(jnp.int32, plane.shape, 0)
    return jnp.where(at == rows - 1, beyond, pltpu.roll(plane, rows - 1, 0))


def row_down(plane, beyond):
    at = lax.broadcasted_iota(jnp.int32, plane.shape, 0)
    return jnp.where(at == 0, beyond, pltpu.roll(plane, 1, 0))


def lane_up(plane, beyond):
    cells = plane.shape[1]
    at = lax.broadcasted_iota(jnp.int32, plane.shape, 1)
    return jnp.where(at == cells - 1, beyond, pltpu.roll(plane, cells - 1, 1))


def lane_down(plane, beyond):
    at = lax.broadcasted_iota(jnp.int32, plane.shape, 1)
    return jnp.where(at == 0, beyond, pltpu.roll(plane, 1, 1))


def mu_inverse(ex, ey, ez):
    return 1.0 / (2.0 + (ex * ex + ey * ey + ez * ez))


def lam_inverse(center, total):
    return 1.0 / (0.5 + 0.125 * (6.0 * center + total))


HALO = 4
X_DAMAGE, X_PULL, X_MU, X_SOURCE, X_SLOTS = 0, 3, 9, 11, 17
LATE_DAMAGE, LATE_PULL, LATE_MU, LATE_SOURCE, LATE_SLOTS = 0, 1, 2, 3, 6
Y_HALO = (3, 2, 2, 2, 1, 2, 2, 2)
Y_KNOWN, Y_FIELDS = 8, 12
CORNER_ROWS = sum(Y_HALO) + 8


def edge_row(s, ny, depth):
    return depth if s == 0 else ny - 1 - depth


def known_of(s, damages, pulls, behind_pull, mus, sources, behind):
    planes = damages[0].shape[0]
    (c1, c2), _, _ = weights()
    soft = [soft_of(part) for part in damages]
    less = damages[0] - 1.0
    wx, wy, wz = (less * pull for pull in pulls)
    wy_behind = (damages[1] - 1.0) * behind_pull

    def across(value):
        return pltpu.roll(value, planes - 1, 0), pltpu.roll(value, 1, 0)

    def along(value, fill):
        return lane_up(value, fill), lane_down(value, fill)

    total = soft[0] + soft[2] + sum(across(soft[1])) + sum(along(soft[1], OUTSIDE))
    inverse = lam_inverse(soft[1], total)
    face = 0.125 * (soft[0] + soft[1])
    scale = 0.25 * mu_inverse(*pulls)
    known = [(1.0 + c1) * mus[0] + c2 * scale * (mus[1] + sum(across(mus[0])) + sum(along(mus[0], 0.0)))]
    x_up, x_down = across(wx * mus[0])
    z_up, z_down = along(wz * mus[0], 0.0)
    y_behind = wy_behind * mus[1]
    transfers = (x_up - x_down, y_behind if s == 0 else -y_behind, z_up - z_down)
    for c in range(3):
        known.append((1.0 + c1) * sources[c] + c2 * (face * (inverse * behind[c]) + transfers[c]))
    return scale, wy, known


def put_rows(s, put, damage, strain, seed_damage, seed_disp, ready=lambda field: None):
    ny = damage.shape[1]
    first, second, third = (edge_row(s, ny, depth) for depth in range(3))
    ready(0)
    damages = [damage[:, row, :] for row in (first, second, third)]
    ready(1)
    pulls = [strain[c, :, first, :] for c in range(3)]
    pulls_behind = [strain[c, :, second, :] for c in range(3)]
    ready(2)
    mus = [
        seed_damage[:, first, :] * mu_inverse(*pulls),
        seed_damage[:, second, :] * mu_inverse(*pulls_behind),
    ]
    ready(3)
    sources = [seed_disp[c, :, first, :] for c in range(3)]
    behind = [seed_disp[c, :, second, :] for c in range(3)]
    scale, wy, known = known_of(s, damages, pulls, pulls_behind[1], mus, sources, behind)
    for slot, value in enumerate(damages[:2] + [wy, mus[0], scale] + sources + known):
        put(slot, value)


def even(axis):
    return lax.rem(lax.axis_index(axis), 2) == 0


def pal_rows_kernel(
    damage_in, strain_in, seed_in, sources_in, out, token,
    damage, strain, seed_damage, seed_disp, rows, sems, out_sem,
):
    nx = damage.shape[0]
    token[0, 0] = 0.0
    copies = [
        pltpu.make_async_copy(damage_in, damage, sems.at[0]),
        pltpu.make_async_copy(strain_in, strain, sems.at[1]),
        pltpu.make_async_copy(seed_in, seed_damage, sems.at[2]),
        pltpu.make_async_copy(sources_in, seed_disp, sems.at[3]),
    ]
    for copy in copies:
        copy.start()

    def put(slot, value):
        rows[slot * nx : (slot + 1) * nx, :] = value

    for s in range(2):

        @pl.when(even("gy") == (s == 1))
        def _():
            put_rows(s, put, damage, strain, seed_damage, seed_disp, lambda field: copies[field].wait())

    copy = pltpu.make_async_copy(rows, out, out_sem)
    copy.start()
    copy.wait()


def faces_kernel(
    damage, strain, seed_damage, seed_disp, _, near, near_late, far, far_late, rows
):
    nx = damage.shape[0]

    def put(slot, value):
        rows[slot * nx : (slot + 1) * nx, :] = value

    for s in range(2):

        @pl.when(even("gy") == (s == 0))
        def _():
            put_rows(s, put, damage, strain, seed_damage, seed_disp)

    for out, late, high in ((near, near_late, even("gx")), (far, far_late, ~even("gx"))):
        for depth in range(4):
            at = jnp.where(high, nx - 1 - depth, depth)
            if depth == 3:
                late[LATE_DAMAGE] = damage[at]
                continue
            out[X_DAMAGE + depth] = damage[at]
            pulls = [strain[c, at] for c in range(3)]
            mu = seed_damage[at] * mu_inverse(*pulls)
            if depth == 2:
                late[LATE_PULL] = pulls[0]
                late[LATE_MU] = mu
            else:
                out[X_MU + depth] = mu
            for c in range(3):
                if depth == 2:
                    late[LATE_SOURCE + c] = seed_disp[c, at]
                else:
                    out[X_PULL + 2 * c + depth] = pulls[c]
                    out[X_SOURCE + 2 * c + depth] = seed_disp[c, at]


def received_x(near, far, side):
    from_near = even("gx") == (side == 1)

    def plane(slot, row=None):
        at = slot if row is None else (slice(slot, slot + 1), row)
        return jnp.where(from_near, near[at], far[at])

    return plane


def received_y(pal, other, side):
    from_pal = even("gy") == (side == 1)
    return lambda first, count: jnp.where(from_pal, pal[first : first + count, :], other[first : first + count, :])


def deal(pal, other, low, high):
    first = even("gy")
    low, high = low[...], high[...]
    pal[...] = jnp.where(first, high, low)
    other[...] = jnp.where(first, low, high)


def corners_kernel(
    damage, strain, seed_damage, seed_disp, near, far, _, pal, other, field, low, high
):
    nx, ny, _ = damage.shape
    for s, out in enumerate((low, high)):
        first, second, third = (edge_row(s, ny, depth) for depth in range(3))
        for side in range(2):
            x_in = received_x(near, far, side)
            ours = slice(3, 8) if side == 0 else slice(0, 5)
            planes = slice(0, 5) if side == 0 else slice(nx - 5, nx)

            def put_x(slot, first, count, row):
                for far_off in range(count):
                    at = 2 - far_off if side == 0 else 5 + far_off
                    field[slot, at : at + 1, :] = x_in(first + far_off, row)

            for depth, row in enumerate((first, second, third)):
                field[depth, ours, :] = damage[planes, row, :]
                put_x(depth, X_DAMAGE, 3, row)
            for depth, row in enumerate((first, second)):
                pulls = [strain[c, planes, row, :] for c in range(3)]
                for c in range(3):
                    if depth == 0:
                        field[3 + c, ours, :] = pulls[c]
                        put_x(3 + c, X_PULL + 2 * c, 2, row)
                    field[9 + 3 * depth + c, ours, :] = seed_disp[c, planes, row, :]
                    put_x(9 + 3 * depth + c, X_SOURCE + 2 * c, 2, row)
                if depth == 1:
                    field[6, ours, :] = pulls[1]
                    put_x(6, X_PULL + 2, 2, row)
                field[7 + depth, ours, :] = seed_damage[planes, row, :] * mu_inverse(*pulls)
                put_x(7 + depth, X_MU, 2, row)
            got = [field[slot] for slot in range(15)]
            scale, wy, known = known_of(s, got[:3], got[3:6], got[6], got[7:9], got[9:12], got[12:15])
            row = side * CORNER_ROWS
            for slot, value in enumerate(got[:2] + [wy, got[7], scale] + got[9:12]):
                count = Y_HALO[slot]
                start = 3 - count if side == 0 else 5
                out[row : row + count, :] = value[start : start + count, :]
                row += count
            for value in known:
                start = 2 if side == 0 else 4
                out[row : row + 2, :] = value[start : start + 2, :]
                row += 2
    deal(pal, other, low, high)


def in_grid():
    here = lax.axis_index("gx")
    return here > 0, here < lax.axis_size("gx") - 1


def prepare(first, last, soft, pull, raw, g, k, state0):
    planes, ny, nz = soft.shape
    inside = in_grid()
    lane = lax.broadcasted_iota(jnp.int32, (ny, nz), 1)
    row = lax.broadcasted_iota(jnp.int32, (ny, nz), 0)
    inner = (row > 0) & (row < ny - 1)

    def step(at, _):
        center = soft[at]
        sides = [
            soft[at + 1],
            soft[at - 1],
            pltpu.roll(center, ny - 1, 0),
            pltpu.roll(center, 1, 0),
            lane_up(center, OUTSIDE),
            lane_down(center, OUTSIDE),
        ]
        outside = ((at < HALO) & ~inside[0]) | ((at >= planes - HALO) & ~inside[1])
        inverse = jnp.where(inner & ~outside, lam_inverse(center, sum(sides)), 0.0)
        eighth = 0.125 * inverse
        for j in range(6):
            face = eighth * (center + sides[j])
            if j == 4:
                face = jnp.where(lane == nz - 1, 0.0, face)
            if j == 5:
                face = jnp.where(lane == 0, 0.0, face)
            g[j, at] = face
        k[0, at] = inverse * pull[0, at + 1]
        k[1, at] = -inverse * pull[0, at - 1]
        k[2, at] = inverse * pltpu.roll(pull[1, at], ny - 1, 0)
        k[3, at] = -inverse * pltpu.roll(pull[1, at], 1, 0)
        k[4, at] = inverse * lane_up(pull[2, at], 0.0)
        k[5, at] = -inverse * lane_down(pull[2, at], 0.0)
        for c in range(3):
            state0[1 + c, at] = inverse * raw[c, at]
        return 0

    lax.fori_loop(first, last, step, 0)


def reach_of(grad, count):
    square = sum(part * part for part in grad)
    scale = 1.0 / jnp.maximum(square, NORMAL_FLOOR)
    power = 1.0 - RELAX_RATE * (1.0 + NORMAL_WEIGHT * square * scale)
    series = 1.0 + power
    for _ in range(2):
        power = power * power
        series = series * (1.0 + power)
    power = power * power
    repeats = jnp.ones_like(power)
    for level in range(1, 4):
        repeats = jnp.where(count > level, 1.0 + power * repeats, repeats)
    return (RELAX_RATE * NORMAL_WEIGHT * scale) * (series * repeats)


def slopes(first, last, count, less, grads):
    ny = less.shape[1]

    def step(at, _):
        own = less[at]
        grad = [
            0.5 * (less[at + 1] - less[at - 1]),
            0.5 * (pltpu.roll(own, ny - 1, 0) - pltpu.roll(own, 1, 0)),
            0.5 * (lane_up(own, -1.0) - lane_down(own, -1.0)),
        ]
        for c in range(3):
            grads[c, at - HALO] = grad[c]
        grads[3, at - HALO] = reach_of(grad, count)
        return 0

    lax.fori_loop(first, last, step, 0)


def first_sweep(ranges, state0, state1, g, k, mu_scale):
    (c1, c2), _, _ = weights()

    def advance(at, f, own, moved):
        state1[f, at] = (1.0 + c1) * own + c2 * moved

    for first, last in ranges:
        sweep(first, last, state0, g, k, mu_scale, None, advance)


def inner_kernel(
    damage, strain, seed_damage, seed_disp, less, soft, pull, mu_scale, raw, g, k, state0, state1
):
    nx = damage.shape[0]

    def fill(i, _):
        at = HALO + i
        own = damage[i]
        sx, sy, sz = strain[0, i], strain[1, i], strain[2, i]
        soft[at] = soft_of(own)
        own = own - 1.0
        less[at] = own
        pull[0, at] = own * sx
        pull[1, at] = own * sy
        pull[2, at] = own * sz
        mu_inv = mu_inverse(sx, sy, sz)
        mu_scale[at] = 0.25 * mu_inv
        state0[0, at] = mu_inv * seed_damage[i]
        for c in range(3):
            raw[c, at] = seed_disp[c, i]
        return 0

    lax.fori_loop(0, nx, fill, 0)
    low, high = HALO, HALO + nx
    prepare(low + 1, high - 1, soft, pull, raw, g, k, state0)
    first_sweep([(low + 2, high - 2)], state0, state1, g, k, mu_scale)


def sides_kernel(
    work, near, near_late, far, far_late,
    less_in, soft_in, pull_in, scale_in, raw_in, g_in, k_in, state0_in, state1_in,
    less, soft, pull, mu_scale, raw, g, k, state0, state1, grads,
):
    nx = soft.shape[0] - 2 * HALO
    low, high = HALO, HALO + nx
    inside = in_grid()
    for s in range(2):
        x_in, late = received_x(near, far, s), received_x(near_late, far_late, s)
        for depth in range(4):
            at = low - 1 - depth if s == 0 else high + depth
            own = late(LATE_DAMAGE) if depth == 3 else x_in(X_DAMAGE + depth)
            soft[at] = soft_of(own)
            if depth == 3:
                continue
            own = own - 1.0
            if depth == 0:
                less[at] = own
            if depth == 2:
                pull[0, at] = own * late(LATE_PULL)
                state0[0, at] = late(LATE_MU)
            else:
                pulls = [x_in(X_PULL + 2 * c + depth) for c in range(3)]
                mu_scale[at] = jnp.where(inside[s], 0.25 * mu_inverse(*pulls), 0.0)
                state0[0, at] = x_in(X_MU + depth)
            for c in range(3):
                if depth == 2:
                    raw[c, at] = late(LATE_SOURCE + c)
                else:
                    pull[c, at] = own * pulls[c]
                    raw[c, at] = x_in(X_SOURCE + 2 * c + depth)

    for first, last in ((low - 3, low + 1), (high - 1, high + 3)):
        prepare(first, last, soft, pull, raw, g, k, state0)
    slopes(low, high, work[0, 0], less, grads)
    first_sweep([(low - 2, low + 2), (high - 2, high + 2)], state0, state1, g, k, mu_scale)


def edges_kernel(
    soft, pull, mu_scale, raw, g, state0, state1, y_pal, y_other, c_other, c_pal,
    sent_pal, sent_other, coefficients, firsts, seconds, outer,
    field, sent_low, sent_high,
):
    planes, ny, nz = soft.shape
    nx = planes - 2 * HALO
    (c1, c2), (d1, d2), _ = weights()
    lane = lax.broadcasted_iota(jnp.int32, (planes, nz), 1)
    plane = lax.broadcasted_iota(jnp.int32, (planes, nz), 0)
    here, there = lax.axis_index("gx"), lax.axis_index("gy")
    in_x = ((plane >= HALO) | (here > 0)) & ((plane < HALO + nx) | (here < lax.axis_size("gx") - 1))
    in_y = (there > 0, there < lax.axis_size("gy") - 1)

    def around_x(value):
        return [pltpu.roll(value, planes - 1, 0), pltpu.roll(value, 1, 0)]

    def around_z(value, fill):
        return [lane_up(value, fill), lane_down(value, fill)]

    for s, sent in enumerate((sent_low, sent_high)):
        y_in, c_in = received_y(y_pal, y_other, s), received_y(c_pal, c_other, s)
        e0, e1 = edge_row(s, ny, 0), edge_row(s, ny, 1)

        def ordered(inward, outward):
            return [inward, outward] if s == 0 else [outward, inward]

        row = 0
        for f in range(Y_FIELDS):
            field[f, HALO : HALO + nx, :] = y_in(f * nx, nx)
            count, shift = (Y_HALO[f], 0) if f < Y_KNOWN else (2, 1)
            field[f, HALO - count + shift : HALO + shift, :] = c_in(row, count)
            high = HALO + nx - shift
            field[f, high : high + count, :] = c_in(CORNER_ROWS + row, count)
            row += count

        soft_1, soft_2 = soft_of(field[0]), soft_of(field[1])
        soft_e0, soft_e1 = soft[:, e0, :], soft[:, e1, :]

        def total(center, inward, outward):
            return sum(around_x(center) + [inward, outward] + around_z(center, OUTSIDE))

        inverse_1 = lam_inverse(soft_1, total(soft_1, soft_e0, soft_2))
        inverse_1 = jnp.where(in_x & in_y[s], inverse_1, 0.0)
        lam_1 = [inverse_1 * field[5 + c] for c in range(3)]
        inverse_e0 = jnp.where(in_x, lam_inverse(soft_e0, total(soft_e0, soft_e1, soft_1)), 0.0)
        lam_e0 = [inverse_e0 * raw[c, :, e0, :] for c in range(3)]
        mu_1, wy_1 = field[3], field[2]
        mu_e0, mu_e1 = state0[0, :, e0, :], state0[0, :, e1, :]
        lam_e1 = [state0[1 + c, :, e1, :] for c in range(3)]

        def coefficients_of(center, inverse, inward, outward, wx, wy, wz):
            sides = around_x(center) + ordered(inward, outward) + around_z(center, OUTSIDE)
            eighth = 0.125 * inverse
            faces = [eighth * (center + side) for side in sides]
            faces[4] = jnp.where(lane == nz - 1, 0.0, faces[4])
            faces[5] = jnp.where(lane == 0, 0.0, faces[5])
            pulls = around_x(wx) + wy + around_z(wz, 0.0)
            return faces, [inverse * w if j % 2 == 0 else -inverse * w for j, w in enumerate(pulls)]

        def moved_of(faces, pulls, scale, own, inward, outward):
            sides = [
                around_x(own[f]) + ordered(inward[f], outward[f]) + around_z(own[f], 0.0) for f in range(4)
            ]
            moved = [scale * sum(sides[0])]
            for c in range(3):
                part = sum(faces[j] * sides[1 + c][j] for j in range(6))
                moved.append(part + pulls[2 * c] * sides[0][2 * c] + pulls[2 * c + 1] * sides[0][2 * c + 1])
            return moved

        first_1 = [jnp.where(in_x, field[Y_KNOWN] + c2 * field[4] * mu_e0, 0.0)]
        sides = around_x(soft_1) + around_z(soft_1, OUTSIDE) + [soft_e0]
        faces = [0.125 * (soft_1 + side) for side in sides]
        wy_e0 = pull[1, :, e0, :] * mu_e0
        own_1 = [mu_1] + lam_1
        own_e0 = [mu_e0] + lam_e0
        for c in range(3):
            sides = around_x(lam_1[c]) + around_z(lam_1[c], 0.0) + [lam_e0[c]]
            lacked = sum(faces[j] * sides[j] for j in range(5))
            if c == 1:
                lacked += wy_e0 if s == 0 else -wy_e0
            first_1.append(inverse_1 * (field[Y_KNOWN + 1 + c] + c2 * lacked))

        scale_e0 = mu_scale[:, e0, :]
        wy = ordered(pull[1, :, e1, :], wy_1)
        faces, pulls = coefficients_of(
            soft_e0, inverse_e0, soft_e1, soft_1, pull[0, :, e0, :], wy, pull[2, :, e0, :]
        )
        moved = moved_of(faces, pulls, scale_e0, own_e0, [mu_e1] + lam_e1, own_1)
        first_e0 = [(1.0 + c1) * own_e0[f] + c2 * moved[f] for f in range(4)]

        outward_face = g[3 if s == 0 else 2, :, e1, :]
        first_e1 = [state1[0, :, e1, :]]
        for c in range(3):
            first_e1.append(state1[1 + c, :, e1, :] + c2 * outward_face * lam_e0[c])

        moved = moved_of(faces, pulls, scale_e0, first_e0, first_e1, first_1)
        for f in range(4):
            second = first_e0[f] + (d1 - d2) * (first_e0[f] - own_e0[f]) + d2 * moved[f]
            sent[f * nx : (f + 1) * nx, :] = second[HALO : HALO + nx, :]
            firsts[s, f] = first_e0[f]
            outer[s, f] = first_1[f]
        for j in range(6):
            coefficients[s, j] = faces[j]
            coefficients[s, 6 + j] = pulls[j]
        for c in range(3):
            coefficients[s, 12 + c] = lam_e0[c]
            seconds[s, c] = first_e1[1 + c]
    deal(sent_pal, sent_other, sent_low, sent_high)


def sweep(first, last, state, g, k, mu_scale, rows, advance, finish=None):
    _, ny, nz = mu_scale.shape
    lane = lax.broadcasted_iota(jnp.int32, (ny, nz), 1)
    if rows is None:

        def rows(s, f, at):
            return 0.0

    def plane(at, _):
        def around(f):
            own = state[f, at]
            return own, [
                state[f, at + 1],
                state[f, at - 1],
                row_up(own, rows(1, f, at)),
                row_down(own, rows(0, f, at)),
                pltpu.roll(own, nz - 1, 1),
                pltpu.roll(own, 1, 1),
            ]

        mu, mu_sides = around(0)
        ends = [
            jnp.where(lane == nz - 1, 0.0, mu_sides[4]),
            jnp.where(lane == 0, 0.0, mu_sides[5]),
        ]
        results = [advance(at, 0, mu, mu_scale[at] * sum(mu_sides[:4] + ends))]
        faces = [g[j, at] for j in range(6)]
        for c in range(3):
            lam, lam_sides = around(1 + c)
            moved = sum(faces[j] * lam_sides[j] for j in range(6))
            moved += k[2 * c, at] * mu_sides[2 * c] + k[2 * c + 1, at] * mu_sides[2 * c + 1]
            results.append(advance(at, 1 + c, lam, moved))
        if finish is not None:
            finish(at - HALO, results)
        return 0

    lax.fori_loop(first, last, plane, 0)


def wait_kernel(
    work, less, grads, y_pal, y_other,
    mu_scale, coefficients, firsts, seconds, outer, g_in, k_in, state0_in, state1_in,
    out_mu, out_lam, edges, g, k, state0, state1,
    state2, states,
):
    _, nx, ny, _ = grads.shape
    planes = nx + 2 * HALO
    _, (d1, d2), (c1, c2) = weights()
    held = slice(HALO - 2, HALO + nx + 2)
    for s in range(2):
        e0, e1 = edge_row(s, ny, 0), edge_row(s, ny, 1)
        for j in range(6):
            g[j, held, e0, :] = coefficients[s, j, held, :]
            k[j, held, e0, :] = coefficients[s, 6 + j, held, :]
        for c in range(3):
            state0[1 + c, held, e0, :] = coefficients[s, 12 + c, held, :]
            state1[1 + c, held, e1, :] = seconds[s, c, held, :]
        for f in range(4):
            state1[f, held, e0, :] = firsts[s, f, held, :]

    def rows(s, f, at):
        return outer[s, f, pl.ds(at, 1), :]

    def advance_2(at, f, own, moved):
        state2[f, at] = own + (d1 - d2) * (own - state0[f, at]) + d2 * moved

    sweep(HALO - 1, HALO + nx + 1, state1, g, k, mu_scale, rows, advance_2)

    def advance_3(at, f, own, moved):
        return own + c1 * (own - state1[f, at]) + c2 * (state0[f, at] - own + moved)

    def finish(i, results):
        out_mu[i] = results[0]
        along = grads[3, i] * sum(grads[c, i] * results[1 + c] for c in range(3))
        for c in range(3):
            out_lam[c, i] = results[1 + c] - along * grads[c, i]
            states[c, i] = results[1 + c]

    sweep(HALO, HALO + nx, state2, g, k, mu_scale, None, advance_3, finish)

    for s in range(2):
        y_in = received_y(y_pal, y_other, s)
        e0, e1 = edge_row(s, ny, 0), edge_row(s, ny, 1)
        own = less[HALO : HALO + nx, e0, :]
        inward, outward = less[HALO : HALO + nx, e1, :], y_in(0, nx) - 1.0
        grad = [
            0.5 * (less[HALO + 1 : HALO + nx + 1, e0, :] - less[HALO - 1 : HALO + nx - 1, e0, :]),
            0.5 * (inward - outward if s == 0 else outward - inward),
            0.5 * (lane_up(own, -1.0) - lane_down(own, -1.0)),
        ]
        for c in range(3):
            edges[s, c] = grad[c]
            edges[s, 4 + c] = states[c, :, e0, :]
        edges[s, 3] = reach_of(grad, work[0, 0])


def last_kernel(
    mu_scale, coefficients, edges, y_other, y_pal, mu_in, lam_in,
    out_mu, out_lam, mu, lam,
    sems,
):
    nx, ny, nz = mu.shape
    inner = slice(HALO, HALO + nx)
    _, _, (_, c2) = weights()
    for s in range(2):
        y_in = received_y(y_pal, y_other, s)
        e0 = edge_row(s, ny, 0)
        outward = 3 if s == 0 else 2

        def got(f):
            return y_in(f * nx, nx)

        mu[:, e0, :] = mu[:, e0, :] + c2 * mu_scale[inner, e0, :] * got(0)
        face = c2 * coefficients[s, outward, inner, :]
        ends = []
        for c in range(3):
            end = edges[s, 4 + c] + face * got(1 + c)
            if c == 1:
                end += c2 * coefficients[s, 6 + outward, inner, :] * got(0)
            ends.append(end)
        along = edges[s, 3] * sum(edges[s, c] * ends[c] for c in range(3))
        for c in range(3):
            lam[c, :, e0, :] = ends[c] - along * edges[s, c]
    copies = [
        pltpu.make_async_copy(mu, out_mu, sems.at[0]),
        pltpu.make_async_copy(lam, out_lam, sems.at[1]),
    ]
    for copy in copies:
        copy.start()
    for copy in copies:
        copy.wait()


VMEM = pl.BlockSpec(memory_space=pltpu.VMEM)
SMEM = pl.BlockSpec(memory_space=pltpu.SMEM)
HBM = pl.BlockSpec(memory_space=pltpu.HBM)
ANY = pl.BlockSpec(memory_space=pl.ANY)
MIB = 1024 * 1024


def call(kernel, ins, outs, scratch=(), in_specs=None, out_specs=None, aliases=None, grant=24 * MIB):
    return pl.pallas_call(
        kernel,
        out_shape=[jax.ShapeDtypeStruct(shape, F32) for shape in outs],
        in_specs=in_specs or [VMEM] * len(ins),
        out_specs=out_specs or [VMEM] * len(outs),
        scratch_shapes=[pltpu.VMEM(shape, F32) if isinstance(shape, tuple) else shape for shape in scratch],
        input_output_aliases=aliases or {},
        compiler_params=pltpu.CompilerParams(vmem_limit_bytes=grant),
    )(*ins)


def trade(value, axis, first):
    pairs = [(i, i + 1) for i in range(first, lax.axis_size(axis) - 1, 2)]
    return lax.ppermute(value, axis, pairs + [(j, i) for i, j in pairs])


def body(damage, strain, seed_damage, seed_disp, brick_work):
    nx, ny, nz = damage.shape
    plane = (ny, nz)
    brick = (nx,) + plane
    bricks = (3,) + brick
    framed = (nx + 2 * HALO,) + plane
    state = (4,) + framed
    row = (nx + 2 * HALO, nz)
    fields = (damage, strain, seed_damage, seed_disp)

    y_rows = (Y_FIELDS * nx, nz)
    pal, token = call(
        pal_rows_kernel, fields, [y_rows, (1, 1)],
        [brick, bricks, brick, bricks, y_rows, pltpu.SemaphoreType.DMA((4,)), pltpu.SemaphoreType.DMA],
        in_specs=[HBM] * 4, out_specs=[HBM, SMEM], grant=56 * MIB,
    )
    x_faces = [(X_SLOTS,) + plane, (LATE_SLOTS,) + plane]
    near, near_late, far, far_late, other = call(
        faces_kernel, fields + (token,), x_faces * 2 + [y_rows], in_specs=[VMEM] * 4 + [SMEM]
    )
    y_in = (trade(pal, "gy", 0), trade(other, "gy", 1))
    far, far_late = trade(far, "gx", 1), trade(far_late, "gx", 1)
    near, near_late = trade(near, "gx", 0), trade(near_late, "gx", 0)
    inner = tuple(call(
        inner_kernel, fields,
        [framed, framed, (3,) + framed, framed, (3,) + framed, (6,) + framed, (6,) + framed, state, state],
    ))
    c_rows = (2 * CORNER_ROWS, nz)
    pal, other = call(
        corners_kernel, fields + (near, far, inner[0]), [c_rows] * 2,
        [(15,) + plane, c_rows, c_rows], in_specs=[VMEM] * 6 + [ANY],
    )
    other = trade(other, "gy", 1)
    c_in = (other, trade(pal, "gy", 0))
    less, soft, pull, mu_scale, raw, g, k, state0, state1, grads = call(
        sides_kernel, (brick_work, near, near_late, far, far_late) + inner,
        [part.shape for part in inner] + [(4,) + brick],
        in_specs=[SMEM] + [VMEM] * 13, aliases={5 + part: part for part in range(9)},
    )
    sent = (4 * nx, nz)
    pal, other, coefficients, firsts, seconds, outer = call(
        edges_kernel, (soft, pull, mu_scale, raw, g, state0, state1) + y_in + c_in,
        [sent] * 2 + [(2, 15) + row, (2, 4) + row, (2, 3) + row, (2, 4) + row],
        [(Y_FIELDS,) + row, sent, sent],
    )
    other = trade(other, "gy", 1)
    halo = (other, trade(pal, "gy", 0))
    ins = (brick_work, less, grads) + y_in + (mu_scale, coefficients, firsts, seconds, outer, g, k, state0, state1)
    mu, lam, edges, *_ = call(
        wait_kernel, ins,
        [brick, bricks, (2, 7, nx, nz), (6,) + framed, (6,) + framed, state, state],
        [state, bricks],
        in_specs=[SMEM] + [VMEM] * (len(ins) - 1),
        aliases={10: 3, 11: 4, 12: 5, 13: 6},
    )
    out_mu, out_lam, *_ = call(
        last_kernel, (mu_scale, coefficients, edges) + halo + (mu, lam),
        [brick, bricks, brick, bricks], [pltpu.SemaphoreType.DMA((2,))],
        out_specs=[HBM, HBM, VMEM, VMEM], aliases={5: 2, 6: 3},
    )
    return out_mu, out_lam


def solution(mesh):
    placed = (
        P("gx", "gy", None),
        P(None, "gx", "gy", None),
        P("gx", "gy", None),
        P(None, "gx", "gy", None),
        P("gx", "gy"),
    )
    return jax.shard_map(
        body,
        mesh=mesh,
        in_specs=placed,
        out_specs=(P("gx", "gy", None), P(None, "gx", "gy", None)),
        check_vma=False,
    )
```

```python
import functools

import jax
import jax.numpy as jnp
from jax import lax
from jax.experimental import pallas as pl
from jax.experimental.pallas import tpu as pltpu
from jax.sharding import PartitionSpec as P

RELAX_INNER = 8
RESIDUAL_STIFFNESS = 0.001
CENTER_VALUE = 1.0
HALF_WIDTH = 0.75
NORMAL_WEIGHT = 1.5
RELAX_RATE = 0.5 / RELAX_INNER
NORMAL_FLOOR = 0.05
OUTSIDE = 1.0 + RESIDUAL_STIFFNESS
F32 = jnp.float32


def weights():
    ratio = CENTER_VALUE / HALF_WIDTH
    rho = 1.0 / ratio
    found = []
    for _ in range(3):
        rho_next = 1.0 / (2.0 * ratio - rho)
        found.append((rho_next * rho, 2.0 * rho_next / HALF_WIDTH))
        rho = rho_next
    return found


def soft_of(damage):
    return (1.0 - damage) ** 2 + RESIDUAL_STIFFNESS


def row_up(plane, beyond):
    rows = plane.shape[0]
    at = lax.broadcasted_iota(jnp.int32, plane.shape, 0)
    return jnp.where(at == rows - 1, beyond, pltpu.roll(plane, rows - 1, 0))


def row_down(plane, beyond):
    at = lax.broadcasted_iota(jnp.int32, plane.shape, 0)
    return jnp.where(at == 0, beyond, pltpu.roll(plane, 1, 0))


def lane_up(plane, beyond):
    cells = plane.shape[1]
    at = lax.broadcasted_iota(jnp.int32, plane.shape, 1)
    return jnp.where(at == cells - 1, beyond, pltpu.roll(plane, cells - 1, 1))


def lane_down(plane, beyond):
    at = lax.broadcasted_iota(jnp.int32, plane.shape, 1)
    return jnp.where(at == 0, beyond, pltpu.roll(plane, 1, 1))


def mu_inverse(ex, ey, ez):
    return 1.0 / (2.0 + (ex * ex + ey * ey + ez * ez))


def lam_inverse(center, total):
    return 1.0 / (0.5 + 0.125 * (6.0 * center + total))


HALO = 4
X_DAMAGE, X_PULL, X_MU, X_SOURCE, X_SLOTS = 0, 3, 9, 11, 17
LATE_DAMAGE, LATE_PULL, LATE_MU, LATE_SOURCE, LATE_SLOTS = 0, 1, 2, 3, 6
Y_HALO = (3, 2, 2, 2, 1, 2, 2, 2)
Y_KNOWN, Y_FIELDS = 8, 12
CORNER_ROWS = sum(Y_HALO) + 8


def edge_row(s, ny, depth):
    return depth if s == 0 else ny - 1 - depth


def known_of(s, damages, pulls, behind_pull, mus, sources, behind):
    planes = damages[0].shape[0]
    (c1, c2), _, _ = weights()
    soft = [soft_of(part) for part in damages]
    less = damages[0] - 1.0
    wx, wy, wz = (less * pull for pull in pulls)
    wy_behind = (damages[1] - 1.0) * behind_pull

    def across(value):
        return pltpu.roll(value, planes - 1, 0), pltpu.roll(value, 1, 0)

    def along(value, fill):
        return lane_up(value, fill), lane_down(value, fill)

    total = soft[0] + soft[2] + sum(across(soft[1])) + sum(along(soft[1], OUTSIDE))
    inverse = lam_inverse(soft[1], total)
    face = 0.125 * (soft[0] + soft[1])
    scale = 0.25 * mu_inverse(*pulls)
    known = [(1.0 + c1) * mus[0] + c2 * scale * (mus[1] + sum(across(mus[0])) + sum(along(mus[0], 0.0)))]
    x_up, x_down = across(wx * mus[0])
    z_up, z_down = along(wz * mus[0], 0.0)
    y_behind = wy_behind * mus[1]
    transfers = (x_up - x_down, y_behind if s == 0 else -y_behind, z_up - z_down)
    for c in range(3):
        known.append((1.0 + c1) * sources[c] + c2 * (face * (inverse * behind[c]) + transfers[c]))
    return scale, wy, known


def put_rows(s, put, damage, strain, seed_damage, seed_disp, ready=lambda field: None):
    ny = damage.shape[1]
    first, second, third = (edge_row(s, ny, depth) for depth in range(3))
    ready(0)
    damages = [damage[:, row, :] for row in (first, second, third)]
    ready(1)
    pulls = [strain[c, :, first, :] for c in range(3)]
    pulls_behind = [strain[c, :, second, :] for c in range(3)]
    ready(2)
    mus = [
        seed_damage[:, first, :] * mu_inverse(*pulls),
        seed_damage[:, second, :] * mu_inverse(*pulls_behind),
    ]
    ready(3)
    sources = [seed_disp[c, :, first, :] for c in range(3)]
    behind = [seed_disp[c, :, second, :] for c in range(3)]
    scale, wy, known = known_of(s, damages, pulls, pulls_behind[1], mus, sources, behind)
    for slot, value in enumerate(damages[:2] + [wy, mus[0], scale] + sources + known):
        put(slot, value)


def even(axis):
    return lax.rem(lax.axis_index(axis), 2) == 0


def halves(source, target, sems, first):
    half = source.shape[0] // 2
    parts = (pl.ds(0, half), pl.ds(half, half))
    return [pltpu.make_async_copy(source.at[part], target.at[part], sems.at[first + i]) for i, part in enumerate(parts)]


def pal_rows_kernel(
    damage_in, strain_in, seed_in, sources_in, out, token,
    damage, strain, seed_damage, seed_disp, rows, sems, out_sems,
):
    nx = damage.shape[0]
    token[0, 0] = 0.0
    copies = [halves(damage_in, damage, sems, 0), [], halves(seed_in, seed_damage, sems, 2), []]
    for c in range(3):
        copies[1] += halves(strain_in.at[c], strain.at[c], sems, 4 + 2 * c)
        copies[3] += halves(sources_in.at[c], seed_disp.at[c], sems, 10 + 2 * c)
    for group in copies:
        for copy in group:
            copy.start()

    def ready(field):
        for copy in copies[field]:
            copy.wait()

    sent = []

    def put(slot, value):
        rows[slot * nx : (slot + 1) * nx, :] = value
        if slot % 4 == 3:
            part = pl.ds((slot - 3) * nx, 4 * nx)
            copy = pltpu.make_async_copy(rows.at[part], out.at[part], out_sems.at[slot // 4])
            copy.start()

    for s in range(2):

        @pl.when(even("gy") == (s == 1))
        def _():
            put_rows(s, put, damage, strain, seed_damage, seed_disp, ready)

    for group in range(Y_FIELDS // 4):
        part = pl.ds(group * 4 * nx, 4 * nx)
        pltpu.make_async_copy(rows.at[part], out.at[part], out_sems.at[group]).wait()


def faces_kernel(
    damage, strain, seed_damage, seed_disp, _, near, near_late, far, far_late, rows
):
    nx = damage.shape[0]

    def put(slot, value):
        rows[slot * nx : (slot + 1) * nx, :] = value

    for s in range(2):

        @pl.when(even("gy") == (s == 0))
        def _():
            put_rows(s, put, damage, strain, seed_damage, seed_disp)

    for out, late, high in ((near, near_late, even("gx")), (far, far_late, ~even("gx"))):
        for depth in range(4):
            at = jnp.where(high, nx - 1 - depth, depth)
            if depth == 3:
                late[LATE_DAMAGE] = damage[at]
                continue
            out[X_DAMAGE + depth] = damage[at]
            pulls = [strain[c, at] for c in range(3)]
            mu = seed_damage[at] * mu_inverse(*pulls)
            if depth == 2:
                late[LATE_PULL] = pulls[0]
                late[LATE_MU] = mu
            else:
                out[X_MU + depth] = mu
            for c in range(3):
                if depth == 2:
                    late[LATE_SOURCE + c] = seed_disp[c, at]
                else:
                    out[X_PULL + 2 * c + depth] = pulls[c]
                    out[X_SOURCE + 2 * c + depth] = seed_disp[c, at]


def received_x(near, far, side):
    from_near = even("gx") == (side == 1)

    def plane(slot, row=None):
        at = slot if row is None else (slice(slot, slot + 1), row)
        return jnp.where(from_near, near[at], far[at])

    return plane


def received_y(pal, other, side):
    from_pal = even("gy") == (side == 1)
    return lambda first, count: jnp.where(from_pal, pal[first : first + count, :], other[first : first + count, :])


def deal(pal, other, low, high):
    first = even("gy")
    low, high = low[...], high[...]
    pal[...] = jnp.where(first, high, low)
    other[...] = jnp.where(first, low, high)


def corners_kernel(
    damage, strain, seed_damage, seed_disp, near, far, _, pal, other, field, low, high
):
    nx, ny, _ = damage.shape
    for s, out in enumerate((low, high)):
        first, second, third = (edge_row(s, ny, depth) for depth in range(3))
        for side in range(2):
            x_in = received_x(near, far, side)
            ours = slice(3, 8) if side == 0 else slice(0, 5)
            planes = slice(0, 5) if side == 0 else slice(nx - 5, nx)

            def put_x(slot, first, count, row):
                for far_off in range(count):
                    at = 2 - far_off if side == 0 else 5 + far_off
                    field[slot, at : at + 1, :] = x_in(first + far_off, row)

            for depth, row in enumerate((first, second, third)):
                field[depth, ours, :] = damage[planes, row, :]
                put_x(depth, X_DAMAGE, 3, row)
            for depth, row in enumerate((first, second)):
                pulls = [strain[c, planes, row, :] for c in range(3)]
                for c in range(3):
                    if depth == 0:
                        field[3 + c, ours, :] = pulls[c]
                        put_x(3 + c, X_PULL + 2 * c, 2, row)
                    field[9 + 3 * depth + c, ours, :] = seed_disp[c, planes, row, :]
                    put_x(9 + 3 * depth + c, X_SOURCE + 2 * c, 2, row)
                if depth == 1:
                    field[6, ours, :] = pulls[1]
                    put_x(6, X_PULL + 2, 2, row)
                field[7 + depth, ours, :] = seed_damage[planes, row, :] * mu_inverse(*pulls)
                put_x(7 + depth, X_MU, 2, row)
            got = [field[slot] for slot in range(15)]
            scale, wy, known = known_of(s, got[:3], got[3:6], got[6], got[7:9], got[9:12], got[12:15])
            row = side * CORNER_ROWS
            for slot, value in enumerate(got[:2] + [wy, got[7], scale] + got[9:12]):
                count = Y_HALO[slot]
                start = 3 - count if side == 0 else 5
                out[row : row + count, :] = value[start : start + count, :]
                row += count
            for value in known:
                start = 2 if side == 0 else 4
                out[row : row + 2, :] = value[start : start + 2, :]
                row += 2
    deal(pal, other, low, high)


def in_grid():
    here = lax.axis_index("gx")
    return here > 0, here < lax.axis_size("gx") - 1


def prepare(first, last, soft, pull, raw, g, k, state0):
    planes, ny, nz = soft.shape
    inside = in_grid()
    lane = lax.broadcasted_iota(jnp.int32, (ny, nz), 1)
    row = lax.broadcasted_iota(jnp.int32, (ny, nz), 0)
    inner = (row > 0) & (row < ny - 1)

    def step(at, _):
        center = soft[at]
        sides = [
            soft[at + 1],
            soft[at - 1],
            pltpu.roll(center, ny - 1, 0),
            pltpu.roll(center, 1, 0),
            lane_up(center, OUTSIDE),
            lane_down(center, OUTSIDE),
        ]
        outside = ((at < HALO) & ~inside[0]) | ((at >= planes - HALO) & ~inside[1])
        inverse = jnp.where(inner & ~outside, lam_inverse(center, sum(sides)), 0.0)
        eighth = 0.125 * inverse
        for j in range(6):
            face = eighth * (center + sides[j])
            if j == 4:
                face = jnp.where(lane == nz - 1, 0.0, face)
            if j == 5:
                face = jnp.where(lane == 0, 0.0, face)
            g[j, at] = face
        k[0, at] = inverse * pull[0, at + 1]
        k[1, at] = -inverse * pull[0, at - 1]
        k[2, at] = inverse * pltpu.roll(pull[1, at], ny - 1, 0)
        k[3, at] = -inverse * pltpu.roll(pull[1, at], 1, 0)
        k[4, at] = inverse * lane_up(pull[2, at], 0.0)
        k[5, at] = -inverse * lane_down(pull[2, at], 0.0)
        for c in range(3):
            state0[1 + c, at] = inverse * raw[c, at]
        return 0

    lax.fori_loop(first, last, step, 0)


def reach_of(grad, count):
    square = sum(part * part for part in grad)
    scale = 1.0 / jnp.maximum(square, NORMAL_FLOOR)
    power = 1.0 - RELAX_RATE * (1.0 + NORMAL_WEIGHT * square * scale)
    series = 1.0 + power
    for _ in range(2):
        power = power * power
        series = series * (1.0 + power)
    power = power * power
    repeats = jnp.ones_like(power)
    for level in range(1, 4):
        repeats = jnp.where(count > level, 1.0 + power * repeats, repeats)
    return (RELAX_RATE * NORMAL_WEIGHT * scale) * (series * repeats)


def slopes(first, last, count, less, grads):
    ny = less.shape[1]

    def step(at, _):
        own = less[at]
        grad = [
            0.5 * (less[at + 1] - less[at - 1]),
            0.5 * (pltpu.roll(own, ny - 1, 0) - pltpu.roll(own, 1, 0)),
            0.5 * (lane_up(own, -1.0) - lane_down(own, -1.0)),
        ]
        for c in range(3):
            grads[c, at - HALO] = grad[c]
        grads[3, at - HALO] = reach_of(grad, count)
        return 0

    lax.fori_loop(first, last, step, 0)


def first_sweep(ranges, state0, state1, g, k, mu_scale):
    (c1, c2), _, _ = weights()

    def advance(at, f, own, moved):
        state1[f, at] = (1.0 + c1) * own + c2 * moved

    for first, last in ranges:
        sweep(first, last, state0, g, k, mu_scale, None, advance)


def inner_kernel(
    damage, strain, seed_damage, seed_disp, less, soft, pull, mu_scale, raw, g, k, state0, state1
):
    nx = damage.shape[0]

    def fill(i, _):
        at = HALO + i
        own = damage[i]
        sx, sy, sz = strain[0, i], strain[1, i], strain[2, i]
        soft[at] = soft_of(own)
        own = own - 1.0
        less[at] = own
        pull[0, at] = own * sx
        pull[1, at] = own * sy
        pull[2, at] = own * sz
        mu_inv = mu_inverse(sx, sy, sz)
        mu_scale[at] = 0.25 * mu_inv
        state0[0, at] = mu_inv * seed_damage[i]
        for c in range(3):
            raw[c, at] = seed_disp[c, i]
        return 0

    lax.fori_loop(0, nx, fill, 0)
    low, high = HALO, HALO + nx
    prepare(low + 1, high - 1, soft, pull, raw, g, k, state0)
    first_sweep([(low + 2, high - 2)], state0, state1, g, k, mu_scale)


def sides_kernel(
    work, near, near_late, far, far_late,
    less_in, soft_in, pull_in, scale_in, raw_in, g_in, k_in, state0_in, state1_in,
    less, soft, pull, mu_scale, raw, g, k, state0, state1, grads,
):
    nx = soft.shape[0] - 2 * HALO
    low, high = HALO, HALO + nx
    inside = in_grid()
    for s in range(2):
        x_in, late = received_x(near, far, s), received_x(near_late, far_late, s)
        for depth in range(4):
            at = low - 1 - depth if s == 0 else high + depth
            own = late(LATE_DAMAGE) if depth == 3 else x_in(X_DAMAGE + depth)
            soft[at] = soft_of(own)
            if depth == 3:
                continue
            own = own - 1.0
            if depth == 0:
                less[at] = own
            if depth == 2:
                pull[0, at] = own * late(LATE_PULL)
                state0[0, at] = late(LATE_MU)
            else:
                pulls = [x_in(X_PULL + 2 * c + depth) for c in range(3)]
                mu_scale[at] = jnp.where(inside[s], 0.25 * mu_inverse(*pulls), 0.0)
                state0[0, at] = x_in(X_MU + depth)
            for c in range(3):
                if depth == 2:
                    raw[c, at] = late(LATE_SOURCE + c)
                else:
                    pull[c, at] = own * pulls[c]
                    raw[c, at] = x_in(X_SOURCE + 2 * c + depth)

    for first, last in ((low - 3, low + 1), (high - 1, high + 3)):
        prepare(first, last, soft, pull, raw, g, k, state0)
    slopes(low, high, work[0, 0], less, grads)
    first_sweep([(low - 2, low + 2), (high - 2, high + 2)], state0, state1, g, k, mu_scale)


def edges_kernel(
    soft, pull, mu_scale, raw, g, state0, state1, y_pal, y_other, c_pal, c_other,
    sent_pal, sent_other, coefficients, firsts, seconds, outer,
    field, sent_low, sent_high,
):
    planes, ny, nz = soft.shape
    nx = planes - 2 * HALO
    (c1, c2), (d1, d2), _ = weights()
    lane = lax.broadcasted_iota(jnp.int32, (planes, nz), 1)
    plane = lax.broadcasted_iota(jnp.int32, (planes, nz), 0)
    here, there = lax.axis_index("gx"), lax.axis_index("gy")
    in_x = ((plane >= HALO) | (here > 0)) & ((plane < HALO + nx) | (here < lax.axis_size("gx") - 1))
    in_y = (there > 0, there < lax.axis_size("gy") - 1)

    def around_x(value):
        return [pltpu.roll(value, planes - 1, 0), pltpu.roll(value, 1, 0)]

    def around_z(value, fill):
        return [lane_up(value, fill), lane_down(value, fill)]

    for s, sent in enumerate((sent_low, sent_high)):
        y_in, c_in = received_y(y_pal, y_other, s), received_y(c_pal, c_other, s)
        e0, e1 = edge_row(s, ny, 0), edge_row(s, ny, 1)

        def ordered(inward, outward):
            return [inward, outward] if s == 0 else [outward, inward]

        row = 0
        for f in range(Y_FIELDS):
            field[f, HALO : HALO + nx, :] = y_in(f * nx, nx)
            count, shift = (Y_HALO[f], 0) if f < Y_KNOWN else (2, 1)
            field[f, HALO - count + shift : HALO + shift, :] = c_in(row, count)
            high = HALO + nx - shift
            field[f, high : high + count, :] = c_in(CORNER_ROWS + row, count)
            row += count

        soft_1, soft_2 = soft_of(field[0]), soft_of(field[1])
        soft_e0, soft_e1 = soft[:, e0, :], soft[:, e1, :]

        def total(center, inward, outward):
            return sum(around_x(center) + [inward, outward] + around_z(center, OUTSIDE))

        inverse_1 = lam_inverse(soft_1, total(soft_1, soft_e0, soft_2))
        inverse_1 = jnp.where(in_x & in_y[s], inverse_1, 0.0)
        lam_1 = [inverse_1 * field[5 + c] for c in range(3)]
        inverse_e0 = jnp.where(in_x, lam_inverse(soft_e0, total(soft_e0, soft_e1, soft_1)), 0.0)
        lam_e0 = [inverse_e0 * raw[c, :, e0, :] for c in range(3)]
        mu_1, wy_1 = field[3], field[2]
        mu_e0, mu_e1 = state0[0, :, e0, :], state0[0, :, e1, :]
        lam_e1 = [state0[1 + c, :, e1, :] for c in range(3)]

        def coefficients_of(center, inverse, inward, outward, wx, wy, wz):
            sides = around_x(center) + ordered(inward, outward) + around_z(center, OUTSIDE)
            eighth = 0.125 * inverse
            faces = [eighth * (center + side) for side in sides]
            faces[4] = jnp.where(lane == nz - 1, 0.0, faces[4])
            faces[5] = jnp.where(lane == 0, 0.0, faces[5])
            pulls = around_x(wx) + wy + around_z(wz, 0.0)
            return faces, [inverse * w if j % 2 == 0 else -inverse * w for j, w in enumerate(pulls)]

        def moved_of(faces, pulls, scale, own, inward, outward):
            sides = [
                around_x(own[f]) + ordered(inward[f], outward[f]) + around_z(own[f], 0.0) for f in range(4)
            ]
            moved = [scale * sum(sides[0])]
            for c in range(3):
                part = sum(faces[j] * sides[1 + c][j] for j in range(6))
                moved.append(part + pulls[2 * c] * sides[0][2 * c] + pulls[2 * c + 1] * sides[0][2 * c + 1])
            return moved

        first_1 = [jnp.where(in_x, field[Y_KNOWN] + c2 * field[4] * mu_e0, 0.0)]
        sides = around_x(soft_1) + around_z(soft_1, OUTSIDE) + [soft_e0]
        faces = [0.125 * (soft_1 + side) for side in sides]
        wy_e0 = pull[1, :, e0, :] * mu_e0
        own_1 = [mu_1] + lam_1
        own_e0 = [mu_e0] + lam_e0
        for c in range(3):
            sides = around_x(lam_1[c]) + around_z(lam_1[c], 0.0) + [lam_e0[c]]
            lacked = sum(faces[j] * sides[j] for j in range(5))
            if c == 1:
                lacked += wy_e0 if s == 0 else -wy_e0
            first_1.append(inverse_1 * (field[Y_KNOWN + 1 + c] + c2 * lacked))

        scale_e0 = mu_scale[:, e0, :]
        wy = ordered(pull[1, :, e1, :], wy_1)
        faces, pulls = coefficients_of(
            soft_e0, inverse_e0, soft_e1, soft_1, pull[0, :, e0, :], wy, pull[2, :, e0, :]
        )
        moved = moved_of(faces, pulls, scale_e0, own_e0, [mu_e1] + lam_e1, own_1)
        first_e0 = [(1.0 + c1) * own_e0[f] + c2 * moved[f] for f in range(4)]

        outward_face = g[3 if s == 0 else 2, :, e1, :]
        first_e1 = [state1[0, :, e1, :]]
        for c in range(3):
            first_e1.append(state1[1 + c, :, e1, :] + c2 * outward_face * lam_e0[c])

        moved = moved_of(faces, pulls, scale_e0, first_e0, first_e1, first_1)
        for f in range(4):
            second = first_e0[f] + (d1 - d2) * (first_e0[f] - own_e0[f]) + d2 * moved[f]
            sent[f * nx : (f + 1) * nx, :] = second[HALO : HALO + nx, :]
            firsts[s, f] = first_e0[f]
            outer[s, f] = first_1[f]
        for j in range(6):
            coefficients[s, j] = faces[j]
            coefficients[s, 6 + j] = pulls[j]
        for c in range(3):
            coefficients[s, 12 + c] = lam_e0[c]
            seconds[s, c] = first_e1[1 + c]
    deal(sent_pal, sent_other, sent_low, sent_high)


def sweep(first, last, state, g, k, mu_scale, rows, advance, finish=None):
    _, ny, nz = mu_scale.shape
    lane = lax.broadcasted_iota(jnp.int32, (ny, nz), 1)
    if rows is None:

        def rows(s, f, at):
            return 0.0

    def plane(at, _):
        def around(f):
            own = state[f, at]
            return own, [
                state[f, at + 1],
                state[f, at - 1],
                row_up(own, rows(1, f, at)),
                row_down(own, rows(0, f, at)),
                pltpu.roll(own, nz - 1, 1),
                pltpu.roll(own, 1, 1),
            ]

        mu, mu_sides = around(0)
        ends = [
            jnp.where(lane == nz - 1, 0.0, mu_sides[4]),
            jnp.where(lane == 0, 0.0, mu_sides[5]),
        ]
        results = [advance(at, 0, mu, mu_scale[at] * sum(mu_sides[:4] + ends))]
        faces = [g[j, at] for j in range(6)]
        for c in range(3):
            lam, lam_sides = around(1 + c)
            moved = sum(faces[j] * lam_sides[j] for j in range(6))
            moved += k[2 * c, at] * mu_sides[2 * c] + k[2 * c + 1, at] * mu_sides[2 * c + 1]
            results.append(advance(at, 1 + c, lam, moved))
        if finish is not None:
            finish(at - HALO, results)
        return 0

    lax.fori_loop(first, last, plane, 0)


def wait_kernel(
    work, less, grads, y_pal, y_other,
    mu_scale, coefficients, firsts, seconds, outer, g_in, k_in, state0_in, state1_in,
    out_mu, out_lam, edges, g, k, state0, state1,
    state2, states,
):
    _, nx, ny, _ = grads.shape
    planes = nx + 2 * HALO
    _, (d1, d2), (c1, c2) = weights()
    held = slice(HALO - 2, HALO + nx + 2)
    for s in range(2):
        e0, e1 = edge_row(s, ny, 0), edge_row(s, ny, 1)
        for j in range(6):
            g[j, held, e0, :] = coefficients[s, j, held, :]
            k[j, held, e0, :] = coefficients[s, 6 + j, held, :]
        for c in range(3):
            state0[1 + c, held, e0, :] = coefficients[s, 12 + c, held, :]
            state1[1 + c, held, e1, :] = seconds[s, c, held, :]
        for f in range(4):
            state1[f, held, e0, :] = firsts[s, f, held, :]

    def rows(s, f, at):
        return outer[s, f, pl.ds(at, 1), :]

    def advance_2(at, f, own, moved):
        state2[f, at] = own + (d1 - d2) * (own - state0[f, at]) + d2 * moved

    sweep(HALO - 1, HALO + nx + 1, state1, g, k, mu_scale, rows, advance_2)

    def advance_3(at, f, own, moved):
        return own + c1 * (own - state1[f, at]) + c2 * (state0[f, at] - own + moved)

    def finish(i, results):
        out_mu[i] = results[0]
        along = grads[3, i] * sum(grads[c, i] * results[1 + c] for c in range(3))
        for c in range(3):
            out_lam[c, i] = results[1 + c] - along * grads[c, i]
            states[c, i] = results[1 + c]

    sweep(HALO, HALO + nx, state2, g, k, mu_scale, None, advance_3, finish)

    for s in range(2):
        y_in = received_y(y_pal, y_other, s)
        e0, e1 = edge_row(s, ny, 0), edge_row(s, ny, 1)
        own = less[HALO : HALO + nx, e0, :]
        inward, outward = less[HALO : HALO + nx, e1, :], y_in(0, nx) - 1.0
        grad = [
            0.5 * (less[HALO + 1 : HALO + nx + 1, e0, :] - less[HALO - 1 : HALO + nx - 1, e0, :]),
            0.5 * (inward - outward if s == 0 else outward - inward),
            0.5 * (lane_up(own, -1.0) - lane_down(own, -1.0)),
        ]
        for c in range(3):
            edges[s, c] = grad[c]
            edges[s, 4 + c] = states[c, :, e0, :]
        edges[s, 3] = reach_of(grad, work[0, 0])


def last_kernel(
    mu_scale, coefficients, edges, y_pal, y_other, mu_in, lam_in,
    out_mu, out_lam, mu, lam,
    sems,
):
    nx, ny, nz = mu.shape
    inner = slice(HALO, HALO + nx)
    _, _, (_, c2) = weights()
    for s in range(2):
        y_in = received_y(y_pal, y_other, s)
        e0 = edge_row(s, ny, 0)
        outward = 3 if s == 0 else 2

        def got(f):
            return y_in(f * nx, nx)

        mu[:, e0, :] = mu[:, e0, :] + c2 * mu_scale[inner, e0, :] * got(0)
        face = c2 * coefficients[s, outward, inner, :]
        ends = []
        for c in range(3):
            end = edges[s, 4 + c] + face * got(1 + c)
            if c == 1:
                end += c2 * coefficients[s, 6 + outward, inner, :] * got(0)
            ends.append(end)
        along = edges[s, 3] * sum(edges[s, c] * ends[c] for c in range(3))
        for c in range(3):
            lam[c, :, e0, :] = ends[c] - along * edges[s, c]
    copies = halves(mu, out_mu, sems, 0)
    for c in range(3):
        copies += halves(lam.at[c], out_lam.at[c], sems, 2 + 2 * c)
    for copy in copies:
        copy.start()
    for copy in copies:
        copy.wait()


VMEM = pl.BlockSpec(memory_space=pltpu.VMEM)
SMEM = pl.BlockSpec(memory_space=pltpu.SMEM)
HBM = pl.BlockSpec(memory_space=pltpu.HBM)
ANY = pl.BlockSpec(memory_space=pl.ANY)
MIB = 1024 * 1024


def call(kernel, ins, outs, scratch=(), in_specs=None, out_specs=None, aliases=None, grant=24 * MIB):
    return pl.pallas_call(
        kernel,
        out_shape=[jax.ShapeDtypeStruct(shape, F32) for shape in outs],
        in_specs=in_specs or [VMEM] * len(ins),
        out_specs=out_specs or [VMEM] * len(outs),
        scratch_shapes=[pltpu.VMEM(shape, F32) if isinstance(shape, tuple) else shape for shape in scratch],
        input_output_aliases=aliases or {},
        compiler_params=pltpu.CompilerParams(vmem_limit_bytes=grant),
    )(*ins)


def trade(value, axis, first):
    pairs = [(i, i + 1) for i in range(first, lax.axis_size(axis) - 1, 2)]
    return lax.ppermute(value, axis, pairs + [(j, i) for i, j in pairs])


def body(damage, strain, seed_damage, seed_disp, brick_work):
    nx, ny, nz = damage.shape
    plane = (ny, nz)
    brick = (nx,) + plane
    bricks = (3,) + brick
    framed = (nx + 2 * HALO,) + plane
    state = (4,) + framed
    row = (nx + 2 * HALO, nz)
    fields = (damage, strain, seed_damage, seed_disp)

    y_rows = (Y_FIELDS * nx, nz)
    pal, token = call(
        pal_rows_kernel, fields, [y_rows, (1, 1)],
        [brick, bricks, brick, bricks, y_rows, pltpu.SemaphoreType.DMA((16,)), pltpu.SemaphoreType.DMA((3,))],
        in_specs=[HBM] * 4, out_specs=[HBM, SMEM], grant=56 * MIB,
    )
    x_faces = [(X_SLOTS,) + plane, (LATE_SLOTS,) + plane]
    near, near_late, far, far_late, other = call(
        faces_kernel, fields + (token,), x_faces * 2 + [y_rows], in_specs=[VMEM] * 4 + [SMEM]
    )
    y_in = (trade(pal, "gy", 0), trade(other, "gy", 1))
    far, far_late = trade(far, "gx", 1), trade(far_late, "gx", 1)
    near, near_late = trade(near, "gx", 0), trade(near_late, "gx", 0)
    inner = tuple(call(
        inner_kernel, fields,
        [framed, framed, (3,) + framed, framed, (3,) + framed, (6,) + framed, (6,) + framed, state, state],
    ))
    c_rows = (2 * CORNER_ROWS, nz)
    pal, other = call(
        corners_kernel, fields + (near, far, inner[0]), [c_rows] * 2,
        [(15,) + plane, c_rows, c_rows], in_specs=[VMEM] * 6 + [ANY],
    )
    c_in = (trade(pal, "gy", 0), trade(other, "gy", 1))
    less, soft, pull, mu_scale, raw, g, k, state0, state1, grads = call(
        sides_kernel, (brick_work, near, near_late, far, far_late) + inner,
        [part.shape for part in inner] + [(4,) + brick],
        in_specs=[SMEM] + [VMEM] * 13, aliases={5 + part: part for part in range(9)},
    )
    sent = (4 * nx, nz)
    pal, other, coefficients, firsts, seconds, outer = call(
        edges_kernel, (soft, pull, mu_scale, raw, g, state0, state1) + y_in + c_in,
        [sent] * 2 + [(2, 15) + row, (2, 4) + row, (2, 3) + row, (2, 4) + row],
        [(Y_FIELDS,) + row, sent, sent],
    )
    halo = (trade(pal, "gy", 0), trade(other, "gy", 1))
    ins = (brick_work, less, grads) + y_in + (mu_scale, coefficients, firsts, seconds, outer, g, k, state0, state1)
    mu, lam, edges, *_ = call(
        wait_kernel, ins,
        [brick, bricks, (2, 7, nx, nz), (6,) + framed, (6,) + framed, state, state],
        [state, bricks],
        in_specs=[SMEM] + [VMEM] * (len(ins) - 1),
        aliases={10: 3, 11: 4, 12: 5, 13: 6},
    )
    out_mu, out_lam, *_ = call(
        last_kernel, (mu_scale, coefficients, edges) + halo + (mu, lam),
        [brick, bricks, brick, bricks], [pltpu.SemaphoreType.DMA((8,))],
        out_specs=[HBM, HBM, VMEM, VMEM], aliases={5: 2, 6: 3},
    )
    return out_mu, out_lam


def solution(mesh):
    placed = (
        P("gx", "gy", None),
        P(None, "gx", "gy", None),
        P("gx", "gy", None),
        P(None, "gx", "gy", None),
        P("gx", "gy"),
    )
    return jax.shard_map(
        body,
        mesh=mesh,
        in_specs=placed,
        out_specs=(P("gx", "gy", None), P(None, "gx", "gy", None)),
        check_vma=False,
    )
```

```python
import functools

import jax
import jax.numpy as jnp
from jax import lax
from jax.experimental import pallas as pl
from jax.experimental.pallas import tpu as pltpu
from jax.sharding import PartitionSpec as P

RELAX_INNER = 8
RESIDUAL_STIFFNESS = 0.001
CENTER_VALUE = 1.0
HALF_WIDTH = 0.75
NORMAL_WEIGHT = 1.5
RELAX_RATE = 0.5 / RELAX_INNER
NORMAL_FLOOR = 0.05
OUTSIDE = 1.0 + RESIDUAL_STIFFNESS
F32 = jnp.float32


def weights():
    ratio = CENTER_VALUE / HALF_WIDTH
    rho = 1.0 / ratio
    found = []
    for _ in range(3):
        rho_next = 1.0 / (2.0 * ratio - rho)
        found.append((rho_next * rho, 2.0 * rho_next / HALF_WIDTH))
        rho = rho_next
    return found


def soft_of(damage):
    return (1.0 - damage) ** 2 + RESIDUAL_STIFFNESS


def row_up(plane, beyond):
    rows = plane.shape[0]
    at = lax.broadcasted_iota(jnp.int32, plane.shape, 0)
    return jnp.where(at == rows - 1, beyond, pltpu.roll(plane, rows - 1, 0))


def row_down(plane, beyond):
    at = lax.broadcasted_iota(jnp.int32, plane.shape, 0)
    return jnp.where(at == 0, beyond, pltpu.roll(plane, 1, 0))


def lane_up(plane, beyond):
    cells = plane.shape[1]
    at = lax.broadcasted_iota(jnp.int32, plane.shape, 1)
    return jnp.where(at == cells - 1, beyond, pltpu.roll(plane, cells - 1, 1))


def lane_down(plane, beyond):
    at = lax.broadcasted_iota(jnp.int32, plane.shape, 1)
    return jnp.where(at == 0, beyond, pltpu.roll(plane, 1, 1))


def mu_inverse(ex, ey, ez):
    return 1.0 / (2.0 + (ex * ex + ey * ey + ez * ez))


def lam_inverse(center, total):
    return 1.0 / (0.5 + 0.125 * (6.0 * center + total))


HALO = 4
X_DAMAGE, X_PULL, X_MU, X_SOURCE, X_SLOTS = 0, 3, 9, 11, 17
LATE_DAMAGE, LATE_PULL, LATE_MU, LATE_SOURCE, LATE_SLOTS = 0, 1, 2, 3, 6
Y_HALO = (3, 2, 2, 2, 1, 2, 2, 2)
Y_KNOWN, Y_FIELDS = 8, 12
CORNER_ROWS = sum(Y_HALO) + 8


def edge_row(s, ny, depth):
    return depth if s == 0 else ny - 1 - depth


def known_of(s, damages, pulls, behind_pull, mus, sources, behind):
    planes = damages[0].shape[0]
    (c1, c2), _, _ = weights()
    soft = [soft_of(part) for part in damages]
    less = damages[0] - 1.0
    wx, wy, wz = (less * pull for pull in pulls)
    wy_behind = (damages[1] - 1.0) * behind_pull

    def across(value):
        return pltpu.roll(value, planes - 1, 0), pltpu.roll(value, 1, 0)

    def along(value, fill):
        return lane_up(value, fill), lane_down(value, fill)

    total = soft[0] + soft[2] + sum(across(soft[1])) + sum(along(soft[1], OUTSIDE))
    inverse = lam_inverse(soft[1], total)
    face = 0.125 * (soft[0] + soft[1])
    scale = 0.25 * mu_inverse(*pulls)
    known = [(1.0 + c1) * mus[0] + c2 * scale * (mus[1] + sum(across(mus[0])) + sum(along(mus[0], 0.0)))]
    x_up, x_down = across(wx * mus[0])
    z_up, z_down = along(wz * mus[0], 0.0)
    y_behind = wy_behind * mus[1]
    transfers = (x_up - x_down, y_behind if s == 0 else -y_behind, z_up - z_down)
    for c in range(3):
        known.append((1.0 + c1) * sources[c] + c2 * (face * (inverse * behind[c]) + transfers[c]))
    return scale, wy, known


def put_rows(s, put, damage, strain, seed_damage, seed_disp):
    ny = damage.shape[1]
    first, second, third = (edge_row(s, ny, depth) for depth in range(3))
    damages = [damage[:, row, :] for row in (first, second, third)]
    pulls = [strain[c, :, first, :] for c in range(3)]
    pulls_behind = [strain[c, :, second, :] for c in range(3)]
    mus = [
        seed_damage[:, first, :] * mu_inverse(*pulls),
        seed_damage[:, second, :] * mu_inverse(*pulls_behind),
    ]
    sources = [seed_disp[c, :, first, :] for c in range(3)]
    behind = [seed_disp[c, :, second, :] for c in range(3)]
    scale, wy, known = known_of(s, damages, pulls, pulls_behind[1], mus, sources, behind)
    for slot, value in enumerate(damages[:2] + [wy, mus[0], scale] + sources + known):
        put(slot, value)


def even(axis):
    return lax.rem(lax.axis_index(axis), 2) == 0


def faces_kernel(
    damage_in, strain_in, seed_in, sources_in, pal_out, other_out, near_out, near_late_out, far_out, far_late_out,
    damage, strain, seed_damage, seed_disp, pal, other, near, near_late, far, far_late, sems, out_sems,
):
    nx = damage.shape[0]
    copies = [
        pltpu.make_async_copy(damage_in, damage, sems.at[0]),
        pltpu.make_async_copy(strain_in, strain, sems.at[1]),
        pltpu.make_async_copy(seed_in, seed_damage, sems.at[2]),
        pltpu.make_async_copy(sources_in, seed_disp, sems.at[3]),
    ]
    for copy in copies:
        copy.start()
    sent = []

    def send(source, target):
        sent.append(pltpu.make_async_copy(source, target, out_sems.at[len(sent)]))
        sent[-1].start()

    def put_planes(out, late, high):
        for depth in range(4):
            at = jnp.where(high, nx - 1 - depth, depth)
            if depth == 3:
                late[LATE_DAMAGE] = damage[at]
                continue
            out[X_DAMAGE + depth] = damage[at]
            pulls = [strain[c, at] for c in range(3)]
            mu = seed_damage[at] * mu_inverse(*pulls)
            if depth == 2:
                late[LATE_PULL] = pulls[0]
                late[LATE_MU] = mu
            else:
                out[X_MU + depth] = mu
            for c in range(3):
                if depth == 2:
                    late[LATE_SOURCE + c] = seed_disp[c, at]
                else:
                    out[X_PULL + 2 * c + depth] = pulls[c]
                    out[X_SOURCE + 2 * c + depth] = seed_disp[c, at]

    for copy in copies:
        copy.wait()
    for out, target, first in ((pal, pal_out, True), (other, other_out, False)):

        def put(slot, value):
            out[slot * nx : (slot + 1) * nx, :] = value

        for s in range(2):

            @pl.when(even("gy") == ((s == 1) == first))
            def _():
                put_rows(s, put, damage, strain, seed_damage, seed_disp)

        send(out, target)
    for out, late, target, late_target, high in (
        (near, near_late, near_out, near_late_out, even("gx")),
        (far, far_late, far_out, far_late_out, ~even("gx")),
    ):
        put_planes(out, late, high)
        send(out, target)
        send(late, late_target)
    for copy in sent:
        copy.wait()


def received_x(near, far, side):
    from_near = even("gx") == (side == 1)

    def plane(slot, row=None):
        at = slot if row is None else (slice(slot, slot + 1), row)
        return jnp.where(from_near, near[at], far[at])

    return plane


def received_y(pal, other, side):
    from_pal = even("gy") == (side == 1)
    return lambda first, count: jnp.where(from_pal, pal[first : first + count, :], other[first : first + count, :])


def deal(pal, other, low, high):
    first = even("gy")
    low, high = low[...], high[...]
    pal[...] = jnp.where(first, high, low)
    other[...] = jnp.where(first, low, high)


def corners_kernel(
    damage, strain, seed_damage, seed_disp, near, far, _, pal, other, field, low, high
):
    nx, ny, _ = damage.shape
    for s, out in enumerate((low, high)):
        first, second, third = (edge_row(s, ny, depth) for depth in range(3))
        for side in range(2):
            x_in = received_x(near, far, side)
            ours = slice(3, 8) if side == 0 else slice(0, 5)
            planes = slice(0, 5) if side == 0 else slice(nx - 5, nx)

            def put_x(slot, first, count, row):
                for far_off in range(count):
                    at = 2 - far_off if side == 0 else 5 + far_off
                    field[slot, at : at + 1, :] = x_in(first + far_off, row)

            for depth, row in enumerate((first, second, third)):
                field[depth, ours, :] = damage[planes, row, :]
                put_x(depth, X_DAMAGE, 3, row)
            for depth, row in enumerate((first, second)):
                pulls = [strain[c, planes, row, :] for c in range(3)]
                for c in range(3):
                    if depth == 0:
                        field[3 + c, ours, :] = pulls[c]
                        put_x(3 + c, X_PULL + 2 * c, 2, row)
                    field[9 + 3 * depth + c, ours, :] = seed_disp[c, planes, row, :]
                    put_x(9 + 3 * depth + c, X_SOURCE + 2 * c, 2, row)
                if depth == 1:
                    field[6, ours, :] = pulls[1]
                    put_x(6, X_PULL + 2, 2, row)
                field[7 + depth, ours, :] = seed_damage[planes, row, :] * mu_inverse(*pulls)
                put_x(7 + depth, X_MU, 2, row)
            got = [field[slot] for slot in range(15)]
            scale, wy, known = known_of(s, got[:3], got[3:6], got[6], got[7:9], got[9:12], got[12:15])
            row = side * CORNER_ROWS
            for slot, value in enumerate(got[:2] + [wy, got[7], scale] + got[9:12]):
                count = Y_HALO[slot]
                start = 3 - count if side == 0 else 5
                out[row : row + count, :] = value[start : start + count, :]
                row += count
            for value in known:
                start = 2 if side == 0 else 4
                out[row : row + 2, :] = value[start : start + 2, :]
                row += 2
    deal(pal, other, low, high)


def in_grid():
    here = lax.axis_index("gx")
    return here > 0, here < lax.axis_size("gx") - 1


def prepare(first, last, soft, pull, raw, g, k, state0):
    planes, ny, nz = soft.shape
    inside = in_grid()
    lane = lax.broadcasted_iota(jnp.int32, (ny, nz), 1)
    row = lax.broadcasted_iota(jnp.int32, (ny, nz), 0)
    inner = (row > 0) & (row < ny - 1)

    def step(at, _):
        center = soft[at]
        sides = [
            soft[at + 1],
            soft[at - 1],
            pltpu.roll(center, ny - 1, 0),
            pltpu.roll(center, 1, 0),
            lane_up(center, OUTSIDE),
            lane_down(center, OUTSIDE),
        ]
        outside = ((at < HALO) & ~inside[0]) | ((at >= planes - HALO) & ~inside[1])
        inverse = jnp.where(inner & ~outside, lam_inverse(center, sum(sides)), 0.0)
        eighth = 0.125 * inverse
        for j in range(6):
            face = eighth * (center + sides[j])
            if j == 4:
                face = jnp.where(lane == nz - 1, 0.0, face)
            if j == 5:
                face = jnp.where(lane == 0, 0.0, face)
            g[j, at] = face
        k[0, at] = inverse * pull[0, at + 1]
        k[1, at] = -inverse * pull[0, at - 1]
        k[2, at] = inverse * pltpu.roll(pull[1, at], ny - 1, 0)
        k[3, at] = -inverse * pltpu.roll(pull[1, at], 1, 0)
        k[4, at] = inverse * lane_up(pull[2, at], 0.0)
        k[5, at] = -inverse * lane_down(pull[2, at], 0.0)
        for c in range(3):
            state0[1 + c, at] = inverse * raw[c, at]
        return 0

    lax.fori_loop(first, last, step, 0)


def reach_of(grad, count):
    square = sum(part * part for part in grad)
    scale = 1.0 / jnp.maximum(square, NORMAL_FLOOR)
    power = 1.0 - RELAX_RATE * (1.0 + NORMAL_WEIGHT * square * scale)
    series = 1.0 + power
    for _ in range(2):
        power = power * power
        series = series * (1.0 + power)
    power = power * power
    repeats = jnp.ones_like(power)
    for level in range(1, 4):
        repeats = jnp.where(count > level, 1.0 + power * repeats, repeats)
    return (RELAX_RATE * NORMAL_WEIGHT * scale) * (series * repeats)


def slopes(first, last, count, less, grads):
    ny = less.shape[1]

    def step(at, _):
        own = less[at]
        grad = [
            0.5 * (less[at + 1] - less[at - 1]),
            0.5 * (pltpu.roll(own, ny - 1, 0) - pltpu.roll(own, 1, 0)),
            0.5 * (lane_up(own, -1.0) - lane_down(own, -1.0)),
        ]
        for c in range(3):
            grads[c, at - HALO] = grad[c]
        grads[3, at - HALO] = reach_of(grad, count)
        return 0

    lax.fori_loop(first, last, step, 0)


def first_sweep(ranges, state0, state1, g, k, mu_scale):
    (c1, c2), _, _ = weights()

    def advance(at, f, own, moved):
        state1[f, at] = (1.0 + c1) * own + c2 * moved

    for first, last in ranges:
        sweep(first, last, state0, g, k, mu_scale, None, advance)


def inner_kernel(
    damage, strain, seed_damage, seed_disp, less, soft, pull, mu_scale, raw, g, k, state0, state1
):
    nx = damage.shape[0]

    def fill(i, _):
        at = HALO + i
        own = damage[i]
        sx, sy, sz = strain[0, i], strain[1, i], strain[2, i]
        soft[at] = soft_of(own)
        own = own - 1.0
        less[at] = own
        pull[0, at] = own * sx
        pull[1, at] = own * sy
        pull[2, at] = own * sz
        mu_inv = mu_inverse(sx, sy, sz)
        mu_scale[at] = 0.25 * mu_inv
        state0[0, at] = mu_inv * seed_damage[i]
        for c in range(3):
            raw[c, at] = seed_disp[c, i]
        return 0

    lax.fori_loop(0, nx, fill, 0)
    low, high = HALO, HALO + nx
    prepare(low + 1, high - 1, soft, pull, raw, g, k, state0)
    first_sweep([(low + 2, high - 2)], state0, state1, g, k, mu_scale)


def sides_kernel(
    work, near, near_late, far, far_late,
    less_in, soft_in, pull_in, scale_in, raw_in, g_in, k_in, state0_in, state1_in,
    less, soft, pull, mu_scale, raw, g, k, state0, state1, grads,
):
    nx = soft.shape[0] - 2 * HALO
    low, high = HALO, HALO + nx
    inside = in_grid()
    for s in range(2):
        x_in, late = received_x(near, far, s), received_x(near_late, far_late, s)
        for depth in range(4):
            at = low - 1 - depth if s == 0 else high + depth
            own = late(LATE_DAMAGE) if depth == 3 else x_in(X_DAMAGE + depth)
            soft[at] = soft_of(own)
            if depth == 3:
                continue
            own = own - 1.0
            if depth == 0:
                less[at] = own
            if depth == 2:
                pull[0, at] = own * late(LATE_PULL)
                state0[0, at] = late(LATE_MU)
            else:
                pulls = [x_in(X_PULL + 2 * c + depth) for c in range(3)]
                mu_scale[at] = jnp.where(inside[s], 0.25 * mu_inverse(*pulls), 0.0)
                state0[0, at] = x_in(X_MU + depth)
            for c in range(3):
                if depth == 2:
                    raw[c, at] = late(LATE_SOURCE + c)
                else:
                    pull[c, at] = own * pulls[c]
                    raw[c, at] = x_in(X_SOURCE + 2 * c + depth)

    for first, last in ((low - 3, low + 1), (high - 1, high + 3)):
        prepare(first, last, soft, pull, raw, g, k, state0)
    slopes(low, high, work[0, 0], less, grads)
    first_sweep([(low - 2, low + 2), (high - 2, high + 2)], state0, state1, g, k, mu_scale)


def edges_kernel(
    soft, pull, mu_scale, raw, g, state0, state1, y_pal, y_other, c_pal, c_other,
    sent_pal, sent_other, coefficients, firsts, seconds, outer,
    field, sent_low, sent_high,
):
    planes, ny, nz = soft.shape
    nx = planes - 2 * HALO
    (c1, c2), (d1, d2), _ = weights()
    lane = lax.broadcasted_iota(jnp.int32, (planes, nz), 1)
    plane = lax.broadcasted_iota(jnp.int32, (planes, nz), 0)
    here, there = lax.axis_index("gx"), lax.axis_index("gy")
    in_x = ((plane >= HALO) | (here > 0)) & ((plane < HALO + nx) | (here < lax.axis_size("gx") - 1))
    in_y = (there > 0, there < lax.axis_size("gy") - 1)

    def around_x(value):
        return [pltpu.roll(value, planes - 1, 0), pltpu.roll(value, 1, 0)]

    def around_z(value, fill):
        return [lane_up(value, fill), lane_down(value, fill)]

    for s, sent in enumerate((sent_low, sent_high)):
        y_in, c_in = received_y(y_pal, y_other, s), received_y(c_pal, c_other, s)
        e0, e1 = edge_row(s, ny, 0), edge_row(s, ny, 1)

        def ordered(inward, outward):
            return [inward, outward] if s == 0 else [outward, inward]

        row = 0
        for f in range(Y_FIELDS):
            field[f, HALO : HALO + nx, :] = y_in(f * nx, nx)
            count, shift = (Y_HALO[f], 0) if f < Y_KNOWN else (2, 1)
            field[f, HALO - count + shift : HALO + shift, :] = c_in(row, count)
            high = HALO + nx - shift
            field[f, high : high + count, :] = c_in(CORNER_ROWS + row, count)
            row += count

        soft_1, soft_2 = soft_of(field[0]), soft_of(field[1])
        soft_e0, soft_e1 = soft[:, e0, :], soft[:, e1, :]

        def total(center, inward, outward):
            return sum(around_x(center) + [inward, outward] + around_z(center, OUTSIDE))

        inverse_1 = lam_inverse(soft_1, total(soft_1, soft_e0, soft_2))
        inverse_1 = jnp.where(in_x & in_y[s], inverse_1, 0.0)
        lam_1 = [inverse_1 * field[5 + c] for c in range(3)]
        inverse_e0 = jnp.where(in_x, lam_inverse(soft_e0, total(soft_e0, soft_e1, soft_1)), 0.0)
        lam_e0 = [inverse_e0 * raw[c, :, e0, :] for c in range(3)]
        mu_1, wy_1 = field[3], field[2]
        mu_e0, mu_e1 = state0[0, :, e0, :], state0[0, :, e1, :]
        lam_e1 = [state0[1 + c, :, e1, :] for c in range(3)]

        def coefficients_of(center, inverse, inward, outward, wx, wy, wz):
            sides = around_x(center) + ordered(inward, outward) + around_z(center, OUTSIDE)
            eighth = 0.125 * inverse
            faces = [eighth * (center + side) for side in sides]
            faces[4] = jnp.where(lane == nz - 1, 0.0, faces[4])
            faces[5] = jnp.where(lane == 0, 0.0, faces[5])
            pulls = around_x(wx) + wy + around_z(wz, 0.0)
            return faces, [inverse * w if j % 2 == 0 else -inverse * w for j, w in enumerate(pulls)]

        def moved_of(faces, pulls, scale, own, inward, outward):
            sides = [
                around_x(own[f]) + ordered(inward[f], outward[f]) + around_z(own[f], 0.0) for f in range(4)
            ]
            moved = [scale * sum(sides[0])]
            for c in range(3):
                part = sum(faces[j] * sides[1 + c][j] for j in range(6))
                moved.append(part + pulls[2 * c] * sides[0][2 * c] + pulls[2 * c + 1] * sides[0][2 * c + 1])
            return moved

        first_1 = [jnp.where(in_x, field[Y_KNOWN] + c2 * field[4] * mu_e0, 0.0)]
        sides = around_x(soft_1) + around_z(soft_1, OUTSIDE) + [soft_e0]
        faces = [0.125 * (soft_1 + side) for side in sides]
        wy_e0 = pull[1, :, e0, :] * mu_e0
        own_1 = [mu_1] + lam_1
        own_e0 = [mu_e0] + lam_e0
        for c in range(3):
            sides = around_x(lam_1[c]) + around_z(lam_1[c], 0.0) + [lam_e0[c]]
            lacked = sum(faces[j] * sides[j] for j in range(5))
            if c == 1:
                lacked += wy_e0 if s == 0 else -wy_e0
            first_1.append(inverse_1 * (field[Y_KNOWN + 1 + c] + c2 * lacked))

        scale_e0 = mu_scale[:, e0, :]
        wy = ordered(pull[1, :, e1, :], wy_1)
        faces, pulls = coefficients_of(
            soft_e0, inverse_e0, soft_e1, soft_1, pull[0, :, e0, :], wy, pull[2, :, e0, :]
        )
        moved = moved_of(faces, pulls, scale_e0, own_e0, [mu_e1] + lam_e1, own_1)
        first_e0 = [(1.0 + c1) * own_e0[f] + c2 * moved[f] for f in range(4)]

        outward_face = g[3 if s == 0 else 2, :, e1, :]
        first_e1 = [state1[0, :, e1, :]]
        for c in range(3):
            first_e1.append(state1[1 + c, :, e1, :] + c2 * outward_face * lam_e0[c])

        moved = moved_of(faces, pulls, scale_e0, first_e0, first_e1, first_1)
        for f in range(4):
            second = first_e0[f] + (d1 - d2) * (first_e0[f] - own_e0[f]) + d2 * moved[f]
            sent[f * nx : (f + 1) * nx, :] = second[HALO : HALO + nx, :]
            firsts[s, f] = first_e0[f]
            outer[s, f] = first_1[f]
        for j in range(6):
            coefficients[s, j] = faces[j]
            coefficients[s, 6 + j] = pulls[j]
        for c in range(3):
            coefficients[s, 12 + c] = lam_e0[c]
            seconds[s, c] = first_e1[1 + c]
    deal(sent_pal, sent_other, sent_low, sent_high)


def sweep(first, last, state, g, k, mu_scale, rows, advance, finish=None):
    _, ny, nz = mu_scale.shape
    lane = lax.broadcasted_iota(jnp.int32, (ny, nz), 1)
    if rows is None:

        def rows(s, f, at):
            return 0.0

    def plane(at, _):
        def around(f):
            own = state[f, at]
            return own, [
                state[f, at + 1],
                state[f, at - 1],
                row_up(own, rows(1, f, at)),
                row_down(own, rows(0, f, at)),
                pltpu.roll(own, nz - 1, 1),
                pltpu.roll(own, 1, 1),
            ]

        mu, mu_sides = around(0)
        ends = [
            jnp.where(lane == nz - 1, 0.0, mu_sides[4]),
            jnp.where(lane == 0, 0.0, mu_sides[5]),
        ]
        results = [advance(at, 0, mu, mu_scale[at] * sum(mu_sides[:4] + ends))]
        faces = [g[j, at] for j in range(6)]
        for c in range(3):
            lam, lam_sides = around(1 + c)
            moved = sum(faces[j] * lam_sides[j] for j in range(6))
            moved += k[2 * c, at] * mu_sides[2 * c] + k[2 * c + 1, at] * mu_sides[2 * c + 1]
            results.append(advance(at, 1 + c, lam, moved))
        if finish is not None:
            finish(at - HALO, results)
        return 0

    lax.fori_loop(first, last, plane, 0)


def wait_kernel(
    work, less, grads, y_pal, y_other,
    mu_scale, coefficients, firsts, seconds, outer, g_in, k_in, state0_in, state1_in,
    out_mu, out_lam, edges, g, k, state0, state1,
    state2, states,
):
    _, nx, ny, _ = grads.shape
    planes = nx + 2 * HALO
    _, (d1, d2), (c1, c2) = weights()
    held = slice(HALO - 2, HALO + nx + 2)
    for s in range(2):
        e0, e1 = edge_row(s, ny, 0), edge_row(s, ny, 1)
        for j in range(6):
            g[j, held, e0, :] = coefficients[s, j, held, :]
            k[j, held, e0, :] = coefficients[s, 6 + j, held, :]
        for c in range(3):
            state0[1 + c, held, e0, :] = coefficients[s, 12 + c, held, :]
            state1[1 + c, held, e1, :] = seconds[s, c, held, :]
        for f in range(4):
            state1[f, held, e0, :] = firsts[s, f, held, :]

    def rows(s, f, at):
        return outer[s, f, pl.ds(at, 1), :]

    def advance_2(at, f, own, moved):
        state2[f, at] = own + (d1 - d2) * (own - state0[f, at]) + d2 * moved

    sweep(HALO - 1, HALO + nx + 1, state1, g, k, mu_scale, rows, advance_2)

    def advance_3(at, f, own, moved):
        return own + c1 * (own - state1[f, at]) + c2 * (state0[f, at] - own + moved)

    def finish(i, results):
        out_mu[i] = results[0]
        along = grads[3, i] * sum(grads[c, i] * results[1 + c] for c in range(3))
        for c in range(3):
            out_lam[c, i] = results[1 + c] - along * grads[c, i]
            states[c, i] = results[1 + c]

    sweep(HALO, HALO + nx, state2, g, k, mu_scale, None, advance_3, finish)

    for s in range(2):
        y_in = received_y(y_pal, y_other, s)
        e0, e1 = edge_row(s, ny, 0), edge_row(s, ny, 1)
        own = less[HALO : HALO + nx, e0, :]
        inward, outward = less[HALO : HALO + nx, e1, :], y_in(0, nx) - 1.0
        grad = [
            0.5 * (less[HALO + 1 : HALO + nx + 1, e0, :] - less[HALO - 1 : HALO + nx - 1, e0, :]),
            0.5 * (inward - outward if s == 0 else outward - inward),
            0.5 * (lane_up(own, -1.0) - lane_down(own, -1.0)),
        ]
        for c in range(3):
            edges[s, c] = grad[c]
            edges[s, 4 + c] = states[c, :, e0, :]
        edges[s, 3] = reach_of(grad, work[0, 0])


def last_kernel(
    mu_scale, coefficients, edges, y_pal, y_other, mu_in, lam_in,
    out_mu, out_lam, mu, lam,
    sems,
):
    nx, ny, nz = mu.shape
    inner = slice(HALO, HALO + nx)
    _, _, (_, c2) = weights()
    for s in range(2):
        y_in = received_y(y_pal, y_other, s)
        e0 = edge_row(s, ny, 0)
        outward = 3 if s == 0 else 2

        def got(f):
            return y_in(f * nx, nx)

        mu[:, e0, :] = mu[:, e0, :] + c2 * mu_scale[inner, e0, :] * got(0)
        face = c2 * coefficients[s, outward, inner, :]
        ends = []
        for c in range(3):
            end = edges[s, 4 + c] + face * got(1 + c)
            if c == 1:
                end += c2 * coefficients[s, 6 + outward, inner, :] * got(0)
            ends.append(end)
        along = edges[s, 3] * sum(edges[s, c] * ends[c] for c in range(3))
        for c in range(3):
            lam[c, :, e0, :] = ends[c] - along * edges[s, c]
    copies = [
        pltpu.make_async_copy(mu, out_mu, sems.at[0]),
        pltpu.make_async_copy(lam, out_lam, sems.at[1]),
    ]
    for copy in copies:
        copy.start()
    for copy in copies:
        copy.wait()


VMEM = pl.BlockSpec(memory_space=pltpu.VMEM)
SMEM = pl.BlockSpec(memory_space=pltpu.SMEM)
HBM = pl.BlockSpec(memory_space=pltpu.HBM)
ANY = pl.BlockSpec(memory_space=pl.ANY)
MIB = 1024 * 1024


def call(kernel, ins, outs, scratch=(), in_specs=None, out_specs=None, aliases=None, grant=24 * MIB):
    return pl.pallas_call(
        kernel,
        out_shape=[jax.ShapeDtypeStruct(shape, F32) for shape in outs],
        in_specs=in_specs or [VMEM] * len(ins),
        out_specs=out_specs or [VMEM] * len(outs),
        scratch_shapes=[pltpu.VMEM(shape, F32) if isinstance(shape, tuple) else shape for shape in scratch],
        input_output_aliases=aliases or {},
        compiler_params=pltpu.CompilerParams(vmem_limit_bytes=grant),
    )(*ins)


def trade(value, axis, first):
    pairs = [(i, i + 1) for i in range(first, lax.axis_size(axis) - 1, 2)]
    return lax.ppermute(value, axis, pairs + [(j, i) for i, j in pairs])


def body(damage, strain, seed_damage, seed_disp, brick_work):
    nx, ny, nz = damage.shape
    plane = (ny, nz)
    brick = (nx,) + plane
    bricks = (3,) + brick
    framed = (nx + 2 * HALO,) + plane
    state = (4,) + framed
    row = (nx + 2 * HALO, nz)
    fields = (damage, strain, seed_damage, seed_disp)

    y_rows = (Y_FIELDS * nx, nz)
    x_faces = [(X_SLOTS,) + plane, (LATE_SLOTS,) + plane]
    faces = [y_rows] * 2 + x_faces * 2
    pal, other, near, near_late, far, far_late = call(
        faces_kernel, fields, faces,
        [brick, bricks, brick, bricks] + faces + [pltpu.SemaphoreType.DMA((4,)), pltpu.SemaphoreType.DMA((6,))],
        in_specs=[HBM] * 4, out_specs=[HBM] * 6, grant=56 * MIB,
    )
    y_in = (trade(pal, "gy", 0), trade(other, "gy", 1))
    far, far_late = trade(far, "gx", 1), trade(far_late, "gx", 1)
    near, near_late = trade(near, "gx", 0), trade(near_late, "gx", 0)
    inner = tuple(call(
        inner_kernel, fields,
        [framed, framed, (3,) + framed, framed, (3,) + framed, (6,) + framed, (6,) + framed, state, state],
    ))
    c_rows = (2 * CORNER_ROWS, nz)
    pal, other = call(
        corners_kernel, fields + (near, far, inner[0]), [c_rows] * 2,
        [(15,) + plane, c_rows, c_rows], in_specs=[VMEM] * 6 + [ANY],
    )
    c_in = (trade(pal, "gy", 0), trade(other, "gy", 1))
    less, soft, pull, mu_scale, raw, g, k, state0, state1, grads = call(
        sides_kernel, (brick_work, near, near_late, far, far_late) + inner,
        [part.shape for part in inner] + [(4,) + brick],
        in_specs=[SMEM] + [VMEM] * 13, aliases={5 + part: part for part in range(9)},
    )
    sent = (4 * nx, nz)
    pal, other, coefficients, firsts, seconds, outer = call(
        edges_kernel, (soft, pull, mu_scale, raw, g, state0, state1) + y_in + c_in,
        [sent] * 2 + [(2, 15) + row, (2, 4) + row, (2, 3) + row, (2, 4) + row],
        [(Y_FIELDS,) + row, sent, sent],
    )
    halo = (trade(pal, "gy", 0), trade(other, "gy", 1))
    ins = (brick_work, less, grads) + y_in + (mu_scale, coefficients, firsts, seconds, outer, g, k, state0, state1)
    mu, lam, edges, *_ = call(
        wait_kernel, ins,
        [brick, bricks, (2, 7, nx, nz), (6,) + framed, (6,) + framed, state, state],
        [state, bricks],
        in_specs=[SMEM] + [VMEM] * (len(ins) - 1),
        aliases={10: 3, 11: 4, 12: 5, 13: 6},
    )
    out_mu, out_lam, *_ = call(
        last_kernel, (mu_scale, coefficients, edges) + halo + (mu, lam),
        [brick, bricks, brick, bricks], [pltpu.SemaphoreType.DMA((2,))],
        out_specs=[HBM, HBM, VMEM, VMEM], aliases={5: 2, 6: 3},
    )
    return out_mu, out_lam


def solution(mesh):
    placed = (
        P("gx", "gy", None),
        P(None, "gx", "gy", None),
        P("gx", "gy", None),
        P(None, "gx", "gy", None),
        P("gx", "gy"),
    )
    return jax.shard_map(
        body,
        mesh=mesh,
        in_specs=placed,
        out_specs=(P("gx", "gy", None), P(None, "gx", "gy", None)),
        check_vma=False,
    )
```

```python
import functools

import jax
import jax.numpy as jnp
from jax import lax
from jax.experimental import pallas as pl
from jax.experimental.pallas import tpu as pltpu
from jax.sharding import PartitionSpec as P

RELAX_INNER = 8
RESIDUAL_STIFFNESS = 0.001
CENTER_VALUE = 1.0
HALF_WIDTH = 0.75
NORMAL_WEIGHT = 1.5
RELAX_RATE = 0.5 / RELAX_INNER
NORMAL_FLOOR = 0.05
OUTSIDE = 1.0 + RESIDUAL_STIFFNESS
F32 = jnp.float32


def weights():
    ratio = CENTER_VALUE / HALF_WIDTH
    rho = 1.0 / ratio
    found = []
    for _ in range(3):
        rho_next = 1.0 / (2.0 * ratio - rho)
        found.append((rho_next * rho, 2.0 * rho_next / HALF_WIDTH))
        rho = rho_next
    return found


def soft_of(damage):
    return (1.0 - damage) ** 2 + RESIDUAL_STIFFNESS


def row_up(plane, beyond):
    rows = plane.shape[0]
    at = lax.broadcasted_iota(jnp.int32, plane.shape, 0)
    return jnp.where(at == rows - 1, beyond, pltpu.roll(plane, rows - 1, 0))


def row_down(plane, beyond):
    at = lax.broadcasted_iota(jnp.int32, plane.shape, 0)
    return jnp.where(at == 0, beyond, pltpu.roll(plane, 1, 0))


def lane_up(plane, beyond):
    cells = plane.shape[1]
    at = lax.broadcasted_iota(jnp.int32, plane.shape, 1)
    return jnp.where(at == cells - 1, beyond, pltpu.roll(plane, cells - 1, 1))


def lane_down(plane, beyond):
    at = lax.broadcasted_iota(jnp.int32, plane.shape, 1)
    return jnp.where(at == 0, beyond, pltpu.roll(plane, 1, 1))


def mu_inverse(ex, ey, ez):
    return 1.0 / (2.0 + (ex * ex + ey * ey + ez * ez))


def lam_inverse(center, total):
    return 1.0 / (0.5 + 0.125 * (6.0 * center + total))


HALO = 4
X_DAMAGE, X_PULL, X_MU, X_SOURCE, X_SLOTS = 0, 3, 9, 11, 17
LATE_DAMAGE, LATE_PULL, LATE_MU, LATE_SOURCE, LATE_SLOTS = 0, 1, 2, 3, 6
Y_HALO = (3, 2, 2, 2, 1, 2, 2, 2)
Y_KNOWN, Y_FIELDS = 8, 12
CORNER_ROWS = sum(Y_HALO) + 8


def edge_row(s, ny, depth):
    return depth if s == 0 else ny - 1 - depth


def known_of(s, damages, pulls, behind_pull, mus, sources, behind):
    planes = damages[0].shape[0]
    (c1, c2), _, _ = weights()
    soft = [soft_of(part) for part in damages]
    less = damages[0] - 1.0
    wx, wy, wz = (less * pull for pull in pulls)
    wy_behind = (damages[1] - 1.0) * behind_pull

    def across(value):
        return pltpu.roll(value, planes - 1, 0), pltpu.roll(value, 1, 0)

    def along(value, fill):
        return lane_up(value, fill), lane_down(value, fill)

    total = soft[0] + soft[2] + sum(across(soft[1])) + sum(along(soft[1], OUTSIDE))
    inverse = lam_inverse(soft[1], total)
    face = 0.125 * (soft[0] + soft[1])
    scale = 0.25 * mu_inverse(*pulls)
    known = [(1.0 + c1) * mus[0] + c2 * scale * (mus[1] + sum(across(mus[0])) + sum(along(mus[0], 0.0)))]
    x_up, x_down = across(wx * mus[0])
    z_up, z_down = along(wz * mus[0], 0.0)
    y_behind = wy_behind * mus[1]
    transfers = (x_up - x_down, y_behind if s == 0 else -y_behind, z_up - z_down)
    for c in range(3):
        known.append((1.0 + c1) * sources[c] + c2 * (face * (inverse * behind[c]) + transfers[c]))
    return scale, wy, known


def put_rows(s, put, damage, strain, seed_damage, seed_disp):
    ny = damage.shape[1]
    first, second, third = (edge_row(s, ny, depth) for depth in range(3))
    damages = [damage[:, row, :] for row in (first, second, third)]
    pulls = [strain[c, :, first, :] for c in range(3)]
    pulls_behind = [strain[c, :, second, :] for c in range(3)]
    mus = [
        seed_damage[:, first, :] * mu_inverse(*pulls),
        seed_damage[:, second, :] * mu_inverse(*pulls_behind),
    ]
    sources = [seed_disp[c, :, first, :] for c in range(3)]
    behind = [seed_disp[c, :, second, :] for c in range(3)]
    scale, wy, known = known_of(s, damages, pulls, pulls_behind[1], mus, sources, behind)
    for slot, value in enumerate(damages[:2] + [wy, mus[0], scale] + sources + known):
        put(slot, value)


def even(axis):
    return lax.rem(lax.axis_index(axis), 2) == 0


def faces_kernel(
    damage_in, strain_in, seed_in, sources_in, pal_out, other_out, near_out, near_late_out, far_out, far_late_out,
    damage, strain, seed_damage, seed_disp, pal, other, near, near_late, far, far_late, sems, out_sems,
):
    nx = damage.shape[0]
    copies = [
        pltpu.make_async_copy(damage_in, damage, sems.at[0]),
        pltpu.make_async_copy(strain_in, strain, sems.at[1]),
        pltpu.make_async_copy(seed_in, seed_damage, sems.at[2]),
        pltpu.make_async_copy(sources_in, seed_disp, sems.at[3]),
    ]
    for copy in copies:
        copy.start(priority=1)
    sent = []

    def send(source, target):
        sent.append(pltpu.make_async_copy(source, target, out_sems.at[len(sent)]))
        sent[-1].start()

    def put_planes(out, late, high):
        for depth in range(4):
            at = jnp.where(high, nx - 1 - depth, depth)
            if depth == 3:
                late[LATE_DAMAGE] = damage[at]
                continue
            out[X_DAMAGE + depth] = damage[at]
            pulls = [strain[c, at] for c in range(3)]
            mu = seed_damage[at] * mu_inverse(*pulls)
            if depth == 2:
                late[LATE_PULL] = pulls[0]
                late[LATE_MU] = mu
            else:
                out[X_MU + depth] = mu
            for c in range(3):
                if depth == 2:
                    late[LATE_SOURCE + c] = seed_disp[c, at]
                else:
                    out[X_PULL + 2 * c + depth] = pulls[c]
                    out[X_SOURCE + 2 * c + depth] = seed_disp[c, at]

    for copy in copies:
        copy.wait()
    for out, target, first in ((pal, pal_out, True), (other, other_out, False)):

        def put(slot, value):
            out[slot * nx : (slot + 1) * nx, :] = value

        for s in range(2):

            @pl.when(even("gy") == ((s == 1) == first))
            def _():
                put_rows(s, put, damage, strain, seed_damage, seed_disp)

        send(out, target)
    for out, late, target, late_target, high in (
        (near, near_late, near_out, near_late_out, even("gx")),
        (far, far_late, far_out, far_late_out, ~even("gx")),
    ):
        put_planes(out, late, high)
        send(out, target)
        send(late, late_target)
    for copy in sent:
        copy.wait()


def received_x(near, far, side):
    from_near = even("gx") == (side == 1)

    def plane(slot, row=None):
        at = slot if row is None else (slice(slot, slot + 1), row)
        return jnp.where(from_near, near[at], far[at])

    return plane


def received_y(pal, other, side):
    from_pal = even("gy") == (side == 1)
    return lambda first, count: jnp.where(from_pal, pal[first : first + count, :], other[first : first + count, :])


def deal(pal, other, low, high):
    first = even("gy")
    low, high = low[...], high[...]
    pal[...] = jnp.where(first, high, low)
    other[...] = jnp.where(first, low, high)


def corners_kernel(
    damage, strain, seed_damage, seed_disp, near, far, _, pal, other, field, low, high
):
    nx, ny, _ = damage.shape
    for s, out in enumerate((low, high)):
        first, second, third = (edge_row(s, ny, depth) for depth in range(3))
        for side in range(2):
            x_in = received_x(near, far, side)
            ours = slice(3, 8) if side == 0 else slice(0, 5)
            planes = slice(0, 5) if side == 0 else slice(nx - 5, nx)

            def put_x(slot, first, count, row):
                for far_off in range(count):
                    at = 2 - far_off if side == 0 else 5 + far_off
                    field[slot, at : at + 1, :] = x_in(first + far_off, row)

            for depth, row in enumerate((first, second, third)):
                field[depth, ours, :] = damage[planes, row, :]
                put_x(depth, X_DAMAGE, 3, row)
            for depth, row in enumerate((first, second)):
                pulls = [strain[c, planes, row, :] for c in range(3)]
                for c in range(3):
                    if depth == 0:
                        field[3 + c, ours, :] = pulls[c]
                        put_x(3 + c, X_PULL + 2 * c, 2, row)
                    field[9 + 3 * depth + c, ours, :] = seed_disp[c, planes, row, :]
                    put_x(9 + 3 * depth + c, X_SOURCE + 2 * c, 2, row)
                if depth == 1:
                    field[6, ours, :] = pulls[1]
                    put_x(6, X_PULL + 2, 2, row)
                field[7 + depth, ours, :] = seed_damage[planes, row, :] * mu_inverse(*pulls)
                put_x(7 + depth, X_MU, 2, row)
            got = [field[slot] for slot in range(15)]
            scale, wy, known = known_of(s, got[:3], got[3:6], got[6], got[7:9], got[9:12], got[12:15])
            row = side * CORNER_ROWS
            for slot, value in enumerate(got[:2] + [wy, got[7], scale] + got[9:12]):
                count = Y_HALO[slot]
                start = 3 - count if side == 0 else 5
                out[row : row + count, :] = value[start : start + count, :]
                row += count
            for value in known:
                start = 2 if side == 0 else 4
                out[row : row + 2, :] = value[start : start + 2, :]
                row += 2
    deal(pal, other, low, high)


def in_grid():
    here = lax.axis_index("gx")
    return here > 0, here < lax.axis_size("gx") - 1


def prepare(first, last, soft, pull, raw, g, k, state0):
    planes, ny, nz = soft.shape
    inside = in_grid()
    lane = lax.broadcasted_iota(jnp.int32, (ny, nz), 1)
    row = lax.broadcasted_iota(jnp.int32, (ny, nz), 0)
    inner = (row > 0) & (row < ny - 1)

    def step(at, _):
        center = soft[at]
        sides = [
            soft[at + 1],
            soft[at - 1],
            pltpu.roll(center, ny - 1, 0),
            pltpu.roll(center, 1, 0),
            lane_up(center, OUTSIDE),
            lane_down(center, OUTSIDE),
        ]
        outside = ((at < HALO) & ~inside[0]) | ((at >= planes - HALO) & ~inside[1])
        inverse = jnp.where(inner & ~outside, lam_inverse(center, sum(sides)), 0.0)
        eighth = 0.125 * inverse
        for j in range(6):
            face = eighth * (center + sides[j])
            if j == 4:
                face = jnp.where(lane == nz - 1, 0.0, face)
            if j == 5:
                face = jnp.where(lane == 0, 0.0, face)
            g[j, at] = face
        k[0, at] = inverse * pull[0, at + 1]
        k[1, at] = -inverse * pull[0, at - 1]
        k[2, at] = inverse * pltpu.roll(pull[1, at], ny - 1, 0)
        k[3, at] = -inverse * pltpu.roll(pull[1, at], 1, 0)
        k[4, at] = inverse * lane_up(pull[2, at], 0.0)
        k[5, at] = -inverse * lane_down(pull[2, at], 0.0)
        for c in range(3):
            state0[1 + c, at] = inverse * raw[c, at]
        return 0

    lax.fori_loop(first, last, step, 0)


def reach_of(grad, count):
    square = sum(part * part for part in grad)
    scale = 1.0 / jnp.maximum(square, NORMAL_FLOOR)
    power = 1.0 - RELAX_RATE * (1.0 + NORMAL_WEIGHT * square * scale)
    series = 1.0 + power
    for _ in range(2):
        power = power * power
        series = series * (1.0 + power)
    power = power * power
    repeats = jnp.ones_like(power)
    for level in range(1, 4):
        repeats = jnp.where(count > level, 1.0 + power * repeats, repeats)
    return (RELAX_RATE * NORMAL_WEIGHT * scale) * (series * repeats)


def slopes(first, last, count, less, grads):
    ny = less.shape[1]

    def step(at, _):
        own = less[at]
        grad = [
            0.5 * (less[at + 1] - less[at - 1]),
            0.5 * (pltpu.roll(own, ny - 1, 0) - pltpu.roll(own, 1, 0)),
            0.5 * (lane_up(own, -1.0) - lane_down(own, -1.0)),
        ]
        for c in range(3):
            grads[c, at - HALO] = grad[c]
        grads[3, at - HALO] = reach_of(grad, count)
        return 0

    lax.fori_loop(first, last, step, 0)


def first_sweep(ranges, state0, state1, g, k, mu_scale):
    (c1, c2), _, _ = weights()

    def advance(at, f, own, moved):
        state1[f, at] = (1.0 + c1) * own + c2 * moved

    for first, last in ranges:
        sweep(first, last, state0, g, k, mu_scale, None, advance)


def inner_kernel(
    damage, strain, seed_damage, seed_disp, less, soft, pull, mu_scale, raw, g, k, state0, state1
):
    nx = damage.shape[0]

    def fill(i, _):
        at = HALO + i
        own = damage[i]
        sx, sy, sz = strain[0, i], strain[1, i], strain[2, i]
        soft[at] = soft_of(own)
        own = own - 1.0
        less[at] = own
        pull[0, at] = own * sx
        pull[1, at] = own * sy
        pull[2, at] = own * sz
        mu_inv = mu_inverse(sx, sy, sz)
        mu_scale[at] = 0.25 * mu_inv
        state0[0, at] = mu_inv * seed_damage[i]
        for c in range(3):
            raw[c, at] = seed_disp[c, i]
        return 0

    lax.fori_loop(0, nx, fill, 0)
    low, high = HALO, HALO + nx
    prepare(low + 1, high - 1, soft, pull, raw, g, k, state0)
    first_sweep([(low + 2, high - 2)], state0, state1, g, k, mu_scale)


def sides_kernel(
    work, near, near_late, far, far_late,
    less_in, soft_in, pull_in, scale_in, raw_in, g_in, k_in, state0_in, state1_in,
    less, soft, pull, mu_scale, raw, g, k, state0, state1, grads,
):
    nx = soft.shape[0] - 2 * HALO
    low, high = HALO, HALO + nx
    inside = in_grid()
    for s in range(2):
        x_in, late = received_x(near, far, s), received_x(near_late, far_late, s)
        for depth in range(4):
            at = low - 1 - depth if s == 0 else high + depth
            own = late(LATE_DAMAGE) if depth == 3 else x_in(X_DAMAGE + depth)
            soft[at] = soft_of(own)
            if depth == 3:
                continue
            own = own - 1.0
            if depth == 0:
                less[at] = own
            if depth == 2:
                pull[0, at] = own * late(LATE_PULL)
                state0[0, at] = late(LATE_MU)
            else:
                pulls = [x_in(X_PULL + 2 * c + depth) for c in range(3)]
                mu_scale[at] = jnp.where(inside[s], 0.25 * mu_inverse(*pulls), 0.0)
                state0[0, at] = x_in(X_MU + depth)
            for c in range(3):
                if depth == 2:
                    raw[c, at] = late(LATE_SOURCE + c)
                else:
                    pull[c, at] = own * pulls[c]
                    raw[c, at] = x_in(X_SOURCE + 2 * c + depth)

    for first, last in ((low - 3, low + 1), (high - 1, high + 3)):
        prepare(first, last, soft, pull, raw, g, k, state0)
    slopes(low, high, work[0, 0], less, grads)
    first_sweep([(low - 2, low + 2), (high - 2, high + 2)], state0, state1, g, k, mu_scale)


def edges_kernel(
    soft, pull, mu_scale, raw, g, state0, state1, y_pal, y_other, c_pal, c_other,
    sent_pal, sent_other, coefficients, firsts, seconds, outer,
    field, sent_low, sent_high,
):
    planes, ny, nz = soft.shape
    nx = planes - 2 * HALO
    (c1, c2), (d1, d2), _ = weights()
    lane = lax.broadcasted_iota(jnp.int32, (planes, nz), 1)
    plane = lax.broadcasted_iota(jnp.int32, (planes, nz), 0)
    here, there = lax.axis_index("gx"), lax.axis_index("gy")
    in_x = ((plane >= HALO) | (here > 0)) & ((plane < HALO + nx) | (here < lax.axis_size("gx") - 1))
    in_y = (there > 0, there < lax.axis_size("gy") - 1)

    def around_x(value):
        return [pltpu.roll(value, planes - 1, 0), pltpu.roll(value, 1, 0)]

    def around_z(value, fill):
        return [lane_up(value, fill), lane_down(value, fill)]

    for s, sent in enumerate((sent_low, sent_high)):
        y_in, c_in = received_y(y_pal, y_other, s), received_y(c_pal, c_other, s)
        e0, e1 = edge_row(s, ny, 0), edge_row(s, ny, 1)

        def ordered(inward, outward):
            return [inward, outward] if s == 0 else [outward, inward]

        row = 0
        for f in range(Y_FIELDS):
            field[f, HALO : HALO + nx, :] = y_in(f * nx, nx)
            count, shift = (Y_HALO[f], 0) if f < Y_KNOWN else (2, 1)
            field[f, HALO - count + shift : HALO + shift, :] = c_in(row, count)
            high = HALO + nx - shift
            field[f, high : high + count, :] = c_in(CORNER_ROWS + row, count)
            row += count

        soft_1, soft_2 = soft_of(field[0]), soft_of(field[1])
        soft_e0, soft_e1 = soft[:, e0, :], soft[:, e1, :]

        def total(center, inward, outward):
            return sum(around_x(center) + [inward, outward] + around_z(center, OUTSIDE))

        inverse_1 = lam_inverse(soft_1, total(soft_1, soft_e0, soft_2))
        inverse_1 = jnp.where(in_x & in_y[s], inverse_1, 0.0)
        lam_1 = [inverse_1 * field[5 + c] for c in range(3)]
        inverse_e0 = jnp.where(in_x, lam_inverse(soft_e0, total(soft_e0, soft_e1, soft_1)), 0.0)
        lam_e0 = [inverse_e0 * raw[c, :, e0, :] for c in range(3)]
        mu_1, wy_1 = field[3], field[2]
        mu_e0, mu_e1 = state0[0, :, e0, :], state0[0, :, e1, :]
        lam_e1 = [state0[1 + c, :, e1, :] for c in range(3)]

        def coefficients_of(center, inverse, inward, outward, wx, wy, wz):
            sides = around_x(center) + ordered(inward, outward) + around_z(center, OUTSIDE)
            eighth = 0.125 * inverse
            faces = [eighth * (center + side) for side in sides]
            faces[4] = jnp.where(lane == nz - 1, 0.0, faces[4])
            faces[5] = jnp.where(lane == 0, 0.0, faces[5])
            pulls = around_x(wx) + wy + around_z(wz, 0.0)
            return faces, [inverse * w if j % 2 == 0 else -inverse * w for j, w in enumerate(pulls)]

        def moved_of(faces, pulls, scale, own, inward, outward):
            sides = [
                around_x(own[f]) + ordered(inward[f], outward[f]) + around_z(own[f], 0.0) for f in range(4)
            ]
            moved = [scale * sum(sides[0])]
            for c in range(3):
                part = sum(faces[j] * sides[1 + c][j] for j in range(6))
                moved.append(part + pulls[2 * c] * sides[0][2 * c] + pulls[2 * c + 1] * sides[0][2 * c + 1])
            return moved

        first_1 = [jnp.where(in_x, field[Y_KNOWN] + c2 * field[4] * mu_e0, 0.0)]
        sides = around_x(soft_1) + around_z(soft_1, OUTSIDE) + [soft_e0]
        faces = [0.125 * (soft_1 + side) for side in sides]
        wy_e0 = pull[1, :, e0, :] * mu_e0
        own_1 = [mu_1] + lam_1
        own_e0 = [mu_e0] + lam_e0
        for c in range(3):
            sides = around_x(lam_1[c]) + around_z(lam_1[c], 0.0) + [lam_e0[c]]
            lacked = sum(faces[j] * sides[j] for j in range(5))
            if c == 1:
                lacked += wy_e0 if s == 0 else -wy_e0
            first_1.append(inverse_1 * (field[Y_KNOWN + 1 + c] + c2 * lacked))

        scale_e0 = mu_scale[:, e0, :]
        wy = ordered(pull[1, :, e1, :], wy_1)
        faces, pulls = coefficients_of(
            soft_e0, inverse_e0, soft_e1, soft_1, pull[0, :, e0, :], wy, pull[2, :, e0, :]
        )
        moved = moved_of(faces, pulls, scale_e0, own_e0, [mu_e1] + lam_e1, own_1)
        first_e0 = [(1.0 + c1) * own_e0[f] + c2 * moved[f] for f in range(4)]

        outward_face = g[3 if s == 0 else 2, :, e1, :]
        first_e1 = [state1[0, :, e1, :]]
        for c in range(3):
            first_e1.append(state1[1 + c, :, e1, :] + c2 * outward_face * lam_e0[c])

        moved = moved_of(faces, pulls, scale_e0, first_e0, first_e1, first_1)
        for f in range(4):
            second = first_e0[f] + (d1 - d2) * (first_e0[f] - own_e0[f]) + d2 * moved[f]
            sent[f * nx : (f + 1) * nx, :] = second[HALO : HALO + nx, :]
            firsts[s, f] = first_e0[f]
            outer[s, f] = first_1[f]
        for j in range(6):
            coefficients[s, j] = faces[j]
            coefficients[s, 6 + j] = pulls[j]
        for c in range(3):
            coefficients[s, 12 + c] = lam_e0[c]
            seconds[s, c] = first_e1[1 + c]
    deal(sent_pal, sent_other, sent_low, sent_high)


def sweep(first, last, state, g, k, mu_scale, rows, advance, finish=None):
    _, ny, nz = mu_scale.shape
    lane = lax.broadcasted_iota(jnp.int32, (ny, nz), 1)
    if rows is None:

        def rows(s, f, at):
            return 0.0

    def plane(at, _):
        def around(f):
            own = state[f, at]
            return own, [
                state[f, at + 1],
                state[f, at - 1],
                row_up(own, rows(1, f, at)),
                row_down(own, rows(0, f, at)),
                pltpu.roll(own, nz - 1, 1),
                pltpu.roll(own, 1, 1),
            ]

        mu, mu_sides = around(0)
        ends = [
            jnp.where(lane == nz - 1, 0.0, mu_sides[4]),
            jnp.where(lane == 0, 0.0, mu_sides[5]),
        ]
        results = [advance(at, 0, mu, mu_scale[at] * sum(mu_sides[:4] + ends))]
        faces = [g[j, at] for j in range(6)]
        for c in range(3):
            lam, lam_sides = around(1 + c)
            moved = sum(faces[j] * lam_sides[j] for j in range(6))
            moved += k[2 * c, at] * mu_sides[2 * c] + k[2 * c + 1, at] * mu_sides[2 * c + 1]
            results.append(advance(at, 1 + c, lam, moved))
        if finish is not None:
            finish(at - HALO, results)
        return 0

    lax.fori_loop(first, last, plane, 0)


def wait_kernel(
    work, less, grads, y_pal, y_other,
    mu_scale, coefficients, firsts, seconds, outer, g_in, k_in, state0_in, state1_in,
    out_mu, out_lam, edges, g, k, state0, state1,
    state2, states,
):
    _, nx, ny, _ = grads.shape
    planes = nx + 2 * HALO
    _, (d1, d2), (c1, c2) = weights()
    held = slice(HALO - 2, HALO + nx + 2)
    for s in range(2):
        e0, e1 = edge_row(s, ny, 0), edge_row(s, ny, 1)
        for j in range(6):
            g[j, held, e0, :] = coefficients[s, j, held, :]
            k[j, held, e0, :] = coefficients[s, 6 + j, held, :]
        for c in range(3):
            state0[1 + c, held, e0, :] = coefficients[s, 12 + c, held, :]
            state1[1 + c, held, e1, :] = seconds[s, c, held, :]
        for f in range(4):
            state1[f, held, e0, :] = firsts[s, f, held, :]

    def rows(s, f, at):
        return outer[s, f, pl.ds(at, 1), :]

    def advance_2(at, f, own, moved):
        state2[f, at] = own + (d1 - d2) * (own - state0[f, at]) + d2 * moved

    sweep(HALO - 1, HALO + nx + 1, state1, g, k, mu_scale, rows, advance_2)

    def advance_3(at, f, own, moved):
        return own + c1 * (own - state1[f, at]) + c2 * (state0[f, at] - own + moved)

    def finish(i, results):
        out_mu[i] = results[0]
        along = grads[3, i] * sum(grads[c, i] * results[1 + c] for c in range(3))
        for c in range(3):
            out_lam[c, i] = results[1 + c] - along * grads[c, i]
            states[c, i] = results[1 + c]

    sweep(HALO, HALO + nx, state2, g, k, mu_scale, None, advance_3, finish)

    for s in range(2):
        y_in = received_y(y_pal, y_other, s)
        e0, e1 = edge_row(s, ny, 0), edge_row(s, ny, 1)
        own = less[HALO : HALO + nx, e0, :]
        inward, outward = less[HALO : HALO + nx, e1, :], y_in(0, nx) - 1.0
        grad = [
            0.5 * (less[HALO + 1 : HALO + nx + 1, e0, :] - less[HALO - 1 : HALO + nx - 1, e0, :]),
            0.5 * (inward - outward if s == 0 else outward - inward),
            0.5 * (lane_up(own, -1.0) - lane_down(own, -1.0)),
        ]
        for c in range(3):
            edges[s, c] = grad[c]
            edges[s, 4 + c] = states[c, :, e0, :]
        edges[s, 3] = reach_of(grad, work[0, 0])


def last_kernel(
    mu_scale, coefficients, edges, y_pal, y_other, mu_in, lam_in,
    out_mu, out_lam, mu, lam,
    sems,
):
    nx, ny, nz = mu.shape
    inner = slice(HALO, HALO + nx)
    _, _, (_, c2) = weights()
    for s in range(2):
        y_in = received_y(y_pal, y_other, s)
        e0 = edge_row(s, ny, 0)
        outward = 3 if s == 0 else 2

        def got(f):
            return y_in(f * nx, nx)

        mu[:, e0, :] = mu[:, e0, :] + c2 * mu_scale[inner, e0, :] * got(0)
        face = c2 * coefficients[s, outward, inner, :]
        ends = []
        for c in range(3):
            end = edges[s, 4 + c] + face * got(1 + c)
            if c == 1:
                end += c2 * coefficients[s, 6 + outward, inner, :] * got(0)
            ends.append(end)
        along = edges[s, 3] * sum(edges[s, c] * ends[c] for c in range(3))
        for c in range(3):
            lam[c, :, e0, :] = ends[c] - along * edges[s, c]
    copies = [
        pltpu.make_async_copy(mu, out_mu, sems.at[0]),
        pltpu.make_async_copy(lam, out_lam, sems.at[1]),
    ]
    for copy in copies:
        copy.start()
    for copy in copies:
        copy.wait()


VMEM = pl.BlockSpec(memory_space=pltpu.VMEM)
SMEM = pl.BlockSpec(memory_space=pltpu.SMEM)
HBM = pl.BlockSpec(memory_space=pltpu.HBM)
ANY = pl.BlockSpec(memory_space=pl.ANY)
MIB = 1024 * 1024


def call(kernel, ins, outs, scratch=(), in_specs=None, out_specs=None, aliases=None, grant=24 * MIB):
    return pl.pallas_call(
        kernel,
        out_shape=[jax.ShapeDtypeStruct(shape, F32) for shape in outs],
        in_specs=in_specs or [VMEM] * len(ins),
        out_specs=out_specs or [VMEM] * len(outs),
        scratch_shapes=[pltpu.VMEM(shape, F32) if isinstance(shape, tuple) else shape for shape in scratch],
        input_output_aliases=aliases or {},
        compiler_params=pltpu.CompilerParams(vmem_limit_bytes=grant),
    )(*ins)


def trade(value, axis, first):
    pairs = [(i, i + 1) for i in range(first, lax.axis_size(axis) - 1, 2)]
    return lax.ppermute(value, axis, pairs + [(j, i) for i, j in pairs])


def body(damage, strain, seed_damage, seed_disp, brick_work):
    nx, ny, nz = damage.shape
    plane = (ny, nz)
    brick = (nx,) + plane
    bricks = (3,) + brick
    framed = (nx + 2 * HALO,) + plane
    state = (4,) + framed
    row = (nx + 2 * HALO, nz)
    fields = (damage, strain, seed_damage, seed_disp)

    y_rows = (Y_FIELDS * nx, nz)
    x_faces = [(X_SLOTS,) + plane, (LATE_SLOTS,) + plane]
    faces = [y_rows] * 2 + x_faces * 2
    pal, other, near, near_late, far, far_late = call(
        faces_kernel, fields, faces,
        [brick, bricks, brick, bricks] + faces + [pltpu.SemaphoreType.DMA((4,)), pltpu.SemaphoreType.DMA((6,))],
        in_specs=[HBM] * 4, out_specs=[HBM] * 6, grant=56 * MIB,
    )
    y_in = (trade(pal, "gy", 0), trade(other, "gy", 1))
    far, far_late = trade(far, "gx", 1), trade(far_late, "gx", 1)
    near, near_late = trade(near, "gx", 0), trade(near_late, "gx", 0)
    inner = tuple(call(
        inner_kernel, fields,
        [framed, framed, (3,) + framed, framed, (3,) + framed, (6,) + framed, (6,) + framed, state, state],
    ))
    c_rows = (2 * CORNER_ROWS, nz)
    pal, other = call(
        corners_kernel, fields + (near, far, inner[0]), [c_rows] * 2,
        [(15,) + plane, c_rows, c_rows], in_specs=[VMEM] * 6 + [ANY],
    )
    c_in = (trade(pal, "gy", 0), trade(other, "gy", 1))
    less, soft, pull, mu_scale, raw, g, k, state0, state1, grads = call(
        sides_kernel, (brick_work, near, near_late, far, far_late) + inner,
        [part.shape for part in inner] + [(4,) + brick],
        in_specs=[SMEM] + [VMEM] * 13, aliases={5 + part: part for part in range(9)},
    )
    sent = (4 * nx, nz)
    pal, other, coefficients, firsts, seconds, outer = call(
        edges_kernel, (soft, pull, mu_scale, raw, g, state0, state1) + y_in + c_in,
        [sent] * 2 + [(2, 15) + row, (2, 4) + row, (2, 3) + row, (2, 4) + row],
        [(Y_FIELDS,) + row, sent, sent],
    )
    halo = (trade(pal, "gy", 0), trade(other, "gy", 1))
    ins = (brick_work, less, grads) + y_in + (mu_scale, coefficients, firsts, seconds, outer, g, k, state0, state1)
    mu, lam, edges, *_ = call(
        wait_kernel, ins,
        [brick, bricks, (2, 7, nx, nz), (6,) + framed, (6,) + framed, state, state],
        [state, bricks],
        in_specs=[SMEM] + [VMEM] * (len(ins) - 1),
        aliases={10: 3, 11: 4, 12: 5, 13: 6},
    )
    out_mu, out_lam, *_ = call(
        last_kernel, (mu_scale, coefficients, edges) + halo + (mu, lam),
        [brick, bricks, brick, bricks], [pltpu.SemaphoreType.DMA((2,))],
        out_specs=[HBM, HBM, VMEM, VMEM], aliases={5: 2, 6: 3},
    )
    return out_mu, out_lam


def solution(mesh):
    placed = (
        P("gx", "gy", None),
        P(None, "gx", "gy", None),
        P("gx", "gy", None),
        P(None, "gx", "gy", None),
        P("gx", "gy"),
    )
    return jax.shard_map(
        body,
        mesh=mesh,
        in_specs=placed,
        out_specs=(P("gx", "gy", None), P(None, "gx", "gy", None)),
        check_vma=False,
    )
```

```python
import functools

import jax
import jax.numpy as jnp
from jax import lax
from jax.experimental import pallas as pl
from jax.experimental.pallas import tpu as pltpu
from jax.sharding import PartitionSpec as P

RELAX_INNER = 8
RESIDUAL_STIFFNESS = 0.001
CENTER_VALUE = 1.0
HALF_WIDTH = 0.75
NORMAL_WEIGHT = 1.5
RELAX_RATE = 0.5 / RELAX_INNER
NORMAL_FLOOR = 0.05
OUTSIDE = 1.0 + RESIDUAL_STIFFNESS
F32 = jnp.float32


def weights():
    ratio = CENTER_VALUE / HALF_WIDTH
    rho = 1.0 / ratio
    found = []
    for _ in range(3):
        rho_next = 1.0 / (2.0 * ratio - rho)
        found.append((rho_next * rho, 2.0 * rho_next / HALF_WIDTH))
        rho = rho_next
    return found


def by_pairs(first, last, step):
    width = 2 if (last - first) % 2 == 0 else 1

    def turn(i, _):
        for part in range(width):
            step(first + width * i + part)
        return 0

    lax.fori_loop(0, (last - first) // width, turn, 0)


def soft_of(damage):
    return (1.0 - damage) ** 2 + RESIDUAL_STIFFNESS


def row_up(plane, beyond):
    rows = plane.shape[0]
    at = lax.broadcasted_iota(jnp.int32, plane.shape, 0)
    return jnp.where(at == rows - 1, beyond, pltpu.roll(plane, rows - 1, 0))


def row_down(plane, beyond):
    at = lax.broadcasted_iota(jnp.int32, plane.shape, 0)
    return jnp.where(at == 0, beyond, pltpu.roll(plane, 1, 0))


def lane_up(plane, beyond):
    cells = plane.shape[1]
    at = lax.broadcasted_iota(jnp.int32, plane.shape, 1)
    return jnp.where(at == cells - 1, beyond, pltpu.roll(plane, cells - 1, 1))


def lane_down(plane, beyond):
    at = lax.broadcasted_iota(jnp.int32, plane.shape, 1)
    return jnp.where(at == 0, beyond, pltpu.roll(plane, 1, 1))


def mu_inverse(ex, ey, ez):
    return 1.0 / (2.0 + (ex * ex + ey * ey + ez * ez))


def lam_inverse(center, total):
    return 1.0 / (0.5 + 0.125 * (6.0 * center + total))


HALO = 4
X_DAMAGE, X_PULL, X_MU, X_SOURCE, X_SLOTS = 0, 3, 9, 11, 17
LATE_DAMAGE, LATE_PULL, LATE_MU, LATE_SOURCE, LATE_SLOTS = 0, 1, 2, 3, 6
Y_HALO = (3, 2, 2, 2, 1, 2, 2, 2)
Y_KNOWN, Y_FIELDS = 8, 12
CORNER_ROWS = sum(Y_HALO) + 8


def edge_row(s, ny, depth):
    return depth if s == 0 else ny - 1 - depth


def known_of(s, damages, pulls, behind_pull, mus, sources, behind):
    planes = damages[0].shape[0]
    (c1, c2), _, _ = weights()
    soft = [soft_of(part) for part in damages]
    less = damages[0] - 1.0
    wx, wy, wz = (less * pull for pull in pulls)
    wy_behind = (damages[1] - 1.0) * behind_pull

    def across(value):
        return pltpu.roll(value, planes - 1, 0), pltpu.roll(value, 1, 0)

    def along(value, fill):
        return lane_up(value, fill), lane_down(value, fill)

    total = soft[0] + soft[2] + sum(across(soft[1])) + sum(along(soft[1], OUTSIDE))
    inverse = lam_inverse(soft[1], total)
    face = 0.125 * (soft[0] + soft[1])
    scale = 0.25 * mu_inverse(*pulls)
    known = [(1.0 + c1) * mus[0] + c2 * scale * (mus[1] + sum(across(mus[0])) + sum(along(mus[0], 0.0)))]
    x_up, x_down = across(wx * mus[0])
    z_up, z_down = along(wz * mus[0], 0.0)
    y_behind = wy_behind * mus[1]
    transfers = (x_up - x_down, y_behind if s == 0 else -y_behind, z_up - z_down)
    for c in range(3):
        known.append((1.0 + c1) * sources[c] + c2 * (face * (inverse * behind[c]) + transfers[c]))
    return scale, wy, known


def put_rows(s, put, damage, strain, seed_damage, seed_disp):
    ny = damage.shape[1]
    first, second, third = (edge_row(s, ny, depth) for depth in range(3))
    damages = [damage[:, row, :] for row in (first, second, third)]
    pulls = [strain[c, :, first, :] for c in range(3)]
    pulls_behind = [strain[c, :, second, :] for c in range(3)]
    mus = [
        seed_damage[:, first, :] * mu_inverse(*pulls),
        seed_damage[:, second, :] * mu_inverse(*pulls_behind),
    ]
    sources = [seed_disp[c, :, first, :] for c in range(3)]
    behind = [seed_disp[c, :, second, :] for c in range(3)]
    scale, wy, known = known_of(s, damages, pulls, pulls_behind[1], mus, sources, behind)
    for slot, value in enumerate(damages[:2] + [wy, mus[0], scale] + sources + known):
        put(slot, value)


def even(axis):
    return lax.rem(lax.axis_index(axis), 2) == 0


def faces_kernel(
    damage_in, strain_in, seed_in, sources_in, pal_out, other_out, near_out, near_late_out, far_out, far_late_out,
    damage, strain, seed_damage, seed_disp, pal, other, near, near_late, far, far_late, sems, out_sems,
):
    nx = damage.shape[0]
    copies = [
        pltpu.make_async_copy(damage_in, damage, sems.at[0]),
        pltpu.make_async_copy(strain_in, strain, sems.at[1]),
        pltpu.make_async_copy(seed_in, seed_damage, sems.at[2]),
        pltpu.make_async_copy(sources_in, seed_disp, sems.at[3]),
    ]
    for copy in copies:
        copy.start()
    sent = []

    def send(source, target):
        sent.append(pltpu.make_async_copy(source, target, out_sems.at[len(sent)]))
        sent[-1].start()

    def put_planes(out, late, high):
        for depth in range(4):
            at = jnp.where(high, nx - 1 - depth, depth)
            if depth == 3:
                late[LATE_DAMAGE] = damage[at]
                continue
            out[X_DAMAGE + depth] = damage[at]
            pulls = [strain[c, at] for c in range(3)]
            mu = seed_damage[at] * mu_inverse(*pulls)
            if depth == 2:
                late[LATE_PULL] = pulls[0]
                late[LATE_MU] = mu
            else:
                out[X_MU + depth] = mu
            for c in range(3):
                if depth == 2:
                    late[LATE_SOURCE + c] = seed_disp[c, at]
                else:
                    out[X_PULL + 2 * c + depth] = pulls[c]
                    out[X_SOURCE + 2 * c + depth] = seed_disp[c, at]

    for copy in copies:
        copy.wait()
    for out, target, first in ((pal, pal_out, True), (other, other_out, False)):

        def put(slot, value):
            out[slot * nx : (slot + 1) * nx, :] = value

        for s in range(2):

            @pl.when(even("gy") == ((s == 1) == first))
            def _():
                put_rows(s, put, damage, strain, seed_damage, seed_disp)

        send(out, target)
    for out, late, target, late_target, high in (
        (near, near_late, near_out, near_late_out, even("gx")),
        (far, far_late, far_out, far_late_out, ~even("gx")),
    ):
        put_planes(out, late, high)
        send(out, target)
        send(late, late_target)
    for copy in sent:
        copy.wait()


def received_x(near, far, side):
    from_near = even("gx") == (side == 1)

    def plane(slot, row=None):
        at = slot if row is None else (slice(slot, slot + 1), row)
        return jnp.where(from_near, near[at], far[at])

    return plane


def received_y(pal, other, side):
    from_pal = even("gy") == (side == 1)
    return lambda first, count: jnp.where(from_pal, pal[first : first + count, :], other[first : first + count, :])


def deal(pal, other, low, high):
    first = even("gy")
    low, high = low[...], high[...]
    pal[...] = jnp.where(first, high, low)
    other[...] = jnp.where(first, low, high)


def corners_kernel(
    damage, strain, seed_damage, seed_disp, near, far, _, pal, other, field, low, high
):
    nx, ny, _ = damage.shape
    for s, out in enumerate((low, high)):
        first, second, third = (edge_row(s, ny, depth) for depth in range(3))
        for side in range(2):
            x_in = received_x(near, far, side)
            ours = slice(3, 8) if side == 0 else slice(0, 5)
            planes = slice(0, 5) if side == 0 else slice(nx - 5, nx)

            def put_x(slot, first, count, row):
                for far_off in range(count):
                    at = 2 - far_off if side == 0 else 5 + far_off
                    field[slot, at : at + 1, :] = x_in(first + far_off, row)

            for depth, row in enumerate((first, second, third)):
                field[depth, ours, :] = damage[planes, row, :]
                put_x(depth, X_DAMAGE, 3, row)
            for depth, row in enumerate((first, second)):
                pulls = [strain[c, planes, row, :] for c in range(3)]
                for c in range(3):
                    if depth == 0:
                        field[3 + c, ours, :] = pulls[c]
                        put_x(3 + c, X_PULL + 2 * c, 2, row)
                    field[9 + 3 * depth + c, ours, :] = seed_disp[c, planes, row, :]
                    put_x(9 + 3 * depth + c, X_SOURCE + 2 * c, 2, row)
                if depth == 1:
                    field[6, ours, :] = pulls[1]
                    put_x(6, X_PULL + 2, 2, row)
                field[7 + depth, ours, :] = seed_damage[planes, row, :] * mu_inverse(*pulls)
                put_x(7 + depth, X_MU, 2, row)
            got = [field[slot] for slot in range(15)]
            scale, wy, known = known_of(s, got[:3], got[3:6], got[6], got[7:9], got[9:12], got[12:15])
            row = side * CORNER_ROWS
            for slot, value in enumerate(got[:2] + [wy, got[7], scale] + got[9:12]):
                count = Y_HALO[slot]
                start = 3 - count if side == 0 else 5
                out[row : row + count, :] = value[start : start + count, :]
                row += count
            for value in known:
                start = 2 if side == 0 else 4
                out[row : row + 2, :] = value[start : start + 2, :]
                row += 2
    deal(pal, other, low, high)


def in_grid():
    here = lax.axis_index("gx")
    return here > 0, here < lax.axis_size("gx") - 1


def prepare(first, last, soft, pull, raw, g, k, state0):
    planes, ny, nz = soft.shape
    inside = in_grid()
    lane = lax.broadcasted_iota(jnp.int32, (ny, nz), 1)
    row = lax.broadcasted_iota(jnp.int32, (ny, nz), 0)
    inner = (row > 0) & (row < ny - 1)

    def step(at):
        center = soft[at]
        sides = [
            soft[at + 1],
            soft[at - 1],
            pltpu.roll(center, ny - 1, 0),
            pltpu.roll(center, 1, 0),
            lane_up(center, OUTSIDE),
            lane_down(center, OUTSIDE),
        ]
        outside = ((at < HALO) & ~inside[0]) | ((at >= planes - HALO) & ~inside[1])
        inverse = jnp.where(inner & ~outside, lam_inverse(center, sum(sides)), 0.0)
        eighth = 0.125 * inverse
        for j in range(6):
            face = eighth * (center + sides[j])
            if j == 4:
                face = jnp.where(lane == nz - 1, 0.0, face)
            if j == 5:
                face = jnp.where(lane == 0, 0.0, face)
            g[j, at] = face
        k[0, at] = inverse * pull[0, at + 1]
        k[1, at] = -inverse * pull[0, at - 1]
        k[2, at] = inverse * pltpu.roll(pull[1, at], ny - 1, 0)
        k[3, at] = -inverse * pltpu.roll(pull[1, at], 1, 0)
        k[4, at] = inverse * lane_up(pull[2, at], 0.0)
        k[5, at] = -inverse * lane_down(pull[2, at], 0.0)
        for c in range(3):
            state0[1 + c, at] = inverse * raw[c, at]

    by_pairs(first, last, step)


def reach_of(grad, count):
    square = sum(part * part for part in grad)
    scale = 1.0 / jnp.maximum(square, NORMAL_FLOOR)
    power = 1.0 - RELAX_RATE * (1.0 + NORMAL_WEIGHT * square * scale)
    series = 1.0 + power
    for _ in range(2):
        power = power * power
        series = series * (1.0 + power)
    power = power * power
    repeats = jnp.ones_like(power)
    for level in range(1, 4):
        repeats = jnp.where(count > level, 1.0 + power * repeats, repeats)
    return (RELAX_RATE * NORMAL_WEIGHT * scale) * (series * repeats)


def slopes(first, last, count, less, grads):
    ny = less.shape[1]

    def step(at):
        own = less[at]
        grad = [
            0.5 * (less[at + 1] - less[at - 1]),
            0.5 * (pltpu.roll(own, ny - 1, 0) - pltpu.roll(own, 1, 0)),
            0.5 * (lane_up(own, -1.0) - lane_down(own, -1.0)),
        ]
        for c in range(3):
            grads[c, at - HALO] = grad[c]
        grads[3, at - HALO] = reach_of(grad, count)

    by_pairs(first, last, step)


def first_sweep(ranges, state0, state1, g, k, mu_scale):
    (c1, c2), _, _ = weights()

    def advance(at, f, own, moved):
        state1[f, at] = (1.0 + c1) * own + c2 * moved

    for first, last in ranges:
        sweep(first, last, state0, g, k, mu_scale, None, advance)


def inner_kernel(
    damage, strain, seed_damage, seed_disp, less, soft, pull, mu_scale, raw, g, k, state0, state1
):
    nx = damage.shape[0]

    def fill(i, _):
        at = HALO + i
        own = damage[i]
        sx, sy, sz = strain[0, i], strain[1, i], strain[2, i]
        soft[at] = soft_of(own)
        own = own - 1.0
        less[at] = own
        pull[0, at] = own * sx
        pull[1, at] = own * sy
        pull[2, at] = own * sz
        mu_inv = mu_inverse(sx, sy, sz)
        mu_scale[at] = 0.25 * mu_inv
        state0[0, at] = mu_inv * seed_damage[i]
        for c in range(3):
            raw[c, at] = seed_disp[c, i]
        return 0

    lax.fori_loop(0, nx, fill, 0)
    low, high = HALO, HALO + nx
    prepare(low + 1, high - 1, soft, pull, raw, g, k, state0)
    first_sweep([(low + 2, high - 2)], state0, state1, g, k, mu_scale)


def sides_kernel(
    work, near, near_late, far, far_late,
    less_in, soft_in, pull_in, scale_in, raw_in, g_in, k_in, state0_in, state1_in,
    less, soft, pull, mu_scale, raw, g, k, state0, state1, grads,
):
    nx = soft.shape[0] - 2 * HALO
    low, high = HALO, HALO + nx
    inside = in_grid()
    for s in range(2):
        x_in, late = received_x(near, far, s), received_x(near_late, far_late, s)
        for depth in range(4):
            at = low - 1 - depth if s == 0 else high + depth
            own = late(LATE_DAMAGE) if depth == 3 else x_in(X_DAMAGE + depth)
            soft[at] = soft_of(own)
            if depth == 3:
                continue
            own = own - 1.0
            if depth == 0:
                less[at] = own
            if depth == 2:
                pull[0, at] = own * late(LATE_PULL)
                state0[0, at] = late(LATE_MU)
            else:
                pulls = [x_in(X_PULL + 2 * c + depth) for c in range(3)]
                mu_scale[at] = jnp.where(inside[s], 0.25 * mu_inverse(*pulls), 0.0)
                state0[0, at] = x_in(X_MU + depth)
            for c in range(3):
                if depth == 2:
                    raw[c, at] = late(LATE_SOURCE + c)
                else:
                    pull[c, at] = own * pulls[c]
                    raw[c, at] = x_in(X_SOURCE + 2 * c + depth)

    for first, last in ((low - 3, low + 1), (high - 1, high + 3)):
        prepare(first, last, soft, pull, raw, g, k, state0)
    slopes(low, high, work[0, 0], less, grads)
    first_sweep([(low - 2, low + 2), (high - 2, high + 2)], state0, state1, g, k, mu_scale)


def edges_kernel(
    soft, pull, mu_scale, raw, g, state0, state1, y_pal, y_other, c_pal, c_other,
    sent_pal, sent_other, coefficients, firsts, seconds, outer,
    field, sent_low, sent_high,
):
    planes, ny, nz = soft.shape
    nx = planes - 2 * HALO
    (c1, c2), (d1, d2), _ = weights()
    lane = lax.broadcasted_iota(jnp.int32, (planes, nz), 1)
    plane = lax.broadcasted_iota(jnp.int32, (planes, nz), 0)
    here, there = lax.axis_index("gx"), lax.axis_index("gy")
    in_x = ((plane >= HALO) | (here > 0)) & ((plane < HALO + nx) | (here < lax.axis_size("gx") - 1))
    in_y = (there > 0, there < lax.axis_size("gy") - 1)

    def around_x(value):
        return [pltpu.roll(value, planes - 1, 0), pltpu.roll(value, 1, 0)]

    def around_z(value, fill):
        return [lane_up(value, fill), lane_down(value, fill)]

    for s, sent in enumerate((sent_low, sent_high)):
        y_in, c_in = received_y(y_pal, y_other, s), received_y(c_pal, c_other, s)
        e0, e1 = edge_row(s, ny, 0), edge_row(s, ny, 1)

        def ordered(inward, outward):
            return [inward, outward] if s == 0 else [outward, inward]

        row = 0
        for f in range(Y_FIELDS):
            field[f, HALO : HALO + nx, :] = y_in(f * nx, nx)
            count, shift = (Y_HALO[f], 0) if f < Y_KNOWN else (2, 1)
            field[f, HALO - count + shift : HALO + shift, :] = c_in(row, count)
            high = HALO + nx - shift
            field[f, high : high + count, :] = c_in(CORNER_ROWS + row, count)
            row += count

        soft_1, soft_2 = soft_of(field[0]), soft_of(field[1])
        soft_e0, soft_e1 = soft[:, e0, :], soft[:, e1, :]

        def total(center, inward, outward):
            return sum(around_x(center) + [inward, outward] + around_z(center, OUTSIDE))

        inverse_1 = lam_inverse(soft_1, total(soft_1, soft_e0, soft_2))
        inverse_1 = jnp.where(in_x & in_y[s], inverse_1, 0.0)
        lam_1 = [inverse_1 * field[5 + c] for c in range(3)]
        inverse_e0 = jnp.where(in_x, lam_inverse(soft_e0, total(soft_e0, soft_e1, soft_1)), 0.0)
        lam_e0 = [inverse_e0 * raw[c, :, e0, :] for c in range(3)]
        mu_1, wy_1 = field[3], field[2]
        mu_e0, mu_e1 = state0[0, :, e0, :], state0[0, :, e1, :]
        lam_e1 = [state0[1 + c, :, e1, :] for c in range(3)]

        def coefficients_of(center, inverse, inward, outward, wx, wy, wz):
            sides = around_x(center) + ordered(inward, outward) + around_z(center, OUTSIDE)
            eighth = 0.125 * inverse
            faces = [eighth * (center + side) for side in sides]
            faces[4] = jnp.where(lane == nz - 1, 0.0, faces[4])
            faces[5] = jnp.where(lane == 0, 0.0, faces[5])
            pulls = around_x(wx) + wy + around_z(wz, 0.0)
            return faces, [inverse * w if j % 2 == 0 else -inverse * w for j, w in enumerate(pulls)]

        def moved_of(faces, pulls, scale, own, inward, outward):
            sides = [
                around_x(own[f]) + ordered(inward[f], outward[f]) + around_z(own[f], 0.0) for f in range(4)
            ]
            moved = [scale * sum(sides[0])]
            for c in range(3):
                part = sum(faces[j] * sides[1 + c][j] for j in range(6))
                moved.append(part + pulls[2 * c] * sides[0][2 * c] + pulls[2 * c + 1] * sides[0][2 * c + 1])
            return moved

        first_1 = [jnp.where(in_x, field[Y_KNOWN] + c2 * field[4] * mu_e0, 0.0)]
        sides = around_x(soft_1) + around_z(soft_1, OUTSIDE) + [soft_e0]
        faces = [0.125 * (soft_1 + side) for side in sides]
        wy_e0 = pull[1, :, e0, :] * mu_e0
        own_1 = [mu_1] + lam_1
        own_e0 = [mu_e0] + lam_e0
        for c in range(3):
            sides = around_x(lam_1[c]) + around_z(lam_1[c], 0.0) + [lam_e0[c]]
            lacked = sum(faces[j] * sides[j] for j in range(5))
            if c == 1:
                lacked += wy_e0 if s == 0 else -wy_e0
            first_1.append(inverse_1 * (field[Y_KNOWN + 1 + c] + c2 * lacked))

        scale_e0 = mu_scale[:, e0, :]
        wy = ordered(pull[1, :, e1, :], wy_1)
        faces, pulls = coefficients_of(
            soft_e0, inverse_e0, soft_e1, soft_1, pull[0, :, e0, :], wy, pull[2, :, e0, :]
        )
        moved = moved_of(faces, pulls, scale_e0, own_e0, [mu_e1] + lam_e1, own_1)
        first_e0 = [(1.0 + c1) * own_e0[f] + c2 * moved[f] for f in range(4)]

        outward_face = g[3 if s == 0 else 2, :, e1, :]
        first_e1 = [state1[0, :, e1, :]]
        for c in range(3):
            first_e1.append(state1[1 + c, :, e1, :] + c2 * outward_face * lam_e0[c])

        moved = moved_of(faces, pulls, scale_e0, first_e0, first_e1, first_1)
        for f in range(4):
            second = first_e0[f] + (d1 - d2) * (first_e0[f] - own_e0[f]) + d2 * moved[f]
            sent[f * nx : (f + 1) * nx, :] = second[HALO : HALO + nx, :]
            firsts[s, f] = first_e0[f]
            outer[s, f] = first_1[f]
        for j in range(6):
            coefficients[s, j] = faces[j]
            coefficients[s, 6 + j] = pulls[j]
        for c in range(3):
            coefficients[s, 12 + c] = lam_e0[c]
            seconds[s, c] = first_e1[1 + c]
    deal(sent_pal, sent_other, sent_low, sent_high)


def sweep(first, last, state, g, k, mu_scale, rows, advance, finish=None):
    _, ny, nz = mu_scale.shape
    lane = lax.broadcasted_iota(jnp.int32, (ny, nz), 1)
    if rows is None:

        def rows(s, f, at):
            return 0.0

    def plane(at):
        def around(f):
            own = state[f, at]
            return own, [
                state[f, at + 1],
                state[f, at - 1],
                row_up(own, rows(1, f, at)),
                row_down(own, rows(0, f, at)),
                pltpu.roll(own, nz - 1, 1),
                pltpu.roll(own, 1, 1),
            ]

        mu, mu_sides = around(0)
        ends = [
            jnp.where(lane == nz - 1, 0.0, mu_sides[4]),
            jnp.where(lane == 0, 0.0, mu_sides[5]),
        ]
        results = [advance(at, 0, mu, mu_scale[at] * sum(mu_sides[:4] + ends))]
        faces = [g[j, at] for j in range(6)]
        for c in range(3):
            lam, lam_sides = around(1 + c)
            moved = sum(faces[j] * lam_sides[j] for j in range(6))
            moved += k[2 * c, at] * mu_sides[2 * c] + k[2 * c + 1, at] * mu_sides[2 * c + 1]
            results.append(advance(at, 1 + c, lam, moved))
        if finish is not None:
            finish(at - HALO, results)

    by_pairs(first, last, plane)


def wait_kernel(
    work, less, grads, y_pal, y_other,
    mu_scale, coefficients, firsts, seconds, outer, g_in, k_in, state0_in, state1_in,
    out_mu, out_lam, edges, g, k, state0, state1,
    state2, states,
):
    _, nx, ny, _ = grads.shape
    planes = nx + 2 * HALO
    _, (d1, d2), (c1, c2) = weights()
    held = slice(HALO - 2, HALO + nx + 2)
    for s in range(2):
        e0, e1 = edge_row(s, ny, 0), edge_row(s, ny, 1)
        for j in range(6):
            g[j, held, e0, :] = coefficients[s, j, held, :]
            k[j, held, e0, :] = coefficients[s, 6 + j, held, :]
        for c in range(3):
            state0[1 + c, held, e0, :] = coefficients[s, 12 + c, held, :]
            state1[1 + c, held, e1, :] = seconds[s, c, held, :]
        for f in range(4):
            state1[f, held, e0, :] = firsts[s, f, held, :]

    def rows(s, f, at):
        return outer[s, f, pl.ds(at, 1), :]

    def advance_2(at, f, own, moved):
        state2[f, at] = own + (d1 - d2) * (own - state0[f, at]) + d2 * moved

    sweep(HALO - 1, HALO + nx + 1, state1, g, k, mu_scale, rows, advance_2)

    def advance_3(at, f, own, moved):
        return own + c1 * (own - state1[f, at]) + c2 * (state0[f, at] - own + moved)

    def finish(i, results):
        out_mu[i] = results[0]
        along = grads[3, i] * sum(grads[c, i] * results[1 + c] for c in range(3))
        for c in range(3):
            out_lam[c, i] = results[1 + c] - along * grads[c, i]
            states[c, i] = results[1 + c]

    sweep(HALO, HALO + nx, state2, g, k, mu_scale, None, advance_3, finish)

    for s in range(2):
        y_in = received_y(y_pal, y_other, s)
        e0, e1 = edge_row(s, ny, 0), edge_row(s, ny, 1)
        own = less[HALO : HALO + nx, e0, :]
        inward, outward = less[HALO : HALO + nx, e1, :], y_in(0, nx) - 1.0
        grad = [
            0.5 * (less[HALO + 1 : HALO + nx + 1, e0, :] - less[HALO - 1 : HALO + nx - 1, e0, :]),
            0.5 * (inward - outward if s == 0 else outward - inward),
            0.5 * (lane_up(own, -1.0) - lane_down(own, -1.0)),
        ]
        for c in range(3):
            edges[s, c] = grad[c]
            edges[s, 4 + c] = states[c, :, e0, :]
        edges[s, 3] = reach_of(grad, work[0, 0])


def last_kernel(
    mu_scale, coefficients, edges, y_pal, y_other, mu_in, lam_in,
    out_mu, out_lam, mu, lam,
    sems,
):
    nx, ny, nz = mu.shape
    inner = slice(HALO, HALO + nx)
    _, _, (_, c2) = weights()
    for s in range(2):
        y_in = received_y(y_pal, y_other, s)
        e0 = edge_row(s, ny, 0)
        outward = 3 if s == 0 else 2

        def got(f):
            return y_in(f * nx, nx)

        mu[:, e0, :] = mu[:, e0, :] + c2 * mu_scale[inner, e0, :] * got(0)
        face = c2 * coefficients[s, outward, inner, :]
        ends = []
        for c in range(3):
            end = edges[s, 4 + c] + face * got(1 + c)
            if c == 1:
                end += c2 * coefficients[s, 6 + outward, inner, :] * got(0)
            ends.append(end)
        along = edges[s, 3] * sum(edges[s, c] * ends[c] for c in range(3))
        for c in range(3):
            lam[c, :, e0, :] = ends[c] - along * edges[s, c]
    copies = [
        pltpu.make_async_copy(mu, out_mu, sems.at[0]),
        pltpu.make_async_copy(lam, out_lam, sems.at[1]),
    ]
    for copy in copies:
        copy.start()
    for copy in copies:
        copy.wait()


VMEM = pl.BlockSpec(memory_space=pltpu.VMEM)
SMEM = pl.BlockSpec(memory_space=pltpu.SMEM)
HBM = pl.BlockSpec(memory_space=pltpu.HBM)
ANY = pl.BlockSpec(memory_space=pl.ANY)
MIB = 1024 * 1024


def call(kernel, ins, outs, scratch=(), in_specs=None, out_specs=None, aliases=None, grant=24 * MIB):
    return pl.pallas_call(
        kernel,
        out_shape=[jax.ShapeDtypeStruct(shape, F32) for shape in outs],
        in_specs=in_specs or [VMEM] * len(ins),
        out_specs=out_specs or [VMEM] * len(outs),
        scratch_shapes=[pltpu.VMEM(shape, F32) if isinstance(shape, tuple) else shape for shape in scratch],
        input_output_aliases=aliases or {},
        compiler_params=pltpu.CompilerParams(vmem_limit_bytes=grant),
    )(*ins)


def trade(value, axis, first):
    pairs = [(i, i + 1) for i in range(first, lax.axis_size(axis) - 1, 2)]
    return lax.ppermute(value, axis, pairs + [(j, i) for i, j in pairs])


def body(damage, strain, seed_damage, seed_disp, brick_work):
    nx, ny, nz = damage.shape
    plane = (ny, nz)
    brick = (nx,) + plane
    bricks = (3,) + brick
    framed = (nx + 2 * HALO,) + plane
    state = (4,) + framed
    row = (nx + 2 * HALO, nz)
    fields = (damage, strain, seed_damage, seed_disp)

    y_rows = (Y_FIELDS * nx, nz)
    x_faces = [(X_SLOTS,) + plane, (LATE_SLOTS,) + plane]
    faces = [y_rows] * 2 + x_faces * 2
    pal, other, near, near_late, far, far_late = call(
        faces_kernel, fields, faces,
        [brick, bricks, brick, bricks] + faces + [pltpu.SemaphoreType.DMA((4,)), pltpu.SemaphoreType.DMA((6,))],
        in_specs=[HBM] * 4, out_specs=[HBM] * 6, grant=56 * MIB,
    )
    y_in = (trade(pal, "gy", 0), trade(other, "gy", 1))
    far, far_late = trade(far, "gx", 1), trade(far_late, "gx", 1)
    near, near_late = trade(near, "gx", 0), trade(near_late, "gx", 0)
    inner = tuple(call(
        inner_kernel, fields,
        [framed, framed, (3,) + framed, framed, (3,) + framed, (6,) + framed, (6,) + framed, state, state],
    ))
    c_rows = (2 * CORNER_ROWS, nz)
    pal, other = call(
        corners_kernel, fields + (near, far, inner[0]), [c_rows] * 2,
        [(15,) + plane, c_rows, c_rows], in_specs=[VMEM] * 6 + [ANY],
    )
    c_in = (trade(pal, "gy", 0), trade(other, "gy", 1))
    less, soft, pull, mu_scale, raw, g, k, state0, state1, grads = call(
        sides_kernel, (brick_work, near, near_late, far, far_late) + inner,
        [part.shape for part in inner] + [(4,) + brick],
        in_specs=[SMEM] + [VMEM] * 13, aliases={5 + part: part for part in range(9)},
    )
    sent = (4 * nx, nz)
    pal, other, coefficients, firsts, seconds, outer = call(
        edges_kernel, (soft, pull, mu_scale, raw, g, state0, state1) + y_in + c_in,
        [sent] * 2 + [(2, 15) + row, (2, 4) + row, (2, 3) + row, (2, 4) + row],
        [(Y_FIELDS,) + row, sent, sent],
    )
    halo = (trade(pal, "gy", 0), trade(other, "gy", 1))
    ins = (brick_work, less, grads) + y_in + (mu_scale, coefficients, firsts, seconds, outer, g, k, state0, state1)
    mu, lam, edges, *_ = call(
        wait_kernel, ins,
        [brick, bricks, (2, 7, nx, nz), (6,) + framed, (6,) + framed, state, state],
        [state, bricks],
        in_specs=[SMEM] + [VMEM] * (len(ins) - 1),
        aliases={10: 3, 11: 4, 12: 5, 13: 6},
    )
    out_mu, out_lam, *_ = call(
        last_kernel, (mu_scale, coefficients, edges) + halo + (mu, lam),
        [brick, bricks, brick, bricks], [pltpu.SemaphoreType.DMA((2,))],
        out_specs=[HBM, HBM, VMEM, VMEM], aliases={5: 2, 6: 3},
    )
    return out_mu, out_lam


def solution(mesh):
    placed = (
        P("gx", "gy", None),
        P(None, "gx", "gy", None),
        P("gx", "gy", None),
        P(None, "gx", "gy", None),
        P("gx", "gy"),
    )
    return jax.shard_map(
        body,
        mesh=mesh,
        in_specs=placed,
        out_specs=(P("gx", "gy", None), P(None, "gx", "gy", None)),
        check_vma=False,
    )
```

```python
import functools

import jax
import jax.numpy as jnp
from jax import lax
from jax.experimental import pallas as pl
from jax.experimental.pallas import tpu as pltpu
from jax.sharding import PartitionSpec as P

RELAX_INNER = 8
RESIDUAL_STIFFNESS = 0.001
CENTER_VALUE = 1.0
HALF_WIDTH = 0.75
NORMAL_WEIGHT = 1.5
RELAX_RATE = 0.5 / RELAX_INNER
NORMAL_FLOOR = 0.05
OUTSIDE = 1.0 + RESIDUAL_STIFFNESS
F32 = jnp.float32


def weights():
    ratio = CENTER_VALUE / HALF_WIDTH
    rho = 1.0 / ratio
    found = []
    for _ in range(3):
        rho_next = 1.0 / (2.0 * ratio - rho)
        found.append((rho_next * rho, 2.0 * rho_next / HALF_WIDTH))
        rho = rho_next
    return found


def by_pairs(first, last, step):
    width = 2 if (last - first) % 2 == 0 else 1

    def turn(i, _):
        for part in range(width):
            step(first + width * i + part)
        return 0

    lax.fori_loop(0, (last - first) // width, turn, 0)


def soft_of(damage):
    return (1.0 - damage) ** 2 + RESIDUAL_STIFFNESS


def row_up(plane, beyond):
    rows = plane.shape[0]
    at = lax.broadcasted_iota(jnp.int32, plane.shape, 0)
    return jnp.where(at == rows - 1, beyond, pltpu.roll(plane, rows - 1, 0))


def row_down(plane, beyond):
    at = lax.broadcasted_iota(jnp.int32, plane.shape, 0)
    return jnp.where(at == 0, beyond, pltpu.roll(plane, 1, 0))


def lane_up(plane, beyond):
    cells = plane.shape[1]
    at = lax.broadcasted_iota(jnp.int32, plane.shape, 1)
    return jnp.where(at == cells - 1, beyond, pltpu.roll(plane, cells - 1, 1))


def lane_down(plane, beyond):
    at = lax.broadcasted_iota(jnp.int32, plane.shape, 1)
    return jnp.where(at == 0, beyond, pltpu.roll(plane, 1, 1))


def mu_inverse(ex, ey, ez):
    return 1.0 / (2.0 + (ex * ex + ey * ey + ez * ez))


def lam_inverse(center, total):
    return 1.0 / (0.5 + 0.125 * (6.0 * center + total))


HALO = 4
X_DAMAGE, X_PULL, X_MU, X_SOURCE, X_SLOTS = 0, 3, 9, 11, 17
LATE_DAMAGE, LATE_PULL, LATE_MU, LATE_SOURCE, LATE_SLOTS = 0, 1, 2, 3, 6
Y_HALO = (2, 1, 1, 1, 0, 1, 1, 1)
Y_KNOWN, Y_FIELDS = 8, 12
CORNER_ROWS = sum(Y_HALO) + 4


def edge_row(s, ny, depth):
    return depth if s == 0 else ny - 1 - depth


def known_of(s, damages, pulls, behind_pull, mus, sources, behind):
    planes = damages[0].shape[0]
    (c1, c2), _, _ = weights()
    soft = [soft_of(part) for part in damages]
    less = damages[0] - 1.0
    wx, wy, wz = (less * pull for pull in pulls)
    wy_behind = (damages[1] - 1.0) * behind_pull

    def across(value):
        return pltpu.roll(value, planes - 1, 0), pltpu.roll(value, 1, 0)

    def along(value, fill):
        return lane_up(value, fill), lane_down(value, fill)

    total = soft[0] + soft[2] + sum(across(soft[1])) + sum(along(soft[1], OUTSIDE))
    inverse = lam_inverse(soft[1], total)
    face = 0.125 * (soft[0] + soft[1])
    scale = 0.25 * mu_inverse(*pulls)
    known = [(1.0 + c1) * mus[0] + c2 * scale * (mus[1] + sum(across(mus[0])) + sum(along(mus[0], 0.0)))]
    x_up, x_down = across(wx * mus[0])
    z_up, z_down = along(wz * mus[0], 0.0)
    y_behind = wy_behind * mus[1]
    transfers = (x_up - x_down, y_behind if s == 0 else -y_behind, z_up - z_down)
    for c in range(3):
        known.append((1.0 + c1) * sources[c] + c2 * (face * (inverse * behind[c]) + transfers[c]))
    return scale, wy, known


def put_rows(s, put, damage, strain, seed_damage, seed_disp):
    ny = damage.shape[1]
    first, second, third = (edge_row(s, ny, depth) for depth in range(3))
    damages = [damage[:, row, :] for row in (first, second, third)]
    pulls = [strain[c, :, first, :] for c in range(3)]
    pulls_behind = [strain[c, :, second, :] for c in range(3)]
    mus = [
        seed_damage[:, first, :] * mu_inverse(*pulls),
        seed_damage[:, second, :] * mu_inverse(*pulls_behind),
    ]
    sources = [seed_disp[c, :, first, :] for c in range(3)]
    behind = [seed_disp[c, :, second, :] for c in range(3)]
    scale, wy, known = known_of(s, damages, pulls, pulls_behind[1], mus, sources, behind)
    for slot, value in enumerate(damages[:2] + [wy, mus[0], scale] + sources + known):
        put(slot, value)


def even(axis):
    return lax.rem(lax.axis_index(axis), 2) == 0


def faces_kernel(
    damage_in, strain_in, seed_in, sources_in, pal_out, other_out, near_out, near_late_out, far_out, far_late_out,
    damage, strain, seed_damage, seed_disp, pal, other, near, near_late, far, far_late, sems, out_sems,
):
    nx = damage.shape[0]
    copies = [
        pltpu.make_async_copy(damage_in, damage, sems.at[0]),
        pltpu.make_async_copy(strain_in, strain, sems.at[1]),
        pltpu.make_async_copy(seed_in, seed_damage, sems.at[2]),
        pltpu.make_async_copy(sources_in, seed_disp, sems.at[3]),
    ]
    for copy in copies:
        copy.start()
    sent = []

    def send(source, target):
        sent.append(pltpu.make_async_copy(source, target, out_sems.at[len(sent)]))
        sent[-1].start()

    def put_planes(out, late, high):
        for depth in range(4):
            at = jnp.where(high, nx - 1 - depth, depth)
            if depth == 3:
                late[LATE_DAMAGE] = damage[at]
                continue
            out[X_DAMAGE + depth] = damage[at]
            pulls = [strain[c, at] for c in range(3)]
            mu = seed_damage[at] * mu_inverse(*pulls)
            if depth == 2:
                late[LATE_PULL] = pulls[0]
                late[LATE_MU] = mu
            else:
                out[X_MU + depth] = mu
            for c in range(3):
                if depth == 2:
                    late[LATE_SOURCE + c] = seed_disp[c, at]
                else:
                    out[X_PULL + 2 * c + depth] = pulls[c]
                    out[X_SOURCE + 2 * c + depth] = seed_disp[c, at]

    for copy in copies:
        copy.wait()
    for out, target, first in ((pal, pal_out, True), (other, other_out, False)):

        def put(slot, value):
            out[slot * nx : (slot + 1) * nx, :] = value

        for s in range(2):

            @pl.when(even("gy") == ((s == 1) == first))
            def _():
                put_rows(s, put, damage, strain, seed_damage, seed_disp)

        send(out, target)
    for out, late, target, late_target, high in (
        (near, near_late, near_out, near_late_out, even("gx")),
        (far, far_late, far_out, far_late_out, ~even("gx")),
    ):
        put_planes(out, late, high)
        send(out, target)
        send(late, late_target)
    for copy in sent:
        copy.wait()


def received_x(near, far, side):
    from_near = even("gx") == (side == 1)

    def plane(slot, row=None):
        at = slot if row is None else (slice(slot, slot + 1), row)
        return jnp.where(from_near, near[at], far[at])

    return plane


def received_y(pal, other, side):
    from_pal = even("gy") == (side == 1)
    return lambda first, count: jnp.where(from_pal, pal[first : first + count, :], other[first : first + count, :])


def deal(pal, other, low, high, axis="gy"):
    first = even(axis)
    low, high = low[...], high[...]
    pal[...] = jnp.where(first, high, low)
    other[...] = jnp.where(first, low, high)


def corners_kernel(
    damage, strain, seed_damage, seed_disp, near, far, _, pal, other, field, low, high
):
    nx, ny, _ = damage.shape
    for s, out in enumerate((low, high)):
        first, second, third = (edge_row(s, ny, depth) for depth in range(3))
        for side in range(2):
            x_in = received_x(near, far, side)
            ours = slice(3, 8) if side == 0 else slice(0, 5)
            planes = slice(0, 5) if side == 0 else slice(nx - 5, nx)

            def put_x(slot, first, count, row):
                for far_off in range(count):
                    at = 2 - far_off if side == 0 else 5 + far_off
                    field[slot, at : at + 1, :] = x_in(first + far_off, row)

            for depth, row in enumerate((first, second, third)):
                field[depth, ours, :] = damage[planes, row, :]
                put_x(depth, X_DAMAGE, 3, row)
            for depth, row in enumerate((first, second)):
                pulls = [strain[c, planes, row, :] for c in range(3)]
                for c in range(3):
                    if depth == 0:
                        field[3 + c, ours, :] = pulls[c]
                        put_x(3 + c, X_PULL + 2 * c, 2, row)
                    field[9 + 3 * depth + c, ours, :] = seed_disp[c, planes, row, :]
                    put_x(9 + 3 * depth + c, X_SOURCE + 2 * c, 2, row)
                if depth == 1:
                    field[6, ours, :] = pulls[1]
                    put_x(6, X_PULL + 2, 2, row)
                field[7 + depth, ours, :] = seed_damage[planes, row, :] * mu_inverse(*pulls)
                put_x(7 + depth, X_MU, 2, row)
            got = [field[slot] for slot in range(15)]
            scale, wy, known = known_of(s, got[:3], got[3:6], got[6], got[7:9], got[9:12], got[12:15])
            row = side * CORNER_ROWS
            for slot, value in enumerate(got[:2] + [wy, got[7], scale] + got[9:12]):
                count = Y_HALO[slot]
                if count == 0:
                    continue
                start = 3 - count if side == 0 else 5
                out[row : row + count, :] = value[start : start + count, :]
                row += count
            for value in known:
                edge = 3 if side == 0 else 4
                out[row : row + 1, :] = value[edge : edge + 1, :]
                row += 1
    deal(pal, other, low, high)


def in_grid():
    here = lax.axis_index("gx")
    return here > 0, here < lax.axis_size("gx") - 1


def prepare(first, last, soft, pull, raw, g, k, state0):
    planes, ny, nz = soft.shape
    inside = in_grid()
    lane = lax.broadcasted_iota(jnp.int32, (ny, nz), 1)
    row = lax.broadcasted_iota(jnp.int32, (ny, nz), 0)
    inner = (row > 0) & (row < ny - 1)

    def step(at):
        center = soft[at]
        sides = [
            soft[at + 1],
            soft[at - 1],
            pltpu.roll(center, ny - 1, 0),
            pltpu.roll(center, 1, 0),
            lane_up(center, OUTSIDE),
            lane_down(center, OUTSIDE),
        ]
        outside = ((at < HALO) & ~inside[0]) | ((at >= planes - HALO) & ~inside[1])
        inverse = jnp.where(inner & ~outside, lam_inverse(center, sum(sides)), 0.0)
        eighth = 0.125 * inverse
        for j in range(6):
            face = eighth * (center + sides[j])
            if j == 4:
                face = jnp.where(lane == nz - 1, 0.0, face)
            if j == 5:
                face = jnp.where(lane == 0, 0.0, face)
            g[j, at] = face
        k[0, at] = inverse * pull[0, at + 1]
        k[1, at] = -inverse * pull[0, at - 1]
        k[2, at] = inverse * pltpu.roll(pull[1, at], ny - 1, 0)
        k[3, at] = -inverse * pltpu.roll(pull[1, at], 1, 0)
        k[4, at] = inverse * lane_up(pull[2, at], 0.0)
        k[5, at] = -inverse * lane_down(pull[2, at], 0.0)
        for c in range(3):
            state0[1 + c, at] = inverse * raw[c, at]

    by_pairs(first, last, step)


def reach_of(grad, count):
    square = sum(part * part for part in grad)
    scale = 1.0 / jnp.maximum(square, NORMAL_FLOOR)
    power = 1.0 - RELAX_RATE * (1.0 + NORMAL_WEIGHT * square * scale)
    series = 1.0 + power
    for _ in range(2):
        power = power * power
        series = series * (1.0 + power)
    power = power * power
    repeats = jnp.ones_like(power)
    for level in range(1, 4):
        repeats = jnp.where(count > level, 1.0 + power * repeats, repeats)
    return (RELAX_RATE * NORMAL_WEIGHT * scale) * (series * repeats)


def slopes(first, last, count, less, grads):
    ny = less.shape[1]

    def step(at):
        own = less[at]
        grad = [
            0.5 * (less[at + 1] - less[at - 1]),
            0.5 * (pltpu.roll(own, ny - 1, 0) - pltpu.roll(own, 1, 0)),
            0.5 * (lane_up(own, -1.0) - lane_down(own, -1.0)),
        ]
        for c in range(3):
            grads[c, at - HALO] = grad[c]
        grads[3, at - HALO] = reach_of(grad, count)

    by_pairs(first, last, step)


def first_sweep(ranges, state0, state1, g, k, mu_scale):
    (c1, c2), _, _ = weights()

    def advance(at, f, own, moved):
        state1[f, at] = (1.0 + c1) * own + c2 * moved

    for first, last in ranges:
        sweep(first, last, state0, g, k, mu_scale, None, advance)


def inner_kernel(
    damage, strain, seed_damage, seed_disp, less, soft, pull, mu_scale, raw, g, k, state0, state1
):
    nx = damage.shape[0]

    def fill(i, _):
        at = HALO + i
        own = damage[i]
        sx, sy, sz = strain[0, i], strain[1, i], strain[2, i]
        soft[at] = soft_of(own)
        own = own - 1.0
        less[at] = own
        pull[0, at] = own * sx
        pull[1, at] = own * sy
        pull[2, at] = own * sz
        mu_inv = mu_inverse(sx, sy, sz)
        mu_scale[at] = 0.25 * mu_inv
        state0[0, at] = mu_inv * seed_damage[i]
        for c in range(3):
            raw[c, at] = seed_disp[c, i]
        return 0

    lax.fori_loop(0, nx, fill, 0)
    low, high = HALO, HALO + nx
    prepare(low + 1, high - 1, soft, pull, raw, g, k, state0)
    first_sweep([(low + 2, high - 2)], state0, state1, g, k, mu_scale)


def sides_kernel(
    work, near, near_late, far, far_late,
    less_in, soft_in, pull_in, scale_in, raw_in, g_in, k_in, state0_in, state1_in,
    less, soft, pull, mu_scale, raw, g, k, state0, state1, grads,
):
    nx = soft.shape[0] - 2 * HALO
    low, high = HALO, HALO + nx
    inside = in_grid()
    for s in range(2):
        x_in, late = received_x(near, far, s), received_x(near_late, far_late, s)
        for depth in range(4):
            at = low - 1 - depth if s == 0 else high + depth
            own = late(LATE_DAMAGE) if depth == 3 else x_in(X_DAMAGE + depth)
            soft[at] = soft_of(own)
            if depth == 3:
                continue
            own = own - 1.0
            if depth == 0:
                less[at] = own
            if depth == 2:
                pull[0, at] = own * late(LATE_PULL)
                state0[0, at] = late(LATE_MU)
            else:
                pulls = [x_in(X_PULL + 2 * c + depth) for c in range(3)]
                mu_scale[at] = jnp.where(inside[s], 0.25 * mu_inverse(*pulls), 0.0)
                state0[0, at] = x_in(X_MU + depth)
            for c in range(3):
                if depth == 2:
                    raw[c, at] = late(LATE_SOURCE + c)
                else:
                    pull[c, at] = own * pulls[c]
                    raw[c, at] = x_in(X_SOURCE + 2 * c + depth)

    for first, last in ((low - 3, low + 1), (high - 1, high + 3)):
        prepare(first, last, soft, pull, raw, g, k, state0)
    slopes(low, high, work[0, 0], less, grads)
    first_sweep([(low - 2, low + 2), (high - 2, high + 2)], state0, state1, g, k, mu_scale)


def edges_kernel(
    soft, pull, mu_scale, raw, g, state0, state1, y_pal, y_other, c_pal, c_other,
    sent_pal, sent_other, sent_near, sent_far, coefficients, firsts, seconds, outer,
    field, sent_low, sent_high, x_low, x_high,
):
    planes, ny, nz = soft.shape
    nx = planes - 2 * HALO
    (c1, c2), (d1, d2), _ = weights()
    lane = lax.broadcasted_iota(jnp.int32, (planes, nz), 1)
    plane = lax.broadcasted_iota(jnp.int32, (planes, nz), 0)
    here, there = lax.axis_index("gx"), lax.axis_index("gy")
    in_x = ((plane >= HALO) | (here > 0)) & ((plane < HALO + nx) | (here < lax.axis_size("gx") - 1))
    in_y = (there > 0, there < lax.axis_size("gy") - 1)

    def around_x(value):
        return [pltpu.roll(value, planes - 1, 0), pltpu.roll(value, 1, 0)]

    def around_z(value, fill):
        return [lane_up(value, fill), lane_down(value, fill)]

    for s, sent in enumerate((sent_low, sent_high)):
        y_in, c_in = received_y(y_pal, y_other, s), received_y(c_pal, c_other, s)
        e0, e1 = edge_row(s, ny, 0), edge_row(s, ny, 1)

        def ordered(inward, outward):
            return [inward, outward] if s == 0 else [outward, inward]

        row = 0
        for f in range(Y_FIELDS):
            field[f, HALO : HALO + nx, :] = y_in(f * nx, nx)
            count, shift = (Y_HALO[f], 0) if f < Y_KNOWN else (1, 1)
            if count == 0:
                continue
            field[f, HALO - count + shift : HALO + shift, :] = c_in(row, count)
            high = HALO + nx - shift
            field[f, high : high + count, :] = c_in(CORNER_ROWS + row, count)
            row += count

        soft_1, soft_2 = soft_of(field[0]), soft_of(field[1])
        soft_e0, soft_e1 = soft[:, e0, :], soft[:, e1, :]

        def total(center, inward, outward):
            return sum(around_x(center) + [inward, outward] + around_z(center, OUTSIDE))

        inverse_1 = lam_inverse(soft_1, total(soft_1, soft_e0, soft_2))
        inverse_1 = jnp.where(in_x & in_y[s], inverse_1, 0.0)
        lam_1 = [inverse_1 * field[5 + c] for c in range(3)]
        inverse_e0 = jnp.where(in_x, lam_inverse(soft_e0, total(soft_e0, soft_e1, soft_1)), 0.0)
        lam_e0 = [inverse_e0 * raw[c, :, e0, :] for c in range(3)]
        mu_1, wy_1 = field[3], field[2]
        mu_e0, mu_e1 = state0[0, :, e0, :], state0[0, :, e1, :]
        lam_e1 = [state0[1 + c, :, e1, :] for c in range(3)]

        def coefficients_of(center, inverse, inward, outward, wx, wy, wz):
            sides = around_x(center) + ordered(inward, outward) + around_z(center, OUTSIDE)
            eighth = 0.125 * inverse
            faces = [eighth * (center + side) for side in sides]
            faces[4] = jnp.where(lane == nz - 1, 0.0, faces[4])
            faces[5] = jnp.where(lane == 0, 0.0, faces[5])
            pulls = around_x(wx) + wy + around_z(wz, 0.0)
            return faces, [inverse * w if j % 2 == 0 else -inverse * w for j, w in enumerate(pulls)]

        def moved_of(faces, pulls, scale, own, inward, outward):
            sides = [
                around_x(own[f]) + ordered(inward[f], outward[f]) + around_z(own[f], 0.0) for f in range(4)
            ]
            moved = [scale * sum(sides[0])]
            for c in range(3):
                part = sum(faces[j] * sides[1 + c][j] for j in range(6))
                moved.append(part + pulls[2 * c] * sides[0][2 * c] + pulls[2 * c + 1] * sides[0][2 * c + 1])
            return moved

        first_1 = [jnp.where(in_x, field[Y_KNOWN] + c2 * field[4] * mu_e0, 0.0)]
        sides = around_x(soft_1) + around_z(soft_1, OUTSIDE) + [soft_e0]
        faces = [0.125 * (soft_1 + side) for side in sides]
        wy_e0 = pull[1, :, e0, :] * mu_e0
        own_1 = [mu_1] + lam_1
        own_e0 = [mu_e0] + lam_e0
        for c in range(3):
            sides = around_x(lam_1[c]) + around_z(lam_1[c], 0.0) + [lam_e0[c]]
            lacked = sum(faces[j] * sides[j] for j in range(5))
            if c == 1:
                lacked += wy_e0 if s == 0 else -wy_e0
            first_1.append(inverse_1 * (field[Y_KNOWN + 1 + c] + c2 * lacked))

        scale_e0 = mu_scale[:, e0, :]
        wy = ordered(pull[1, :, e1, :], wy_1)
        faces, pulls = coefficients_of(
            soft_e0, inverse_e0, soft_e1, soft_1, pull[0, :, e0, :], wy, pull[2, :, e0, :]
        )
        moved = moved_of(faces, pulls, scale_e0, own_e0, [mu_e1] + lam_e1, own_1)
        first_e0 = [(1.0 + c1) * own_e0[f] + c2 * moved[f] for f in range(4)]

        outward_face = g[3 if s == 0 else 2, :, e1, :]
        first_e1 = [state1[0, :, e1, :]]
        for c in range(3):
            first_e1.append(state1[1 + c, :, e1, :] + c2 * outward_face * lam_e0[c])

        moved = moved_of(faces, pulls, scale_e0, first_e0, first_e1, first_1)
        for f in range(4):
            second = first_e0[f] + (d1 - d2) * (first_e0[f] - own_e0[f]) + d2 * moved[f]
            sent[f * nx : (f + 1) * nx, :] = second[HALO : HALO + nx, :]
            x_low[4 * s + f : 4 * s + f + 1, :] = second[HALO : HALO + 1, :]
            x_high[4 * s + f : 4 * s + f + 1, :] = second[HALO + nx - 1 : HALO + nx, :]
            firsts[s, f] = first_e0[f]
            outer[s, f] = first_1[f]
        for j in range(6):
            coefficients[s, j] = faces[j]
            coefficients[s, 6 + j] = pulls[j]
        for c in range(3):
            coefficients[s, 12 + c] = lam_e0[c]
            seconds[s, c] = first_e1[1 + c]
    deal(sent_pal, sent_other, sent_low, sent_high)
    deal(sent_near, sent_far, x_low, x_high, "gx")


def sweep(first, last, state, g, k, mu_scale, rows, advance, finish=None):
    _, ny, nz = mu_scale.shape
    lane = lax.broadcasted_iota(jnp.int32, (ny, nz), 1)
    if rows is None:

        def rows(s, f, at):
            return 0.0

    def plane(at):
        def around(f):
            own = state[f, at]
            return own, [
                state[f, at + 1],
                state[f, at - 1],
                row_up(own, rows(1, f, at)),
                row_down(own, rows(0, f, at)),
                pltpu.roll(own, nz - 1, 1),
                pltpu.roll(own, 1, 1),
            ]

        mu, mu_sides = around(0)
        ends = [
            jnp.where(lane == nz - 1, 0.0, mu_sides[4]),
            jnp.where(lane == 0, 0.0, mu_sides[5]),
        ]
        results = [advance(at, 0, mu, mu_scale[at] * sum(mu_sides[:4] + ends))]
        faces = [g[j, at] for j in range(6)]
        for c in range(3):
            lam, lam_sides = around(1 + c)
            moved = sum(faces[j] * lam_sides[j] for j in range(6))
            moved += k[2 * c, at] * mu_sides[2 * c] + k[2 * c + 1, at] * mu_sides[2 * c + 1]
            results.append(advance(at, 1 + c, lam, moved))
        if finish is not None:
            finish(at - HALO, results)

    by_pairs(first, last, plane)


def wait_kernel(
    work, less, grads, y_pal, y_other,
    mu_scale, coefficients, firsts, seconds, outer, g_in, k_in, state0_in, state1_in,
    out_mu, out_lam, edges, g, k, state0, state1,
    state2, states,
):
    _, nx, ny, _ = grads.shape
    planes = nx + 2 * HALO
    _, (d1, d2), (c1, c2) = weights()
    held = slice(HALO - 2, HALO + nx + 2)
    for s in range(2):
        e0, e1 = edge_row(s, ny, 0), edge_row(s, ny, 1)
        for j in range(6):
            g[j, held, e0, :] = coefficients[s, j, held, :]
            k[j, held, e0, :] = coefficients[s, 6 + j, held, :]
        for c in range(3):
            state0[1 + c, held, e0, :] = coefficients[s, 12 + c, held, :]
            state1[1 + c, held, e1, :] = seconds[s, c, held, :]
        for f in range(4):
            state1[f, held, e0, :] = firsts[s, f, held, :]

    def rows(s, f, at):
        return outer[s, f, pl.ds(at, 1), :]

    def advance_2(at, f, own, moved):
        state2[f, at] = own + (d1 - d2) * (own - state0[f, at]) + d2 * moved

    sweep(HALO - 1, HALO + nx + 1, state1, g, k, mu_scale, rows, advance_2)
    nothing = jnp.zeros((1, state2.shape[3]), F32)
    for s in range(2):
        e0 = edge_row(s, ny, 0)
        for f in range(4):
            for at in (HALO - 1, HALO + nx):
                state2[f, at, e0 : e0 + 1, :] = nothing

    def advance_3(at, f, own, moved):
        return own + c1 * (own - state1[f, at]) + c2 * (state0[f, at] - own + moved)

    def finish(i, results):
        out_mu[i] = results[0]
        along = grads[3, i] * sum(grads[c, i] * results[1 + c] for c in range(3))
        for c in range(3):
            out_lam[c, i] = results[1 + c] - along * grads[c, i]
            states[c, i] = results[1 + c]

    sweep(HALO, HALO + nx, state2, g, k, mu_scale, None, advance_3, finish)

    for s in range(2):
        y_in = received_y(y_pal, y_other, s)
        e0, e1 = edge_row(s, ny, 0), edge_row(s, ny, 1)
        own = less[HALO : HALO + nx, e0, :]
        inward, outward = less[HALO : HALO + nx, e1, :], y_in(0, nx) - 1.0
        grad = [
            0.5 * (less[HALO + 1 : HALO + nx + 1, e0, :] - less[HALO - 1 : HALO + nx - 1, e0, :]),
            0.5 * (inward - outward if s == 0 else outward - inward),
            0.5 * (lane_up(own, -1.0) - lane_down(own, -1.0)),
        ]
        for c in range(3):
            edges[s, c] = grad[c]
            edges[s, 4 + c] = states[c, :, e0, :]
        edges[s, 3] = reach_of(grad, work[0, 0])


def last_kernel(
    mu_scale, coefficients, edges, y_pal, y_other, x_near, x_far, mu_in, lam_in,
    out_mu, out_lam, mu, lam,
    sems,
):
    nx, ny, nz = mu.shape
    inner = slice(HALO, HALO + nx)
    _, _, (_, c2) = weights()
    for s in range(2):
        y_in = received_y(y_pal, y_other, s)
        e0 = edge_row(s, ny, 0)
        outward = 3 if s == 0 else 2

        def got(f):
            return y_in(f * nx, nx)

        ends_x = []
        for side, at, way in ((0, HALO, 1), (1, HALO + nx - 1, 0)):
            x_in = received_x(x_near, x_far, side)
            sides_x = [x_in(slice(4 * s + f, 4 * s + f + 1)) for f in range(4)]
            face = c2 * coefficients[s, way, at : at + 1, :]
            end = [c2 * mu_scale[at, e0 : e0 + 1, :] * sides_x[0]] + [face * sides_x[1 + c] for c in range(3)]
            end[1] += c2 * coefficients[s, 6 + way, at : at + 1, :] * sides_x[0]
            ends_x.append(end)
        plane = lax.broadcasted_iota(jnp.int32, (nx, nz), 0)

        def from_x(f):
            return jnp.where(plane == 0, ends_x[0][f], jnp.where(plane == nx - 1, ends_x[1][f], 0.0))

        mu[:, e0, :] = mu[:, e0, :] + c2 * mu_scale[inner, e0, :] * got(0) + from_x(0)
        face = c2 * coefficients[s, outward, inner, :]
        ends = []
        for c in range(3):
            end = edges[s, 4 + c] + face * got(1 + c) + from_x(1 + c)
            if c == 1:
                end += c2 * coefficients[s, 6 + outward, inner, :] * got(0)
            ends.append(end)
        along = edges[s, 3] * sum(edges[s, c] * ends[c] for c in range(3))
        for c in range(3):
            lam[c, :, e0, :] = ends[c] - along * edges[s, c]
    copies = [
        pltpu.make_async_copy(mu, out_mu, sems.at[0]),
        pltpu.make_async_copy(lam, out_lam, sems.at[1]),
    ]
    for copy in copies:
        copy.start()
    for copy in copies:
        copy.wait()


VMEM = pl.BlockSpec(memory_space=pltpu.VMEM)
SMEM = pl.BlockSpec(memory_space=pltpu.SMEM)
HBM = pl.BlockSpec(memory_space=pltpu.HBM)
ANY = pl.BlockSpec(memory_space=pl.ANY)
MIB = 1024 * 1024


def call(kernel, ins, outs, scratch=(), in_specs=None, out_specs=None, aliases=None, grant=24 * MIB):
    return pl.pallas_call(
        kernel,
        out_shape=[jax.ShapeDtypeStruct(shape, F32) for shape in outs],
        in_specs=in_specs or [VMEM] * len(ins),
        out_specs=out_specs or [VMEM] * len(outs),
        scratch_shapes=[pltpu.VMEM(shape, F32) if isinstance(shape, tuple) else shape for shape in scratch],
        input_output_aliases=aliases or {},
        compiler_params=pltpu.CompilerParams(vmem_limit_bytes=grant),
    )(*ins)


def trade(value, axis, first):
    pairs = [(i, i + 1) for i in range(first, lax.axis_size(axis) - 1, 2)]
    return lax.ppermute(value, axis, pairs + [(j, i) for i, j in pairs])


def body(damage, strain, seed_damage, seed_disp, brick_work):
    nx, ny, nz = damage.shape
    plane = (ny, nz)
    brick = (nx,) + plane
    bricks = (3,) + brick
    framed = (nx + 2 * HALO,) + plane
    state = (4,) + framed
    row = (nx + 2 * HALO, nz)
    fields = (damage, strain, seed_damage, seed_disp)

    y_rows = (Y_FIELDS * nx, nz)
    x_faces = [(X_SLOTS,) + plane, (LATE_SLOTS,) + plane]
    faces = [y_rows] * 2 + x_faces * 2
    pal, other, near, near_late, far, far_late = call(
        faces_kernel, fields, faces,
        [brick, bricks, brick, bricks] + faces + [pltpu.SemaphoreType.DMA((4,)), pltpu.SemaphoreType.DMA((6,))],
        in_specs=[HBM] * 4, out_specs=[HBM] * 6, grant=56 * MIB,
    )
    y_in = (trade(pal, "gy", 0), trade(other, "gy", 1))
    far, far_late = trade(far, "gx", 1), trade(far_late, "gx", 1)
    near, near_late = trade(near, "gx", 0), trade(near_late, "gx", 0)
    inner = tuple(call(
        inner_kernel, fields,
        [framed, framed, (3,) + framed, framed, (3,) + framed, (6,) + framed, (6,) + framed, state, state],
    ))
    c_rows = (2 * CORNER_ROWS, nz)
    pal, other = call(
        corners_kernel, fields + (near, far, inner[0]), [c_rows] * 2,
        [(15,) + plane, c_rows, c_rows], in_specs=[VMEM] * 6 + [ANY],
    )
    c_in = (trade(pal, "gy", 0), trade(other, "gy", 1))
    less, soft, pull, mu_scale, raw, g, k, state0, state1, grads = call(
        sides_kernel, (brick_work, near, near_late, far, far_late) + inner,
        [part.shape for part in inner] + [(4,) + brick],
        in_specs=[SMEM] + [VMEM] * 13, aliases={5 + part: part for part in range(9)},
    )
    sent = (4 * nx, nz)
    x_sent = (8, nz)
    pal, other, near, far, coefficients, firsts, seconds, outer = call(
        edges_kernel, (soft, pull, mu_scale, raw, g, state0, state1) + y_in + c_in,
        [sent] * 2 + [x_sent] * 2 + [(2, 15) + row, (2, 4) + row, (2, 3) + row, (2, 4) + row],
        [(Y_FIELDS,) + row, sent, sent, x_sent, x_sent],
    )
    halo = (trade(pal, "gy", 0), trade(other, "gy", 1), trade(near, "gx", 0), trade(far, "gx", 1))
    ins = (brick_work, less, grads) + y_in + (mu_scale, coefficients, firsts, seconds, outer, g, k, state0, state1)
    mu, lam, edges, *_ = call(
        wait_kernel, ins,
        [brick, bricks, (2, 7, nx, nz), (6,) + framed, (6,) + framed, state, state],
        [state, bricks],
        in_specs=[SMEM] + [VMEM] * (len(ins) - 1),
        aliases={10: 3, 11: 4, 12: 5, 13: 6},
    )
    out_mu, out_lam, *_ = call(
        last_kernel, (mu_scale, coefficients, edges) + halo + (mu, lam),
        [brick, bricks, brick, bricks], [pltpu.SemaphoreType.DMA((2,))],
        out_specs=[HBM, HBM, VMEM, VMEM], aliases={7: 2, 8: 3},
    )
    return out_mu, out_lam


def solution(mesh):
    placed = (
        P("gx", "gy", None),
        P(None, "gx", "gy", None),
        P("gx", "gy", None),
        P(None, "gx", "gy", None),
        P("gx", "gy"),
    )
    return jax.shard_map(
        body,
        mesh=mesh,
        in_specs=placed,
        out_specs=(P("gx", "gy", None), P(None, "gx", "gy", None)),
        check_vma=False,
    )
```

```python
import functools

import jax
import jax.numpy as jnp
from jax import lax
from jax.experimental import pallas as pl
from jax.experimental.pallas import tpu as pltpu
from jax.sharding import PartitionSpec as P

RELAX_INNER = 8
RESIDUAL_STIFFNESS = 0.001
CENTER_VALUE = 1.0
HALF_WIDTH = 0.75
NORMAL_WEIGHT = 1.5
RELAX_RATE = 0.5 / RELAX_INNER
NORMAL_FLOOR = 0.05
OUTSIDE = 1.0 + RESIDUAL_STIFFNESS
F32 = jnp.float32


def weights():
    ratio = CENTER_VALUE / HALF_WIDTH
    rho = 1.0 / ratio
    found = []
    for _ in range(3):
        rho_next = 1.0 / (2.0 * ratio - rho)
        found.append((rho_next * rho, 2.0 * rho_next / HALF_WIDTH))
        rho = rho_next
    return found


def by_pairs(first, last, step):
    width = 2 if (last - first) % 2 == 0 else 1

    def turn(i, _):
        for part in range(width):
            step(first + width * i + part)
        return 0

    lax.fori_loop(0, (last - first) // width, turn, 0)


def soft_of(damage):
    return (1.0 - damage) ** 2 + RESIDUAL_STIFFNESS


def row_up(plane, beyond):
    rows = plane.shape[0]
    at = lax.broadcasted_iota(jnp.int32, plane.shape, 0)
    return jnp.where(at == rows - 1, beyond, pltpu.roll(plane, rows - 1, 0))


def row_down(plane, beyond):
    at = lax.broadcasted_iota(jnp.int32, plane.shape, 0)
    return jnp.where(at == 0, beyond, pltpu.roll(plane, 1, 0))


def lane_up(plane, beyond):
    cells = plane.shape[1]
    at = lax.broadcasted_iota(jnp.int32, plane.shape, 1)
    return jnp.where(at == cells - 1, beyond, pltpu.roll(plane, cells - 1, 1))


def lane_down(plane, beyond):
    at = lax.broadcasted_iota(jnp.int32, plane.shape, 1)
    return jnp.where(at == 0, beyond, pltpu.roll(plane, 1, 1))


def mu_inverse(ex, ey, ez):
    return 1.0 / (2.0 + (ex * ex + ey * ey + ez * ez))


def lam_inverse(center, total):
    return 1.0 / (0.5 + 0.125 * (6.0 * center + total))


HALO = 4
X_DAMAGE, X_PULL, X_MU, X_SOURCE, X_SLOTS = 0, 3, 9, 11, 17
LATE_DAMAGE, LATE_PULL, LATE_MU, LATE_SOURCE, LATE_SLOTS = 0, 1, 2, 3, 6
Y_HALO = (2, 1, 1, 1, 0, 1, 1, 1)
Y_KNOWN, Y_FIELDS = 8, 12
CORNER_ROWS = sum(Y_HALO) + 4
MORE_ROWS = 12


def edge_row(s, ny, depth):
    return depth if s == 0 else ny - 1 - depth


def known_of(s, damages, pulls, behind_pull, mus, sources, behind):
    planes = damages[0].shape[0]
    (c1, c2), _, _ = weights()
    soft = [soft_of(part) for part in damages]
    less = damages[0] - 1.0
    wx, wy, wz = (less * pull for pull in pulls)
    wy_behind = (damages[1] - 1.0) * behind_pull

    def across(value):
        return pltpu.roll(value, planes - 1, 0), pltpu.roll(value, 1, 0)

    def along(value, fill):
        return lane_up(value, fill), lane_down(value, fill)

    total = soft[0] + soft[2] + sum(across(soft[1])) + sum(along(soft[1], OUTSIDE))
    inverse = lam_inverse(soft[1], total)
    face = 0.125 * (soft[0] + soft[1])
    scale = 0.25 * mu_inverse(*pulls)
    known = [(1.0 + c1) * mus[0] + c2 * scale * (mus[1] + sum(across(mus[0])) + sum(along(mus[0], 0.0)))]
    x_up, x_down = across(wx * mus[0])
    z_up, z_down = along(wz * mus[0], 0.0)
    y_behind = wy_behind * mus[1]
    transfers = (x_up - x_down, y_behind if s == 0 else -y_behind, z_up - z_down)
    for c in range(3):
        known.append((1.0 + c1) * sources[c] + c2 * (face * (inverse * behind[c]) + transfers[c]))
    return scale, wy, known


def put_rows(s, put, damage, strain, seed_damage, seed_disp):
    ny = damage.shape[1]
    first, second, third = (edge_row(s, ny, depth) for depth in range(3))
    damages = [damage[:, row, :] for row in (first, second, third)]
    pulls = [strain[c, :, first, :] for c in range(3)]
    pulls_behind = [strain[c, :, second, :] for c in range(3)]
    mus = [
        seed_damage[:, first, :] * mu_inverse(*pulls),
        seed_damage[:, second, :] * mu_inverse(*pulls_behind),
    ]
    sources = [seed_disp[c, :, first, :] for c in range(3)]
    behind = [seed_disp[c, :, second, :] for c in range(3)]
    scale, wy, known = known_of(s, damages, pulls, pulls_behind[1], mus, sources, behind)
    for slot, value in enumerate(damages[:2] + [wy, mus[0], scale] + sources + known):
        put(slot, value)


def even(axis):
    return lax.rem(lax.axis_index(axis), 2) == 0


def faces_kernel(
    damage_in, strain_in, seed_in, sources_in, pal_out, other_out, near_out, near_late_out, far_out, far_late_out,
    damage, strain, seed_damage, seed_disp, pal, other, near, near_late, far, far_late, sems, out_sems,
):
    nx = damage.shape[0]
    copies = [
        pltpu.make_async_copy(damage_in, damage, sems.at[0]),
        pltpu.make_async_copy(strain_in, strain, sems.at[1]),
        pltpu.make_async_copy(seed_in, seed_damage, sems.at[2]),
        pltpu.make_async_copy(sources_in, seed_disp, sems.at[3]),
    ]
    for copy in copies:
        copy.start()
    sent = []

    def send(source, target):
        sent.append(pltpu.make_async_copy(source, target, out_sems.at[len(sent)]))
        sent[-1].start()

    def put_planes(out, late, high):
        for depth in range(4):
            at = jnp.where(high, nx - 1 - depth, depth)
            if depth == 3:
                late[LATE_DAMAGE] = damage[at]
                continue
            out[X_DAMAGE + depth] = damage[at]
            pulls = [strain[c, at] for c in range(3)]
            mu = seed_damage[at] * mu_inverse(*pulls)
            if depth == 2:
                late[LATE_PULL] = pulls[0]
                late[LATE_MU] = mu
            else:
                out[X_MU + depth] = mu
            for c in range(3):
                if depth == 2:
                    late[LATE_SOURCE + c] = seed_disp[c, at]
                else:
                    out[X_PULL + 2 * c + depth] = pulls[c]
                    out[X_SOURCE + 2 * c + depth] = seed_disp[c, at]

    for copy in copies:
        copy.wait()
    for out, target, first in ((pal, pal_out, True), (other, other_out, False)):

        def put(slot, value):
            out[slot * nx : (slot + 1) * nx, :] = value

        for s in range(2):

            @pl.when(even("gy") == ((s == 1) == first))
            def _():
                put_rows(s, put, damage, strain, seed_damage, seed_disp)

        send(out, target)
    for out, late, target, late_target, high in (
        (near, near_late, near_out, near_late_out, even("gx")),
        (far, far_late, far_out, far_late_out, ~even("gx")),
    ):
        put_planes(out, late, high)
        send(out, target)
        send(late, late_target)
    for copy in sent:
        copy.wait()


def received_x(near, far, side):
    from_near = even("gx") == (side == 1)

    def plane(slot, row=None):
        at = slot if row is None else (slice(slot, slot + 1), row)
        return jnp.where(from_near, near[at], far[at])

    return plane


def received_y(pal, other, side):
    from_pal = even("gy") == (side == 1)
    return lambda first, count: jnp.where(from_pal, pal[first : first + count, :], other[first : first + count, :])


def deal(pal, other, low, high):
    first = even("gy")
    low, high = low[...], high[...]
    pal[...] = jnp.where(first, high, low)
    other[...] = jnp.where(first, low, high)


def corners_kernel(
    damage, strain, seed_damage, seed_disp, near, far, _, pal, other, field, low, high, more
):
    nx, ny, _ = damage.shape
    for s, out in enumerate((low, high)):
        first, second, third = (edge_row(s, ny, depth) for depth in range(3))
        for side in range(2):
            x_in = received_x(near, far, side)
            ours = slice(3, 8) if side == 0 else slice(0, 5)
            planes = slice(0, 5) if side == 0 else slice(nx - 5, nx)

            def put_x(slot, first, count, row):
                for far_off in range(count):
                    at = 2 - far_off if side == 0 else 5 + far_off
                    field[slot, at : at + 1, :] = x_in(first + far_off, row)

            for depth, row in enumerate((first, second, third)):
                field[depth, ours, :] = damage[planes, row, :]
                put_x(depth, X_DAMAGE, 3, row)
            for depth, row in enumerate((first, second)):
                pulls = [strain[c, planes, row, :] for c in range(3)]
                for c in range(3):
                    if depth == 0:
                        field[3 + c, ours, :] = pulls[c]
                        put_x(3 + c, X_PULL + 2 * c, 2, row)
                    field[9 + 3 * depth + c, ours, :] = seed_disp[c, planes, row, :]
                    put_x(9 + 3 * depth + c, X_SOURCE + 2 * c, 2, row)
                if depth == 1:
                    field[6, ours, :] = pulls[1]
                    put_x(6, X_PULL + 2, 2, row)
                field[7 + depth, ours, :] = seed_damage[planes, row, :] * mu_inverse(*pulls)
                put_x(7 + depth, X_MU, 2, row)
            got = [field[slot] for slot in range(15)]
            scale, wy, known = known_of(s, got[:3], got[3:6], got[6], got[7:9], got[9:12], got[12:15])
            row = side * CORNER_ROWS
            for slot, value in enumerate(got[:2] + [wy, got[7], scale] + got[9:12]):
                count = Y_HALO[slot]
                behind = 2 - count if side == 0 else 5 + count
                more[side, slot : slot + 1, :] = value[behind : behind + 1, :]
                if count == 0:
                    continue
                start = 3 - count if side == 0 else 5
                out[row : row + count, :] = value[start : start + count, :]
                row += count
            for slot, value in enumerate(known):
                edge, behind = (3, 2) if side == 0 else (4, 5)
                out[row : row + 1, :] = value[edge : edge + 1, :]
                slot += Y_KNOWN
                more[side, slot : slot + 1, :] = value[behind : behind + 1, :]
                row += 1
        out[2 * CORNER_ROWS :, :] = jnp.where(even("gx"), more[0], more[1])
    deal(pal, other, low, high)


def in_grid():
    here = lax.axis_index("gx")
    return here > 0, here < lax.axis_size("gx") - 1


def prepare(first, last, soft, pull, raw, g, k, state0):
    planes, ny, nz = soft.shape
    inside = in_grid()
    lane = lax.broadcasted_iota(jnp.int32, (ny, nz), 1)
    row = lax.broadcasted_iota(jnp.int32, (ny, nz), 0)
    inner = (row > 0) & (row < ny - 1)

    def step(at):
        center = soft[at]
        sides = [
            soft[at + 1],
            soft[at - 1],
            pltpu.roll(center, ny - 1, 0),
            pltpu.roll(center, 1, 0),
            lane_up(center, OUTSIDE),
            lane_down(center, OUTSIDE),
        ]
        outside = ((at < HALO) & ~inside[0]) | ((at >= planes - HALO) & ~inside[1])
        inverse = jnp.where(inner & ~outside, lam_inverse(center, sum(sides)), 0.0)
        eighth = 0.125 * inverse
        for j in range(6):
            face = eighth * (center + sides[j])
            if j == 4:
                face = jnp.where(lane == nz - 1, 0.0, face)
            if j == 5:
                face = jnp.where(lane == 0, 0.0, face)
            g[j, at] = face
        k[0, at] = inverse * pull[0, at + 1]
        k[1, at] = -inverse * pull[0, at - 1]
        k[2, at] = inverse * pltpu.roll(pull[1, at], ny - 1, 0)
        k[3, at] = -inverse * pltpu.roll(pull[1, at], 1, 0)
        k[4, at] = inverse * lane_up(pull[2, at], 0.0)
        k[5, at] = -inverse * lane_down(pull[2, at], 0.0)
        for c in range(3):
            state0[1 + c, at] = inverse * raw[c, at]

    by_pairs(first, last, step)


def reach_of(grad, count):
    square = sum(part * part for part in grad)
    scale = 1.0 / jnp.maximum(square, NORMAL_FLOOR)
    power = 1.0 - RELAX_RATE * (1.0 + NORMAL_WEIGHT * square * scale)
    series = 1.0 + power
    for _ in range(2):
        power = power * power
        series = series * (1.0 + power)
    power = power * power
    repeats = jnp.ones_like(power)
    for level in range(1, 4):
        repeats = jnp.where(count > level, 1.0 + power * repeats, repeats)
    return (RELAX_RATE * NORMAL_WEIGHT * scale) * (series * repeats)


def slopes(first, last, count, less, grads):
    ny = less.shape[1]

    def step(at):
        own = less[at]
        grad = [
            0.5 * (less[at + 1] - less[at - 1]),
            0.5 * (pltpu.roll(own, ny - 1, 0) - pltpu.roll(own, 1, 0)),
            0.5 * (lane_up(own, -1.0) - lane_down(own, -1.0)),
        ]
        for c in range(3):
            grads[c, at - HALO] = grad[c]
        grads[3, at - HALO] = reach_of(grad, count)

    by_pairs(first, last, step)


def first_sweep(ranges, state0, state1, g, k, mu_scale):
    (c1, c2), _, _ = weights()

    def advance(at, f, own, moved):
        state1[f, at] = (1.0 + c1) * own + c2 * moved

    for first, last in ranges:
        sweep(first, last, state0, g, k, mu_scale, None, advance)


def inner_kernel(
    damage, strain, seed_damage, seed_disp, less, soft, pull, mu_scale, raw, g, k, state0, state1
):
    nx = damage.shape[0]

    def fill(i, _):
        at = HALO + i
        own = damage[i]
        sx, sy, sz = strain[0, i], strain[1, i], strain[2, i]
        soft[at] = soft_of(own)
        own = own - 1.0
        less[at] = own
        pull[0, at] = own * sx
        pull[1, at] = own * sy
        pull[2, at] = own * sz
        mu_inv = mu_inverse(sx, sy, sz)
        mu_scale[at] = 0.25 * mu_inv
        state0[0, at] = mu_inv * seed_damage[i]
        for c in range(3):
            raw[c, at] = seed_disp[c, i]
        return 0

    lax.fori_loop(0, nx, fill, 0)
    low, high = HALO, HALO + nx
    prepare(low + 1, high - 1, soft, pull, raw, g, k, state0)
    first_sweep([(low + 2, high - 2)], state0, state1, g, k, mu_scale)


def sides_kernel(
    work, near, near_late, far, far_late,
    less_in, soft_in, pull_in, scale_in, raw_in, g_in, k_in, state0_in, state1_in,
    less, soft, pull, mu_scale, raw, g, k, state0, state1, grads,
):
    nx = soft.shape[0] - 2 * HALO
    low, high = HALO, HALO + nx
    inside = in_grid()
    for s in range(2):
        x_in, late = received_x(near, far, s), received_x(near_late, far_late, s)
        for depth in range(4):
            at = low - 1 - depth if s == 0 else high + depth
            own = late(LATE_DAMAGE) if depth == 3 else x_in(X_DAMAGE + depth)
            soft[at] = soft_of(own)
            if depth == 3:
                continue
            own = own - 1.0
            if depth == 0:
                less[at] = own
            if depth == 2:
                pull[0, at] = own * late(LATE_PULL)
                state0[0, at] = late(LATE_MU)
            else:
                pulls = [x_in(X_PULL + 2 * c + depth) for c in range(3)]
                mu_scale[at] = jnp.where(inside[s], 0.25 * mu_inverse(*pulls), 0.0)
                state0[0, at] = x_in(X_MU + depth)
            for c in range(3):
                if depth == 2:
                    raw[c, at] = late(LATE_SOURCE + c)
                else:
                    pull[c, at] = own * pulls[c]
                    raw[c, at] = x_in(X_SOURCE + 2 * c + depth)

    for first, last in ((low - 3, low + 1), (high - 1, high + 3)):
        prepare(first, last, soft, pull, raw, g, k, state0)
    slopes(low, high, work[0, 0], less, grads)
    first_sweep([(low - 2, low + 2), (high - 2, high + 2)], state0, state1, g, k, mu_scale)


def edges_kernel(
    soft, pull, mu_scale, raw, g, state0, state1, y_pal, y_other, c_pal, c_other,
    sent_pal, sent_other, sent_near, coefficients, firsts, seconds, outer,
    field, sent_low, sent_high, x_low, x_high,
):
    planes, ny, nz = soft.shape
    nx = planes - 2 * HALO
    (c1, c2), (d1, d2), _ = weights()
    lane = lax.broadcasted_iota(jnp.int32, (planes, nz), 1)
    plane = lax.broadcasted_iota(jnp.int32, (planes, nz), 0)
    here, there = lax.axis_index("gx"), lax.axis_index("gy")
    in_x = ((plane >= HALO) | (here > 0)) & ((plane < HALO + nx) | (here < lax.axis_size("gx") - 1))
    in_y = (there > 0, there < lax.axis_size("gy") - 1)

    def around_x(value):
        return [pltpu.roll(value, planes - 1, 0), pltpu.roll(value, 1, 0)]

    def around_z(value, fill):
        return [lane_up(value, fill), lane_down(value, fill)]

    for s, sent in enumerate((sent_low, sent_high)):
        y_in, c_in = received_y(y_pal, y_other, s), received_y(c_pal, c_other, s)
        e0, e1 = edge_row(s, ny, 0), edge_row(s, ny, 1)

        def ordered(inward, outward):
            return [inward, outward] if s == 0 else [outward, inward]

        row = 0
        for f in range(Y_FIELDS):
            field[f, HALO : HALO + nx, :] = y_in(f * nx, nx)
            count, shift = (Y_HALO[f], 0) if f < Y_KNOWN else (1, 1)
            behind = HALO - count - 1 + shift
            for at in (behind, planes - 1 - behind):
                field[f, at : at + 1, :] = c_in(2 * CORNER_ROWS + f, 1)
            if count == 0:
                continue
            field[f, HALO - count + shift : HALO + shift, :] = c_in(row, count)
            high = HALO + nx - shift
            field[f, high : high + count, :] = c_in(CORNER_ROWS + row, count)
            row += count

        soft_1, soft_2 = soft_of(field[0]), soft_of(field[1])
        soft_e0, soft_e1 = soft[:, e0, :], soft[:, e1, :]

        def total(center, inward, outward):
            return sum(around_x(center) + [inward, outward] + around_z(center, OUTSIDE))

        inverse_1 = lam_inverse(soft_1, total(soft_1, soft_e0, soft_2))
        inverse_1 = jnp.where(in_x & in_y[s], inverse_1, 0.0)
        lam_1 = [inverse_1 * field[5 + c] for c in range(3)]
        inverse_e0 = jnp.where(in_x, lam_inverse(soft_e0, total(soft_e0, soft_e1, soft_1)), 0.0)
        lam_e0 = [inverse_e0 * raw[c, :, e0, :] for c in range(3)]
        mu_1, wy_1 = field[3], field[2]
        mu_e0, mu_e1 = state0[0, :, e0, :], state0[0, :, e1, :]
        lam_e1 = [state0[1 + c, :, e1, :] for c in range(3)]

        def coefficients_of(center, inverse, inward, outward, wx, wy, wz):
            sides = around_x(center) + ordered(inward, outward) + around_z(center, OUTSIDE)
            eighth = 0.125 * inverse
            faces = [eighth * (center + side) for side in sides]
            faces[4] = jnp.where(lane == nz - 1, 0.0, faces[4])
            faces[5] = jnp.where(lane == 0, 0.0, faces[5])
            pulls = around_x(wx) + wy + around_z(wz, 0.0)
            return faces, [inverse * w if j % 2 == 0 else -inverse * w for j, w in enumerate(pulls)]

        def moved_of(faces, pulls, scale, own, inward, outward):
            sides = [
                around_x(own[f]) + ordered(inward[f], outward[f]) + around_z(own[f], 0.0) for f in range(4)
            ]
            moved = [scale * sum(sides[0])]
            for c in range(3):
                part = sum(faces[j] * sides[1 + c][j] for j in range(6))
                moved.append(part + pulls[2 * c] * sides[0][2 * c] + pulls[2 * c + 1] * sides[0][2 * c + 1])
            return moved

        first_1 = [jnp.where(in_x, field[Y_KNOWN] + c2 * field[4] * mu_e0, 0.0)]
        sides = around_x(soft_1) + around_z(soft_1, OUTSIDE) + [soft_e0]
        faces = [0.125 * (soft_1 + side) for side in sides]
        wy_e0 = pull[1, :, e0, :] * mu_e0
        own_1 = [mu_1] + lam_1
        own_e0 = [mu_e0] + lam_e0
        for c in range(3):
            sides = around_x(lam_1[c]) + around_z(lam_1[c], 0.0) + [lam_e0[c]]
            lacked = sum(faces[j] * sides[j] for j in range(5))
            if c == 1:
                lacked += wy_e0 if s == 0 else -wy_e0
            first_1.append(inverse_1 * (field[Y_KNOWN + 1 + c] + c2 * lacked))

        scale_e0 = mu_scale[:, e0, :]
        wy = ordered(pull[1, :, e1, :], wy_1)
        faces, pulls = coefficients_of(
            soft_e0, inverse_e0, soft_e1, soft_1, pull[0, :, e0, :], wy, pull[2, :, e0, :]
        )
        moved = moved_of(faces, pulls, scale_e0, own_e0, [mu_e1] + lam_e1, own_1)
        first_e0 = [(1.0 + c1) * own_e0[f] + c2 * moved[f] for f in range(4)]

        outward_face = g[3 if s == 0 else 2, :, e1, :]
        first_e1 = [state1[0, :, e1, :]]
        for c in range(3):
            first_e1.append(state1[1 + c, :, e1, :] + c2 * outward_face * lam_e0[c])

        moved = moved_of(faces, pulls, scale_e0, first_e0, first_e1, first_1)
        for f in range(4):
            second = first_e0[f] + (d1 - d2) * (first_e0[f] - own_e0[f]) + d2 * moved[f]
            sent[f * nx : (f + 1) * nx, :] = second[HALO : HALO + nx, :]
            x_low[4 * s + f : 4 * s + f + 1, :] = second[HALO : HALO + 1, :]
            x_high[4 * s + f : 4 * s + f + 1, :] = second[HALO + nx - 1 : HALO + nx, :]
            firsts[s, f] = first_e0[f]
            outer[s, f] = first_1[f]
        for j in range(6):
            coefficients[s, j] = faces[j]
            coefficients[s, 6 + j] = pulls[j]
        for c in range(3):
            coefficients[s, 12 + c] = lam_e0[c]
            seconds[s, c] = first_e1[1 + c]
    deal(sent_pal, sent_other, sent_low, sent_high)
    sent_near[...] = jnp.where(even("gx"), x_high[...], x_low[...])


def sweep(first, last, state, g, k, mu_scale, rows, advance, finish=None):
    _, ny, nz = mu_scale.shape
    lane = lax.broadcasted_iota(jnp.int32, (ny, nz), 1)
    if rows is None:

        def rows(s, f, at):
            return 0.0

    def plane(at):
        def around(f):
            own = state[f, at]
            return own, [
                state[f, at + 1],
                state[f, at - 1],
                row_up(own, rows(1, f, at)),
                row_down(own, rows(0, f, at)),
                pltpu.roll(own, nz - 1, 1),
                pltpu.roll(own, 1, 1),
            ]

        mu, mu_sides = around(0)
        ends = [
            jnp.where(lane == nz - 1, 0.0, mu_sides[4]),
            jnp.where(lane == 0, 0.0, mu_sides[5]),
        ]
        results = [advance(at, 0, mu, mu_scale[at] * sum(mu_sides[:4] + ends))]
        faces = [g[j, at] for j in range(6)]
        for c in range(3):
            lam, lam_sides = around(1 + c)
            moved = sum(faces[j] * lam_sides[j] for j in range(6))
            moved += k[2 * c, at] * mu_sides[2 * c] + k[2 * c + 1, at] * mu_sides[2 * c + 1]
            results.append(advance(at, 1 + c, lam, moved))
        if finish is not None:
            finish(at - HALO, results)

    by_pairs(first, last, plane)


def wait_kernel(
    work, less, grads, y_pal, y_other,
    mu_scale, coefficients, firsts, seconds, outer, g_in, k_in, state0_in, state1_in,
    out_mu, out_lam, edges, g, k, state0, state1,
    state2, states,
):
    _, nx, ny, _ = grads.shape
    planes = nx + 2 * HALO
    _, (d1, d2), (c1, c2) = weights()
    held = slice(HALO - 2, HALO + nx + 2)
    for s in range(2):
        e0, e1 = edge_row(s, ny, 0), edge_row(s, ny, 1)
        for j in range(6):
            g[j, held, e0, :] = coefficients[s, j, held, :]
            k[j, held, e0, :] = coefficients[s, 6 + j, held, :]
        for c in range(3):
            state0[1 + c, held, e0, :] = coefficients[s, 12 + c, held, :]
            state1[1 + c, held, e1, :] = seconds[s, c, held, :]
        for f in range(4):
            state1[f, held, e0, :] = firsts[s, f, held, :]

    def rows(s, f, at):
        return outer[s, f, pl.ds(at, 1), :]

    def advance_2(at, f, own, moved):
        state2[f, at] = own + (d1 - d2) * (own - state0[f, at]) + d2 * moved

    sweep(HALO - 1, HALO + nx + 1, state1, g, k, mu_scale, rows, advance_2)
    nothing = jnp.zeros((1, state2.shape[3]), F32)
    at = jnp.where(even("gx"), HALO + nx, HALO - 1)
    for s in range(2):
        e0 = edge_row(s, ny, 0)
        for f in range(4):
            state2[f, at, e0 : e0 + 1, :] = nothing

    def advance_3(at, f, own, moved):
        return own + c1 * (own - state1[f, at]) + c2 * (state0[f, at] - own + moved)

    def finish(i, results):
        out_mu[i] = results[0]
        along = grads[3, i] * sum(grads[c, i] * results[1 + c] for c in range(3))
        for c in range(3):
            out_lam[c, i] = results[1 + c] - along * grads[c, i]
            states[c, i] = results[1 + c]

    sweep(HALO, HALO + nx, state2, g, k, mu_scale, None, advance_3, finish)

    for s in range(2):
        y_in = received_y(y_pal, y_other, s)
        e0, e1 = edge_row(s, ny, 0), edge_row(s, ny, 1)
        own = less[HALO : HALO + nx, e0, :]
        inward, outward = less[HALO : HALO + nx, e1, :], y_in(0, nx) - 1.0
        grad = [
            0.5 * (less[HALO + 1 : HALO + nx + 1, e0, :] - less[HALO - 1 : HALO + nx - 1, e0, :]),
            0.5 * (inward - outward if s == 0 else outward - inward),
            0.5 * (lane_up(own, -1.0) - lane_down(own, -1.0)),
        ]
        for c in range(3):
            edges[s, c] = grad[c]
            edges[s, 4 + c] = states[c, :, e0, :]
        edges[s, 3] = reach_of(grad, work[0, 0])


def last_kernel(
    mu_scale, coefficients, edges, y_pal, y_other, x_near, mu_in, lam_in,
    out_mu, out_lam, mu, lam,
    sems,
):
    nx, ny, nz = mu.shape
    inner = slice(HALO, HALO + nx)
    _, _, (_, c2) = weights()
    for s in range(2):
        y_in = received_y(y_pal, y_other, s)
        e0 = edge_row(s, ny, 0)
        outward = 3 if s == 0 else 2

        def got(f):
            return y_in(f * nx, nx)

        ends_x = []
        for side, at, way in ((0, HALO, 1), (1, HALO + nx - 1, 0)):
            got_x = jnp.where(even("gx") == (side == 1), x_near[4 * s : 4 * s + 4, :], 0.0)
            sides_x = [got_x[f : f + 1, :] for f in range(4)]
            face = c2 * coefficients[s, way, at : at + 1, :]
            end = [c2 * mu_scale[at, e0 : e0 + 1, :] * sides_x[0]] + [face * sides_x[1 + c] for c in range(3)]
            end[1] += c2 * coefficients[s, 6 + way, at : at + 1, :] * sides_x[0]
            ends_x.append(end)
        plane = lax.broadcasted_iota(jnp.int32, (nx, nz), 0)

        def from_x(f):
            return jnp.where(plane == 0, ends_x[0][f], jnp.where(plane == nx - 1, ends_x[1][f], 0.0))

        mu[:, e0, :] = mu[:, e0, :] + c2 * mu_scale[inner, e0, :] * got(0) + from_x(0)
        face = c2 * coefficients[s, outward, inner, :]
        ends = []
        for c in range(3):
            end = edges[s, 4 + c] + face * got(1 + c) + from_x(1 + c)
            if c == 1:
                end += c2 * coefficients[s, 6 + outward, inner, :] * got(0)
            ends.append(end)
        along = edges[s, 3] * sum(edges[s, c] * ends[c] for c in range(3))
        for c in range(3):
            lam[c, :, e0, :] = ends[c] - along * edges[s, c]
    copies = [
        pltpu.make_async_copy(mu, out_mu, sems.at[0]),
        pltpu.make_async_copy(lam, out_lam, sems.at[1]),
    ]
    for copy in copies:
        copy.start()
    for copy in copies:
        copy.wait()


VMEM = pl.BlockSpec(memory_space=pltpu.VMEM)
SMEM = pl.BlockSpec(memory_space=pltpu.SMEM)
HBM = pl.BlockSpec(memory_space=pltpu.HBM)
ANY = pl.BlockSpec(memory_space=pl.ANY)
MIB = 1024 * 1024


def call(kernel, ins, outs, scratch=(), in_specs=None, out_specs=None, aliases=None, grant=24 * MIB):
    return pl.pallas_call(
        kernel,
        out_shape=[jax.ShapeDtypeStruct(shape, F32) for shape in outs],
        in_specs=in_specs or [VMEM] * len(ins),
        out_specs=out_specs or [VMEM] * len(outs),
        scratch_shapes=[pltpu.VMEM(shape, F32) if isinstance(shape, tuple) else shape for shape in scratch],
        input_output_aliases=aliases or {},
        compiler_params=pltpu.CompilerParams(vmem_limit_bytes=grant),
    )(*ins)


def trade(value, axis, first):
    pairs = [(i, i + 1) for i in range(first, lax.axis_size(axis) - 1, 2)]
    return lax.ppermute(value, axis, pairs + [(j, i) for i, j in pairs])


def body(damage, strain, seed_damage, seed_disp, brick_work):
    nx, ny, nz = damage.shape
    plane = (ny, nz)
    brick = (nx,) + plane
    bricks = (3,) + brick
    framed = (nx + 2 * HALO,) + plane
    state = (4,) + framed
    row = (nx + 2 * HALO, nz)
    fields = (damage, strain, seed_damage, seed_disp)

    y_rows = (Y_FIELDS * nx, nz)
    x_faces = [(X_SLOTS,) + plane, (LATE_SLOTS,) + plane]
    faces = [y_rows] * 2 + x_faces * 2
    pal, other, near, near_late, far, far_late = call(
        faces_kernel, fields, faces,
        [brick, bricks, brick, bricks] + faces + [pltpu.SemaphoreType.DMA((4,)), pltpu.SemaphoreType.DMA((6,))],
        in_specs=[HBM] * 4, out_specs=[HBM] * 6, grant=56 * MIB,
    )
    y_in = (trade(pal, "gy", 0), trade(other, "gy", 1))
    far, far_late = trade(far, "gx", 1), trade(far_late, "gx", 1)
    near, near_late = trade(near, "gx", 0), trade(near_late, "gx", 0)
    inner = tuple(call(
        inner_kernel, fields,
        [framed, framed, (3,) + framed, framed, (3,) + framed, (6,) + framed, (6,) + framed, state, state],
    ))
    c_rows = (2 * CORNER_ROWS + MORE_ROWS, nz)
    pal, other = call(
        corners_kernel, fields + (near, far, inner[0]), [c_rows] * 2,
        [(15,) + plane, c_rows, c_rows, (2, MORE_ROWS, nz)], in_specs=[VMEM] * 6 + [ANY],
    )
    c_in = (trade(pal, "gy", 0), trade(other, "gy", 1))
    less, soft, pull, mu_scale, raw, g, k, state0, state1, grads = call(
        sides_kernel, (brick_work, near, near_late, far, far_late) + inner,
        [part.shape for part in inner] + [(4,) + brick],
        in_specs=[SMEM] + [VMEM] * 13, aliases={5 + part: part for part in range(9)},
    )
    sent = (4 * nx, nz)
    x_sent = (8, nz)
    pal, other, near, coefficients, firsts, seconds, outer = call(
        edges_kernel, (soft, pull, mu_scale, raw, g, state0, state1) + y_in + c_in,
        [sent] * 2 + [x_sent] + [(2, 15) + row, (2, 4) + row, (2, 3) + row, (2, 4) + row],
        [(Y_FIELDS,) + row, sent, sent, x_sent, x_sent],
    )
    halo = (trade(pal, "gy", 0), trade(other, "gy", 1), trade(near, "gx", 0))
    ins = (brick_work, less, grads) + y_in + (mu_scale, coefficients, firsts, seconds, outer, g, k, state0, state1)
    mu, lam, edges, *_ = call(
        wait_kernel, ins,
        [brick, bricks, (2, 7, nx, nz), (6,) + framed, (6,) + framed, state, state],
        [state, bricks],
        in_specs=[SMEM] + [VMEM] * (len(ins) - 1),
        aliases={10: 3, 11: 4, 12: 5, 13: 6},
    )
    out_mu, out_lam, *_ = call(
        last_kernel, (mu_scale, coefficients, edges) + halo + (mu, lam),
        [brick, bricks, brick, bricks], [pltpu.SemaphoreType.DMA((2,))],
        out_specs=[HBM, HBM, VMEM, VMEM], aliases={6: 2, 7: 3},
    )
    return out_mu, out_lam


def solution(mesh):
    placed = (
        P("gx", "gy", None),
        P(None, "gx", "gy", None),
        P("gx", "gy", None),
        P(None, "gx", "gy", None),
        P("gx", "gy"),
    )
    return jax.shard_map(
        body,
        mesh=mesh,
        in_specs=placed,
        out_specs=(P("gx", "gy", None), P(None, "gx", "gy", None)),
        check_vma=False,
    )
```

```python
import functools

import jax
import jax.numpy as jnp
from jax import lax
from jax.experimental import pallas as pl
from jax.experimental.pallas import tpu as pltpu
from jax.sharding import PartitionSpec as P

RELAX_INNER = 8
RESIDUAL_STIFFNESS = 0.001
CENTER_VALUE = 1.0
HALF_WIDTH = 0.75
NORMAL_WEIGHT = 1.5
RELAX_RATE = 0.5 / RELAX_INNER
NORMAL_FLOOR = 0.05
OUTSIDE = 1.0 + RESIDUAL_STIFFNESS
F32 = jnp.float32


def weights():
    ratio = CENTER_VALUE / HALF_WIDTH
    rho = 1.0 / ratio
    found = []
    for _ in range(3):
        rho_next = 1.0 / (2.0 * ratio - rho)
        found.append((rho_next * rho, 2.0 * rho_next / HALF_WIDTH))
        rho = rho_next
    return found


def by_pairs(first, last, step):
    width = 2 if (last - first) % 2 == 0 else 1

    def turn(i, _):
        for part in range(width):
            step(first + width * i + part)
        return 0

    lax.fori_loop(0, (last - first) // width, turn, 0)


def soft_of(damage):
    return (1.0 - damage) ** 2 + RESIDUAL_STIFFNESS


def row_up(plane, beyond):
    rows = plane.shape[0]
    at = lax.broadcasted_iota(jnp.int32, plane.shape, 0)
    return jnp.where(at == rows - 1, beyond, pltpu.roll(plane, rows - 1, 0))


def row_down(plane, beyond):
    at = lax.broadcasted_iota(jnp.int32, plane.shape, 0)
    return jnp.where(at == 0, beyond, pltpu.roll(plane, 1, 0))


def lane_up(plane, beyond):
    cells = plane.shape[1]
    at = lax.broadcasted_iota(jnp.int32, plane.shape, 1)
    return jnp.where(at == cells - 1, beyond, pltpu.roll(plane, cells - 1, 1))


def lane_down(plane, beyond):
    at = lax.broadcasted_iota(jnp.int32, plane.shape, 1)
    return jnp.where(at == 0, beyond, pltpu.roll(plane, 1, 1))


def mu_inverse(ex, ey, ez):
    return 1.0 / (2.0 + (ex * ex + ey * ey + ez * ez))


def lam_inverse(center, total):
    return 1.0 / (0.5 + 0.125 * (6.0 * center + total))


HALO = 4
X_DAMAGE, X_PULL, X_MU, X_SOURCE, X_SLOTS = 0, 3, 9, 11, 17
LATE_DAMAGE, LATE_PULL, LATE_MU, LATE_SOURCE, LATE_SLOTS = 0, 1, 2, 3, 6
Y_HALO = (2, 1, 1, 1, 0, 1, 1, 1)
Y_KNOWN, Y_FIELDS = 8, 12
CORNER_ROWS = sum(Y_HALO) + 4
MORE_ROWS = 12


def edge_row(s, ny, depth):
    return depth if s == 0 else ny - 1 - depth


def known_of(s, damages, pulls, behind_pull, mus, sources, behind):
    planes = damages[0].shape[0]
    (c1, c2), _, _ = weights()
    soft = [soft_of(part) for part in damages]
    less = damages[0] - 1.0
    wx, wy, wz = (less * pull for pull in pulls)
    wy_behind = (damages[1] - 1.0) * behind_pull

    def across(value):
        return pltpu.roll(value, planes - 1, 0), pltpu.roll(value, 1, 0)

    def along(value, fill):
        return lane_up(value, fill), lane_down(value, fill)

    total = soft[0] + soft[2] + sum(across(soft[1])) + sum(along(soft[1], OUTSIDE))
    inverse = lam_inverse(soft[1], total)
    face = 0.125 * (soft[0] + soft[1])
    scale = 0.25 * mu_inverse(*pulls)
    known = [(1.0 + c1) * mus[0] + c2 * scale * (mus[1] + sum(across(mus[0])) + sum(along(mus[0], 0.0)))]
    x_up, x_down = across(wx * mus[0])
    z_up, z_down = along(wz * mus[0], 0.0)
    y_behind = wy_behind * mus[1]
    transfers = (x_up - x_down, y_behind if s == 0 else -y_behind, z_up - z_down)
    for c in range(3):
        known.append((1.0 + c1) * sources[c] + c2 * (face * (inverse * behind[c]) + transfers[c]))
    return scale, wy, known


def put_rows(s, put, damage, strain, seed_damage, seed_disp):
    ny = damage.shape[1]
    first, second, third = (edge_row(s, ny, depth) for depth in range(3))
    damages = [damage[:, row, :] for row in (first, second, third)]
    pulls = [strain[c, :, first, :] for c in range(3)]
    pulls_behind = [strain[c, :, second, :] for c in range(3)]
    mus = [
        seed_damage[:, first, :] * mu_inverse(*pulls),
        seed_damage[:, second, :] * mu_inverse(*pulls_behind),
    ]
    sources = [seed_disp[c, :, first, :] for c in range(3)]
    behind = [seed_disp[c, :, second, :] for c in range(3)]
    scale, wy, known = known_of(s, damages, pulls, pulls_behind[1], mus, sources, behind)
    for slot, value in enumerate(damages[:2] + [wy, mus[0], scale] + sources + known):
        put(slot, value)


def even(axis):
    return lax.rem(lax.axis_index(axis), 2) == 0


def faces_kernel(
    damage_in, strain_in, seed_in, sources_in, pal_out, other_out, near_out, near_late_out, far_out, far_late_out,
    damage, strain, seed_damage, seed_disp, pal, other, near, near_late, far, far_late, sems, out_sems,
):
    nx = damage.shape[0]
    copies = [
        pltpu.make_async_copy(damage_in, damage, sems.at[0]),
        pltpu.make_async_copy(strain_in, strain, sems.at[1]),
        pltpu.make_async_copy(seed_in, seed_damage, sems.at[2]),
        pltpu.make_async_copy(sources_in, seed_disp, sems.at[3]),
    ]
    for copy in copies:
        copy.start()
    sent = []

    def send(source, target):
        sent.append(pltpu.make_async_copy(source, target, out_sems.at[len(sent)]))
        sent[-1].start()

    def put_planes(out, late, high):
        for depth in range(4):
            at = jnp.where(high, nx - 1 - depth, depth)
            if depth == 3:
                late[LATE_DAMAGE] = damage[at]
                continue
            out[X_DAMAGE + depth] = damage[at]
            pulls = [strain[c, at] for c in range(3)]
            mu = seed_damage[at] * mu_inverse(*pulls)
            if depth == 2:
                late[LATE_PULL] = pulls[0]
                late[LATE_MU] = mu
            else:
                out[X_MU + depth] = mu
            for c in range(3):
                if depth == 2:
                    late[LATE_SOURCE + c] = seed_disp[c, at]
                else:
                    out[X_PULL + 2 * c + depth] = pulls[c]
                    out[X_SOURCE + 2 * c + depth] = seed_disp[c, at]

    for copy in copies:
        copy.wait()
    for out, target, first in ((pal, pal_out, True), (other, other_out, False)):

        def put(slot, value):
            out[slot * nx : (slot + 1) * nx, :] = value

        for s in range(2):

            @pl.when(even("gy") == ((s == 1) == first))
            def _():
                put_rows(s, put, damage, strain, seed_damage, seed_disp)

        send(out, target)
    for out, late, target, late_target, high in (
        (near, near_late, near_out, near_late_out, even("gx")),
        (far, far_late, far_out, far_late_out, ~even("gx")),
    ):
        put_planes(out, late, high)
        send(out, target)
        send(late, late_target)
    for copy in sent:
        copy.wait()


def received_x(near, far, side):
    from_near = even("gx") == (side == 1)

    def plane(slot, row=None):
        at = slot if row is None else (slice(slot, slot + 1), row)
        return jnp.where(from_near, near[at], far[at])

    return plane


def received_y(pal, other, side):
    from_pal = even("gy") == (side == 1)
    return lambda first, count: jnp.where(from_pal, pal[first : first + count, :], other[first : first + count, :])


def deal(pal, other, low, high):
    first = even("gy")
    low, high = low[...], high[...]
    pal[...] = jnp.where(first, high, low)
    other[...] = jnp.where(first, low, high)


def corners_kernel(
    damage, strain, seed_damage, seed_disp, near, far, _, pal, other, fields, low, high, more
):
    nx, ny, _ = damage.shape
    for s, out in enumerate((low, high)):
        first, second, third = (edge_row(s, ny, depth) for depth in range(3))
        for side in range(2):
            field = fields.at[2 * s + side]
            x_in = received_x(near, far, side)
            ours = slice(3, 8) if side == 0 else slice(0, 5)
            planes = slice(0, 5) if side == 0 else slice(nx - 5, nx)

            def put_x(slot, first, count, row):
                for far_off in range(count):
                    at = 2 - far_off if side == 0 else 5 + far_off
                    field[slot, at : at + 1, :] = x_in(first + far_off, row)

            for depth, row in enumerate((first, second, third)):
                field[depth, ours, :] = damage[planes, row, :]
                put_x(depth, X_DAMAGE, 3, row)
            for depth, row in enumerate((first, second)):
                pulls = [strain[c, planes, row, :] for c in range(3)]
                for c in range(3):
                    if depth == 0:
                        field[3 + c, ours, :] = pulls[c]
                        put_x(3 + c, X_PULL + 2 * c, 2, row)
                    field[9 + 3 * depth + c, ours, :] = seed_disp[c, planes, row, :]
                    put_x(9 + 3 * depth + c, X_SOURCE + 2 * c, 2, row)
                if depth == 1:
                    field[6, ours, :] = pulls[1]
                    put_x(6, X_PULL + 2, 2, row)
                field[7 + depth, ours, :] = seed_damage[planes, row, :] * mu_inverse(*pulls)
                put_x(7 + depth, X_MU, 2, row)
            got = [field[slot] for slot in range(15)]
            scale, wy, known = known_of(s, got[:3], got[3:6], got[6], got[7:9], got[9:12], got[12:15])
            row = side * CORNER_ROWS
            for slot, value in enumerate(got[:2] + [wy, got[7], scale] + got[9:12]):
                count = Y_HALO[slot]
                behind = 2 - count if side == 0 else 5 + count
                more[s, side, slot : slot + 1, :] = value[behind : behind + 1, :]
                if count == 0:
                    continue
                start = 3 - count if side == 0 else 5
                out[row : row + count, :] = value[start : start + count, :]
                row += count
            for slot, value in enumerate(known):
                edge, behind = (3, 2) if side == 0 else (4, 5)
                out[row : row + 1, :] = value[edge : edge + 1, :]
                slot += Y_KNOWN
                more[s, side, slot : slot + 1, :] = value[behind : behind + 1, :]
                row += 1
        out[2 * CORNER_ROWS :, :] = jnp.where(even("gx"), more[s, 0], more[s, 1])
    deal(pal, other, low, high)


def in_grid():
    here = lax.axis_index("gx")
    return here > 0, here < lax.axis_size("gx") - 1


def prepare(first, last, soft, pull, raw, g, k, state0):
    planes, ny, nz = soft.shape
    inside = in_grid()
    lane = lax.broadcasted_iota(jnp.int32, (ny, nz), 1)
    row = lax.broadcasted_iota(jnp.int32, (ny, nz), 0)
    inner = (row > 0) & (row < ny - 1)

    def step(at):
        center = soft[at]
        sides = [
            soft[at + 1],
            soft[at - 1],
            pltpu.roll(center, ny - 1, 0),
            pltpu.roll(center, 1, 0),
            lane_up(center, OUTSIDE),
            lane_down(center, OUTSIDE),
        ]
        outside = ((at < HALO) & ~inside[0]) | ((at >= planes - HALO) & ~inside[1])
        inverse = jnp.where(inner & ~outside, lam_inverse(center, sum(sides)), 0.0)
        eighth = 0.125 * inverse
        for j in range(6):
            face = eighth * (center + sides[j])
            if j == 4:
                face = jnp.where(lane == nz - 1, 0.0, face)
            if j == 5:
                face = jnp.where(lane == 0, 0.0, face)
            g[j, at] = face
        k[0, at] = inverse * pull[0, at + 1]
        k[1, at] = -inverse * pull[0, at - 1]
        k[2, at] = inverse * pltpu.roll(pull[1, at], ny - 1, 0)
        k[3, at] = -inverse * pltpu.roll(pull[1, at], 1, 0)
        k[4, at] = inverse * lane_up(pull[2, at], 0.0)
        k[5, at] = -inverse * lane_down(pull[2, at], 0.0)
        for c in range(3):
            state0[1 + c, at] = inverse * raw[c, at]

    by_pairs(first, last, step)


def reach_of(grad, count):
    square = sum(part * part for part in grad)
    scale = 1.0 / jnp.maximum(square, NORMAL_FLOOR)
    power = 1.0 - RELAX_RATE * (1.0 + NORMAL_WEIGHT * square * scale)
    series = 1.0 + power
    for _ in range(2):
        power = power * power
        series = series * (1.0 + power)
    power = power * power
    repeats = jnp.ones_like(power)
    for level in range(1, 4):
        repeats = jnp.where(count > level, 1.0 + power * repeats, repeats)
    return (RELAX_RATE * NORMAL_WEIGHT * scale) * (series * repeats)


def slopes(first, last, count, less, grads):
    ny = less.shape[1]

    def step(at):
        own = less[at]
        grad = [
            0.5 * (less[at + 1] - less[at - 1]),
            0.5 * (pltpu.roll(own, ny - 1, 0) - pltpu.roll(own, 1, 0)),
            0.5 * (lane_up(own, -1.0) - lane_down(own, -1.0)),
        ]
        for c in range(3):
            grads[c, at - HALO] = grad[c]
        grads[3, at - HALO] = reach_of(grad, count)

    by_pairs(first, last, step)


def first_sweep(ranges, state0, state1, g, k, mu_scale):
    (c1, c2), _, _ = weights()

    def advance(at, f, own, moved):
        state1[f, at] = (1.0 + c1) * own + c2 * moved

    for first, last in ranges:
        sweep(first, last, state0, g, k, mu_scale, None, advance)


def inner_kernel(
    damage, strain, seed_damage, seed_disp, less, soft, pull, mu_scale, raw, g, k, state0, state1
):
    nx = damage.shape[0]

    def fill(i, _):
        at = HALO + i
        own = damage[i]
        sx, sy, sz = strain[0, i], strain[1, i], strain[2, i]
        soft[at] = soft_of(own)
        own = own - 1.0
        less[at] = own
        pull[0, at] = own * sx
        pull[1, at] = own * sy
        pull[2, at] = own * sz
        mu_inv = mu_inverse(sx, sy, sz)
        mu_scale[at] = 0.25 * mu_inv
        state0[0, at] = mu_inv * seed_damage[i]
        for c in range(3):
            raw[c, at] = seed_disp[c, i]
        return 0

    lax.fori_loop(0, nx, fill, 0)
    low, high = HALO, HALO + nx
    prepare(low + 1, high - 1, soft, pull, raw, g, k, state0)
    first_sweep([(low + 2, high - 2)], state0, state1, g, k, mu_scale)


def sides_kernel(
    work, near, near_late, far, far_late,
    less_in, soft_in, pull_in, scale_in, raw_in, g_in, k_in, state0_in, state1_in,
    less, soft, pull, mu_scale, raw, g, k, state0, state1, grads,
):
    nx = soft.shape[0] - 2 * HALO
    low, high = HALO, HALO + nx
    inside = in_grid()
    for s in range(2):
        x_in, late = received_x(near, far, s), received_x(near_late, far_late, s)
        for depth in range(4):
            at = low - 1 - depth if s == 0 else high + depth
            own = late(LATE_DAMAGE) if depth == 3 else x_in(X_DAMAGE + depth)
            soft[at] = soft_of(own)
            if depth == 3:
                continue
            own = own - 1.0
            if depth == 0:
                less[at] = own
            if depth == 2:
                pull[0, at] = own * late(LATE_PULL)
                state0[0, at] = late(LATE_MU)
            else:
                pulls = [x_in(X_PULL + 2 * c + depth) for c in range(3)]
                mu_scale[at] = jnp.where(inside[s], 0.25 * mu_inverse(*pulls), 0.0)
                state0[0, at] = x_in(X_MU + depth)
            for c in range(3):
                if depth == 2:
                    raw[c, at] = late(LATE_SOURCE + c)
                else:
                    pull[c, at] = own * pulls[c]
                    raw[c, at] = x_in(X_SOURCE + 2 * c + depth)

    for first, last in ((low - 3, low + 1), (high - 1, high + 3)):
        prepare(first, last, soft, pull, raw, g, k, state0)
    slopes(low, high, work[0, 0], less, grads)
    first_sweep([(low - 2, low + 2), (high - 2, high + 2)], state0, state1, g, k, mu_scale)


def edges_kernel(
    soft, pull, mu_scale, raw, g, state0, state1, y_pal, y_other, c_pal, c_other,
    sent_pal, sent_other, sent_near, coefficients, firsts, seconds, outer,
    fields, sent_low, sent_high, x_low, x_high,
):
    planes, ny, nz = soft.shape
    nx = planes - 2 * HALO
    (c1, c2), (d1, d2), _ = weights()
    lane = lax.broadcasted_iota(jnp.int32, (planes, nz), 1)
    plane = lax.broadcasted_iota(jnp.int32, (planes, nz), 0)
    here, there = lax.axis_index("gx"), lax.axis_index("gy")
    in_x = ((plane >= HALO) | (here > 0)) & ((plane < HALO + nx) | (here < lax.axis_size("gx") - 1))
    in_y = (there > 0, there < lax.axis_size("gy") - 1)

    def around_x(value):
        return [pltpu.roll(value, planes - 1, 0), pltpu.roll(value, 1, 0)]

    def around_z(value, fill):
        return [lane_up(value, fill), lane_down(value, fill)]

    for s, sent in enumerate((sent_low, sent_high)):
        field = fields.at[s]
        y_in, c_in = received_y(y_pal, y_other, s), received_y(c_pal, c_other, s)
        e0, e1 = edge_row(s, ny, 0), edge_row(s, ny, 1)

        def ordered(inward, outward):
            return [inward, outward] if s == 0 else [outward, inward]

        row = 0
        for f in range(Y_FIELDS):
            field[f, HALO : HALO + nx, :] = y_in(f * nx, nx)
            count, shift = (Y_HALO[f], 0) if f < Y_KNOWN else (1, 1)
            behind = HALO - count - 1 + shift
            for at in (behind, planes - 1 - behind):
                field[f, at : at + 1, :] = c_in(2 * CORNER_ROWS + f, 1)
            if count == 0:
                continue
            field[f, HALO - count + shift : HALO + shift, :] = c_in(row, count)
            high = HALO + nx - shift
            field[f, high : high + count, :] = c_in(CORNER_ROWS + row, count)
            row += count

        soft_1, soft_2 = soft_of(field[0]), soft_of(field[1])
        soft_e0, soft_e1 = soft[:, e0, :], soft[:, e1, :]

        def total(center, inward, outward):
            return sum(around_x(center) + [inward, outward] + around_z(center, OUTSIDE))

        inverse_1 = lam_inverse(soft_1, total(soft_1, soft_e0, soft_2))
        inverse_1 = jnp.where(in_x & in_y[s], inverse_1, 0.0)
        lam_1 = [inverse_1 * field[5 + c] for c in range(3)]
        inverse_e0 = jnp.where(in_x, lam_inverse(soft_e0, total(soft_e0, soft_e1, soft_1)), 0.0)
        lam_e0 = [inverse_e0 * raw[c, :, e0, :] for c in range(3)]
        mu_1, wy_1 = field[3], field[2]
        mu_e0, mu_e1 = state0[0, :, e0, :], state0[0, :, e1, :]
        lam_e1 = [state0[1 + c, :, e1, :] for c in range(3)]

        def coefficients_of(center, inverse, inward, outward, wx, wy, wz):
            sides = around_x(center) + ordered(inward, outward) + around_z(center, OUTSIDE)
            eighth = 0.125 * inverse
            faces = [eighth * (center + side) for side in sides]
            faces[4] = jnp.where(lane == nz - 1, 0.0, faces[4])
            faces[5] = jnp.where(lane == 0, 0.0, faces[5])
            pulls = around_x(wx) + wy + around_z(wz, 0.0)
            return faces, [inverse * w if j % 2 == 0 else -inverse * w for j, w in enumerate(pulls)]

        def moved_of(faces, pulls, scale, own, inward, outward):
            sides = [
                around_x(own[f]) + ordered(inward[f], outward[f]) + around_z(own[f], 0.0) for f in range(4)
            ]
            moved = [scale * sum(sides[0])]
            for c in range(3):
                part = sum(faces[j] * sides[1 + c][j] for j in range(6))
                moved.append(part + pulls[2 * c] * sides[0][2 * c] + pulls[2 * c + 1] * sides[0][2 * c + 1])
            return moved

        first_1 = [jnp.where(in_x, field[Y_KNOWN] + c2 * field[4] * mu_e0, 0.0)]
        sides = around_x(soft_1) + around_z(soft_1, OUTSIDE) + [soft_e0]
        faces = [0.125 * (soft_1 + side) for side in sides]
        wy_e0 = pull[1, :, e0, :] * mu_e0
        own_1 = [mu_1] + lam_1
        own_e0 = [mu_e0] + lam_e0
        for c in range(3):
            sides = around_x(lam_1[c]) + around_z(lam_1[c], 0.0) + [lam_e0[c]]
            lacked = sum(faces[j] * sides[j] for j in range(5))
            if c == 1:
                lacked += wy_e0 if s == 0 else -wy_e0
            first_1.append(inverse_1 * (field[Y_KNOWN + 1 + c] + c2 * lacked))

        scale_e0 = mu_scale[:, e0, :]
        wy = ordered(pull[1, :, e1, :], wy_1)
        faces, pulls = coefficients_of(
            soft_e0, inverse_e0, soft_e1, soft_1, pull[0, :, e0, :], wy, pull[2, :, e0, :]
        )
        moved = moved_of(faces, pulls, scale_e0, own_e0, [mu_e1] + lam_e1, own_1)
        first_e0 = [(1.0 + c1) * own_e0[f] + c2 * moved[f] for f in range(4)]

        outward_face = g[3 if s == 0 else 2, :, e1, :]
        first_e1 = [state1[0, :, e1, :]]
        for c in range(3):
            first_e1.append(state1[1 + c, :, e1, :] + c2 * outward_face * lam_e0[c])

        moved = moved_of(faces, pulls, scale_e0, first_e0, first_e1, first_1)
        for f in range(4):
            second = first_e0[f] + (d1 - d2) * (first_e0[f] - own_e0[f]) + d2 * moved[f]
            sent[f * nx : (f + 1) * nx, :] = second[HALO : HALO + nx, :]
            x_low[4 * s + f : 4 * s + f + 1, :] = second[HALO : HALO + 1, :]
            x_high[4 * s + f : 4 * s + f + 1, :] = second[HALO + nx - 1 : HALO + nx, :]
            firsts[s, f] = first_e0[f]
            outer[s, f] = first_1[f]
        for j in range(6):
            coefficients[s, j] = faces[j]
            coefficients[s, 6 + j] = pulls[j]
        for c in range(3):
            coefficients[s, 12 + c] = lam_e0[c]
            seconds[s, c] = first_e1[1 + c]
    deal(sent_pal, sent_other, sent_low, sent_high)
    sent_near[...] = jnp.where(even("gx"), x_high[...], x_low[...])


def sweep(first, last, state, g, k, mu_scale, rows, advance, finish=None):
    _, ny, nz = mu_scale.shape
    lane = lax.broadcasted_iota(jnp.int32, (ny, nz), 1)
    if rows is None:

        def rows(s, f, at):
            return 0.0

    def plane(at):
        def around(f):
            own = state[f, at]
            return own, [
                state[f, at + 1],
                state[f, at - 1],
                row_up(own, rows(1, f, at)),
                row_down(own, rows(0, f, at)),
                pltpu.roll(own, nz - 1, 1),
                pltpu.roll(own, 1, 1),
            ]

        mu, mu_sides = around(0)
        ends = [
            jnp.where(lane == nz - 1, 0.0, mu_sides[4]),
            jnp.where(lane == 0, 0.0, mu_sides[5]),
        ]
        results = [advance(at, 0, mu, mu_scale[at] * sum(mu_sides[:4] + ends))]
        faces = [g[j, at] for j in range(6)]
        for c in range(3):
            lam, lam_sides = around(1 + c)
            moved = sum(faces[j] * lam_sides[j] for j in range(6))
            moved += k[2 * c, at] * mu_sides[2 * c] + k[2 * c + 1, at] * mu_sides[2 * c + 1]
            results.append(advance(at, 1 + c, lam, moved))
        if finish is not None:
            finish(at - HALO, results)

    by_pairs(first, last, plane)


def wait_kernel(
    work, less, grads, y_pal, y_other,
    mu_scale, coefficients, firsts, seconds, outer, g_in, k_in, state0_in, state1_in,
    out_mu, out_lam, edges, g, k, state0, state1,
    state2, states, mu, lam, sems,
):
    _, nx, ny, _ = grads.shape
    planes = nx + 2 * HALO
    _, (d1, d2), (c1, c2) = weights()
    held = slice(HALO - 2, HALO + nx + 2)
    for s in range(2):
        e0, e1 = edge_row(s, ny, 0), edge_row(s, ny, 1)
        for j in range(6):
            g[j, held, e0, :] = coefficients[s, j, held, :]
            k[j, held, e0, :] = coefficients[s, 6 + j, held, :]
        for c in range(3):
            state0[1 + c, held, e0, :] = coefficients[s, 12 + c, held, :]
            state1[1 + c, held, e1, :] = seconds[s, c, held, :]
        for f in range(4):
            state1[f, held, e0, :] = firsts[s, f, held, :]

    def rows(s, f, at):
        return outer[s, f, pl.ds(at, 1), :]

    def advance_2(at, f, own, moved):
        state2[f, at] = own + (d1 - d2) * (own - state0[f, at]) + d2 * moved

    sweep(HALO - 1, HALO + nx + 1, state1, g, k, mu_scale, rows, advance_2)
    nothing = jnp.zeros((1, state2.shape[3]), F32)
    at = jnp.where(even("gx"), HALO + nx, HALO - 1)
    for s in range(2):
        e0 = edge_row(s, ny, 0)
        for f in range(4):
            state2[f, at, e0 : e0 + 1, :] = nothing

    def advance_3(at, f, own, moved):
        return own + c1 * (own - state1[f, at]) + c2 * (state0[f, at] - own + moved)

    def copies(i):
        return (
            pltpu.make_async_copy(mu.at[i], out_mu.at[i], sems.at[0, i]),
            pltpu.make_async_copy(lam.at[:, i], out_lam.at[:, i], sems.at[1, i]),
        )

    def finish(i, results):
        mu[i] = results[0]
        along = grads[3, i] * sum(grads[c, i] * results[1 + c] for c in range(3))
        for c in range(3):
            lam[c, i] = results[1 + c] - along * grads[c, i]
            states[c, i] = results[1 + c]
        for copy in copies(i):
            copy.start()

    sweep(HALO, HALO + nx, state2, g, k, mu_scale, None, advance_3, finish)

    for s in range(2):
        y_in = received_y(y_pal, y_other, s)
        e0, e1 = edge_row(s, ny, 0), edge_row(s, ny, 1)
        own = less[HALO : HALO + nx, e0, :]
        inward, outward = less[HALO : HALO + nx, e1, :], y_in(0, nx) - 1.0
        grad = [
            0.5 * (less[HALO + 1 : HALO + nx + 1, e0, :] - less[HALO - 1 : HALO + nx - 1, e0, :]),
            0.5 * (inward - outward if s == 0 else outward - inward),
            0.5 * (lane_up(own, -1.0) - lane_down(own, -1.0)),
        ]
        for c in range(3):
            edges[s, c] = grad[c]
            edges[s, 4 + c] = states[c, :, e0, :]
        edges[s, 3] = reach_of(grad, work[0, 0])
        edges[s, 7] = mu[:, e0, :]

    def settle(i, _):
        for copy in copies(i):
            copy.wait()
        return 0

    lax.fori_loop(0, nx, settle, 0)


def last_kernel(
    mu_scale, coefficients, edges, y_pal, y_other, x_near, mu_in, lam_in,
    out_mu, out_lam,
    rows, sems,
):
    nx, ny, nz = out_mu.shape
    inner = slice(HALO, HALO + nx)
    copies = []
    _, _, (_, c2) = weights()
    for s in range(2):
        y_in = received_y(y_pal, y_other, s)
        e0 = edge_row(s, ny, 0)
        outward = 3 if s == 0 else 2

        def got(f):
            return y_in(f * nx, nx)

        ends_x = []
        for side, at, way in ((0, HALO, 1), (1, HALO + nx - 1, 0)):
            got_x = jnp.where(even("gx") == (side == 1), x_near[4 * s : 4 * s + 4, :], 0.0)
            sides_x = [got_x[f : f + 1, :] for f in range(4)]
            face = c2 * coefficients[s, way, at : at + 1, :]
            end = [c2 * mu_scale[at, e0 : e0 + 1, :] * sides_x[0]] + [face * sides_x[1 + c] for c in range(3)]
            end[1] += c2 * coefficients[s, 6 + way, at : at + 1, :] * sides_x[0]
            ends_x.append(end)
        plane = lax.broadcasted_iota(jnp.int32, (nx, nz), 0)

        def from_x(f):
            return jnp.where(plane == 0, ends_x[0][f], jnp.where(plane == nx - 1, ends_x[1][f], 0.0))

        rows[s, 0] = edges[s, 7] + c2 * mu_scale[inner, e0, :] * got(0) + from_x(0)
        face = c2 * coefficients[s, outward, inner, :]
        ends = []
        for c in range(3):
            end = edges[s, 4 + c] + face * got(1 + c) + from_x(1 + c)
            if c == 1:
                end += c2 * coefficients[s, 6 + outward, inner, :] * got(0)
            ends.append(end)
        along = edges[s, 3] * sum(edges[s, c] * ends[c] for c in range(3))
        for c in range(3):
            rows[s, 1 + c] = ends[c] - along * edges[s, c]
        copies.append(pltpu.make_async_copy(rows.at[s, 0], out_mu.at[:, e0, :], sems.at[s, 0]))
        for c in range(3):
            copies.append(pltpu.make_async_copy(rows.at[s, 1 + c], out_lam.at[c, :, e0, :], sems.at[s, 1 + c]))
        for copy in copies[4 * s :]:
            copy.start()
    for copy in copies:
        copy.wait()


VMEM = pl.BlockSpec(memory_space=pltpu.VMEM)
SMEM = pl.BlockSpec(memory_space=pltpu.SMEM)
HBM = pl.BlockSpec(memory_space=pltpu.HBM)
ANY = pl.BlockSpec(memory_space=pl.ANY)
MIB = 1024 * 1024


def call(kernel, ins, outs, scratch=(), in_specs=None, out_specs=None, aliases=None, grant=24 * MIB):
    return pl.pallas_call(
        kernel,
        out_shape=[jax.ShapeDtypeStruct(shape, F32) for shape in outs],
        in_specs=in_specs or [VMEM] * len(ins),
        out_specs=out_specs or [VMEM] * len(outs),
        scratch_shapes=[pltpu.VMEM(shape, F32) if isinstance(shape, tuple) else shape for shape in scratch],
        input_output_aliases=aliases or {},
        compiler_params=pltpu.CompilerParams(vmem_limit_bytes=grant),
    )(*ins)


def trade(value, axis, first):
    pairs = [(i, i + 1) for i in range(first, lax.axis_size(axis) - 1, 2)]
    return lax.ppermute(value, axis, pairs + [(j, i) for i, j in pairs])


def body(damage, strain, seed_damage, seed_disp, brick_work):
    nx, ny, nz = damage.shape
    plane = (ny, nz)
    brick = (nx,) + plane
    bricks = (3,) + brick
    framed = (nx + 2 * HALO,) + plane
    state = (4,) + framed
    row = (nx + 2 * HALO, nz)
    fields = (damage, strain, seed_damage, seed_disp)

    y_rows = (Y_FIELDS * nx, nz)
    x_faces = [(X_SLOTS,) + plane, (LATE_SLOTS,) + plane]
    faces = [y_rows] * 2 + x_faces * 2
    pal, other, near, near_late, far, far_late = call(
        faces_kernel, fields, faces,
        [brick, bricks, brick, bricks] + faces + [pltpu.SemaphoreType.DMA((4,)), pltpu.SemaphoreType.DMA((6,))],
        in_specs=[HBM] * 4, out_specs=[HBM] * 6, grant=56 * MIB,
    )
    y_in = (trade(pal, "gy", 0), trade(other, "gy", 1))
    far, far_late = trade(far, "gx", 1), trade(far_late, "gx", 1)
    near, near_late = trade(near, "gx", 0), trade(near_late, "gx", 0)
    inner = tuple(call(
        inner_kernel, fields,
        [framed, framed, (3,) + framed, framed, (3,) + framed, (6,) + framed, (6,) + framed, state, state],
    ))
    c_rows = (2 * CORNER_ROWS + MORE_ROWS, nz)
    pal, other = call(
        corners_kernel, fields + (near, far, inner[0]), [c_rows] * 2,
        [(4, 15) + plane, c_rows, c_rows, (2, 2, MORE_ROWS, nz)], in_specs=[VMEM] * 6 + [ANY],
    )
    c_in = (trade(pal, "gy", 0), trade(other, "gy", 1))
    less, soft, pull, mu_scale, raw, g, k, state0, state1, grads = call(
        sides_kernel, (brick_work, near, near_late, far, far_late) + inner,
        [part.shape for part in inner] + [(4,) + brick],
        in_specs=[SMEM] + [VMEM] * 13, aliases={5 + part: part for part in range(9)},
    )
    sent = (4 * nx, nz)
    x_sent = (8, nz)
    pal, other, near, coefficients, firsts, seconds, outer = call(
        edges_kernel, (soft, pull, mu_scale, raw, g, state0, state1) + y_in + c_in,
        [sent] * 2 + [x_sent] + [(2, 15) + row, (2, 4) + row, (2, 3) + row, (2, 4) + row],
        [(2, Y_FIELDS) + row, sent, sent, x_sent, x_sent],
    )
    halo = (trade(pal, "gy", 0), trade(other, "gy", 1), trade(near, "gx", 0))
    ins = (brick_work, less, grads) + y_in + (mu_scale, coefficients, firsts, seconds, outer, g, k, state0, state1)
    mu, lam, edges, *_ = call(
        wait_kernel, ins,
        [brick, bricks, (2, 8, nx, nz), (6,) + framed, (6,) + framed, state, state],
        [state, bricks, brick, bricks, pltpu.SemaphoreType.DMA((2, nx))],
        out_specs=[HBM] * 2 + [VMEM] * 5,
        in_specs=[SMEM] + [VMEM] * (len(ins) - 1),
        aliases={10: 3, 11: 4, 12: 5, 13: 6},
    )
    out_mu, out_lam = call(
        last_kernel, (mu_scale, coefficients, edges) + halo + (mu, lam),
        [brick, bricks], [(2, 4, nx, nz), pltpu.SemaphoreType.DMA((2, 4))],
        in_specs=[VMEM] * 6 + [HBM] * 2, out_specs=[HBM, HBM], aliases={6: 0, 7: 1},
    )
    return out_mu, out_lam


def solution(mesh):
    placed = (
        P("gx", "gy", None),
        P(None, "gx", "gy", None),
        P("gx", "gy", None),
        P(None, "gx", "gy", None),
        P("gx", "gy"),
    )
    return jax.shard_map(
        body,
        mesh=mesh,
        in_specs=placed,
        out_specs=(P("gx", "gy", None), P(None, "gx", "gy", None)),
        check_vma=False,
    )
```

```python
import functools

import jax
import jax.numpy as jnp
from jax import lax
from jax.experimental import pallas as pl
from jax.experimental.pallas import tpu as pltpu
from jax.sharding import PartitionSpec as P

RELAX_INNER = 8
RESIDUAL_STIFFNESS = 0.001
CENTER_VALUE = 1.0
HALF_WIDTH = 0.75
NORMAL_WEIGHT = 1.5
RELAX_RATE = 0.5 / RELAX_INNER
NORMAL_FLOOR = 0.05
OUTSIDE = 1.0 + RESIDUAL_STIFFNESS
F32 = jnp.float32


def weights():
    ratio = CENTER_VALUE / HALF_WIDTH
    rho = 1.0 / ratio
    found = []
    for _ in range(3):
        rho_next = 1.0 / (2.0 * ratio - rho)
        found.append((rho_next * rho, 2.0 * rho_next / HALF_WIDTH))
        rho = rho_next
    return found


def by_pairs(first, last, step):
    width = 2 if (last - first) % 2 == 0 else 1

    def turn(i, _):
        for part in range(width):
            step(first + width * i + part)
        return 0

    lax.fori_loop(0, (last - first) // width, turn, 0)


def soft_of(damage):
    return (1.0 - damage) ** 2 + RESIDUAL_STIFFNESS


def row_up(plane, beyond):
    rows = plane.shape[0]
    at = lax.broadcasted_iota(jnp.int32, plane.shape, 0)
    return jnp.where(at == rows - 1, beyond, pltpu.roll(plane, rows - 1, 0))


def row_down(plane, beyond):
    at = lax.broadcasted_iota(jnp.int32, plane.shape, 0)
    return jnp.where(at == 0, beyond, pltpu.roll(plane, 1, 0))


def lane_up(plane, beyond):
    cells = plane.shape[1]
    at = lax.broadcasted_iota(jnp.int32, plane.shape, 1)
    return jnp.where(at == cells - 1, beyond, pltpu.roll(plane, cells - 1, 1))


def lane_down(plane, beyond):
    at = lax.broadcasted_iota(jnp.int32, plane.shape, 1)
    return jnp.where(at == 0, beyond, pltpu.roll(plane, 1, 1))


def mu_inverse(ex, ey, ez):
    return 1.0 / (2.0 + (ex * ex + ey * ey + ez * ez))


def lam_inverse(center, total):
    return 1.0 / (0.5 + 0.125 * (6.0 * center + total))


HALO = 4
X_DAMAGE, X_PULL, X_MU, X_SOURCE, X_SLOTS = 0, 3, 9, 11, 17
LATE_DAMAGE, LATE_PULL, LATE_MU, LATE_SOURCE, LATE_SLOTS = 0, 1, 2, 3, 6
Y_HALO = (2, 1, 1, 1, 0, 1, 1, 1)
Y_KNOWN, Y_FIELDS = 8, 12
CORNER_ROWS = sum(Y_HALO) + 4
MORE_ROWS = 12


def edge_row(s, ny, depth):
    return depth if s == 0 else ny - 1 - depth


def known_of(s, damages, pulls, behind_pull, mus, sources, behind):
    planes = damages[0].shape[0]
    (c1, c2), _, _ = weights()
    soft = [soft_of(part) for part in damages]
    less = damages[0] - 1.0
    wx, wy, wz = (less * pull for pull in pulls)
    wy_behind = (damages[1] - 1.0) * behind_pull

    def across(value):
        return pltpu.roll(value, planes - 1, 0), pltpu.roll(value, 1, 0)

    def along(value, fill):
        return lane_up(value, fill), lane_down(value, fill)

    total = soft[0] + soft[2] + sum(across(soft[1])) + sum(along(soft[1], OUTSIDE))
    inverse = lam_inverse(soft[1], total)
    face = 0.125 * (soft[0] + soft[1])
    scale = 0.25 * mu_inverse(*pulls)
    known = [(1.0 + c1) * mus[0] + c2 * scale * (mus[1] + sum(across(mus[0])) + sum(along(mus[0], 0.0)))]
    x_up, x_down = across(wx * mus[0])
    z_up, z_down = along(wz * mus[0], 0.0)
    y_behind = wy_behind * mus[1]
    transfers = (x_up - x_down, y_behind if s == 0 else -y_behind, z_up - z_down)
    for c in range(3):
        known.append((1.0 + c1) * sources[c] + c2 * (face * (inverse * behind[c]) + transfers[c]))
    return scale, wy, known


def put_rows(s, put, damage, strain, seed_damage, seed_disp):
    ny = damage.shape[1]
    first, second, third = (edge_row(s, ny, depth) for depth in range(3))
    damages = [damage[:, row, :] for row in (first, second, third)]
    pulls = [strain[c, :, first, :] for c in range(3)]
    pulls_behind = [strain[c, :, second, :] for c in range(3)]
    mus = [
        seed_damage[:, first, :] * mu_inverse(*pulls),
        seed_damage[:, second, :] * mu_inverse(*pulls_behind),
    ]
    sources = [seed_disp[c, :, first, :] for c in range(3)]
    behind = [seed_disp[c, :, second, :] for c in range(3)]
    scale, wy, known = known_of(s, damages, pulls, pulls_behind[1], mus, sources, behind)
    for slot, value in enumerate(damages[:2] + [wy, mus[0], scale] + sources + known):
        put(slot, value)


def even(axis):
    return lax.rem(lax.axis_index(axis), 2) == 0


def faces_kernel(
    damage_in, strain_in, seed_in, sources_in, pal_out, other_out, near_out, near_late_out, far_out, far_late_out,
    damage, strain, seed_damage, seed_disp, pal, other, near, near_late, far, far_late, sems, out_sems,
):
    nx = damage.shape[0]
    copies = [
        pltpu.make_async_copy(damage_in, damage, sems.at[0]),
        pltpu.make_async_copy(strain_in, strain, sems.at[1]),
        pltpu.make_async_copy(seed_in, seed_damage, sems.at[2]),
        pltpu.make_async_copy(sources_in, seed_disp, sems.at[3]),
    ]
    for copy in copies:
        copy.start()
    sent = []

    def send(source, target):
        sent.append(pltpu.make_async_copy(source, target, out_sems.at[len(sent)]))
        sent[-1].start()

    def put_planes(out, late, high):
        for depth in range(4):
            at = jnp.where(high, nx - 1 - depth, depth)
            if depth == 3:
                late[LATE_DAMAGE] = damage[at]
                continue
            out[X_DAMAGE + depth] = damage[at]
            pulls = [strain[c, at] for c in range(3)]
            mu = seed_damage[at] * mu_inverse(*pulls)
            if depth == 2:
                late[LATE_PULL] = pulls[0]
                late[LATE_MU] = mu
            else:
                out[X_MU + depth] = mu
            for c in range(3):
                if depth == 2:
                    late[LATE_SOURCE + c] = seed_disp[c, at]
                else:
                    out[X_PULL + 2 * c + depth] = pulls[c]
                    out[X_SOURCE + 2 * c + depth] = seed_disp[c, at]

    for copy in copies:
        copy.wait()
    for out, target, first in ((pal, pal_out, True), (other, other_out, False)):

        def put(slot, value):
            out[slot * nx : (slot + 1) * nx, :] = value

        for s in range(2):

            @pl.when(even("gy") == ((s == 1) == first))
            def _():
                put_rows(s, put, damage, strain, seed_damage, seed_disp)

        send(out, target)
    for out, late, target, late_target, high in (
        (near, near_late, near_out, near_late_out, even("gx")),
        (far, far_late, far_out, far_late_out, ~even("gx")),
    ):
        put_planes(out, late, high)
        send(out, target)
        send(late, late_target)
    for copy in sent:
        copy.wait()


def received_x(near, far, side):
    from_near = even("gx") == (side == 1)

    def plane(slot, row=None):
        at = slot if row is None else (slice(slot, slot + 1), row)
        return jnp.where(from_near, near[at], far[at])

    return plane


def received_y(pal, other, side):
    from_pal = even("gy") == (side == 1)
    return lambda first, count: jnp.where(from_pal, pal[first : first + count, :], other[first : first + count, :])


def deal(pal, other, low, high):
    first = even("gy")
    low, high = low[...], high[...]
    pal[...] = jnp.where(first, high, low)
    other[...] = jnp.where(first, low, high)


def corners_kernel(
    damage, strain, seed_damage, seed_disp, near, far, _, pal, other, field, low, high, more
):
    nx, ny, _ = damage.shape
    for s, out in enumerate((low, high)):
        first, second, third = (edge_row(s, ny, depth) for depth in range(3))
        for side in range(2):
            x_in = received_x(near, far, side)
            ours = slice(3, 8) if side == 0 else slice(0, 5)
            planes = slice(0, 5) if side == 0 else slice(nx - 5, nx)

            def put_x(slot, first, count, row):
                for far_off in range(count):
                    at = 2 - far_off if side == 0 else 5 + far_off
                    field[slot, at : at + 1, :] = x_in(first + far_off, row)

            for depth, row in enumerate((first, second, third)):
                field[depth, ours, :] = damage[planes, row, :]
                put_x(depth, X_DAMAGE, 3, row)
            for depth, row in enumerate((first, second)):
                pulls = [strain[c, planes, row, :] for c in range(3)]
                for c in range(3):
                    if depth == 0:
                        field[3 + c, ours, :] = pulls[c]
                        put_x(3 + c, X_PULL + 2 * c, 2, row)
                    field[9 + 3 * depth + c, ours, :] = seed_disp[c, planes, row, :]
                    put_x(9 + 3 * depth + c, X_SOURCE + 2 * c, 2, row)
                if depth == 1:
                    field[6, ours, :] = pulls[1]
                    put_x(6, X_PULL + 2, 2, row)
                field[7 + depth, ours, :] = seed_damage[planes, row, :] * mu_inverse(*pulls)
                put_x(7 + depth, X_MU, 2, row)
            got = [field[slot] for slot in range(15)]
            scale, wy, known = known_of(s, got[:3], got[3:6], got[6], got[7:9], got[9:12], got[12:15])
            row = side * CORNER_ROWS
            for slot, value in enumerate(got[:2] + [wy, got[7], scale] + got[9:12]):
                count = Y_HALO[slot]
                behind = 2 - count if side == 0 else 5 + count
                more[side, slot : slot + 1, :] = value[behind : behind + 1, :]
                if count == 0:
                    continue
                start = 3 - count if side == 0 else 5
                out[row : row + count, :] = value[start : start + count, :]
                row += count
            for slot, value in enumerate(known):
                edge, behind = (3, 2) if side == 0 else (4, 5)
                out[row : row + 1, :] = value[edge : edge + 1, :]
                slot += Y_KNOWN
                more[side, slot : slot + 1, :] = value[behind : behind + 1, :]
                row += 1
        out[2 * CORNER_ROWS :, :] = jnp.where(even("gx"), more[0], more[1])
    deal(pal, other, low, high)


def in_grid():
    here = lax.axis_index("gx")
    return here > 0, here < lax.axis_size("gx") - 1


def prepare(first, last, soft, pull, raw, g, k, state0):
    planes, ny, nz = soft.shape
    inside = in_grid()
    lane = lax.broadcasted_iota(jnp.int32, (ny, nz), 1)
    row = lax.broadcasted_iota(jnp.int32, (ny, nz), 0)
    inner = (row > 0) & (row < ny - 1)

    def step(at):
        center = soft[at]
        sides = [
            soft[at + 1],
            soft[at - 1],
            pltpu.roll(center, ny - 1, 0),
            pltpu.roll(center, 1, 0),
            lane_up(center, OUTSIDE),
            lane_down(center, OUTSIDE),
        ]
        outside = ((at < HALO) & ~inside[0]) | ((at >= planes - HALO) & ~inside[1])
        inverse = jnp.where(inner & ~outside, lam_inverse(center, sum(sides)), 0.0)
        eighth = 0.125 * inverse
        for j in range(6):
            face = eighth * (center + sides[j])
            if j == 4:
                face = jnp.where(lane == nz - 1, 0.0, face)
            if j == 5:
                face = jnp.where(lane == 0, 0.0, face)
            g[j, at] = face
        k[0, at] = inverse * pull[0, at + 1]
        k[1, at] = -inverse * pull[0, at - 1]
        k[2, at] = inverse * pltpu.roll(pull[1, at], ny - 1, 0)
        k[3, at] = -inverse * pltpu.roll(pull[1, at], 1, 0)
        k[4, at] = inverse * lane_up(pull[2, at], 0.0)
        k[5, at] = -inverse * lane_down(pull[2, at], 0.0)
        for c in range(3):
            state0[1 + c, at] = inverse * raw[c, at]

    by_pairs(first, last, step)


def reach_of(grad, count):
    square = sum(part * part for part in grad)
    scale = 1.0 / jnp.maximum(square, NORMAL_FLOOR)
    power = 1.0 - RELAX_RATE * (1.0 + NORMAL_WEIGHT * square * scale)
    series = 1.0 + power
    for _ in range(2):
        power = power * power
        series = series * (1.0 + power)
    power = power * power
    repeats = jnp.ones_like(power)
    for level in range(1, 4):
        repeats = jnp.where(count > level, 1.0 + power * repeats, repeats)
    return (RELAX_RATE * NORMAL_WEIGHT * scale) * (series * repeats)


def slopes(first, last, count, less, grads):
    ny = less.shape[1]

    def step(at):
        own = less[at]
        grad = [
            0.5 * (less[at + 1] - less[at - 1]),
            0.5 * (pltpu.roll(own, ny - 1, 0) - pltpu.roll(own, 1, 0)),
            0.5 * (lane_up(own, -1.0) - lane_down(own, -1.0)),
        ]
        for c in range(3):
            grads[c, at - HALO] = grad[c]
        grads[3, at - HALO] = reach_of(grad, count)

    by_pairs(first, last, step)


def first_sweep(ranges, state0, state1, g, k, mu_scale):
    (c1, c2), _, _ = weights()

    def advance(at, f, own, moved):
        state1[f, at] = (1.0 + c1) * own + c2 * moved

    for first, last in ranges:
        sweep(first, last, state0, g, k, mu_scale, None, advance)


def inner_kernel(
    damage, strain, seed_damage, seed_disp, less, soft, pull, mu_scale, raw, g, k, state0, state1
):
    nx = damage.shape[0]

    def fill(i, _):
        at = HALO + i
        own = damage[i]
        sx, sy, sz = strain[0, i], strain[1, i], strain[2, i]
        soft[at] = soft_of(own)
        own = own - 1.0
        less[at] = own
        pull[0, at] = own * sx
        pull[1, at] = own * sy
        pull[2, at] = own * sz
        mu_inv = mu_inverse(sx, sy, sz)
        mu_scale[at] = 0.25 * mu_inv
        state0[0, at] = mu_inv * seed_damage[i]
        for c in range(3):
            raw[c, at] = seed_disp[c, i]
        return 0

    lax.fori_loop(0, nx, fill, 0)
    low, high = HALO, HALO + nx
    prepare(low + 1, high - 1, soft, pull, raw, g, k, state0)
    first_sweep([(low + 2, high - 2)], state0, state1, g, k, mu_scale)


def sides_kernel(
    work, near, near_late, far, far_late,
    less_in, soft_in, pull_in, scale_in, raw_in, g_in, k_in, state0_in, state1_in,
    less, soft, pull, mu_scale, raw, g, k, state0, state1, grads,
):
    nx = soft.shape[0] - 2 * HALO
    low, high = HALO, HALO + nx
    inside = in_grid()
    for s in range(2):
        x_in, late = received_x(near, far, s), received_x(near_late, far_late, s)
        for depth in range(4):
            at = low - 1 - depth if s == 0 else high + depth
            own = late(LATE_DAMAGE) if depth == 3 else x_in(X_DAMAGE + depth)
            soft[at] = soft_of(own)
            if depth == 3:
                continue
            own = own - 1.0
            if depth == 0:
                less[at] = own
            if depth == 2:
                pull[0, at] = own * late(LATE_PULL)
                state0[0, at] = late(LATE_MU)
            else:
                pulls = [x_in(X_PULL + 2 * c + depth) for c in range(3)]
                mu_scale[at] = jnp.where(inside[s], 0.25 * mu_inverse(*pulls), 0.0)
                state0[0, at] = x_in(X_MU + depth)
            for c in range(3):
                if depth == 2:
                    raw[c, at] = late(LATE_SOURCE + c)
                else:
                    pull[c, at] = own * pulls[c]
                    raw[c, at] = x_in(X_SOURCE + 2 * c + depth)

    for first, last in ((low - 3, low + 1), (high - 1, high + 3)):
        prepare(first, last, soft, pull, raw, g, k, state0)
    slopes(low, high, work[0, 0], less, grads)
    first_sweep([(low - 2, low + 2), (high - 2, high + 2)], state0, state1, g, k, mu_scale)


def edges_kernel(first, *refs):
    soft, pull, mu_scale, raw, g, state0, state1, y_got, c_got = refs[:9]
    sent, coefficients, firsts, seconds, outer, x_rows, sent_near, field = refs[-8:]
    planes, ny, nz = soft.shape
    nx = planes - 2 * HALO
    (c1, c2), (d1, d2), _ = weights()
    lane = lax.broadcasted_iota(jnp.int32, (planes, nz), 1)
    plane = lax.broadcasted_iota(jnp.int32, (planes, nz), 0)
    here, there = lax.axis_index("gx"), lax.axis_index("gy")
    in_x = ((plane >= HALO) | (here > 0)) & ((plane < HALO + nx) | (here < lax.axis_size("gx") - 1))
    in_y = (there > 0, there < lax.axis_size("gy") - 1)

    def around_x(value):
        return [pltpu.roll(value, planes - 1, 0), pltpu.roll(value, 1, 0)]

    def around_z(value, fill):
        return [lane_up(value, fill), lane_down(value, fill)]

    def y_in(start, count):
        return y_got[start : start + count, :]

    def c_in(start, count):
        return c_got[start : start + count, :]

    def side(s):
        e0, e1 = edge_row(s, ny, 0), edge_row(s, ny, 1)

        def ordered(inward, outward):
            return [inward, outward] if s == 0 else [outward, inward]

        row = 0
        for f in range(Y_FIELDS):
            field[f, HALO : HALO + nx, :] = y_in(f * nx, nx)
            count, shift = (Y_HALO[f], 0) if f < Y_KNOWN else (1, 1)
            behind = HALO - count - 1 + shift
            for at in (behind, planes - 1 - behind):
                field[f, at : at + 1, :] = c_in(2 * CORNER_ROWS + f, 1)
            if count == 0:
                continue
            field[f, HALO - count + shift : HALO + shift, :] = c_in(row, count)
            high = HALO + nx - shift
            field[f, high : high + count, :] = c_in(CORNER_ROWS + row, count)
            row += count

        soft_1, soft_2 = soft_of(field[0]), soft_of(field[1])
        soft_e0, soft_e1 = soft[:, e0, :], soft[:, e1, :]

        def total(center, inward, outward):
            return sum(around_x(center) + [inward, outward] + around_z(center, OUTSIDE))

        inverse_1 = lam_inverse(soft_1, total(soft_1, soft_e0, soft_2))
        inverse_1 = jnp.where(in_x & in_y[s], inverse_1, 0.0)
        lam_1 = [inverse_1 * field[5 + c] for c in range(3)]
        inverse_e0 = jnp.where(in_x, lam_inverse(soft_e0, total(soft_e0, soft_e1, soft_1)), 0.0)
        lam_e0 = [inverse_e0 * raw[c, :, e0, :] for c in range(3)]
        mu_1, wy_1 = field[3], field[2]
        mu_e0, mu_e1 = state0[0, :, e0, :], state0[0, :, e1, :]
        lam_e1 = [state0[1 + c, :, e1, :] for c in range(3)]

        def coefficients_of(center, inverse, inward, outward, wx, wy, wz):
            sides = around_x(center) + ordered(inward, outward) + around_z(center, OUTSIDE)
            eighth = 0.125 * inverse
            faces = [eighth * (center + side) for side in sides]
            faces[4] = jnp.where(lane == nz - 1, 0.0, faces[4])
            faces[5] = jnp.where(lane == 0, 0.0, faces[5])
            pulls = around_x(wx) + wy + around_z(wz, 0.0)
            return faces, [inverse * w if j % 2 == 0 else -inverse * w for j, w in enumerate(pulls)]

        def moved_of(faces, pulls, scale, own, inward, outward):
            sides = [
                around_x(own[f]) + ordered(inward[f], outward[f]) + around_z(own[f], 0.0) for f in range(4)
            ]
            moved = [scale * sum(sides[0])]
            for c in range(3):
                part = sum(faces[j] * sides[1 + c][j] for j in range(6))
                moved.append(part + pulls[2 * c] * sides[0][2 * c] + pulls[2 * c + 1] * sides[0][2 * c + 1])
            return moved

        first_1 = [jnp.where(in_x, field[Y_KNOWN] + c2 * field[4] * mu_e0, 0.0)]
        sides = around_x(soft_1) + around_z(soft_1, OUTSIDE) + [soft_e0]
        faces = [0.125 * (soft_1 + side) for side in sides]
        wy_e0 = pull[1, :, e0, :] * mu_e0
        own_1 = [mu_1] + lam_1
        own_e0 = [mu_e0] + lam_e0
        for c in range(3):
            sides = around_x(lam_1[c]) + around_z(lam_1[c], 0.0) + [lam_e0[c]]
            lacked = sum(faces[j] * sides[j] for j in range(5))
            if c == 1:
                lacked += wy_e0 if s == 0 else -wy_e0
            first_1.append(inverse_1 * (field[Y_KNOWN + 1 + c] + c2 * lacked))

        scale_e0 = mu_scale[:, e0, :]
        wy = ordered(pull[1, :, e1, :], wy_1)
        faces, pulls = coefficients_of(
            soft_e0, inverse_e0, soft_e1, soft_1, pull[0, :, e0, :], wy, pull[2, :, e0, :]
        )
        moved = moved_of(faces, pulls, scale_e0, own_e0, [mu_e1] + lam_e1, own_1)
        first_e0 = [(1.0 + c1) * own_e0[f] + c2 * moved[f] for f in range(4)]

        outward_face = g[3 if s == 0 else 2, :, e1, :]
        first_e1 = [state1[0, :, e1, :]]
        for c in range(3):
            first_e1.append(state1[1 + c, :, e1, :] + c2 * outward_face * lam_e0[c])

        moved = moved_of(faces, pulls, scale_e0, first_e0, first_e1, first_1)
        for f in range(4):
            second = first_e0[f] + (d1 - d2) * (first_e0[f] - own_e0[f]) + d2 * moved[f]
            sent[f * nx : (f + 1) * nx, :] = second[HALO : HALO + nx, :]
            x_rows[0, 4 * s + f : 4 * s + f + 1, :] = second[HALO : HALO + 1, :]
            x_rows[1, 4 * s + f : 4 * s + f + 1, :] = second[HALO + nx - 1 : HALO + nx, :]
            firsts[s, f] = first_e0[f]
            outer[s, f] = first_1[f]
        for j in range(6):
            coefficients[s, j] = faces[j]
            coefficients[s, 6 + j] = pulls[j]
        for c in range(3):
            coefficients[s, 12 + c] = lam_e0[c]
            seconds[s, c] = first_e1[1 + c]

    for s in range(2):
        pl.when(even("gy") == ((s == 1) == first))(functools.partial(side, s))
    sent_near[...] = jnp.where(even("gx"), x_rows[1], x_rows[0])


def sweep(first, last, state, g, k, mu_scale, rows, advance, finish=None):
    _, ny, nz = mu_scale.shape
    lane = lax.broadcasted_iota(jnp.int32, (ny, nz), 1)
    if rows is None:

        def rows(s, f, at):
            return 0.0

    def plane(at):
        def around(f):
            own = state[f, at]
            return own, [
                state[f, at + 1],
                state[f, at - 1],
                row_up(own, rows(1, f, at)),
                row_down(own, rows(0, f, at)),
                pltpu.roll(own, nz - 1, 1),
                pltpu.roll(own, 1, 1),
            ]

        mu, mu_sides = around(0)
        ends = [
            jnp.where(lane == nz - 1, 0.0, mu_sides[4]),
            jnp.where(lane == 0, 0.0, mu_sides[5]),
        ]
        results = [advance(at, 0, mu, mu_scale[at] * sum(mu_sides[:4] + ends))]
        faces = [g[j, at] for j in range(6)]
        for c in range(3):
            lam, lam_sides = around(1 + c)
            moved = sum(faces[j] * lam_sides[j] for j in range(6))
            moved += k[2 * c, at] * mu_sides[2 * c] + k[2 * c + 1, at] * mu_sides[2 * c + 1]
            results.append(advance(at, 1 + c, lam, moved))
        if finish is not None:
            finish(at - HALO, results)

    by_pairs(first, last, plane)


def wait_kernel(
    work, less, grads, y_pal, y_other,
    mu_scale, coefficients, firsts, seconds, outer, g_in, k_in, state0_in, state1_in,
    out_mu, out_lam, edges, g, k, state0, state1,
    state2, states,
):
    _, nx, ny, _ = grads.shape
    planes = nx + 2 * HALO
    _, (d1, d2), (c1, c2) = weights()
    held = slice(HALO - 2, HALO + nx + 2)
    for s in range(2):
        e0, e1 = edge_row(s, ny, 0), edge_row(s, ny, 1)
        for j in range(6):
            g[j, held, e0, :] = coefficients[s, j, held, :]
            k[j, held, e0, :] = coefficients[s, 6 + j, held, :]
        for c in range(3):
            state0[1 + c, held, e0, :] = coefficients[s, 12 + c, held, :]
            state1[1 + c, held, e1, :] = seconds[s, c, held, :]
        for f in range(4):
            state1[f, held, e0, :] = firsts[s, f, held, :]

    def rows(s, f, at):
        return outer[s, f, pl.ds(at, 1), :]

    def advance_2(at, f, own, moved):
        state2[f, at] = own + (d1 - d2) * (own - state0[f, at]) + d2 * moved

    sweep(HALO - 1, HALO + nx + 1, state1, g, k, mu_scale, rows, advance_2)
    nothing = jnp.zeros((1, state2.shape[3]), F32)
    at = jnp.where(even("gx"), HALO + nx, HALO - 1)
    for s in range(2):
        e0 = edge_row(s, ny, 0)
        for f in range(4):
            state2[f, at, e0 : e0 + 1, :] = nothing

    def advance_3(at, f, own, moved):
        return own + c1 * (own - state1[f, at]) + c2 * (state0[f, at] - own + moved)

    def finish(i, results):
        out_mu[i] = results[0]
        along = grads[3, i] * sum(grads[c, i] * results[1 + c] for c in range(3))
        for c in range(3):
            out_lam[c, i] = results[1 + c] - along * grads[c, i]
            states[c, i] = results[1 + c]

    sweep(HALO, HALO + nx, state2, g, k, mu_scale, None, advance_3, finish)

    for s in range(2):
        y_in = received_y(y_pal, y_other, s)
        e0, e1 = edge_row(s, ny, 0), edge_row(s, ny, 1)
        own = less[HALO : HALO + nx, e0, :]
        inward, outward = less[HALO : HALO + nx, e1, :], y_in(0, nx) - 1.0
        grad = [
            0.5 * (less[HALO + 1 : HALO + nx + 1, e0, :] - less[HALO - 1 : HALO + nx - 1, e0, :]),
            0.5 * (inward - outward if s == 0 else outward - inward),
            0.5 * (lane_up(own, -1.0) - lane_down(own, -1.0)),
        ]
        for c in range(3):
            edges[s, c] = grad[c]
            edges[s, 4 + c] = states[c, :, e0, :]
        edges[s, 3] = reach_of(grad, work[0, 0])


def last_kernel(
    mu_scale, coefficients, edges, y_pal, y_other, x_near, mu_in, lam_in,
    out_mu, out_lam, mu, lam,
    sems,
):
    nx, ny, nz = mu.shape
    inner = slice(HALO, HALO + nx)
    _, _, (_, c2) = weights()
    for s in range(2):
        y_in = received_y(y_pal, y_other, s)
        e0 = edge_row(s, ny, 0)
        outward = 3 if s == 0 else 2

        def got(f):
            return y_in(f * nx, nx)

        ends_x = []
        for side, at, way in ((0, HALO, 1), (1, HALO + nx - 1, 0)):
            got_x = jnp.where(even("gx") == (side == 1), x_near[4 * s : 4 * s + 4, :], 0.0)
            sides_x = [got_x[f : f + 1, :] for f in range(4)]
            face = c2 * coefficients[s, way, at : at + 1, :]
            end = [c2 * mu_scale[at, e0 : e0 + 1, :] * sides_x[0]] + [face * sides_x[1 + c] for c in range(3)]
            end[1] += c2 * coefficients[s, 6 + way, at : at + 1, :] * sides_x[0]
            ends_x.append(end)
        plane = lax.broadcasted_iota(jnp.int32, (nx, nz), 0)

        def from_x(f):
            return jnp.where(plane == 0, ends_x[0][f], jnp.where(plane == nx - 1, ends_x[1][f], 0.0))

        mu[:, e0, :] = mu[:, e0, :] + c2 * mu_scale[inner, e0, :] * got(0) + from_x(0)
        face = c2 * coefficients[s, outward, inner, :]
        ends = []
        for c in range(3):
            end = edges[s, 4 + c] + face * got(1 + c) + from_x(1 + c)
            if c == 1:
                end += c2 * coefficients[s, 6 + outward, inner, :] * got(0)
            ends.append(end)
        along = edges[s, 3] * sum(edges[s, c] * ends[c] for c in range(3))
        for c in range(3):
            lam[c, :, e0, :] = ends[c] - along * edges[s, c]
    copies = [
        pltpu.make_async_copy(mu, out_mu, sems.at[0]),
        pltpu.make_async_copy(lam, out_lam, sems.at[1]),
    ]
    for copy in copies:
        copy.start()
    for copy in copies:
        copy.wait()


VMEM = pl.BlockSpec(memory_space=pltpu.VMEM)
SMEM = pl.BlockSpec(memory_space=pltpu.SMEM)
HBM = pl.BlockSpec(memory_space=pltpu.HBM)
ANY = pl.BlockSpec(memory_space=pl.ANY)
MIB = 1024 * 1024


def call(kernel, ins, outs, scratch=(), in_specs=None, out_specs=None, aliases=None, grant=24 * MIB):
    return pl.pallas_call(
        kernel,
        out_shape=[jax.ShapeDtypeStruct(shape, F32) for shape in outs],
        in_specs=in_specs or [VMEM] * len(ins),
        out_specs=out_specs or [VMEM] * len(outs),
        scratch_shapes=[pltpu.VMEM(shape, F32) if isinstance(shape, tuple) else shape for shape in scratch],
        input_output_aliases=aliases or {},
        compiler_params=pltpu.CompilerParams(vmem_limit_bytes=grant),
    )(*ins)


def trade(value, axis, first):
    pairs = [(i, i + 1) for i in range(first, lax.axis_size(axis) - 1, 2)]
    return lax.ppermute(value, axis, pairs + [(j, i) for i, j in pairs])


def body(damage, strain, seed_damage, seed_disp, brick_work):
    nx, ny, nz = damage.shape
    plane = (ny, nz)
    brick = (nx,) + plane
    bricks = (3,) + brick
    framed = (nx + 2 * HALO,) + plane
    state = (4,) + framed
    row = (nx + 2 * HALO, nz)
    fields = (damage, strain, seed_damage, seed_disp)

    y_rows = (Y_FIELDS * nx, nz)
    x_faces = [(X_SLOTS,) + plane, (LATE_SLOTS,) + plane]
    faces = [y_rows] * 2 + x_faces * 2
    pal, other, near, near_late, far, far_late = call(
        faces_kernel, fields, faces,
        [brick, bricks, brick, bricks] + faces + [pltpu.SemaphoreType.DMA((4,)), pltpu.SemaphoreType.DMA((6,))],
        in_specs=[HBM] * 4, out_specs=[HBM] * 6, grant=56 * MIB,
    )
    y_in = (trade(pal, "gy", 0), trade(other, "gy", 1))
    far, far_late = trade(far, "gx", 1), trade(far_late, "gx", 1)
    near, near_late = trade(near, "gx", 0), trade(near_late, "gx", 0)
    inner = tuple(call(
        inner_kernel, fields,
        [framed, framed, (3,) + framed, framed, (3,) + framed, (6,) + framed, (6,) + framed, state, state],
    ))
    c_rows = (2 * CORNER_ROWS + MORE_ROWS, nz)
    pal, other = call(
        corners_kernel, fields + (near, far, inner[0]), [c_rows] * 2,
        [(15,) + plane, c_rows, c_rows, (2, MORE_ROWS, nz)], in_specs=[VMEM] * 6 + [ANY],
    )
    c_in = (trade(pal, "gy", 0), trade(other, "gy", 1))
    less, soft, pull, mu_scale, raw, g, k, state0, state1, grads = call(
        sides_kernel, (brick_work, near, near_late, far, far_late) + inner,
        [part.shape for part in inner] + [(4,) + brick],
        in_specs=[SMEM] + [VMEM] * 13, aliases={5 + part: part for part in range(9)},
    )
    sent, x_sent = (4 * nx, nz), (8, nz)
    shapes = [(2, 15) + row, (2, 4) + row, (2, 3) + row, (2, 4) + row, (2,) + x_sent]
    ins = (soft, pull, mu_scale, raw, g, state0, state1)
    pal, *found, _ = call(
        functools.partial(edges_kernel, True), ins + (y_in[0], c_in[0]),
        [(4 * nx + 8, nz)] + shapes + [x_sent], [(Y_FIELDS,) + row],
    )
    other, coefficients, firsts, seconds, outer, _, near = call(
        functools.partial(edges_kernel, False), ins + (y_in[1], c_in[1]) + tuple(found),
        [sent] + shapes + [x_sent], [(Y_FIELDS,) + row],
        aliases={9 + part: 1 + part for part in range(5)},
    )
    halo = (trade(pal, "gy", 0), trade(other, "gy", 1), trade(near, "gx", 0))
    ins = (brick_work, less, grads) + y_in + (mu_scale, coefficients, firsts, seconds, outer, g, k, state0, state1)
    mu, lam, edges, *_ = call(
        wait_kernel, ins,
        [brick, bricks, (2, 7, nx, nz), (6,) + framed, (6,) + framed, state, state],
        [state, bricks],
        in_specs=[SMEM] + [VMEM] * (len(ins) - 1),
        aliases={10: 3, 11: 4, 12: 5, 13: 6},
    )
    out_mu, out_lam, *_ = call(
        last_kernel, (mu_scale, coefficients, edges) + halo + (mu, lam),
        [brick, bricks, brick, bricks], [pltpu.SemaphoreType.DMA((2,))],
        out_specs=[HBM, HBM, VMEM, VMEM], aliases={6: 2, 7: 3},
    )
    return out_mu, out_lam


def solution(mesh):
    placed = (
        P("gx", "gy", None),
        P(None, "gx", "gy", None),
        P("gx", "gy", None),
        P(None, "gx", "gy", None),
        P("gx", "gy"),
    )
    return jax.shard_map(
        body,
        mesh=mesh,
        in_specs=placed,
        out_specs=(P("gx", "gy", None), P(None, "gx", "gy", None)),
        check_vma=False,
    )
```

```python
import functools

import jax
import jax.numpy as jnp
from jax import lax
from jax.experimental import pallas as pl
from jax.experimental.pallas import tpu as pltpu
from jax.sharding import PartitionSpec as P

RELAX_INNER = 8
RESIDUAL_STIFFNESS = 0.001
CENTER_VALUE = 1.0
HALF_WIDTH = 0.75
NORMAL_WEIGHT = 1.5
RELAX_RATE = 0.5 / RELAX_INNER
NORMAL_FLOOR = 0.05
OUTSIDE = 1.0 + RESIDUAL_STIFFNESS
F32 = jnp.float32


def weights():
    ratio = CENTER_VALUE / HALF_WIDTH
    rho = 1.0 / ratio
    found = []
    for _ in range(3):
        rho_next = 1.0 / (2.0 * ratio - rho)
        found.append((rho_next * rho, 2.0 * rho_next / HALF_WIDTH))
        rho = rho_next
    return found


def by_pairs(first, last, step):
    width = 2 if (last - first) % 2 == 0 else 1

    def turn(i, _):
        for part in range(width):
            step(first + width * i + part)
        return 0

    lax.fori_loop(0, (last - first) // width, turn, 0)


def soft_of(damage):
    return (1.0 - damage) ** 2 + RESIDUAL_STIFFNESS


def row_up(plane, beyond):
    rows = plane.shape[0]
    at = lax.broadcasted_iota(jnp.int32, plane.shape, 0)
    return jnp.where(at == rows - 1, beyond, pltpu.roll(plane, rows - 1, 0))


def row_down(plane, beyond):
    at = lax.broadcasted_iota(jnp.int32, plane.shape, 0)
    return jnp.where(at == 0, beyond, pltpu.roll(plane, 1, 0))


def lane_up(plane, beyond):
    cells = plane.shape[1]
    at = lax.broadcasted_iota(jnp.int32, plane.shape, 1)
    return jnp.where(at == cells - 1, beyond, pltpu.roll(plane, cells - 1, 1))


def lane_down(plane, beyond):
    at = lax.broadcasted_iota(jnp.int32, plane.shape, 1)
    return jnp.where(at == 0, beyond, pltpu.roll(plane, 1, 1))


def mu_inverse(ex, ey, ez):
    return 1.0 / (2.0 + (ex * ex + ey * ey + ez * ez))


def lam_inverse(center, total):
    return 1.0 / (0.5 + 0.125 * (6.0 * center + total))


HALO = 4
X_DAMAGE, X_PULL, X_MU, X_SOURCE, X_SLOTS = 0, 3, 9, 11, 17
LATE_DAMAGE, LATE_PULL, LATE_MU, LATE_SOURCE, LATE_SLOTS = 0, 1, 2, 3, 6
Y_HALO = (2, 1, 1, 1, 0, 1, 1, 1)
Y_KNOWN, Y_FIELDS = 8, 12
CORNER_ROWS = sum(Y_HALO) + 4
MORE_ROWS = 12


def edge_row(s, ny, depth):
    return depth if s == 0 else ny - 1 - depth


def known_of(s, damages, pulls, behind_pull, mus, sources, behind):
    planes = damages[0].shape[0]
    (c1, c2), _, _ = weights()
    soft = [soft_of(part) for part in damages]
    less = damages[0] - 1.0
    wx, wy, wz = (less * pull for pull in pulls)
    wy_behind = (damages[1] - 1.0) * behind_pull

    def across(value):
        return pltpu.roll(value, planes - 1, 0), pltpu.roll(value, 1, 0)

    def along(value, fill):
        return lane_up(value, fill), lane_down(value, fill)

    total = soft[0] + soft[2] + sum(across(soft[1])) + sum(along(soft[1], OUTSIDE))
    inverse = lam_inverse(soft[1], total)
    face = 0.125 * (soft[0] + soft[1])
    scale = 0.25 * mu_inverse(*pulls)
    known = [(1.0 + c1) * mus[0] + c2 * scale * (mus[1] + sum(across(mus[0])) + sum(along(mus[0], 0.0)))]
    x_up, x_down = across(wx * mus[0])
    z_up, z_down = along(wz * mus[0], 0.0)
    y_behind = wy_behind * mus[1]
    transfers = (x_up - x_down, y_behind if s == 0 else -y_behind, z_up - z_down)
    for c in range(3):
        known.append((1.0 + c1) * sources[c] + c2 * (face * (inverse * behind[c]) + transfers[c]))
    return scale, wy, known


def put_rows(s, put, damage, strain, seed_damage, seed_disp):
    ny = damage.shape[1]
    first, second, third = (edge_row(s, ny, depth) for depth in range(3))
    damages = [damage[:, row, :] for row in (first, second, third)]
    pulls = [strain[c, :, first, :] for c in range(3)]
    pulls_behind = [strain[c, :, second, :] for c in range(3)]
    mus = [
        seed_damage[:, first, :] * mu_inverse(*pulls),
        seed_damage[:, second, :] * mu_inverse(*pulls_behind),
    ]
    sources = [seed_disp[c, :, first, :] for c in range(3)]
    behind = [seed_disp[c, :, second, :] for c in range(3)]
    scale, wy, known = known_of(s, damages, pulls, pulls_behind[1], mus, sources, behind)
    for slot, value in enumerate(damages[:2] + [wy, mus[0], scale] + sources + known):
        put(slot, value)


def even(axis):
    return lax.rem(lax.axis_index(axis), 2) == 0


def faces_kernel(
    damage_in, strain_in, seed_in, sources_in, pal_out, other_out, near_out, near_late_out, far_out, far_late_out,
    damage, strain, seed_damage, seed_disp, pal, other, near, near_late, far, far_late, sems, out_sems,
):
    nx = damage.shape[0]
    copies = [
        pltpu.make_async_copy(damage_in, damage, sems.at[0]),
        pltpu.make_async_copy(strain_in, strain, sems.at[1]),
        pltpu.make_async_copy(seed_in, seed_damage, sems.at[2]),
        pltpu.make_async_copy(sources_in, seed_disp, sems.at[3]),
    ]
    for copy in copies:
        copy.start()
    sent = []

    def send(source, target):
        sent.append(pltpu.make_async_copy(source, target, out_sems.at[len(sent)]))
        sent[-1].start()

    def put_planes(out, late, high):
        for depth in range(4):
            at = jnp.where(high, nx - 1 - depth, depth)
            if depth == 3:
                late[LATE_DAMAGE] = damage[at]
                continue
            out[X_DAMAGE + depth] = damage[at]
            pulls = [strain[c, at] for c in range(3)]
            mu = seed_damage[at] * mu_inverse(*pulls)
            if depth == 2:
                late[LATE_PULL] = pulls[0]
                late[LATE_MU] = mu
            else:
                out[X_MU + depth] = mu
            for c in range(3):
                if depth == 2:
                    late[LATE_SOURCE + c] = seed_disp[c, at]
                else:
                    out[X_PULL + 2 * c + depth] = pulls[c]
                    out[X_SOURCE + 2 * c + depth] = seed_disp[c, at]

    for copy in copies:
        copy.wait()
    for out, target, first in ((pal, pal_out, True), (other, other_out, False)):

        def put(slot, value):
            out[slot * nx : (slot + 1) * nx, :] = value

        for s in range(2):

            @pl.when(even("gy") == ((s == 1) == first))
            def _():
                put_rows(s, put, damage, strain, seed_damage, seed_disp)

        send(out, target)
    for out, late, target, late_target, high in (
        (near, near_late, near_out, near_late_out, even("gx")),
        (far, far_late, far_out, far_late_out, ~even("gx")),
    ):
        put_planes(out, late, high)
        send(out, target)
        send(late, late_target)
    for copy in sent:
        copy.wait()


def received_x(near, far, side):
    from_near = even("gx") == (side == 1)

    def plane(slot, row=None):
        at = slot if row is None else (slice(slot, slot + 1), row)
        return jnp.where(from_near, near[at], far[at])

    return plane


def received_y(pal, other, side):
    from_pal = even("gy") == (side == 1)
    return lambda first, count: jnp.where(from_pal, pal[first : first + count, :], other[first : first + count, :])


def deal(pal, other, low, high):
    first = even("gy")
    low, high = low[...], high[...]
    pal[...] = jnp.where(first, high, low)
    other[...] = jnp.where(first, low, high)


def corners_kernel(
    damage, strain, seed_damage, seed_disp, near, far, _, pal, other, fields, low, high, more
):
    nx, ny, _ = damage.shape
    for s, out in enumerate((low, high)):
        first, second, third = (edge_row(s, ny, depth) for depth in range(3))
        for side in range(2):
            field = fields.at[2 * s + side]
            x_in = received_x(near, far, side)
            ours = slice(3, 8) if side == 0 else slice(0, 5)
            planes = slice(0, 5) if side == 0 else slice(nx - 5, nx)

            def put_x(slot, first, count, row):
                for far_off in range(count):
                    at = 2 - far_off if side == 0 else 5 + far_off
                    field[slot, at : at + 1, :] = x_in(first + far_off, row)

            for depth, row in enumerate((first, second, third)):
                field[depth, ours, :] = damage[planes, row, :]
                put_x(depth, X_DAMAGE, 3, row)
            for depth, row in enumerate((first, second)):
                pulls = [strain[c, planes, row, :] for c in range(3)]
                for c in range(3):
                    if depth == 0:
                        field[3 + c, ours, :] = pulls[c]
                        put_x(3 + c, X_PULL + 2 * c, 2, row)
                    field[9 + 3 * depth + c, ours, :] = seed_disp[c, planes, row, :]
                    put_x(9 + 3 * depth + c, X_SOURCE + 2 * c, 2, row)
                if depth == 1:
                    field[6, ours, :] = pulls[1]
                    put_x(6, X_PULL + 2, 2, row)
                field[7 + depth, ours, :] = seed_damage[planes, row, :] * mu_inverse(*pulls)
                put_x(7 + depth, X_MU, 2, row)
            got = [field[slot] for slot in range(15)]
            scale, wy, known = known_of(s, got[:3], got[3:6], got[6], got[7:9], got[9:12], got[12:15])
            row = side * CORNER_ROWS
            for slot, value in enumerate(got[:2] + [wy, got[7], scale] + got[9:12]):
                count = Y_HALO[slot]
                behind = 2 - count if side == 0 else 5 + count
                more[s, side, slot : slot + 1, :] = value[behind : behind + 1, :]
                if count == 0:
                    continue
                start = 3 - count if side == 0 else 5
                out[row : row + count, :] = value[start : start + count, :]
                row += count
            for slot, value in enumerate(known):
                edge, behind = (3, 2) if side == 0 else (4, 5)
                out[row : row + 1, :] = value[edge : edge + 1, :]
                slot += Y_KNOWN
                more[s, side, slot : slot + 1, :] = value[behind : behind + 1, :]
                row += 1
        out[2 * CORNER_ROWS :, :] = jnp.where(even("gx"), more[s, 0], more[s, 1])
    deal(pal, other, low, high)


def in_grid():
    here = lax.axis_index("gx")
    return here > 0, here < lax.axis_size("gx") - 1


def prepare(first, last, soft, pull, raw, g, k, state0):
    planes, ny, nz = soft.shape
    inside = in_grid()
    lane = lax.broadcasted_iota(jnp.int32, (ny, nz), 1)
    row = lax.broadcasted_iota(jnp.int32, (ny, nz), 0)
    inner = (row > 0) & (row < ny - 1)

    def step(at):
        center = soft[at]
        sides = [
            soft[at + 1],
            soft[at - 1],
            pltpu.roll(center, ny - 1, 0),
            pltpu.roll(center, 1, 0),
            lane_up(center, OUTSIDE),
            lane_down(center, OUTSIDE),
        ]
        outside = ((at < HALO) & ~inside[0]) | ((at >= planes - HALO) & ~inside[1])
        inverse = jnp.where(inner & ~outside, lam_inverse(center, sum(sides)), 0.0)
        eighth = 0.125 * inverse
        for j in range(6):
            face = eighth * (center + sides[j])
            if j == 4:
                face = jnp.where(lane == nz - 1, 0.0, face)
            if j == 5:
                face = jnp.where(lane == 0, 0.0, face)
            g[j, at] = face
        k[0, at] = inverse * pull[0, at + 1]
        k[1, at] = -inverse * pull[0, at - 1]
        k[2, at] = inverse * pltpu.roll(pull[1, at], ny - 1, 0)
        k[3, at] = -inverse * pltpu.roll(pull[1, at], 1, 0)
        k[4, at] = inverse * lane_up(pull[2, at], 0.0)
        k[5, at] = -inverse * lane_down(pull[2, at], 0.0)
        for c in range(3):
            state0[1 + c, at] = inverse * raw[c, at]

    by_pairs(first, last, step)


def reach_of(grad, count):
    square = sum(part * part for part in grad)
    scale = 1.0 / jnp.maximum(square, NORMAL_FLOOR)
    power = 1.0 - RELAX_RATE * (1.0 + NORMAL_WEIGHT * square * scale)
    series = 1.0 + power
    for _ in range(2):
        power = power * power
        series = series * (1.0 + power)
    power = power * power
    repeats = jnp.ones_like(power)
    for level in range(1, 4):
        repeats = jnp.where(count > level, 1.0 + power * repeats, repeats)
    return (RELAX_RATE * NORMAL_WEIGHT * scale) * (series * repeats)


def slopes(first, last, count, less, grads):
    ny = less.shape[1]

    def step(at):
        own = less[at]
        grad = [
            0.5 * (less[at + 1] - less[at - 1]),
            0.5 * (pltpu.roll(own, ny - 1, 0) - pltpu.roll(own, 1, 0)),
            0.5 * (lane_up(own, -1.0) - lane_down(own, -1.0)),
        ]
        for c in range(3):
            grads[c, at - HALO] = grad[c]
        grads[3, at - HALO] = reach_of(grad, count)

    by_pairs(first, last, step)


def first_sweep(ranges, state0, state1, g, k, mu_scale):
    (c1, c2), _, _ = weights()

    def advance(at, f, own, moved):
        state1[f, at] = (1.0 + c1) * own + c2 * moved

    for first, last in ranges:
        sweep(first, last, state0, g, k, mu_scale, None, advance)


def inner_kernel(
    damage, strain, seed_damage, seed_disp, less, soft, pull, mu_scale, raw, g, k, state0, state1
):
    nx = damage.shape[0]

    def fill(i, _):
        at = HALO + i
        own = damage[i]
        sx, sy, sz = strain[0, i], strain[1, i], strain[2, i]
        soft[at] = soft_of(own)
        own = own - 1.0
        less[at] = own
        pull[0, at] = own * sx
        pull[1, at] = own * sy
        pull[2, at] = own * sz
        mu_inv = mu_inverse(sx, sy, sz)
        mu_scale[at] = 0.25 * mu_inv
        state0[0, at] = mu_inv * seed_damage[i]
        for c in range(3):
            raw[c, at] = seed_disp[c, i]
        return 0

    lax.fori_loop(0, nx, fill, 0)
    low, high = HALO, HALO + nx
    prepare(low + 1, high - 1, soft, pull, raw, g, k, state0)
    first_sweep([(low + 2, high - 2)], state0, state1, g, k, mu_scale)


def sides_kernel(
    work, near, near_late, far, far_late,
    less_in, soft_in, pull_in, scale_in, raw_in, g_in, k_in, state0_in, state1_in,
    less, soft, pull, mu_scale, raw, g, k, state0, state1, grads,
):
    nx = soft.shape[0] - 2 * HALO
    low, high = HALO, HALO + nx
    inside = in_grid()
    for s in range(2):
        x_in, late = received_x(near, far, s), received_x(near_late, far_late, s)
        for depth in range(4):
            at = low - 1 - depth if s == 0 else high + depth
            own = late(LATE_DAMAGE) if depth == 3 else x_in(X_DAMAGE + depth)
            soft[at] = soft_of(own)
            if depth == 3:
                continue
            own = own - 1.0
            if depth == 0:
                less[at] = own
            if depth == 2:
                pull[0, at] = own * late(LATE_PULL)
                state0[0, at] = late(LATE_MU)
            else:
                pulls = [x_in(X_PULL + 2 * c + depth) for c in range(3)]
                mu_scale[at] = jnp.where(inside[s], 0.25 * mu_inverse(*pulls), 0.0)
                state0[0, at] = x_in(X_MU + depth)
            for c in range(3):
                if depth == 2:
                    raw[c, at] = late(LATE_SOURCE + c)
                else:
                    pull[c, at] = own * pulls[c]
                    raw[c, at] = x_in(X_SOURCE + 2 * c + depth)

    for first, last in ((low - 3, low + 1), (high - 1, high + 3)):
        prepare(first, last, soft, pull, raw, g, k, state0)
    slopes(low, high, work[0, 0], less, grads)
    first_sweep([(low - 2, low + 2), (high - 2, high + 2)], state0, state1, g, k, mu_scale)


def edges_kernel(
    soft, pull, mu_scale, raw, g, state0, state1, y_pal, y_other, c_pal, c_other,
    sent_pal, sent_other, sent_near, coefficients, firsts, seconds, outer,
    fields, sent_low, sent_high, x_low, x_high,
):
    planes, ny, nz = soft.shape
    nx = planes - 2 * HALO
    (c1, c2), (d1, d2), _ = weights()
    lane = lax.broadcasted_iota(jnp.int32, (planes, nz), 1)
    plane = lax.broadcasted_iota(jnp.int32, (planes, nz), 0)
    here, there = lax.axis_index("gx"), lax.axis_index("gy")
    in_x = ((plane >= HALO) | (here > 0)) & ((plane < HALO + nx) | (here < lax.axis_size("gx") - 1))
    in_y = (there > 0, there < lax.axis_size("gy") - 1)

    def around_x(value):
        return [pltpu.roll(value, planes - 1, 0), pltpu.roll(value, 1, 0)]

    def around_z(value, fill):
        return [lane_up(value, fill), lane_down(value, fill)]

    for s, sent in enumerate((sent_low, sent_high)):
        field = fields.at[s]
        y_in, c_in = received_y(y_pal, y_other, s), received_y(c_pal, c_other, s)
        e0, e1 = edge_row(s, ny, 0), edge_row(s, ny, 1)

        def ordered(inward, outward):
            return [inward, outward] if s == 0 else [outward, inward]

        row = 0
        for f in range(Y_FIELDS):
            field[f, HALO : HALO + nx, :] = y_in(f * nx, nx)
            count, shift = (Y_HALO[f], 0) if f < Y_KNOWN else (1, 1)
            behind = HALO - count - 1 + shift
            for at in (behind, planes - 1 - behind):
                field[f, at : at + 1, :] = c_in(2 * CORNER_ROWS + f, 1)
            if count == 0:
                continue
            field[f, HALO - count + shift : HALO + shift, :] = c_in(row, count)
            high = HALO + nx - shift
            field[f, high : high + count, :] = c_in(CORNER_ROWS + row, count)
            row += count

        soft_1, soft_2 = soft_of(field[0]), soft_of(field[1])
        soft_e0, soft_e1 = soft[:, e0, :], soft[:, e1, :]

        def total(center, inward, outward):
            return sum(around_x(center) + [inward, outward] + around_z(center, OUTSIDE))

        inverse_1 = lam_inverse(soft_1, total(soft_1, soft_e0, soft_2))
        inverse_1 = jnp.where(in_x & in_y[s], inverse_1, 0.0)
        lam_1 = [inverse_1 * field[5 + c] for c in range(3)]
        inverse_e0 = jnp.where(in_x, lam_inverse(soft_e0, total(soft_e0, soft_e1, soft_1)), 0.0)
        lam_e0 = [inverse_e0 * raw[c, :, e0, :] for c in range(3)]
        mu_1, wy_1 = field[3], field[2]
        mu_e0, mu_e1 = state0[0, :, e0, :], state0[0, :, e1, :]
        lam_e1 = [state0[1 + c, :, e1, :] for c in range(3)]

        def coefficients_of(center, inverse, inward, outward, wx, wy, wz):
            sides = around_x(center) + ordered(inward, outward) + around_z(center, OUTSIDE)
            eighth = 0.125 * inverse
            faces = [eighth * (center + side) for side in sides]
            faces[4] = jnp.where(lane == nz - 1, 0.0, faces[4])
            faces[5] = jnp.where(lane == 0, 0.0, faces[5])
            pulls = around_x(wx) + wy + around_z(wz, 0.0)
            return faces, [inverse * w if j % 2 == 0 else -inverse * w for j, w in enumerate(pulls)]

        def moved_of(faces, pulls, scale, own, inward, outward):
            sides = [
                around_x(own[f]) + ordered(inward[f], outward[f]) + around_z(own[f], 0.0) for f in range(4)
            ]
            moved = [scale * sum(sides[0])]
            for c in range(3):
                part = sum(faces[j] * sides[1 + c][j] for j in range(6))
                moved.append(part + pulls[2 * c] * sides[0][2 * c] + pulls[2 * c + 1] * sides[0][2 * c + 1])
            return moved

        first_1 = [jnp.where(in_x, field[Y_KNOWN] + c2 * field[4] * mu_e0, 0.0)]
        sides = around_x(soft_1) + around_z(soft_1, OUTSIDE) + [soft_e0]
        faces = [0.125 * (soft_1 + side) for side in sides]
        wy_e0 = pull[1, :, e0, :] * mu_e0
        own_1 = [mu_1] + lam_1
        own_e0 = [mu_e0] + lam_e0
        for c in range(3):
            sides = around_x(lam_1[c]) + around_z(lam_1[c], 0.0) + [lam_e0[c]]
            lacked = sum(faces[j] * sides[j] for j in range(5))
            if c == 1:
                lacked += wy_e0 if s == 0 else -wy_e0
            first_1.append(inverse_1 * (field[Y_KNOWN + 1 + c] + c2 * lacked))

        scale_e0 = mu_scale[:, e0, :]
        wy = ordered(pull[1, :, e1, :], wy_1)
        faces, pulls = coefficients_of(
            soft_e0, inverse_e0, soft_e1, soft_1, pull[0, :, e0, :], wy, pull[2, :, e0, :]
        )
        moved = moved_of(faces, pulls, scale_e0, own_e0, [mu_e1] + lam_e1, own_1)
        first_e0 = [(1.0 + c1) * own_e0[f] + c2 * moved[f] for f in range(4)]

        outward_face = g[3 if s == 0 else 2, :, e1, :]
        first_e1 = [state1[0, :, e1, :]]
        for c in range(3):
            first_e1.append(state1[1 + c, :, e1, :] + c2 * outward_face * lam_e0[c])

        moved = moved_of(faces, pulls, scale_e0, first_e0, first_e1, first_1)
        for f in range(4):
            second = first_e0[f] + (d1 - d2) * (first_e0[f] - own_e0[f]) + d2 * moved[f]
            sent[f * nx : (f + 1) * nx, :] = second[HALO : HALO + nx, :]
            x_low[4 * s + f : 4 * s + f + 1, :] = second[HALO : HALO + 1, :]
            x_high[4 * s + f : 4 * s + f + 1, :] = second[HALO + nx - 1 : HALO + nx, :]
            firsts[s, f] = first_e0[f]
            outer[s, f] = first_1[f]
        for j in range(6):
            coefficients[s, j] = faces[j]
            coefficients[s, 6 + j] = pulls[j]
        for c in range(3):
            coefficients[s, 12 + c] = lam_e0[c]
            seconds[s, c] = first_e1[1 + c]
    deal(sent_pal, sent_other, sent_low, sent_high)
    sent_near[...] = jnp.where(even("gx"), x_high[...], x_low[...])


def sweep(first, last, state, g, k, mu_scale, rows, advance, finish=None):
    _, ny, nz = mu_scale.shape
    lane = lax.broadcasted_iota(jnp.int32, (ny, nz), 1)
    if rows is None:

        def rows(s, f, at):
            return 0.0

    def plane(at):
        def around(f):
            own = state[f, at]
            return own, [
                state[f, at + 1],
                state[f, at - 1],
                row_up(own, rows(1, f, at)),
                row_down(own, rows(0, f, at)),
                pltpu.roll(own, nz - 1, 1),
                pltpu.roll(own, 1, 1),
            ]

        mu, mu_sides = around(0)
        ends = [
            jnp.where(lane == nz - 1, 0.0, mu_sides[4]),
            jnp.where(lane == 0, 0.0, mu_sides[5]),
        ]
        results = [advance(at, 0, mu, mu_scale[at] * sum(mu_sides[:4] + ends))]
        faces = [g[j, at] for j in range(6)]
        for c in range(3):
            lam, lam_sides = around(1 + c)
            moved = sum(faces[j] * lam_sides[j] for j in range(6))
            moved += k[2 * c, at] * mu_sides[2 * c] + k[2 * c + 1, at] * mu_sides[2 * c + 1]
            results.append(advance(at, 1 + c, lam, moved))
        if finish is not None:
            finish(at - HALO, results)

    by_pairs(first, last, plane)


def wait_kernel(
    work, less, grads, y_pal, y_other,
    mu_scale, coefficients, firsts, seconds, outer, g_in, k_in, state0_in, state1_in,
    out_mu, out_lam, edges, g, k, state0, state1,
    state2, states, mu, lam, sems,
):
    _, nx, ny, _ = grads.shape
    planes = nx + 2 * HALO
    _, (d1, d2), (c1, c2) = weights()
    held = slice(HALO - 2, HALO + nx + 2)
    for s in range(2):
        e0, e1 = edge_row(s, ny, 0), edge_row(s, ny, 1)
        for j in range(6):
            g[j, held, e0, :] = coefficients[s, j, held, :]
            k[j, held, e0, :] = coefficients[s, 6 + j, held, :]
        for c in range(3):
            state0[1 + c, held, e0, :] = coefficients[s, 12 + c, held, :]
            state1[1 + c, held, e1, :] = seconds[s, c, held, :]
        for f in range(4):
            state1[f, held, e0, :] = firsts[s, f, held, :]

    def rows(s, f, at):
        return outer[s, f, pl.ds(at, 1), :]

    def advance_2(at, f, own, moved):
        state2[f, at] = own + (d1 - d2) * (own - state0[f, at]) + d2 * moved

    sweep(HALO - 1, HALO + nx + 1, state1, g, k, mu_scale, rows, advance_2)
    nothing = jnp.zeros((1, state2.shape[3]), F32)
    at = jnp.where(even("gx"), HALO + nx, HALO - 1)
    for s in range(2):
        e0 = edge_row(s, ny, 0)
        for f in range(4):
            state2[f, at, e0 : e0 + 1, :] = nothing

    def advance_3(at, f, own, moved):
        return own + c1 * (own - state1[f, at]) + c2 * (state0[f, at] - own + moved)

    def copies(part):
        planes = pl.ds(part * (nx // 4), nx // 4)
        return (
            pltpu.make_async_copy(mu.at[planes], out_mu.at[planes], sems.at[0, part]),
            pltpu.make_async_copy(lam.at[:, planes], out_lam.at[:, planes], sems.at[1, part]),
        )

    def finish(i, results):
        mu[i] = results[0]
        along = grads[3, i] * sum(grads[c, i] * results[1 + c] for c in range(3))
        for c in range(3):
            lam[c, i] = results[1 + c] - along * grads[c, i]
            states[c, i] = results[1 + c]

    for part in range(4):
        start = HALO + part * (nx // 4)
        sweep(start, start + nx // 4, state2, g, k, mu_scale, None, advance_3, finish)
        for copy in copies(part):
            copy.start()

    for s in range(2):
        y_in = received_y(y_pal, y_other, s)
        e0, e1 = edge_row(s, ny, 0), edge_row(s, ny, 1)
        own = less[HALO : HALO + nx, e0, :]
        inward, outward = less[HALO : HALO + nx, e1, :], y_in(0, nx) - 1.0
        grad = [
            0.5 * (less[HALO + 1 : HALO + nx + 1, e0, :] - less[HALO - 1 : HALO + nx - 1, e0, :]),
            0.5 * (inward - outward if s == 0 else outward - inward),
            0.5 * (lane_up(own, -1.0) - lane_down(own, -1.0)),
        ]
        for c in range(3):
            edges[s, c] = grad[c]
            edges[s, 4 + c] = states[c, :, e0, :]
        edges[s, 3] = reach_of(grad, work[0, 0])
        edges[s, 7] = mu[:, e0, :]

    for part in range(4):
        for copy in copies(part):
            copy.wait()


def last_kernel(
    mu_scale, coefficients, edges, y_pal, y_other, x_near, mu_in, lam_in,
    out_mu, out_lam,
    rows, sems,
):
    nx, ny, nz = out_mu.shape
    inner = slice(HALO, HALO + nx)
    copies = []
    _, _, (_, c2) = weights()
    for s in range(2):
        y_in = received_y(y_pal, y_other, s)
        e0 = edge_row(s, ny, 0)
        outward = 3 if s == 0 else 2

        def got(f):
            return y_in(f * nx, nx)

        ends_x = []
        for side, at, way in ((0, HALO, 1), (1, HALO + nx - 1, 0)):
            got_x = jnp.where(even("gx") == (side == 1), x_near[4 * s : 4 * s + 4, :], 0.0)
            sides_x = [got_x[f : f + 1, :] for f in range(4)]
            face = c2 * coefficients[s, way, at : at + 1, :]
            end = [c2 * mu_scale[at, e0 : e0 + 1, :] * sides_x[0]] + [face * sides_x[1 + c] for c in range(3)]
            end[1] += c2 * coefficients[s, 6 + way, at : at + 1, :] * sides_x[0]
            ends_x.append(end)
        plane = lax.broadcasted_iota(jnp.int32, (nx, nz), 0)

        def from_x(f):
            return jnp.where(plane == 0, ends_x[0][f], jnp.where(plane == nx - 1, ends_x[1][f], 0.0))

        rows[s, 0] = edges[s, 7] + c2 * mu_scale[inner, e0, :] * got(0) + from_x(0)
        face = c2 * coefficients[s, outward, inner, :]
        ends = []
        for c in range(3):
            end = edges[s, 4 + c] + face * got(1 + c) + from_x(1 + c)
            if c == 1:
                end += c2 * coefficients[s, 6 + outward, inner, :] * got(0)
            ends.append(end)
        along = edges[s, 3] * sum(edges[s, c] * ends[c] for c in range(3))
        for c in range(3):
            rows[s, 1 + c] = ends[c] - along * edges[s, c]
        copies.append(pltpu.make_async_copy(rows.at[s, 0], out_mu.at[:, e0, :], sems.at[s, 0]))
        for c in range(3):
            copies.append(pltpu.make_async_copy(rows.at[s, 1 + c], out_lam.at[c, :, e0, :], sems.at[s, 1 + c]))
        for copy in copies[4 * s :]:
            copy.start()
    for copy in copies:
        copy.wait()


VMEM = pl.BlockSpec(memory_space=pltpu.VMEM)
SMEM = pl.BlockSpec(memory_space=pltpu.SMEM)
HBM = pl.BlockSpec(memory_space=pltpu.HBM)
ANY = pl.BlockSpec(memory_space=pl.ANY)
MIB = 1024 * 1024


def call(kernel, ins, outs, scratch=(), in_specs=None, out_specs=None, aliases=None, grant=24 * MIB):
    return pl.pallas_call(
        kernel,
        out_shape=[jax.ShapeDtypeStruct(shape, F32) for shape in outs],
        in_specs=in_specs or [VMEM] * len(ins),
        out_specs=out_specs or [VMEM] * len(outs),
        scratch_shapes=[pltpu.VMEM(shape, F32) if isinstance(shape, tuple) else shape for shape in scratch],
        input_output_aliases=aliases or {},
        compiler_params=pltpu.CompilerParams(vmem_limit_bytes=grant),
    )(*ins)


def trade(value, axis, first):
    pairs = [(i, i + 1) for i in range(first, lax.axis_size(axis) - 1, 2)]
    return lax.ppermute(value, axis, pairs + [(j, i) for i, j in pairs])


def body(damage, strain, seed_damage, seed_disp, brick_work):
    nx, ny, nz = damage.shape
    plane = (ny, nz)
    brick = (nx,) + plane
    bricks = (3,) + brick
    framed = (nx + 2 * HALO,) + plane
    state = (4,) + framed
    row = (nx + 2 * HALO, nz)
    fields = (damage, strain, seed_damage, seed_disp)

    y_rows = (Y_FIELDS * nx, nz)
    x_faces = [(X_SLOTS,) + plane, (LATE_SLOTS,) + plane]
    faces = [y_rows] * 2 + x_faces * 2
    pal, other, near, near_late, far, far_late = call(
        faces_kernel, fields, faces,
        [brick, bricks, brick, bricks] + faces + [pltpu.SemaphoreType.DMA((4,)), pltpu.SemaphoreType.DMA((6,))],
        in_specs=[HBM] * 4, out_specs=[HBM] * 6, grant=56 * MIB,
    )
    y_in = (trade(pal, "gy", 0), trade(other, "gy", 1))
    far, far_late = trade(far, "gx", 1), trade(far_late, "gx", 1)
    near, near_late = trade(near, "gx", 0), trade(near_late, "gx", 0)
    inner = tuple(call(
        inner_kernel, fields,
        [framed, framed, (3,) + framed, framed, (3,) + framed, (6,) + framed, (6,) + framed, state, state],
    ))
    c_rows = (2 * CORNER_ROWS + MORE_ROWS, nz)
    pal, other = call(
        corners_kernel, fields + (near, far, inner[0]), [c_rows] * 2,
        [(4, 15) + plane, c_rows, c_rows, (2, 2, MORE_ROWS, nz)], in_specs=[VMEM] * 6 + [ANY],
    )
    c_in = (trade(pal, "gy", 0), trade(other, "gy", 1))
    less, soft, pull, mu_scale, raw, g, k, state0, state1, grads = call(
        sides_kernel, (brick_work, near, near_late, far, far_late) + inner,
        [part.shape for part in inner] + [(4,) + brick],
        in_specs=[SMEM] + [VMEM] * 13, aliases={5 + part: part for part in range(9)},
    )
    sent = (4 * nx, nz)
    x_sent = (8, nz)
    pal, other, near, coefficients, firsts, seconds, outer = call(
        edges_kernel, (soft, pull, mu_scale, raw, g, state0, state1) + y_in + c_in,
        [sent] * 2 + [x_sent] + [(2, 15) + row, (2, 4) + row, (2, 3) + row, (2, 4) + row],
        [(2, Y_FIELDS) + row, sent, sent, x_sent, x_sent],
    )
    halo = (trade(pal, "gy", 0), trade(other, "gy", 1), trade(near, "gx", 0))
    ins = (brick_work, less, grads) + y_in + (mu_scale, coefficients, firsts, seconds, outer, g, k, state0, state1)
    mu, lam, edges, *_ = call(
        wait_kernel, ins,
        [brick, bricks, (2, 8, nx, nz), (6,) + framed, (6,) + framed, state, state],
        [state, bricks, brick, bricks, pltpu.SemaphoreType.DMA((2, 4))],
        out_specs=[HBM] * 2 + [VMEM] * 5,
        in_specs=[SMEM] + [VMEM] * (len(ins) - 1),
        aliases={10: 3, 11: 4, 12: 5, 13: 6},
    )
    out_mu, out_lam = call(
        last_kernel, (mu_scale, coefficients, edges) + halo + (mu, lam),
        [brick, bricks], [(2, 4, nx, nz), pltpu.SemaphoreType.DMA((2, 4))],
        in_specs=[VMEM] * 6 + [HBM] * 2, out_specs=[HBM, HBM], aliases={6: 0, 7: 1},
    )
    return out_mu, out_lam


def solution(mesh):
    placed = (
        P("gx", "gy", None),
        P(None, "gx", "gy", None),
        P("gx", "gy", None),
        P(None, "gx", "gy", None),
        P("gx", "gy"),
    )
    return jax.shard_map(
        body,
        mesh=mesh,
        in_specs=placed,
        out_specs=(P("gx", "gy", None), P(None, "gx", "gy", None)),
        check_vma=False,
    )
```

```python
import functools

import jax
import jax.numpy as jnp
from jax import lax
from jax.experimental import pallas as pl
from jax.experimental.pallas import tpu as pltpu
from jax.sharding import PartitionSpec as P

RELAX_INNER = 8
RESIDUAL_STIFFNESS = 0.001
CENTER_VALUE = 1.0
HALF_WIDTH = 0.75
NORMAL_WEIGHT = 1.5
RELAX_RATE = 0.5 / RELAX_INNER
NORMAL_FLOOR = 0.05
OUTSIDE = 1.0 + RESIDUAL_STIFFNESS
F32 = jnp.float32


def weights():
    ratio = CENTER_VALUE / HALF_WIDTH
    rho = 1.0 / ratio
    found = []
    for _ in range(3):
        rho_next = 1.0 / (2.0 * ratio - rho)
        found.append((rho_next * rho, 2.0 * rho_next / HALF_WIDTH))
        rho = rho_next
    return found


def by_pairs(first, last, step):
    width = 2 if (last - first) % 2 == 0 else 1

    def turn(i, _):
        for part in range(width):
            step(first + width * i + part)
        return 0

    lax.fori_loop(0, (last - first) // width, turn, 0)


def soft_of(damage):
    return (1.0 - damage) ** 2 + RESIDUAL_STIFFNESS


def row_up(plane, beyond):
    rows = plane.shape[0]
    at = lax.broadcasted_iota(jnp.int32, plane.shape, 0)
    return jnp.where(at == rows - 1, beyond, pltpu.roll(plane, rows - 1, 0))


def row_down(plane, beyond):
    at = lax.broadcasted_iota(jnp.int32, plane.shape, 0)
    return jnp.where(at == 0, beyond, pltpu.roll(plane, 1, 0))


def lane_up(plane, beyond):
    cells = plane.shape[1]
    at = lax.broadcasted_iota(jnp.int32, plane.shape, 1)
    return jnp.where(at == cells - 1, beyond, pltpu.roll(plane, cells - 1, 1))


def lane_down(plane, beyond):
    at = lax.broadcasted_iota(jnp.int32, plane.shape, 1)
    return jnp.where(at == 0, beyond, pltpu.roll(plane, 1, 1))


def mu_inverse(ex, ey, ez):
    return 1.0 / (2.0 + (ex * ex + ey * ey + ez * ez))


def lam_inverse(center, total):
    return 1.0 / (0.5 + 0.125 * (6.0 * center + total))


HALO = 4
X_DAMAGE, X_PULL, X_MU, X_SOURCE, X_SLOTS = 0, 3, 9, 11, 17
LATE_DAMAGE, LATE_PULL, LATE_MU, LATE_SOURCE, LATE_SLOTS = 0, 1, 2, 3, 6
Y_HALO = (2, 1, 1, 1, 0, 1, 1, 1)
Y_KNOWN, Y_FIELDS = 8, 12
CORNER_ROWS = sum(Y_HALO) + 4
MORE_ROWS = 12


def edge_row(s, ny, depth):
    return depth if s == 0 else ny - 1 - depth


def known_of(s, damages, pulls, behind_pull, mus, sources, behind):
    planes = damages[0].shape[0]
    (c1, c2), _, _ = weights()
    soft = [soft_of(part) for part in damages]
    less = damages[0] - 1.0
    wx, wy, wz = (less * pull for pull in pulls)
    wy_behind = (damages[1] - 1.0) * behind_pull

    def across(value):
        return pltpu.roll(value, planes - 1, 0), pltpu.roll(value, 1, 0)

    def along(value, fill):
        return lane_up(value, fill), lane_down(value, fill)

    total = soft[0] + soft[2] + sum(across(soft[1])) + sum(along(soft[1], OUTSIDE))
    inverse = lam_inverse(soft[1], total)
    face = 0.125 * (soft[0] + soft[1])
    scale = 0.25 * mu_inverse(*pulls)
    known = [(1.0 + c1) * mus[0] + c2 * scale * (mus[1] + sum(across(mus[0])) + sum(along(mus[0], 0.0)))]
    x_up, x_down = across(wx * mus[0])
    z_up, z_down = along(wz * mus[0], 0.0)
    y_behind = wy_behind * mus[1]
    transfers = (x_up - x_down, y_behind if s == 0 else -y_behind, z_up - z_down)
    for c in range(3):
        known.append((1.0 + c1) * sources[c] + c2 * (face * (inverse * behind[c]) + transfers[c]))
    return scale, wy, known


def put_rows(s, put, damage, strain, seed_damage, seed_disp):
    ny = damage.shape[1]
    first, second, third = (edge_row(s, ny, depth) for depth in range(3))
    damages = [damage[:, row, :] for row in (first, second, third)]
    pulls = [strain[c, :, first, :] for c in range(3)]
    pulls_behind = [strain[c, :, second, :] for c in range(3)]
    mus = [
        seed_damage[:, first, :] * mu_inverse(*pulls),
        seed_damage[:, second, :] * mu_inverse(*pulls_behind),
    ]
    sources = [seed_disp[c, :, first, :] for c in range(3)]
    behind = [seed_disp[c, :, second, :] for c in range(3)]
    scale, wy, known = known_of(s, damages, pulls, pulls_behind[1], mus, sources, behind)
    for slot, value in enumerate(damages[:2] + [wy, mus[0], scale] + sources + known):
        put(slot, value)


def even(axis):
    return lax.rem(lax.axis_index(axis), 2) == 0


def faces_kernel(
    damage_in, strain_in, seed_in, sources_in, pal_out, other_out, near_out, near_late_out, far_out, far_late_out,
    damage, strain, seed_damage, seed_disp, pal, other, near, near_late, far, far_late, sems, out_sems,
):
    nx = damage.shape[0]
    edges, middle = (pl.ds(0, HALO), pl.ds(nx - HALO, HALO)), (pl.ds(HALO, nx - 2 * HALO),)
    pairs = ((damage_in, damage), (seed_in, seed_damage), (strain_in, strain), (sources_in, seed_disp))
    copies = []
    for planes in edges + middle:
        for source, target in pairs:
            at = planes if len(source.shape) == 3 else (slice(None), planes)
            copies.append(pltpu.make_async_copy(source.at[at], target.at[at], sems.at[len(copies)]))
    for copy in copies:
        copy.start()
    sent = []

    def send(source, target):
        sent.append(pltpu.make_async_copy(source, target, out_sems.at[len(sent)]))
        sent[-1].start()

    def put_planes(out, late, high):
        for depth in range(4):
            at = jnp.where(high, nx - 1 - depth, depth)
            if depth == 3:
                late[LATE_DAMAGE] = damage[at]
                continue
            out[X_DAMAGE + depth] = damage[at]
            pulls = [strain[c, at] for c in range(3)]
            mu = seed_damage[at] * mu_inverse(*pulls)
            if depth == 2:
                late[LATE_PULL] = pulls[0]
                late[LATE_MU] = mu
            else:
                out[X_MU + depth] = mu
            for c in range(3):
                if depth == 2:
                    late[LATE_SOURCE + c] = seed_disp[c, at]
                else:
                    out[X_PULL + 2 * c + depth] = pulls[c]
                    out[X_SOURCE + 2 * c + depth] = seed_disp[c, at]

    for copy in copies[:8]:
        copy.wait()
    for out, late, target, late_target, high in (
        (near, near_late, near_out, near_late_out, even("gx")),
        (far, far_late, far_out, far_late_out, ~even("gx")),
    ):
        put_planes(out, late, high)
        send(out, target)
        send(late, late_target)
    for copy in copies[8:]:
        copy.wait()
    for out, target, first in ((pal, pal_out, True), (other, other_out, False)):

        def put(slot, value):
            out[slot * nx : (slot + 1) * nx, :] = value

        for s in range(2):

            @pl.when(even("gy") == ((s == 1) == first))
            def _():
                put_rows(s, put, damage, strain, seed_damage, seed_disp)

        send(out, target)
    for copy in sent:
        copy.wait()


def received_x(near, far, side):
    from_near = even("gx") == (side == 1)

    def plane(slot, row=None):
        at = slot if row is None else (slice(slot, slot + 1), row)
        return jnp.where(from_near, near[at], far[at])

    return plane


def received_y(pal, other, side):
    from_pal = even("gy") == (side == 1)
    return lambda first, count: jnp.where(from_pal, pal[first : first + count, :], other[first : first + count, :])


def deal(pal, other, low, high):
    first = even("gy")
    low, high = low[...], high[...]
    pal[...] = jnp.where(first, high, low)
    other[...] = jnp.where(first, low, high)


def corners_kernel(
    damage, strain, seed_damage, seed_disp, near, far, _, pal, other, field, low, high, more
):
    nx, ny, _ = damage.shape
    for s, out in enumerate((low, high)):
        first, second, third = (edge_row(s, ny, depth) for depth in range(3))
        for side in range(2):
            x_in = received_x(near, far, side)
            ours = slice(3, 8) if side == 0 else slice(0, 5)
            planes = slice(0, 5) if side == 0 else slice(nx - 5, nx)

            def put_x(slot, first, count, row):
                for far_off in range(count):
                    at = 2 - far_off if side == 0 else 5 + far_off
                    field[slot, at : at + 1, :] = x_in(first + far_off, row)

            for depth, row in enumerate((first, second, third)):
                field[depth, ours, :] = damage[planes, row, :]
                put_x(depth, X_DAMAGE, 3, row)
            for depth, row in enumerate((first, second)):
                pulls = [strain[c, planes, row, :] for c in range(3)]
                for c in range(3):
                    if depth == 0:
                        field[3 + c, ours, :] = pulls[c]
                        put_x(3 + c, X_PULL + 2 * c, 2, row)
                    field[9 + 3 * depth + c, ours, :] = seed_disp[c, planes, row, :]
                    put_x(9 + 3 * depth + c, X_SOURCE + 2 * c, 2, row)
                if depth == 1:
                    field[6, ours, :] = pulls[1]
                    put_x(6, X_PULL + 2, 2, row)
                field[7 + depth, ours, :] = seed_damage[planes, row, :] * mu_inverse(*pulls)
                put_x(7 + depth, X_MU, 2, row)
            got = [field[slot] for slot in range(15)]
            scale, wy, known = known_of(s, got[:3], got[3:6], got[6], got[7:9], got[9:12], got[12:15])
            row = side * CORNER_ROWS
            for slot, value in enumerate(got[:2] + [wy, got[7], scale] + got[9:12]):
                count = Y_HALO[slot]
                behind = 2 - count if side == 0 else 5 + count
                more[side, slot : slot + 1, :] = value[behind : behind + 1, :]
                if count == 0:
                    continue
                start = 3 - count if side == 0 else 5
                out[row : row + count, :] = value[start : start + count, :]
                row += count
            for slot, value in enumerate(known):
                edge, behind = (3, 2) if side == 0 else (4, 5)
                out[row : row + 1, :] = value[edge : edge + 1, :]
                slot += Y_KNOWN
                more[side, slot : slot + 1, :] = value[behind : behind + 1, :]
                row += 1
        out[2 * CORNER_ROWS :, :] = jnp.where(even("gx"), more[0], more[1])
    deal(pal, other, low, high)


def in_grid():
    here = lax.axis_index("gx")
    return here > 0, here < lax.axis_size("gx") - 1


def prepare(first, last, soft, pull, raw, g, k, state0):
    planes, ny, nz = soft.shape
    inside = in_grid()
    lane = lax.broadcasted_iota(jnp.int32, (ny, nz), 1)
    row = lax.broadcasted_iota(jnp.int32, (ny, nz), 0)
    inner = (row > 0) & (row < ny - 1)

    def step(at):
        center = soft[at]
        sides = [
            soft[at + 1],
            soft[at - 1],
            pltpu.roll(center, ny - 1, 0),
            pltpu.roll(center, 1, 0),
            lane_up(center, OUTSIDE),
            lane_down(center, OUTSIDE),
        ]
        outside = ((at < HALO) & ~inside[0]) | ((at >= planes - HALO) & ~inside[1])
        inverse = jnp.where(inner & ~outside, lam_inverse(center, sum(sides)), 0.0)
        eighth = 0.125 * inverse
        for j in range(6):
            face = eighth * (center + sides[j])
            if j == 4:
                face = jnp.where(lane == nz - 1, 0.0, face)
            if j == 5:
                face = jnp.where(lane == 0, 0.0, face)
            g[j, at] = face
        k[0, at] = inverse * pull[0, at + 1]
        k[1, at] = -inverse * pull[0, at - 1]
        k[2, at] = inverse * pltpu.roll(pull[1, at], ny - 1, 0)
        k[3, at] = -inverse * pltpu.roll(pull[1, at], 1, 0)
        k[4, at] = inverse * lane_up(pull[2, at], 0.0)
        k[5, at] = -inverse * lane_down(pull[2, at], 0.0)
        for c in range(3):
            state0[1 + c, at] = inverse * raw[c, at]

    by_pairs(first, last, step)


def reach_of(grad, count):
    square = sum(part * part for part in grad)
    scale = 1.0 / jnp.maximum(square, NORMAL_FLOOR)
    power = 1.0 - RELAX_RATE * (1.0 + NORMAL_WEIGHT * square * scale)
    series = 1.0 + power
    for _ in range(2):
        power = power * power
        series = series * (1.0 + power)
    power = power * power
    repeats = jnp.ones_like(power)
    for level in range(1, 4):
        repeats = jnp.where(count > level, 1.0 + power * repeats, repeats)
    return (RELAX_RATE * NORMAL_WEIGHT * scale) * (series * repeats)


def slopes(first, last, count, less, grads):
    ny = less.shape[1]

    def step(at):
        own = less[at]
        grad = [
            0.5 * (less[at + 1] - less[at - 1]),
            0.5 * (pltpu.roll(own, ny - 1, 0) - pltpu.roll(own, 1, 0)),
            0.5 * (lane_up(own, -1.0) - lane_down(own, -1.0)),
        ]
        for c in range(3):
            grads[c, at - HALO] = grad[c]
        grads[3, at - HALO] = reach_of(grad, count)

    by_pairs(first, last, step)


def first_sweep(ranges, state0, state1, g, k, mu_scale):
    (c1, c2), _, _ = weights()

    def advance(at, f, own, moved):
        state1[f, at] = (1.0 + c1) * own + c2 * moved

    for first, last in ranges:
        sweep(first, last, state0, g, k, mu_scale, None, advance)


def inner_kernel(
    damage, strain, seed_damage, seed_disp, less, soft, pull, mu_scale, raw, g, k, state0, state1
):
    nx = damage.shape[0]

    def fill(i, _):
        at = HALO + i
        own = damage[i]
        sx, sy, sz = strain[0, i], strain[1, i], strain[2, i]
        soft[at] = soft_of(own)
        own = own - 1.0
        less[at] = own
        pull[0, at] = own * sx
        pull[1, at] = own * sy
        pull[2, at] = own * sz
        mu_inv = mu_inverse(sx, sy, sz)
        mu_scale[at] = 0.25 * mu_inv
        state0[0, at] = mu_inv * seed_damage[i]
        for c in range(3):
            raw[c, at] = seed_disp[c, i]
        return 0

    lax.fori_loop(0, nx, fill, 0)
    low, high = HALO, HALO + nx
    prepare(low + 1, high - 1, soft, pull, raw, g, k, state0)
    first_sweep([(low + 2, high - 2)], state0, state1, g, k, mu_scale)


def sides_kernel(
    work, near, near_late, far, far_late,
    less_in, soft_in, pull_in, scale_in, raw_in, g_in, k_in, state0_in, state1_in,
    less, soft, pull, mu_scale, raw, g, k, state0, state1, grads,
):
    nx = soft.shape[0] - 2 * HALO
    low, high = HALO, HALO + nx
    inside = in_grid()
    for s in range(2):
        x_in, late = received_x(near, far, s), received_x(near_late, far_late, s)
        for depth in range(4):
            at = low - 1 - depth if s == 0 else high + depth
            own = late(LATE_DAMAGE) if depth == 3 else x_in(X_DAMAGE + depth)
            soft[at] = soft_of(own)
            if depth == 3:
                continue
            own = own - 1.0
            if depth == 0:
                less[at] = own
            if depth == 2:
                pull[0, at] = own * late(LATE_PULL)
                state0[0, at] = late(LATE_MU)
            else:
                pulls = [x_in(X_PULL + 2 * c + depth) for c in range(3)]
                mu_scale[at] = jnp.where(inside[s], 0.25 * mu_inverse(*pulls), 0.0)
                state0[0, at] = x_in(X_MU + depth)
            for c in range(3):
                if depth == 2:
                    raw[c, at] = late(LATE_SOURCE + c)
                else:
                    pull[c, at] = own * pulls[c]
                    raw[c, at] = x_in(X_SOURCE + 2 * c + depth)

    for first, last in ((low - 3, low + 1), (high - 1, high + 3)):
        prepare(first, last, soft, pull, raw, g, k, state0)
    slopes(low, high, work[0, 0], less, grads)
    first_sweep([(low - 2, low + 2), (high - 2, high + 2)], state0, state1, g, k, mu_scale)


def edges_kernel(
    soft, pull, mu_scale, raw, g, state0, state1, y_pal, y_other, c_pal, c_other,
    sent_pal, sent_other, sent_near, coefficients, firsts, seconds, outer,
    field, sent_low, sent_high, x_low, x_high,
):
    planes, ny, nz = soft.shape
    nx = planes - 2 * HALO
    (c1, c2), (d1, d2), _ = weights()
    lane = lax.broadcasted_iota(jnp.int32, (planes, nz), 1)
    plane = lax.broadcasted_iota(jnp.int32, (planes, nz), 0)
    here, there = lax.axis_index("gx"), lax.axis_index("gy")
    in_x = ((plane >= HALO) | (here > 0)) & ((plane < HALO + nx) | (here < lax.axis_size("gx") - 1))
    in_y = (there > 0, there < lax.axis_size("gy") - 1)

    def around_x(value):
        return [pltpu.roll(value, planes - 1, 0), pltpu.roll(value, 1, 0)]

    def around_z(value, fill):
        return [lane_up(value, fill), lane_down(value, fill)]

    for s, sent in enumerate((sent_low, sent_high)):
        y_in, c_in = received_y(y_pal, y_other, s), received_y(c_pal, c_other, s)
        e0, e1 = edge_row(s, ny, 0), edge_row(s, ny, 1)

        def ordered(inward, outward):
            return [inward, outward] if s == 0 else [outward, inward]

        row = 0
        for f in range(Y_FIELDS):
            field[f, HALO : HALO + nx, :] = y_in(f * nx, nx)
            count, shift = (Y_HALO[f], 0) if f < Y_KNOWN else (1, 1)
            behind = HALO - count - 1 + shift
            for at in (behind, planes - 1 - behind):
                field[f, at : at + 1, :] = c_in(2 * CORNER_ROWS + f, 1)
            if count == 0:
                continue
            field[f, HALO - count + shift : HALO + shift, :] = c_in(row, count)
            high = HALO + nx - shift
            field[f, high : high + count, :] = c_in(CORNER_ROWS + row, count)
            row += count

        soft_1, soft_2 = soft_of(field[0]), soft_of(field[1])
        soft_e0, soft_e1 = soft[:, e0, :], soft[:, e1, :]

        def total(center, inward, outward):
            return sum(around_x(center) + [inward, outward] + around_z(center, OUTSIDE))

        inverse_1 = lam_inverse(soft_1, total(soft_1, soft_e0, soft_2))
        inverse_1 = jnp.where(in_x & in_y[s], inverse_1, 0.0)
        lam_1 = [inverse_1 * field[5 + c] for c in range(3)]
        inverse_e0 = jnp.where(in_x, lam_inverse(soft_e0, total(soft_e0, soft_e1, soft_1)), 0.0)
        lam_e0 = [inverse_e0 * raw[c, :, e0, :] for c in range(3)]
        mu_1, wy_1 = field[3], field[2]
        mu_e0, mu_e1 = state0[0, :, e0, :], state0[0, :, e1, :]
        lam_e1 = [state0[1 + c, :, e1, :] for c in range(3)]

        def coefficients_of(center, inverse, inward, outward, wx, wy, wz):
            sides = around_x(center) + ordered(inward, outward) + around_z(center, OUTSIDE)
            eighth = 0.125 * inverse
            faces = [eighth * (center + side) for side in sides]
            faces[4] = jnp.where(lane == nz - 1, 0.0, faces[4])
            faces[5] = jnp.where(lane == 0, 0.0, faces[5])
            pulls = around_x(wx) + wy + around_z(wz, 0.0)
            return faces, [inverse * w if j % 2 == 0 else -inverse * w for j, w in enumerate(pulls)]

        def moved_of(faces, pulls, scale, own, inward, outward):
            sides = [
                around_x(own[f]) + ordered(inward[f], outward[f]) + around_z(own[f], 0.0) for f in range(4)
            ]
            moved = [scale * sum(sides[0])]
            for c in range(3):
                part = sum(faces[j] * sides[1 + c][j] for j in range(6))
                moved.append(part + pulls[2 * c] * sides[0][2 * c] + pulls[2 * c + 1] * sides[0][2 * c + 1])
            return moved

        first_1 = [jnp.where(in_x, field[Y_KNOWN] + c2 * field[4] * mu_e0, 0.0)]
        sides = around_x(soft_1) + around_z(soft_1, OUTSIDE) + [soft_e0]
        faces = [0.125 * (soft_1 + side) for side in sides]
        wy_e0 = pull[1, :, e0, :] * mu_e0
        own_1 = [mu_1] + lam_1
        own_e0 = [mu_e0] + lam_e0
        for c in range(3):
            sides = around_x(lam_1[c]) + around_z(lam_1[c], 0.0) + [lam_e0[c]]
            lacked = sum(faces[j] * sides[j] for j in range(5))
            if c == 1:
                lacked += wy_e0 if s == 0 else -wy_e0
            first_1.append(inverse_1 * (field[Y_KNOWN + 1 + c] + c2 * lacked))

        scale_e0 = mu_scale[:, e0, :]
        wy = ordered(pull[1, :, e1, :], wy_1)
        faces, pulls = coefficients_of(
            soft_e0, inverse_e0, soft_e1, soft_1, pull[0, :, e0, :], wy, pull[2, :, e0, :]
        )
        moved = moved_of(faces, pulls, scale_e0, own_e0, [mu_e1] + lam_e1, own_1)
        first_e0 = [(1.0 + c1) * own_e0[f] + c2 * moved[f] for f in range(4)]

        outward_face = g[3 if s == 0 else 2, :, e1, :]
        first_e1 = [state1[0, :, e1, :]]
        for c in range(3):
            first_e1.append(state1[1 + c, :, e1, :] + c2 * outward_face * lam_e0[c])

        moved = moved_of(faces, pulls, scale_e0, first_e0, first_e1, first_1)
        for f in range(4):
            second = first_e0[f] + (d1 - d2) * (first_e0[f] - own_e0[f]) + d2 * moved[f]
            sent[f * nx : (f + 1) * nx, :] = second[HALO : HALO + nx, :]
            x_low[4 * s + f : 4 * s + f + 1, :] = second[HALO : HALO + 1, :]
            x_high[4 * s + f : 4 * s + f + 1, :] = second[HALO + nx - 1 : HALO + nx, :]
            firsts[s, f] = first_e0[f]
            outer[s, f] = first_1[f]
        for j in range(6):
            coefficients[s, j] = faces[j]
            coefficients[s, 6 + j] = pulls[j]
        for c in range(3):
            coefficients[s, 12 + c] = lam_e0[c]
            seconds[s, c] = first_e1[1 + c]
    deal(sent_pal, sent_other, sent_low, sent_high)
    sent_near[...] = jnp.where(even("gx"), x_high[...], x_low[...])


def sweep(first, last, state, g, k, mu_scale, rows, advance, finish=None):
    _, ny, nz = mu_scale.shape
    lane = lax.broadcasted_iota(jnp.int32, (ny, nz), 1)
    if rows is None:

        def rows(s, f, at):
            return 0.0

    def plane(at):
        def around(f):
            own = state[f, at]
            return own, [
                state[f, at + 1],
                state[f, at - 1],
                row_up(own, rows(1, f, at)),
                row_down(own, rows(0, f, at)),
                pltpu.roll(own, nz - 1, 1),
                pltpu.roll(own, 1, 1),
            ]

        mu, mu_sides = around(0)
        ends = [
            jnp.where(lane == nz - 1, 0.0, mu_sides[4]),
            jnp.where(lane == 0, 0.0, mu_sides[5]),
        ]
        results = [advance(at, 0, mu, mu_scale[at] * sum(mu_sides[:4] + ends))]
        faces = [g[j, at] for j in range(6)]
        for c in range(3):
            lam, lam_sides = around(1 + c)
            moved = sum(faces[j] * lam_sides[j] for j in range(6))
            moved += k[2 * c, at] * mu_sides[2 * c] + k[2 * c + 1, at] * mu_sides[2 * c + 1]
            results.append(advance(at, 1 + c, lam, moved))
        if finish is not None:
            finish(at - HALO, results)

    by_pairs(first, last, plane)


def wait_kernel(
    work, less, grads, y_pal, y_other,
    mu_scale, coefficients, firsts, seconds, outer, g_in, k_in, state0_in, state1_in,
    out_mu, out_lam, edges, g, k, state0, state1,
    state2, states,
):
    _, nx, ny, _ = grads.shape
    planes = nx + 2 * HALO
    _, (d1, d2), (c1, c2) = weights()
    held = slice(HALO - 2, HALO + nx + 2)
    for s in range(2):
        e0, e1 = edge_row(s, ny, 0), edge_row(s, ny, 1)
        for j in range(6):
            g[j, held, e0, :] = coefficients[s, j, held, :]
            k[j, held, e0, :] = coefficients[s, 6 + j, held, :]
        for c in range(3):
            state0[1 + c, held, e0, :] = coefficients[s, 12 + c, held, :]
            state1[1 + c, held, e1, :] = seconds[s, c, held, :]
        for f in range(4):
            state1[f, held, e0, :] = firsts[s, f, held, :]

    def rows(s, f, at):
        return outer[s, f, pl.ds(at, 1), :]

    def advance_2(at, f, own, moved):
        state2[f, at] = own + (d1 - d2) * (own - state0[f, at]) + d2 * moved

    sweep(HALO - 1, HALO + nx + 1, state1, g, k, mu_scale, rows, advance_2)
    nothing = jnp.zeros((1, state2.shape[3]), F32)
    at = jnp.where(even("gx"), HALO + nx, HALO - 1)
    for s in range(2):
        e0 = edge_row(s, ny, 0)
        for f in range(4):
            state2[f, at, e0 : e0 + 1, :] = nothing

    def advance_3(at, f, own, moved):
        return own + c1 * (own - state1[f, at]) + c2 * (state0[f, at] - own + moved)

    def finish(i, results):
        out_mu[i] = results[0]
        along = grads[3, i] * sum(grads[c, i] * results[1 + c] for c in range(3))
        for c in range(3):
            out_lam[c, i] = results[1 + c] - along * grads[c, i]
            states[c, i] = results[1 + c]

    sweep(HALO, HALO + nx, state2, g, k, mu_scale, None, advance_3, finish)

    for s in range(2):
        y_in = received_y(y_pal, y_other, s)
        e0, e1 = edge_row(s, ny, 0), edge_row(s, ny, 1)
        own = less[HALO : HALO + nx, e0, :]
        inward, outward = less[HALO : HALO + nx, e1, :], y_in(0, nx) - 1.0
        grad = [
            0.5 * (less[HALO + 1 : HALO + nx + 1, e0, :] - less[HALO - 1 : HALO + nx - 1, e0, :]),
            0.5 * (inward - outward if s == 0 else outward - inward),
            0.5 * (lane_up(own, -1.0) - lane_down(own, -1.0)),
        ]
        for c in range(3):
            edges[s, c] = grad[c]
            edges[s, 4 + c] = states[c, :, e0, :]
        edges[s, 3] = reach_of(grad, work[0, 0])


def last_kernel(
    mu_scale, coefficients, edges, y_pal, y_other, x_near, mu_in, lam_in,
    out_mu, out_lam, mu, lam,
    sems,
):
    nx, ny, nz = mu.shape
    inner = slice(HALO, HALO + nx)
    _, _, (_, c2) = weights()
    for s in range(2):
        y_in = received_y(y_pal, y_other, s)
        e0 = edge_row(s, ny, 0)
        outward = 3 if s == 0 else 2

        def got(f):
            return y_in(f * nx, nx)

        ends_x = []
        for side, at, way in ((0, HALO, 1), (1, HALO + nx - 1, 0)):
            got_x = jnp.where(even("gx") == (side == 1), x_near[4 * s : 4 * s + 4, :], 0.0)
            sides_x = [got_x[f : f + 1, :] for f in range(4)]
            face = c2 * coefficients[s, way, at : at + 1, :]
            end = [c2 * mu_scale[at, e0 : e0 + 1, :] * sides_x[0]] + [face * sides_x[1 + c] for c in range(3)]
            end[1] += c2 * coefficients[s, 6 + way, at : at + 1, :] * sides_x[0]
            ends_x.append(end)
        plane = lax.broadcasted_iota(jnp.int32, (nx, nz), 0)

        def from_x(f):
            return jnp.where(plane == 0, ends_x[0][f], jnp.where(plane == nx - 1, ends_x[1][f], 0.0))

        mu[:, e0, :] = mu[:, e0, :] + c2 * mu_scale[inner, e0, :] * got(0) + from_x(0)
        face = c2 * coefficients[s, outward, inner, :]
        ends = []
        for c in range(3):
            end = edges[s, 4 + c] + face * got(1 + c) + from_x(1 + c)
            if c == 1:
                end += c2 * coefficients[s, 6 + outward, inner, :] * got(0)
            ends.append(end)
        along = edges[s, 3] * sum(edges[s, c] * ends[c] for c in range(3))
        for c in range(3):
            lam[c, :, e0, :] = ends[c] - along * edges[s, c]
    copies = [
        pltpu.make_async_copy(mu, out_mu, sems.at[0]),
        pltpu.make_async_copy(lam, out_lam, sems.at[1]),
    ]
    for copy in copies:
        copy.start()
    for copy in copies:
        copy.wait()


VMEM = pl.BlockSpec(memory_space=pltpu.VMEM)
SMEM = pl.BlockSpec(memory_space=pltpu.SMEM)
HBM = pl.BlockSpec(memory_space=pltpu.HBM)
ANY = pl.BlockSpec(memory_space=pl.ANY)
MIB = 1024 * 1024


def call(kernel, ins, outs, scratch=(), in_specs=None, out_specs=None, aliases=None, grant=24 * MIB):
    return pl.pallas_call(
        kernel,
        out_shape=[jax.ShapeDtypeStruct(shape, F32) for shape in outs],
        in_specs=in_specs or [VMEM] * len(ins),
        out_specs=out_specs or [VMEM] * len(outs),
        scratch_shapes=[pltpu.VMEM(shape, F32) if isinstance(shape, tuple) else shape for shape in scratch],
        input_output_aliases=aliases or {},
        compiler_params=pltpu.CompilerParams(vmem_limit_bytes=grant),
    )(*ins)


def trade(value, axis, first):
    pairs = [(i, i + 1) for i in range(first, lax.axis_size(axis) - 1, 2)]
    return lax.ppermute(value, axis, pairs + [(j, i) for i, j in pairs])


def body(damage, strain, seed_damage, seed_disp, brick_work):
    nx, ny, nz = damage.shape
    plane = (ny, nz)
    brick = (nx,) + plane
    bricks = (3,) + brick
    framed = (nx + 2 * HALO,) + plane
    state = (4,) + framed
    row = (nx + 2 * HALO, nz)
    fields = (damage, strain, seed_damage, seed_disp)

    y_rows = (Y_FIELDS * nx, nz)
    x_faces = [(X_SLOTS,) + plane, (LATE_SLOTS,) + plane]
    faces = [y_rows] * 2 + x_faces * 2
    pal, other, near, near_late, far, far_late = call(
        faces_kernel, fields, faces,
        [brick, bricks, brick, bricks] + faces + [pltpu.SemaphoreType.DMA((12,)), pltpu.SemaphoreType.DMA((6,))],
        in_specs=[HBM] * 4, out_specs=[HBM] * 6, grant=56 * MIB,
    )
    y_in = (trade(pal, "gy", 0), trade(other, "gy", 1))
    far, far_late = trade(far, "gx", 1), trade(far_late, "gx", 1)
    near, near_late = trade(near, "gx", 0), trade(near_late, "gx", 0)
    inner = tuple(call(
        inner_kernel, fields,
        [framed, framed, (3,) + framed, framed, (3,) + framed, (6,) + framed, (6,) + framed, state, state],
    ))
    c_rows = (2 * CORNER_ROWS + MORE_ROWS, nz)
    pal, other = call(
        corners_kernel, fields + (near, far, inner[0]), [c_rows] * 2,
        [(15,) + plane, c_rows, c_rows, (2, MORE_ROWS, nz)], in_specs=[VMEM] * 6 + [ANY],
    )
    c_in = (trade(pal, "gy", 0), trade(other, "gy", 1))
    less, soft, pull, mu_scale, raw, g, k, state0, state1, grads = call(
        sides_kernel, (brick_work, near, near_late, far, far_late) + inner,
        [part.shape for part in inner] + [(4,) + brick],
        in_specs=[SMEM] + [VMEM] * 13, aliases={5 + part: part for part in range(9)},
    )
    sent = (4 * nx, nz)
    x_sent = (8, nz)
    pal, other, near, coefficients, firsts, seconds, outer = call(
        edges_kernel, (soft, pull, mu_scale, raw, g, state0, state1) + y_in + c_in,
        [sent] * 2 + [x_sent] + [(2, 15) + row, (2, 4) + row, (2, 3) + row, (2, 4) + row],
        [(Y_FIELDS,) + row, sent, sent, x_sent, x_sent],
    )
    halo = (trade(pal, "gy", 0), trade(other, "gy", 1), trade(near, "gx", 0))
    ins = (brick_work, less, grads) + y_in + (mu_scale, coefficients, firsts, seconds, outer, g, k, state0, state1)
    mu, lam, edges, *_ = call(
        wait_kernel, ins,
        [brick, bricks, (2, 7, nx, nz), (6,) + framed, (6,) + framed, state, state],
        [state, bricks],
        in_specs=[SMEM] + [VMEM] * (len(ins) - 1),
        aliases={10: 3, 11: 4, 12: 5, 13: 6},
    )
    out_mu, out_lam, *_ = call(
        last_kernel, (mu_scale, coefficients, edges) + halo + (mu, lam),
        [brick, bricks, brick, bricks], [pltpu.SemaphoreType.DMA((2,))],
        out_specs=[HBM, HBM, VMEM, VMEM], aliases={6: 2, 7: 3},
    )
    return out_mu, out_lam


def solution(mesh):
    placed = (
        P("gx", "gy", None),
        P(None, "gx", "gy", None),
        P("gx", "gy", None),
        P(None, "gx", "gy", None),
        P("gx", "gy"),
    )
    return jax.shard_map(
        body,
        mesh=mesh,
        in_specs=placed,
        out_specs=(P("gx", "gy", None), P(None, "gx", "gy", None)),
        check_vma=False,
    )
```

```python
import functools

import jax
import jax.numpy as jnp
from jax import lax
from jax.experimental import pallas as pl
from jax.experimental.pallas import tpu as pltpu
from jax.sharding import PartitionSpec as P

RELAX_INNER = 8
RESIDUAL_STIFFNESS = 0.001
CENTER_VALUE = 1.0
HALF_WIDTH = 0.75
NORMAL_WEIGHT = 1.5
RELAX_RATE = 0.5 / RELAX_INNER
NORMAL_FLOOR = 0.05
OUTSIDE = 1.0 + RESIDUAL_STIFFNESS
F32 = jnp.float32


def weights():
    ratio = CENTER_VALUE / HALF_WIDTH
    rho = 1.0 / ratio
    found = []
    for _ in range(3):
        rho_next = 1.0 / (2.0 * ratio - rho)
        found.append((rho_next * rho, 2.0 * rho_next / HALF_WIDTH))
        rho = rho_next
    return found


def by_pairs(first, last, step):
    width = 2 if (last - first) % 2 == 0 else 1

    def turn(i, _):
        for part in range(width):
            step(first + width * i + part)
        return 0

    lax.fori_loop(0, (last - first) // width, turn, 0)


def soft_of(damage):
    return (1.0 - damage) ** 2 + RESIDUAL_STIFFNESS


def row_up(plane, beyond):
    rows = plane.shape[0]
    at = lax.broadcasted_iota(jnp.int32, plane.shape, 0)
    return jnp.where(at == rows - 1, beyond, pltpu.roll(plane, rows - 1, 0))


def row_down(plane, beyond):
    at = lax.broadcasted_iota(jnp.int32, plane.shape, 0)
    return jnp.where(at == 0, beyond, pltpu.roll(plane, 1, 0))


def lane_up(plane, beyond):
    cells = plane.shape[1]
    at = lax.broadcasted_iota(jnp.int32, plane.shape, 1)
    return jnp.where(at == cells - 1, beyond, pltpu.roll(plane, cells - 1, 1))


def lane_down(plane, beyond):
    at = lax.broadcasted_iota(jnp.int32, plane.shape, 1)
    return jnp.where(at == 0, beyond, pltpu.roll(plane, 1, 1))


def mu_inverse(ex, ey, ez):
    return 1.0 / (2.0 + (ex * ex + ey * ey + ez * ez))


def lam_inverse(center, total):
    return 1.0 / (0.5 + 0.125 * (6.0 * center + total))


HALO = 4
X_DAMAGE, X_PULL, X_MU, X_SOURCE, X_SLOTS = 0, 3, 9, 11, 17
LATE_DAMAGE, LATE_PULL, LATE_MU, LATE_SOURCE, LATE_SLOTS = 0, 1, 2, 3, 6
Y_HALO = (2, 1, 1, 1, 0, 1, 1, 1)
Y_KNOWN, Y_FIELDS = 8, 12
CORNER_ROWS = sum(Y_HALO) + 4
MORE_ROWS = 12


def edge_row(s, ny, depth):
    return depth if s == 0 else ny - 1 - depth


def known_of(s, damages, pulls, behind_pull, mus, sources, behind):
    planes = damages[0].shape[0]
    (c1, c2), _, _ = weights()
    soft = [soft_of(part) for part in damages]
    less = damages[0] - 1.0
    wx, wy, wz = (less * pull for pull in pulls)
    wy_behind = (damages[1] - 1.0) * behind_pull

    def across(value):
        return pltpu.roll(value, planes - 1, 0), pltpu.roll(value, 1, 0)

    def along(value, fill):
        return lane_up(value, fill), lane_down(value, fill)

    total = soft[0] + soft[2] + sum(across(soft[1])) + sum(along(soft[1], OUTSIDE))
    inverse = lam_inverse(soft[1], total)
    face = 0.125 * (soft[0] + soft[1])
    scale = 0.25 * mu_inverse(*pulls)
    known = [(1.0 + c1) * mus[0] + c2 * scale * (mus[1] + sum(across(mus[0])) + sum(along(mus[0], 0.0)))]
    x_up, x_down = across(wx * mus[0])
    z_up, z_down = along(wz * mus[0], 0.0)
    y_behind = wy_behind * mus[1]
    transfers = (x_up - x_down, y_behind if s == 0 else -y_behind, z_up - z_down)
    for c in range(3):
        known.append((1.0 + c1) * sources[c] + c2 * (face * (inverse * behind[c]) + transfers[c]))
    return scale, wy, known


def put_rows(s, put, damage, strain, seed_damage, seed_disp):
    ny = damage.shape[1]
    first, second, third = (edge_row(s, ny, depth) for depth in range(3))
    damages = [damage[:, row, :] for row in (first, second, third)]
    pulls = [strain[c, :, first, :] for c in range(3)]
    pulls_behind = [strain[c, :, second, :] for c in range(3)]
    mus = [
        seed_damage[:, first, :] * mu_inverse(*pulls),
        seed_damage[:, second, :] * mu_inverse(*pulls_behind),
    ]
    sources = [seed_disp[c, :, first, :] for c in range(3)]
    behind = [seed_disp[c, :, second, :] for c in range(3)]
    scale, wy, known = known_of(s, damages, pulls, pulls_behind[1], mus, sources, behind)
    for slot, value in enumerate(damages[:2] + [wy, mus[0], scale] + sources + known):
        put(slot, value)


def even(axis):
    return lax.rem(lax.axis_index(axis), 2) == 0


def faces_kernel(
    damage_in, strain_in, seed_in, sources_in, pal_out, other_out, near_out, near_late_out, far_out, far_late_out,
    damage, strain, seed_damage, seed_disp, pal, other, near, near_late, far, far_late, sems, out_sems,
):
    nx = damage.shape[0]
    edges, middle = (pl.ds(0, HALO), pl.ds(nx - HALO, HALO)), (pl.ds(HALO, nx - 2 * HALO),)
    pairs = ((damage_in, damage), (seed_in, seed_damage), (strain_in, strain), (sources_in, seed_disp))
    copies = []
    for planes in edges + middle:
        for source, target in pairs:
            at = planes if len(source.shape) == 3 else (slice(None), planes)
            copies.append(pltpu.make_async_copy(source.at[at], target.at[at], sems.at[len(copies)]))
    for copy in copies:
        copy.start()
    sent = []

    def send(source, target):
        sent.append(pltpu.make_async_copy(source, target, out_sems.at[len(sent)]))
        sent[-1].start()

    def put_planes(out, late, high):
        for depth in range(4):
            at = jnp.where(high, nx - 1 - depth, depth)
            if depth == 3:
                late[LATE_DAMAGE] = damage[at]
                continue
            out[X_DAMAGE + depth] = damage[at]
            pulls = [strain[c, at] for c in range(3)]
            mu = seed_damage[at] * mu_inverse(*pulls)
            if depth == 2:
                late[LATE_PULL] = pulls[0]
                late[LATE_MU] = mu
            else:
                out[X_MU + depth] = mu
            for c in range(3):
                if depth == 2:
                    late[LATE_SOURCE + c] = seed_disp[c, at]
                else:
                    out[X_PULL + 2 * c + depth] = pulls[c]
                    out[X_SOURCE + 2 * c + depth] = seed_disp[c, at]

    for copy in copies[:8]:
        copy.wait()
    for out, late, target, late_target, high in (
        (near, near_late, near_out, near_late_out, even("gx")),
        (far, far_late, far_out, far_late_out, ~even("gx")),
    ):
        put_planes(out, late, high)
        send(out, target)
        send(late, late_target)
    for copy in copies[8:]:
        copy.wait()
    for out, target, first in ((pal, pal_out, True), (other, other_out, False)):

        def put(slot, value):
            out[slot * nx : (slot + 1) * nx, :] = value

        for s in range(2):

            @pl.when(even("gy") == ((s == 1) == first))
            def _():
                put_rows(s, put, damage, strain, seed_damage, seed_disp)

        send(out, target)
    for copy in sent:
        copy.wait()


def received_x(near, far, side):
    from_near = even("gx") == (side == 1)

    def plane(slot, row=None):
        at = slot if row is None else (slice(slot, slot + 1), row)
        return jnp.where(from_near, near[at], far[at])

    return plane


def received_y(pal, other, side):
    from_pal = even("gy") == (side == 1)
    return lambda first, count: jnp.where(from_pal, pal[first : first + count, :], other[first : first + count, :])


def deal(pal, other, low, high):
    first = even("gy")
    low, high = low[...], high[...]
    pal[...] = jnp.where(first, high, low)
    other[...] = jnp.where(first, low, high)


def corners_kernel(
    damage, strain, seed_damage, seed_disp, near, far, _, pal, other, fields, low, high, more
):
    nx, ny, _ = damage.shape
    for s, out in enumerate((low, high)):
        first, second, third = (edge_row(s, ny, depth) for depth in range(3))
        for side in range(2):
            field = fields.at[2 * s + side]
            x_in = received_x(near, far, side)
            ours = slice(3, 8) if side == 0 else slice(0, 5)
            planes = slice(0, 5) if side == 0 else slice(nx - 5, nx)

            def put_x(slot, first, count, row):
                for far_off in range(count):
                    at = 2 - far_off if side == 0 else 5 + far_off
                    field[slot, at : at + 1, :] = x_in(first + far_off, row)

            for depth, row in enumerate((first, second, third)):
                field[depth, ours, :] = damage[planes, row, :]
                put_x(depth, X_DAMAGE, 3, row)
            for depth, row in enumerate((first, second)):
                pulls = [strain[c, planes, row, :] for c in range(3)]
                for c in range(3):
                    if depth == 0:
                        field[3 + c, ours, :] = pulls[c]
                        put_x(3 + c, X_PULL + 2 * c, 2, row)
                    field[9 + 3 * depth + c, ours, :] = seed_disp[c, planes, row, :]
                    put_x(9 + 3 * depth + c, X_SOURCE + 2 * c, 2, row)
                if depth == 1:
                    field[6, ours, :] = pulls[1]
                    put_x(6, X_PULL + 2, 2, row)
                field[7 + depth, ours, :] = seed_damage[planes, row, :] * mu_inverse(*pulls)
                put_x(7 + depth, X_MU, 2, row)
            got = [field[slot] for slot in range(15)]
            scale, wy, known = known_of(s, got[:3], got[3:6], got[6], got[7:9], got[9:12], got[12:15])
            row = side * CORNER_ROWS
            for slot, value in enumerate(got[:2] + [wy, got[7], scale] + got[9:12]):
                count = Y_HALO[slot]
                behind = 2 - count if side == 0 else 5 + count
                more[s, side, slot : slot + 1, :] = value[behind : behind + 1, :]
                if count == 0:
                    continue
                start = 3 - count if side == 0 else 5
                out[row : row + count, :] = value[start : start + count, :]
                row += count
            for slot, value in enumerate(known):
                edge, behind = (3, 2) if side == 0 else (4, 5)
                out[row : row + 1, :] = value[edge : edge + 1, :]
                slot += Y_KNOWN
                more[s, side, slot : slot + 1, :] = value[behind : behind + 1, :]
                row += 1
        out[2 * CORNER_ROWS :, :] = jnp.where(even("gx"), more[s, 0], more[s, 1])
    deal(pal, other, low, high)


def in_grid():
    here = lax.axis_index("gx")
    return here > 0, here < lax.axis_size("gx") - 1


def prepare(first, last, soft, pull, raw, g, k, state0):
    planes, ny, nz = soft.shape
    inside = in_grid()
    lane = lax.broadcasted_iota(jnp.int32, (ny, nz), 1)
    row = lax.broadcasted_iota(jnp.int32, (ny, nz), 0)
    inner = (row > 0) & (row < ny - 1)

    def step(at):
        center = soft[at]
        sides = [
            soft[at + 1],
            soft[at - 1],
            pltpu.roll(center, ny - 1, 0),
            pltpu.roll(center, 1, 0),
            lane_up(center, OUTSIDE),
            lane_down(center, OUTSIDE),
        ]
        outside = ((at < HALO) & ~inside[0]) | ((at >= planes - HALO) & ~inside[1])
        inverse = jnp.where(inner & ~outside, lam_inverse(center, sum(sides)), 0.0)
        eighth = 0.125 * inverse
        for j in range(6):
            face = eighth * (center + sides[j])
            if j == 4:
                face = jnp.where(lane == nz - 1, 0.0, face)
            if j == 5:
                face = jnp.where(lane == 0, 0.0, face)
            g[j, at] = face
        k[0, at] = inverse * pull[0, at + 1]
        k[1, at] = -inverse * pull[0, at - 1]
        k[2, at] = inverse * pltpu.roll(pull[1, at], ny - 1, 0)
        k[3, at] = -inverse * pltpu.roll(pull[1, at], 1, 0)
        k[4, at] = inverse * lane_up(pull[2, at], 0.0)
        k[5, at] = -inverse * lane_down(pull[2, at], 0.0)
        for c in range(3):
            state0[1 + c, at] = inverse * raw[c, at]

    by_pairs(first, last, step)


def reach_of(grad, count):
    square = sum(part * part for part in grad)
    scale = 1.0 / jnp.maximum(square, NORMAL_FLOOR)
    power = 1.0 - RELAX_RATE * (1.0 + NORMAL_WEIGHT * square * scale)
    series = 1.0 + power
    for _ in range(2):
        power = power * power
        series = series * (1.0 + power)
    power = power * power
    repeats = jnp.ones_like(power)
    for level in range(1, 4):
        repeats = jnp.where(count > level, 1.0 + power * repeats, repeats)
    return (RELAX_RATE * NORMAL_WEIGHT * scale) * (series * repeats)


def slopes(first, last, count, less, grads):
    ny = less.shape[1]

    def step(at):
        own = less[at]
        grad = [
            0.5 * (less[at + 1] - less[at - 1]),
            0.5 * (pltpu.roll(own, ny - 1, 0) - pltpu.roll(own, 1, 0)),
            0.5 * (lane_up(own, -1.0) - lane_down(own, -1.0)),
        ]
        for c in range(3):
            grads[c, at - HALO] = grad[c]
        grads[3, at - HALO] = reach_of(grad, count)

    by_pairs(first, last, step)


def first_sweep(ranges, state0, state1, g, k, mu_scale):
    (c1, c2), _, _ = weights()

    def advance(at, f, own, moved):
        state1[f, at] = (1.0 + c1) * own + c2 * moved

    for first, last in ranges:
        sweep(first, last, state0, g, k, mu_scale, None, advance)


def inner_kernel(
    damage, strain, seed_damage, seed_disp, less, soft, pull, mu_scale, raw, g, k, state0, state1
):
    nx = damage.shape[0]

    def fill(i, _):
        at = HALO + i
        own = damage[i]
        sx, sy, sz = strain[0, i], strain[1, i], strain[2, i]
        soft[at] = soft_of(own)
        own = own - 1.0
        less[at] = own
        pull[0, at] = own * sx
        pull[1, at] = own * sy
        pull[2, at] = own * sz
        mu_inv = mu_inverse(sx, sy, sz)
        mu_scale[at] = 0.25 * mu_inv
        state0[0, at] = mu_inv * seed_damage[i]
        for c in range(3):
            raw[c, at] = seed_disp[c, i]
        return 0

    lax.fori_loop(0, nx, fill, 0)
    low, high = HALO, HALO + nx
    prepare(low + 1, high - 1, soft, pull, raw, g, k, state0)
    first_sweep([(low + 2, high - 2)], state0, state1, g, k, mu_scale)


def sides_kernel(
    work, near, near_late, far, far_late,
    less_in, soft_in, pull_in, scale_in, raw_in, g_in, k_in, state0_in, state1_in,
    less, soft, pull, mu_scale, raw, g, k, state0, state1, grads,
):
    nx = soft.shape[0] - 2 * HALO
    low, high = HALO, HALO + nx
    inside = in_grid()
    for s in range(2):
        x_in, late = received_x(near, far, s), received_x(near_late, far_late, s)
        for depth in range(4):
            at = low - 1 - depth if s == 0 else high + depth
            own = late(LATE_DAMAGE) if depth == 3 else x_in(X_DAMAGE + depth)
            soft[at] = soft_of(own)
            if depth == 3:
                continue
            own = own - 1.0
            if depth == 0:
                less[at] = own
            if depth == 2:
                pull[0, at] = own * late(LATE_PULL)
                state0[0, at] = late(LATE_MU)
            else:
                pulls = [x_in(X_PULL + 2 * c + depth) for c in range(3)]
                mu_scale[at] = jnp.where(inside[s], 0.25 * mu_inverse(*pulls), 0.0)
                state0[0, at] = x_in(X_MU + depth)
            for c in range(3):
                if depth == 2:
                    raw[c, at] = late(LATE_SOURCE + c)
                else:
                    pull[c, at] = own * pulls[c]
                    raw[c, at] = x_in(X_SOURCE + 2 * c + depth)

    for first, last in ((low - 3, low + 1), (high - 1, high + 3)):
        prepare(first, last, soft, pull, raw, g, k, state0)
    slopes(low, high, work[0, 0], less, grads)
    first_sweep([(low - 2, low + 2), (high - 2, high + 2)], state0, state1, g, k, mu_scale)


def edges_kernel(
    soft, pull, mu_scale, raw, g, state0, state1, y_pal, y_other, c_pal, c_other,
    sent_pal, sent_other, sent_near, coefficients, firsts, seconds, outer,
    fields, sent_low, sent_high, x_low, x_high,
):
    planes, ny, nz = soft.shape
    nx = planes - 2 * HALO
    (c1, c2), (d1, d2), _ = weights()
    lane = lax.broadcasted_iota(jnp.int32, (planes, nz), 1)
    plane = lax.broadcasted_iota(jnp.int32, (planes, nz), 0)
    here, there = lax.axis_index("gx"), lax.axis_index("gy")
    in_x = ((plane >= HALO) | (here > 0)) & ((plane < HALO + nx) | (here < lax.axis_size("gx") - 1))
    in_y = (there > 0, there < lax.axis_size("gy") - 1)

    def around_x(value):
        return [pltpu.roll(value, planes - 1, 0), pltpu.roll(value, 1, 0)]

    def around_z(value, fill):
        return [lane_up(value, fill), lane_down(value, fill)]

    for s, sent in enumerate((sent_low, sent_high)):
        field = fields.at[s]
        y_in, c_in = received_y(y_pal, y_other, s), received_y(c_pal, c_other, s)
        e0, e1 = edge_row(s, ny, 0), edge_row(s, ny, 1)

        def ordered(inward, outward):
            return [inward, outward] if s == 0 else [outward, inward]

        row = 0
        for f in range(Y_FIELDS):
            field[f, HALO : HALO + nx, :] = y_in(f * nx, nx)
            count, shift = (Y_HALO[f], 0) if f < Y_KNOWN else (1, 1)
            behind = HALO - count - 1 + shift
            for at in (behind, planes - 1 - behind):
                field[f, at : at + 1, :] = c_in(2 * CORNER_ROWS + f, 1)
            if count == 0:
                continue
            field[f, HALO - count + shift : HALO + shift, :] = c_in(row, count)
            high = HALO + nx - shift
            field[f, high : high + count, :] = c_in(CORNER_ROWS + row, count)
            row += count

        soft_1, soft_2 = soft_of(field[0]), soft_of(field[1])
        soft_e0, soft_e1 = soft[:, e0, :], soft[:, e1, :]

        def total(center, inward, outward):
            return sum(around_x(center) + [inward, outward] + around_z(center, OUTSIDE))

        inverse_1 = lam_inverse(soft_1, total(soft_1, soft_e0, soft_2))
        inverse_1 = jnp.where(in_x & in_y[s], inverse_1, 0.0)
        lam_1 = [inverse_1 * field[5 + c] for c in range(3)]
        inverse_e0 = jnp.where(in_x, lam_inverse(soft_e0, total(soft_e0, soft_e1, soft_1)), 0.0)
        lam_e0 = [inverse_e0 * raw[c, :, e0, :] for c in range(3)]
        mu_1, wy_1 = field[3], field[2]
        mu_e0, mu_e1 = state0[0, :, e0, :], state0[0, :, e1, :]
        lam_e1 = [state0[1 + c, :, e1, :] for c in range(3)]

        def coefficients_of(center, inverse, inward, outward, wx, wy, wz):
            sides = around_x(center) + ordered(inward, outward) + around_z(center, OUTSIDE)
            eighth = 0.125 * inverse
            faces = [eighth * (center + side) for side in sides]
            faces[4] = jnp.where(lane == nz - 1, 0.0, faces[4])
            faces[5] = jnp.where(lane == 0, 0.0, faces[5])
            pulls = around_x(wx) + wy + around_z(wz, 0.0)
            return faces, [inverse * w if j % 2 == 0 else -inverse * w for j, w in enumerate(pulls)]

        def moved_of(faces, pulls, scale, own, inward, outward):
            sides = [
                around_x(own[f]) + ordered(inward[f], outward[f]) + around_z(own[f], 0.0) for f in range(4)
            ]
            moved = [scale * sum(sides[0])]
            for c in range(3):
                part = sum(faces[j] * sides[1 + c][j] for j in range(6))
                moved.append(part + pulls[2 * c] * sides[0][2 * c] + pulls[2 * c + 1] * sides[0][2 * c + 1])
            return moved

        first_1 = [jnp.where(in_x, field[Y_KNOWN] + c2 * field[4] * mu_e0, 0.0)]
        sides = around_x(soft_1) + around_z(soft_1, OUTSIDE) + [soft_e0]
        faces = [0.125 * (soft_1 + side) for side in sides]
        wy_e0 = pull[1, :, e0, :] * mu_e0
        own_1 = [mu_1] + lam_1
        own_e0 = [mu_e0] + lam_e0
        for c in range(3):
            sides = around_x(lam_1[c]) + around_z(lam_1[c], 0.0) + [lam_e0[c]]
            lacked = sum(faces[j] * sides[j] for j in range(5))
            if c == 1:
                lacked += wy_e0 if s == 0 else -wy_e0
            first_1.append(inverse_1 * (field[Y_KNOWN + 1 + c] + c2 * lacked))

        scale_e0 = mu_scale[:, e0, :]
        wy = ordered(pull[1, :, e1, :], wy_1)
        faces, pulls = coefficients_of(
            soft_e0, inverse_e0, soft_e1, soft_1, pull[0, :, e0, :], wy, pull[2, :, e0, :]
        )
        moved = moved_of(faces, pulls, scale_e0, own_e0, [mu_e1] + lam_e1, own_1)
        first_e0 = [(1.0 + c1) * own_e0[f] + c2 * moved[f] for f in range(4)]

        outward_face = g[3 if s == 0 else 2, :, e1, :]
        first_e1 = [state1[0, :, e1, :]]
        for c in range(3):
            first_e1.append(state1[1 + c, :, e1, :] + c2 * outward_face * lam_e0[c])

        moved = moved_of(faces, pulls, scale_e0, first_e0, first_e1, first_1)
        for f in range(4):
            second = first_e0[f] + (d1 - d2) * (first_e0[f] - own_e0[f]) + d2 * moved[f]
            sent[f * nx : (f + 1) * nx, :] = second[HALO : HALO + nx, :]
            x_low[4 * s + f : 4 * s + f + 1, :] = second[HALO : HALO + 1, :]
            x_high[4 * s + f : 4 * s + f + 1, :] = second[HALO + nx - 1 : HALO + nx, :]
            firsts[s, f] = first_e0[f]
            outer[s, f] = first_1[f]
        for j in range(6):
            coefficients[s, j] = faces[j]
            coefficients[s, 6 + j] = pulls[j]
        for c in range(3):
            coefficients[s, 12 + c] = lam_e0[c]
            seconds[s, c] = first_e1[1 + c]
    deal(sent_pal, sent_other, sent_low, sent_high)
    sent_near[...] = jnp.where(even("gx"), x_high[...], x_low[...])


def sweep(first, last, state, g, k, mu_scale, rows, advance, finish=None):
    _, ny, nz = mu_scale.shape
    lane = lax.broadcasted_iota(jnp.int32, (ny, nz), 1)
    if rows is None:

        def rows(s, f, at):
            return 0.0

    def plane(at):
        def around(f):
            own = state[f, at]
            return own, [
                state[f, at + 1],
                state[f, at - 1],
                row_up(own, rows(1, f, at)),
                row_down(own, rows(0, f, at)),
                pltpu.roll(own, nz - 1, 1),
                pltpu.roll(own, 1, 1),
            ]

        mu, mu_sides = around(0)
        ends = [
            jnp.where(lane == nz - 1, 0.0, mu_sides[4]),
            jnp.where(lane == 0, 0.0, mu_sides[5]),
        ]
        results = [advance(at, 0, mu, mu_scale[at] * sum(mu_sides[:4] + ends))]
        faces = [g[j, at] for j in range(6)]
        for c in range(3):
            lam, lam_sides = around(1 + c)
            moved = sum(faces[j] * lam_sides[j] for j in range(6))
            moved += k[2 * c, at] * mu_sides[2 * c] + k[2 * c + 1, at] * mu_sides[2 * c + 1]
            results.append(advance(at, 1 + c, lam, moved))
        if finish is not None:
            finish(at - HALO, results)

    by_pairs(first, last, plane)


def wait_kernel(
    work, less, grads, y_pal, y_other,
    mu_scale, coefficients, firsts, seconds, outer, g_in, k_in, state0_in, state1_in,
    out_mu, out_lam, edges, g, k, state0, state1,
    state2, states,
):
    _, nx, ny, _ = grads.shape
    planes = nx + 2 * HALO
    _, (d1, d2), (c1, c2) = weights()
    held = slice(HALO - 2, HALO + nx + 2)
    for s in range(2):
        e0, e1 = edge_row(s, ny, 0), edge_row(s, ny, 1)
        for j in range(6):
            g[j, held, e0, :] = coefficients[s, j, held, :]
            k[j, held, e0, :] = coefficients[s, 6 + j, held, :]
        for c in range(3):
            state0[1 + c, held, e0, :] = coefficients[s, 12 + c, held, :]
            state1[1 + c, held, e1, :] = seconds[s, c, held, :]
        for f in range(4):
            state1[f, held, e0, :] = firsts[s, f, held, :]

    def rows(s, f, at):
        return outer[s, f, pl.ds(at, 1), :]

    def advance_2(at, f, own, moved):
        state2[f, at] = own + (d1 - d2) * (own - state0[f, at]) + d2 * moved

    sweep(HALO - 1, HALO + nx + 1, state1, g, k, mu_scale, rows, advance_2)
    nothing = jnp.zeros((1, state2.shape[3]), F32)
    at = jnp.where(even("gx"), HALO + nx, HALO - 1)
    for s in range(2):
        e0 = edge_row(s, ny, 0)
        for f in range(4):
            state2[f, at, e0 : e0 + 1, :] = nothing

    def advance_3(at, f, own, moved):
        return own + c1 * (own - state1[f, at]) + c2 * (state0[f, at] - own + moved)

    def finish(i, results):
        out_mu[i] = results[0]
        along = grads[3, i] * sum(grads[c, i] * results[1 + c] for c in range(3))
        for c in range(3):
            out_lam[c, i] = results[1 + c] - along * grads[c, i]
            states[c, i] = results[1 + c]

    sweep(HALO, HALO + nx, state2, g, k, mu_scale, None, advance_3, finish)

    for s in range(2):
        y_in = received_y(y_pal, y_other, s)
        e0, e1 = edge_row(s, ny, 0), edge_row(s, ny, 1)
        own = less[HALO : HALO + nx, e0, :]
        inward, outward = less[HALO : HALO + nx, e1, :], y_in(0, nx) - 1.0
        grad = [
            0.5 * (less[HALO + 1 : HALO + nx + 1, e0, :] - less[HALO - 1 : HALO + nx - 1, e0, :]),
            0.5 * (inward - outward if s == 0 else outward - inward),
            0.5 * (lane_up(own, -1.0) - lane_down(own, -1.0)),
        ]
        for c in range(3):
            edges[s, c] = grad[c]
            edges[s, 4 + c] = states[c, :, e0, :]
        edges[s, 3] = reach_of(grad, work[0, 0])


def last_kernel(
    mu_scale, coefficients, edges, y_pal, y_other, x_near, mu_in, lam_in,
    out_mu, out_lam, mu, lam,
    sems,
):
    nx, ny, nz = mu.shape
    inner = slice(HALO, HALO + nx)
    _, _, (_, c2) = weights()
    for s in range(2):
        y_in = received_y(y_pal, y_other, s)
        e0 = edge_row(s, ny, 0)
        outward = 3 if s == 0 else 2

        def got(f):
            return y_in(f * nx, nx)

        ends_x = []
        for side, at, way in ((0, HALO, 1), (1, HALO + nx - 1, 0)):
            got_x = jnp.where(even("gx") == (side == 1), x_near[4 * s : 4 * s + 4, :], 0.0)
            sides_x = [got_x[f : f + 1, :] for f in range(4)]
            face = c2 * coefficients[s, way, at : at + 1, :]
            end = [c2 * mu_scale[at, e0 : e0 + 1, :] * sides_x[0]] + [face * sides_x[1 + c] for c in range(3)]
            end[1] += c2 * coefficients[s, 6 + way, at : at + 1, :] * sides_x[0]
            ends_x.append(end)
        plane = lax.broadcasted_iota(jnp.int32, (nx, nz), 0)

        def from_x(f):
            return jnp.where(plane == 0, ends_x[0][f], jnp.where(plane == nx - 1, ends_x[1][f], 0.0))

        mu[:, e0, :] = mu[:, e0, :] + c2 * mu_scale[inner, e0, :] * got(0) + from_x(0)
        face = c2 * coefficients[s, outward, inner, :]
        ends = []
        for c in range(3):
            end = edges[s, 4 + c] + face * got(1 + c) + from_x(1 + c)
            if c == 1:
                end += c2 * coefficients[s, 6 + outward, inner, :] * got(0)
            ends.append(end)
        along = edges[s, 3] * sum(edges[s, c] * ends[c] for c in range(3))
        for c in range(3):
            lam[c, :, e0, :] = ends[c] - along * edges[s, c]
    copies = [
        pltpu.make_async_copy(mu, out_mu, sems.at[0]),
        pltpu.make_async_copy(lam, out_lam, sems.at[1]),
    ]
    for copy in copies:
        copy.start()
    for copy in copies:
        copy.wait()


VMEM = pl.BlockSpec(memory_space=pltpu.VMEM)
SMEM = pl.BlockSpec(memory_space=pltpu.SMEM)
HBM = pl.BlockSpec(memory_space=pltpu.HBM)
ANY = pl.BlockSpec(memory_space=pl.ANY)
MIB = 1024 * 1024


def call(kernel, ins, outs, scratch=(), in_specs=None, out_specs=None, aliases=None, grant=24 * MIB):
    return pl.pallas_call(
        kernel,
        out_shape=[jax.ShapeDtypeStruct(shape, F32) for shape in outs],
        in_specs=in_specs or [VMEM] * len(ins),
        out_specs=out_specs or [VMEM] * len(outs),
        scratch_shapes=[pltpu.VMEM(shape, F32) if isinstance(shape, tuple) else shape for shape in scratch],
        input_output_aliases=aliases or {},
        compiler_params=pltpu.CompilerParams(vmem_limit_bytes=grant),
    )(*ins)


def trade(value, axis, first):
    pairs = [(i, i + 1) for i in range(first, lax.axis_size(axis) - 1, 2)]
    return lax.ppermute(value, axis, pairs + [(j, i) for i, j in pairs])


def body(damage, strain, seed_damage, seed_disp, brick_work):
    nx, ny, nz = damage.shape
    plane = (ny, nz)
    brick = (nx,) + plane
    bricks = (3,) + brick
    framed = (nx + 2 * HALO,) + plane
    state = (4,) + framed
    row = (nx + 2 * HALO, nz)
    fields = (damage, strain, seed_damage, seed_disp)

    y_rows = (Y_FIELDS * nx, nz)
    x_faces = [(X_SLOTS,) + plane, (LATE_SLOTS,) + plane]
    faces = [y_rows] * 2 + x_faces * 2
    pal, other, near, near_late, far, far_late = call(
        faces_kernel, fields, faces,
        [brick, bricks, brick, bricks] + faces + [pltpu.SemaphoreType.DMA((12,)), pltpu.SemaphoreType.DMA((6,))],
        in_specs=[HBM] * 4, out_specs=[HBM] * 6, grant=56 * MIB,
    )
    y_in = (trade(pal, "gy", 0), trade(other, "gy", 1))
    far, far_late = trade(far, "gx", 1), trade(far_late, "gx", 1)
    near, near_late = trade(near, "gx", 0), trade(near_late, "gx", 0)
    inner = tuple(call(
        inner_kernel, fields,
        [framed, framed, (3,) + framed, framed, (3,) + framed, (6,) + framed, (6,) + framed, state, state],
    ))
    c_rows = (2 * CORNER_ROWS + MORE_ROWS, nz)
    pal, other = call(
        corners_kernel, fields + (near, far, inner[0]), [c_rows] * 2,
        [(4, 15) + plane, c_rows, c_rows, (2, 2, MORE_ROWS, nz)], in_specs=[VMEM] * 6 + [ANY],
    )
    c_in = (trade(pal, "gy", 0), trade(other, "gy", 1))
    less, soft, pull, mu_scale, raw, g, k, state0, state1, grads = call(
        sides_kernel, (brick_work, near, near_late, far, far_late) + inner,
        [part.shape for part in inner] + [(4,) + brick],
        in_specs=[SMEM] + [VMEM] * 13, aliases={5 + part: part for part in range(9)},
    )
    sent = (4 * nx, nz)
    x_sent = (8, nz)
    pal, other, near, coefficients, firsts, seconds, outer = call(
        edges_kernel, (soft, pull, mu_scale, raw, g, state0, state1) + y_in + c_in,
        [sent] * 2 + [x_sent] + [(2, 15) + row, (2, 4) + row, (2, 3) + row, (2, 4) + row],
        [(2, Y_FIELDS) + row, sent, sent, x_sent, x_sent],
    )
    halo = (trade(pal, "gy", 0), trade(other, "gy", 1), trade(near, "gx", 0))
    ins = (brick_work, less, grads) + y_in + (mu_scale, coefficients, firsts, seconds, outer, g, k, state0, state1)
    mu, lam, edges, *_ = call(
        wait_kernel, ins,
        [brick, bricks, (2, 7, nx, nz), (6,) + framed, (6,) + framed, state, state],
        [state, bricks],
        in_specs=[SMEM] + [VMEM] * (len(ins) - 1),
        aliases={10: 3, 11: 4, 12: 5, 13: 6},
    )
    out_mu, out_lam, *_ = call(
        last_kernel, (mu_scale, coefficients, edges) + halo + (mu, lam),
        [brick, bricks, brick, bricks], [pltpu.SemaphoreType.DMA((2,))],
        out_specs=[HBM, HBM, VMEM, VMEM], aliases={6: 2, 7: 3},
    )
    return out_mu, out_lam


def solution(mesh):
    placed = (
        P("gx", "gy", None),
        P(None, "gx", "gy", None),
        P("gx", "gy", None),
        P(None, "gx", "gy", None),
        P("gx", "gy"),
    )
    return jax.shard_map(
        body,
        mesh=mesh,
        in_specs=placed,
        out_specs=(P("gx", "gy", None), P(None, "gx", "gy", None)),
        check_vma=False,
    )
```
